32 devices in a mesh: dp: 8 (over z, x), fsdp: 4 (over y, core).
Axes of the slice: x: 2, y: 2, z: 4, core: 2. Of those that a mesh axis runs over, the one named last changes fastest.
Arguments:
- chars: int32 [2, 1024, 6], P(None, ('dp', 'fsdp')), may hold values from 0 to 274
- resets: int32 [2, 1024, 6], P(None, ('dp', 'fsdp')), may hold values 0 or 1
- targets: int32 [2, 1024, 6], P(None, ('dp', 'fsdp')), may hold values from 0 to 274
- embed: bfloat16 [275, 100], replicated, may hold values from -6 to 6
- w_in: bfloat16 [100, 8192], P(None, ('dp', 'fsdp')), may hold values from -0.625 to 0.625
- bias_in: bfloat16 [8192], P(('dp', 'fsdp')), may hold values from -3 to 3
- w_rec: bfloat16 [2048, 8192], P(('dp', 'fsdp')), may hold values from -0.125 to 0.125
- w_dec: bfloat16 [2048, 275], P(('dp', 'fsdp')), may hold values from -0.59765625 to 0.59765625
- bias_dec: bfloat16 [275], replicated, may hold values from -6 to 6
Outputs:
- loss: float32 [], replicated
- hidden: bfloat16 [2, 1024, 6, 2048], P(None, ('dp', 'fsdp'))
- grad_embed: float32 [275, 100], replicated
- grad_w_in: float32 [100, 8192], P(None, ('dp', 'fsdp'))
- grad_bias_in: float32 [8192], P(('dp', 'fsdp'))
- grad_w_rec: float32 [2048, 8192], P(('dp', 'fsdp'))
- grad_w_dec: float32 [2048, 275], P(('dp', 'fsdp'))
- grad_bias_dec: float32 [275], replicated
The draws below stay inside these ranges and needn't reach their ends.
All inputs are finite; a program needn't handle non-finite values. No bound on the sum of `resets` on one device may be relied on, other than what follows from the above.
Results may differ from the reference program's by a relative error of at most 0.0027.
Values may be sent and summed in bfloat16 or wider, within the bound.
A program may use at most 192 MiB of HBM per device.

```python
import math
import jax
import jax.numpy as jnp
import numpy as np
from jax import lax

HID = 2048
EMB = 100
VOCAB = 275
SEQ = 6
MICRO = 2
GATES = 8192
ROWS = 1024


def with_ends(result, key, smallest, high):
    index_at = [jax.random.randint(jax.random.fold_in(key, axis), (), 0, length) for axis, length in enumerate(result.shape)]
    longest = result.shape.index(max(result.shape))
    neighbour = index_at[:longest] + [(index_at[longest] + 1) % result.shape[longest]] + index_at[longest + 1:]
    return result.at[tuple(index_at)].set(smallest).at[tuple(neighbour)].set(high)


def steps_of(own_key, shape, cuts, low, high):
    gain, own = 1.0, jax.random.fold_in(own_key, 6)
    for dim, shards_of in cuts:
        draws = jnp.exp(jax.random.uniform(jax.random.fold_in(own, dim), (shards_of,), jnp.float32, low / len(cuts), high / len(cuts)))
        gain = gain * jnp.repeat(draws, shape[dim] // shards_of).reshape([-1 if axis == dim else 1 for axis in range(len(shape))])
    return gain


def cumulative_ranks(amount, skew):
    weights = [(1 << 20) // math.isqrt(standing ** skew) + 1 for standing in range(1, amount + 1)]
    scale = 1 + sum(weights) // (1 << 30)
    return np.cumsum(np.array([max(1, weight // scale) for weight in weights]))


def ranked(stream_key, shape, number_of, skew):
    grid = cumulative_ranks(number_of, skew)
    pick = jax.random.randint(jax.random.fold_in(stream_key, 1), shape, 0, int(grid[number_of - 1]))
    grade = jnp.searchsorted(jnp.asarray(grid, jnp.int32), pick, side="right")
    return jax.random.permutation(jax.random.fold_in(stream_key, 2), number_of)[grade].astype(jnp.int32)


def normal_values(stream_key, dims, scale, most, cuts=(), kind=jnp.bfloat16):
    result = jax.random.normal(stream_key, dims, jnp.float32) * scale
    if len(cuts) > 0:
        result = steps_of(stream_key, dims, cuts, -0.22, 0.18) * result
    return jnp.clip(result, min=-most, max=most).astype(kind)


def setup_inputs(seed: int = 0) -> dict:
    keys = jax.random.split(jax.random.key(seed), 10)
    return {
        "chars": with_ends(ranked(keys[0], (MICRO, ROWS, SEQ), VOCAB, 2), jax.random.fold_in(keys[0], 3), 0, VOCAB - 1).astype(jnp.int32),
        "resets": with_ends((jax.random.randint(keys[1], (MICRO, ROWS, SEQ), 0, 6) < 1).astype(jnp.int32), jax.random.fold_in(keys[1], 1), 0, 1),
        "targets": with_ends(ranked(keys[2], (MICRO, ROWS, SEQ), VOCAB, 2), jax.random.fold_in(keys[2], 3), 0, VOCAB - 1).astype(jnp.int32),
        "embed": normal_values(keys[3], (VOCAB, EMB), 1.0, 6.0),
        "w_in": normal_values(keys[4], (EMB, GATES), EMB ** -0.5, 0.625, ((1, 32),)),
        "bias_in": normal_values(keys[5], (GATES,), 0.5, 3.0, ((0, 32),)),
        "w_rec": normal_values(keys[6], (HID, GATES), HID ** -0.5, 0.125, ((0, 32),)),
        "w_dec": normal_values(keys[7], (HID, VOCAB), 0.1, 0.59765625, ((0, 32),)),
        "bias_dec": normal_values(keys[8], (VOCAB,), 1.0, 6.0),
    }


@jax.custom_vjp
def low(v):
    return lax.optimization_barrier(v.astype(jnp.bfloat16)).astype(jnp.float32)

@jax.custom_vjp
def low_back(v):
    return v

def low_keep(v):
    return (low(v), None)

def low_pass(kept, grad):
    return (grad,)

def back_keep(v):
    return (v, None)

def back_low(kept, grad):
    return (low(grad),)
low.defvjp(low_keep, low_pass)
low_back.defvjp(back_keep, back_low)

def dense(left, right):
    return jnp.dot(left, right, precision=lax.Precision.HIGHEST, preferred_element_type=jnp.float32)

def forward(embed, w_in, bias_in, w_rec, w_dec, bias_dec, chars, resets, targets):
    letters = jnp.arange(VOCAB, dtype=jnp.int32)
    width = w_rec.shape[0]

    def advance(state, slot):
        hidden_now, cell = state
        ids, marks, goals = slot
        keep = (1 - marks).astype(jnp.float32)[:, None]
        onehot = (ids[:, None] == letters[None, :]).astype(jnp.float32)
        feature = dense(onehot, embed)
        prev_hidden = hidden_now * keep
        pre = low_back(dense(feature, w_in) + bias_in + dense(prev_hidden, w_rec))
        gin, gforget, gcand, gout = jnp.split(pre, 4, axis=1)
        cell_new = jax.nn.sigmoid(gforget) * (cell * keep) + jax.nn.sigmoid(gin) * jnp.tanh(gcand)
        hid_new = low(jax.nn.sigmoid(gout) * jnp.tanh(cell_new))
        logits = low_back(dense(hid_new, w_dec) + bias_dec)
        top = lax.optimization_barrier(jnp.max(logits, axis=1, keepdims=True))
        lse = top[:, 0] + jnp.log(lax.optimization_barrier(jnp.sum(jnp.exp(logits - top), axis=1)))
        goal_hot = (goals[:, None] == letters[None, :]).astype(jnp.float32)
        part = jnp.sum(lse) - jnp.sum(goal_hot * logits)
        return ((hid_new, cell_new), (part, hid_new))

    def micro_step(total, batch):
        ids, marks, goals = batch
        count = ids.shape[0]
        start = (jnp.zeros((count, width), jnp.float32), jnp.zeros((count, width), jnp.float32))
        state, outputs = lax.scan(jax.checkpoint(advance), start, (ids.T, marks.T, goals.T))
        parts, hiddens = outputs
        return (total + jnp.sum(parts), jnp.transpose(hiddens, (1, 0, 2)))
    total, hidden = lax.scan(jax.checkpoint(micro_step), jnp.zeros((), jnp.float32), (chars, resets, targets))
    return (total, hidden)

def reference(chars, resets, targets, embed, w_in, bias_in, w_rec, w_dec, bias_dec):
    params = tuple((p.astype(jnp.float32) for p in (embed, w_in, bias_in, w_rec, w_dec, bias_dec)))

    def objective(embed_f, w_in_f, bias_in_f, w_rec_f, w_dec_f, bias_dec_f):
        return forward(embed_f, w_in_f, bias_in_f, w_rec_f, w_dec_f, bias_dec_f, chars, resets, targets)
    outputs, pullback = jax.vjp(objective, *params)
    total, hidden = outputs
    grads = pullback((jnp.ones((), jnp.float32), jnp.zeros_like(hidden)))
    loss = total / (MICRO * ROWS * SEQ)
    return (loss, hidden.astype(jnp.bfloat16), grads[0], grads[1], grads[2], grads[3], grads[4], grads[5])
```

```python
import functools

import jax
import jax.numpy as jnp
from jax import lax
from jax.experimental import pallas as pl
from jax.experimental.pallas import tpu as pltpu
from jax.sharding import PartitionSpec as P

MESH = pl.DeviceIdType.MESH
NN = ((1,), (0,))
NT = ((1,), (1,))
TN = ((0,), (0,))
F32 = jnp.float32
BF = jnp.bfloat16

VPAD = 384
EPAD = 128
RING = 4
SMALL = 112


def mm(left, right, dims):
    return lax.dot_general(left, right, (dims, ((), ())), preferred_element_type=F32)


def sigmoid(v):
    return 0.5 * jnp.tanh(0.5 * v) + 0.5


def lstm_kernel(
    steps, rows,
    w_rec, w_in, w_dec, emb_t, bias_dec, ids_in,
    out_rec, out_in, out_dec, out_hid, out_small,
    W, WIN, WDEC, IDS, H, HT, HTS, HSEND, A, C, D, DS, DRAW, DL,
    PR, STG, OWN, DCN, SY, RY, SM, RM, EMBT, LV, BD, GWD, GS, GY, GM, DWI, IS, IY, IM, RSM,
    s_ids, r_ids, s_win, r_win, s_wa, r_wa, s_wm, r_wm, s_wy, r_wy, s_ws, r_ws,
    s_da, r_da, s_dm, r_dm, s_dy, r_dy, s_ds, r_ds, s_h, r_h, s_ht, r_ht, s_d, r_d,
    s_pr, r_pr, s_gd, r_gd, s_gi, r_gi, s_sm, r_sm, s_ry, r_ry, s_rm, r_rm, s_ra, r_ra,
    l_sem, hid_sem,
):
    last = steps - 1
    dp, fs = lax.axis_index("dp"), lax.axis_index("fsdp")
    z, x, y, c = dp // 2, dp % 2, fs // 2, fs % 2
    zh = z // 2
    a = z + zh * (3 - 2 * z)

    def dev(zz, xx, yy, cc):
        return (zz * 2 + xx, yy * 2 + cc)

    def block(zz, xx, yy, cc):
        return zz * 8 + xx * 4 + yy * 2 + cc

    def kx(k):
        return x + (k % 2) * (1 - 2 * x)

    def kz(k):
        return z + (k // 2) * (1 - 2 * (z % 2))

    def ka(k):
        return a + (k // 2) * (1 - 2 * a)

    def kdev(k):
        return dev(kz(k), kx(k), y, c)

    def member(k):
        return 2 * kx(k) + ka(k)

    def unit_block(k, j):
        return 2 * (ka(k) + j * (3 - 2 * ka(k))) + kx(k)

    def lanes(ub):
        return pl.ds(pl.multiple_of(256 * ub, 256), 256)

    mir, ydev, sib = dev(3 - z, x, y, c), dev(z, x, 1 - y, c), dev(z, x, y, 1 - c)
    perm = dev(2 * x + y, c, z // 2, z % 2)
    back = dev(2 * y + c, z // 2, z % 2, x)
    stays = jnp.logical_and(perm[0] == dp, perm[1] == fs)
    moved = jnp.logical_not(stays)

    def rc(src, dst, ss, rs, to):
        return pltpu.make_async_remote_copy(
            src_ref=src, dst_ref=dst, send_sem=ss, recv_sem=rs, device_id=to, device_id_type=MESH
        )

    barrier = pltpu.get_barrier_semaphore()

    def greet(to):
        pl.semaphore_signal(barrier, inc=1, device_id=to, device_id_type=MESH)

    for k in (1, 2, 3):
        greet(kdev(k))
    for to in (mir, ydev, sib):
        greet(to)

    @pl.when(moved)
    def _():
        greet(perm)
        greet(back)

    pl.semaphore_wait(barrier, 6 + 2 * moved.astype(jnp.int32))

    me = block(z, x, y, c)

    def w_slot(b):
        return W.at[:, pl.ds(pl.multiple_of(64 * b, 64), 64), :]

    def d_slot(b):
        return WDEC.at[pl.ds(pl.multiple_of(64 * b, 64), 64), :]

    def wa(k, j, b):
        return rc(
            w_rec.at[unit_block(k, j)],
            W.at[pl.ds(4 * j, 4), pl.ds(pl.multiple_of(64 * b, 64), 64), :],
            s_wa.at[k - 1, j], r_wa.at[k - 1, j], kdev(k),
        )

    def ids_copy(k, mem):
        return rc(ids_in, IDS.at[:, mem], s_ids.at[k - 1], r_ids.at[k - 1], kdev(k))

    def own_w(j):
        return pltpu.make_async_copy(
            w_rec.at[unit_block(0, j)],
            W.at[pl.ds(4 * j, 4), pl.ds(pl.multiple_of(64 * me, 64), 64), :],
            l_sem.at[j],
        )

    own_w(0).start()
    own_w(1).start()
    for k in (1, 2, 3):
        ids_copy(k, member(0)).start()

    def win_perm(jj, gy, gc):
        return rc(w_in, WIN.at[jj, gy, gc], s_win.at[0], r_win.at[0], perm)

    def win_local():
        return pltpu.make_async_copy(w_in, WIN.at[x, z // 2, z % 2], l_sem.at[2])

    @pl.when(moved)
    def _():
        win_perm(x, z // 2, z % 2).start()

    @pl.when(stays)
    def _():
        win_local().start()

    for k in (3, 1, 2):
        for j in (0, 1):
            wa(k, j, me).start()

    def to_mir(k):
        b = block(kz(k), kx(k), y, c)
        return rc(w_slot(b), w_slot(b), s_wm.at[k], r_wm.at[k], mir)

    def from_mir(k):
        b = block(3 - kz(k), kx(k), y, c)
        return rc(w_slot(b), w_slot(b), s_wm.at[k], r_wm.at[k], mir)

    def group_block(i, yy, cc):
        k, far = i % 4, i // 4
        zz = kz(k)
        return block(zz + far * (3 - 2 * zz), kx(k), yy, cc)

    def to_y(i, slot=None):
        b = group_block(i, y, c)
        return rc(w_slot(b), w_slot(b), s_wy.at[i], r_wy.at[i], ydev)

    def from_y(i):
        b = group_block(i, 1 - y, c)
        return rc(w_slot(b), w_slot(b), s_wy.at[i], r_wy.at[i], ydev)

    def to_s(i):
        b = group_block(i % 8, y + (i // 8) * (1 - 2 * y), c)
        return rc(w_slot(b), w_slot(b), s_ws.at[i], r_ws.at[i], sib)

    def from_s(i):
        b = group_block(i % 8, y + (i // 8) * (1 - 2 * y), 1 - c)
        return rc(w_slot(b), w_slot(b), s_ws.at[i], r_ws.at[i], sib)

    own_w(0).wait()
    own_w(1).wait()
    to_mir(0).start()
    to_y(0).start()
    to_s(0).start()

    IDS[:, member(0)] = ids_in[...]

    for k in (1, 2, 3):
        for j in (0, 1):
            wa(k, j, block(kz(k), kx(k), y, c)).wait_recv()
        to_mir(k).start()
        to_y(k).start()
        to_s(k).start()

    def da(k, b):
        return rc(w_dec, d_slot(b), s_da.at[k - 1], r_da.at[k - 1], kdev(k))

    for k in (1, 2, 3):
        da(k, me).start()
    own_dec = pltpu.make_async_copy(w_dec, d_slot(me), l_sem.at[3])
    own_dec.start()

    def win_mir(jj):
        return rc(WIN.at[jj, y, c], WIN.at[jj, y, c], s_win.at[1], r_win.at[1], mir)

    def win_y(yy):
        return rc(WIN.at[:, yy, c], WIN.at[:, yy, c], s_win.at[2], r_win.at[2], ydev)

    def win_s(cc):
        return rc(WIN.at[:, :, cc], WIN.at[:, :, cc], s_win.at[3], r_win.at[3], sib)

    @pl.when(moved)
    def _():
        win_perm(zh, y, c).wait_recv()

    @pl.when(stays)
    def _():
        win_local().wait()

    win_mir(zh).start()

    for k in (1, 2, 3):
        ids_copy(k, member(k)).wait_recv()
    lane = lax.broadcasted_iota(jnp.int32, (rows, 128), 1)
    wide = lax.broadcasted_iota(jnp.int32, (rows, VPAD), 1).astype(F32)

    def column(at, s):
        packed = IDS[s].reshape(rows, 128)
        return jnp.sum(jnp.where(lane == at, packed, 0).astype(F32), axis=1, keepdims=True)

    def keep_of(t, s):
        return 1.0 - column(8 + t, s)

    def letter(t, s):
        return jnp.where(column(t, s) == wide, 1.0, 0.0).astype(BF)

    EMBT[...] = jnp.zeros_like(EMBT)
    LV[...] = jnp.zeros_like(LV)
    BD[...] = jnp.zeros_like(BD)
    GWD[...] = jnp.zeros_like(GWD)
    DWI[...] = jnp.zeros_like(DWI)
    DCN[...] = jnp.zeros_like(DCN)

    win_mir(1 - zh).wait_recv()
    win_y(y).start()
    from_y(0).wait_recv()
    to_s(8).start()
    from_mir(0).wait_recv()
    to_y(4).start()
    to_s(4).start()
    from_y(1).wait_recv()
    to_s(9).start()
    win_y(1 - y).wait_recv()
    win_s(c).start()
    win_s(1 - c).wait_recv()

    def h_copy(t, s, k, j, ub):
        part = H.at[t % RING, s, :, lanes(ub)]
        return rc(part, part, s_h.at[t, s, k - 1, j], r_h.at[t, s, k - 1, j], kdev(k))

    def wait_h(t, s):
        for k in (1, 2, 3):
            for j in (0, 1):
                h_copy(t, s, k, j, unit_block(k, j)).wait_recv()

    def gates(t, s, first):
        keep = None if first else keep_of(t, s)
        feature = mm(letter(t, s), emb_t[...], NT).astype(BF)
        for j in (0, 1):
            pre = []
            for g in range(4):
                drive = mm(feature, WIN[j, g // 2, g % 2], NN)
                if not first:
                    drive = drive + keep * mm(H[(t - 1) % RING, s], W[4 * j + g], NN)
                pre.append(drive)
            s_i, s_f, t_g, s_o = sigmoid(pre[0]), sigmoid(pre[1]), jnp.tanh(pre[2]), sigmoid(pre[3])
            cell = s_i * t_g
            if not first:
                cell = s_f * (C[t - 1, s, j] * keep) + cell
            for g, v in enumerate((s_i, s_f, t_g, s_o)):
                A[t, s, 4 * j + g] = v
            C[t, s, j] = cell
            ub = unit_block(0, j)
            H[t % RING, s, :, lanes(ub)] = (s_o * jnp.tanh(cell)).astype(BF)
            for k in (3, 1, 2):
                h_copy(t, s, k, j, ub).start()

    gates(0, 0, True)
    gates(0, 1, True)

    from_y(2).wait_recv()
    to_s(10).start()
    from_mir(1).wait_recv()
    to_y(5).start()
    to_s(5).start()
    from_y(3).wait_recv()
    to_s(11).start()
    from_mir(2).wait_recv()
    to_y(6).start()
    to_s(6).start()
    from_y(4).wait_recv()
    to_s(12).start()
    from_mir(3).wait_recv()
    to_y(7).start()
    to_s(7).start()

    def dec_mir(k, far):
        zz = kz(k)
        b = block(zz + far * (3 - 2 * zz), kx(k), y, c)
        return rc(d_slot(b), d_slot(b), s_dm.at[k], r_dm.at[k], mir)

    def dec_y(i, yy):
        b = group_block(i, yy, c)
        return rc(d_slot(b), d_slot(b), s_dy.at[i], r_dy.at[i], ydev)

    def dec_s(i, cc):
        b = group_block(i % 8, y + (i // 8) * (1 - 2 * y), cc)
        return rc(d_slot(b), d_slot(b), s_ds.at[i], r_ds.at[i], sib)

    own_dec.wait()
    dec_mir(0, 0).start()
    dec_y(0, y).start()
    dec_s(0, c).start()
    for k in (1, 2, 3):
        da(k, block(kz(k), kx(k), y, c)).wait_recv()
        dec_mir(k, 0).start()
        dec_y(k, y).start()
        dec_s(k, c).start()

    for i in (5, 6, 7):
        from_y(i).wait_recv()
        to_s(8 + i).start()

    @pl.loop(0, 16)
    def _(i):
        from_s(i).wait_recv()

    def released(t, s):
        hid_copy(t, s).wait()
        for k in (1, 2, 3):
            for j in (0, 1):
                h_copy(t, s, k, j, unit_block(0, j)).wait_send()

    def forward(t, s):
        wait_h(t - 1, s)

        @pl.when(t >= RING - 1)
        def _():
            released(t - (RING - 1), s)

        gates(t, s, False)

    for s in range(2):
        wait_h(0, s)
        gates(1, s, False)

    for k in range(4):
        dec_mir(k, 1).wait_recv()
        dec_y(4 + k, y).start()
        dec_s(4 + k, c).start()

    row = lax.broadcasted_iota(jnp.int32, (128, 256), 0)
    col = lax.broadcasted_iota(jnp.int32, (128, 256), 1)

    def select(cc):
        yy = y + (row // 64) * (1 - 2 * y)
        return jnp.where(col == 64 * (2 * yy + cc) + row % 64, 1.0, 0.0).astype(BF)

    def lane_slot(t, s):
        return pl.ds(pl.multiple_of((2 * t + s) * rows, rows), rows)

    def ht_copy(t, s, slot):
        return rc(HSEND.at[slot], HTS.at[:, :, lane_slot(t, s)], s_ht.at[t, s], r_ht.at[t, s], sib)

    def hid_copy(t, s):
        mine = H.at[t % RING, s, pl.ds(pl.multiple_of(32 * member(0), 32), 32), :]
        return pltpu.make_async_copy(mine, out_hid.at[s, t], hid_sem.at[t, s])

    def logits_of(t, s):
        scores = mm(H[t % RING, s], WDEC[...], NN) + bias_dec[0:1, :]
        top = jnp.max(scores, axis=1, keepdims=True)
        shifted = jnp.exp(scores - top)
        summed = jnp.sum(shifted, axis=1, keepdims=True)
        goal = jnp.where(column(16 + t, s) == wide, 1.0, 0.0)
        picked = jnp.sum(goal * scores, axis=1, keepdims=True)
        LV[...] += jnp.broadcast_to(top + jnp.log(summed) - picked, (rows, 128))
        DL[t, s] = (shifted / summed - goal).astype(BF)

    def decoder_side(t, s):
        hid_copy(t, s).start()
        grad = DL[t, s]
        BD[...] += mm(jnp.ones((8, rows), BF), grad, NN)
        for j in (0, 1):
            GWD[j] += mm(H[t % RING, s, :, lanes(unit_block(0, j))], grad, TN).reshape(2, 2, 64, VPAD)

    def transposed_side(t, s):
        slot = s
        mine, other = select(c), select(1 - c)

        @pl.when(t >= 1)
        def _():
            ht_copy(t - 1, s, slot).wait_send()

        for tile in range(8):
            part = H[t % RING, s, :, 256 * tile : 256 * (tile + 1)]
            HT[tile, :, lane_slot(t, s)] = mm(mine, part, NT).astype(BF)
            HSEND[slot, tile] = mm(other, part, NT).astype(BF)
        ht_copy(t, s, slot).start()

    for i in range(8):
        dec_y(i, 1 - y).wait_recv()
        dec_s(8 + i, c).start()

    @pl.loop(0, 16)
    def _(i):
        dec_s(i, 1 - c).wait_recv()

    @pl.loop(4, 2 * steps)
    def _(i):
        t, s = i // 2, i % 2
        forward(t, s)
        logits_of(t - 2, s)
        decoder_side(t - 2, s)
        transposed_side(t - 2, s)

    @pl.loop(0, 2)
    def _(s):
        logits_of(last - 1, s)
        decoder_side(last - 1, s)
        transposed_side(last - 1, s)

    def pr_copy(t, s, k, j):
        return rc(STG.at[s, k - 1, j], PR.at[t % 2, s, k - 1, j], s_pr.at[t, s, k - 1, j], r_pr.at[t, s, k - 1, j], kdev(k))

    def d_copy(t, s):
        return rc(D.at[:, t - 1, s], DS.at[:, t - 1, s], s_d.at[t, s], r_d.at[t, s], sib)

    def backward(t, s, newest, oldest):
        if not newest:
            for k in (1, 2, 3):
                for j in (0, 1):
                    pr_copy(t + 1, s, k, j).wait_recv()
        keep = keep_of(t, s)
        for j in (0, 1):
            up = WDEC[lanes(unit_block(0, j)), :]
            dh = mm(DL[t, s], up, NT)
            if not newest:
                rest = PR[(t + 1) % 2, s, 0, j].astype(F32) + PR[(t + 1) % 2, s, 1, j].astype(F32)
                rest = rest + PR[(t + 1) % 2, s, 2, j].astype(F32)
                dh = dh + (OWN[s, j] + rest)
            s_i, s_f, t_g, s_o = (A[t, s, 4 * j + g] for g in range(4))
            t_c = jnp.tanh(C[t, s, j])
            d_o = dh * t_c
            d_c = dh * s_o * (1.0 - t_c * t_c)
            if not newest:
                d_c = d_c + DCN[s, j]
            d_i = d_c * t_g * s_i * (1.0 - s_i)
            d_g = d_c * s_i * (1.0 - t_g * t_g)
            d_o = d_o * s_o * (1.0 - s_o)
            if oldest:
                d_f = jnp.zeros_like(d_i)
            else:
                d_f = d_c * (C[t - 1, s, j] * keep) * s_f * (1.0 - s_f)
                DCN[s, j] = keep * (d_c * s_f)
            for g, v in enumerate((d_i, d_f, d_g, d_o)):
                low = v.astype(BF)
                DRAW[4 * j + g] = low
                if not oldest:
                    D[4 * j + g, t - 1, s] = low * keep.astype(BF)
        if oldest:
            return
        d_copy(t, s).start()
        if not newest:
            for k in (1, 2, 3):
                for j in (0, 1):
                    pr_copy(t + 1, s, k, j).wait_send()
        for k in (3, 1, 2, 0):
            for j in (0, 1):
                ub = unit_block(k, j)
                total = None
                for q in range(8):
                    term = mm(D[q, t - 1, s], W[q, lanes(ub), :], NT)
                    total = term if total is None else total + term
                if k == 0:
                    OWN[s, j] = total
                else:
                    STG[s, k - 1, j] = total.astype(BF)
                    pr_copy(t, s, k, j).start()

    def input_side(t, s):
        onehot = letter(t, s)
        feat_t = mm(emb_t[...], onehot, NT).astype(BF)
        grad_t = None
        for q in range(8):
            jj, gy, gc = q // 4, (q // 2) % 2, q % 2
            DWI[jj, gy, gc] += mm(feat_t, DRAW[q], NN)
            term = mm(WIN[jj, gy, gc], DRAW[q], NT)
            grad_t = term if grad_t is None else grad_t + term
        high = grad_t.astype(BF)
        low = (grad_t - high.astype(F32)).astype(BF)
        EMBT[...] += mm(high, onehot, NN) + mm(low, onehot, NN)

    for s in range(2):
        wait_h(last, s)
        logits_of(last, s)
        backward(last, s, True, False)
        input_side(last, s)
    for s in range(2):
        decoder_side(last, s)

    def gd_s():
        return rc(GWD.at[:, :, 1 - c], GS, s_gd.at[0], r_gd.at[0], sib)

    def gd_y():
        return rc(GWD.at[:, 1 - y, c], GY, s_gd.at[1], r_gd.at[1], ydev)

    def gd_m():
        return rc(GWD.at[1 - zh, y, c], GM, s_gd.at[2], r_gd.at[2], mir)

    gd_s().start()

    @pl.loop(0, 2 * (steps - 2))
    def _(i):
        t, s = last - 1 - i // 2, i % 2
        backward(t, s, False, False)
        input_side(t, s)

        @pl.when(i == 1)
        def _():
            gd_s().wait_recv()
            GWD[:, :, c] += GS[...]
            gd_y().start()

        @pl.when(i == 3)
        def _():
            gd_y().wait_recv()
            GWD[:, y, c] += GY[...]
            gd_m().start()

        @pl.when(i == 5)
        def _():
            gd_m().wait_recv()
            out_dec[...] = GWD[zh, y, c] + GM[...]

    @pl.loop(0, 2 * (steps - 1))
    def _(i):
        ht_copy(i // 2, i % 2, 0).wait_recv()
        d_copy(1 + i // 2, i % 2).wait_recv()

    depth = 2 * (steps - 1) * rows

    def kept(q):
        return A.at[2 + q // 4, (q % 4) // 2, :, pl.ds(pl.multiple_of(64 * (q % 2), 64), 64), :]

    def tile_of(q):
        k, near = q % 4, q // 4
        zz = kz(k)
        return 2 * (3 - zz + near * (2 * zz - 3)) + kx(k)

    def ry_copy(q):
        return rc(SY.at[q % 4], RY.at[q], s_ry.at[q], r_ry.at[q], ydev)

    def rm_copy(k):
        return rc(SM.at[k], RM.at[k], s_rm.at[k], r_rm.at[k], mir)

    def ra_copy(k, j, src_kind):
        src = A.at[3, k // 2, pl.ds(4 * j, 4), pl.ds(pl.multiple_of(64 * (k % 2), 64), 64), :]
        return rc(src, out_rec.at[unit_block(src_kind, j)], s_ra.at[k - 1, j], r_ra.at[k - 1, j], kdev(k))

    def ra_own(j):
        src = A.at[3, 0, pl.ds(4 * j, 4), pl.ds(0, 64), :]
        return pltpu.make_async_copy(src, out_rec.at[unit_block(0, j)], l_sem.at[4 + j])

    def make_tile(q):
        tile = tile_of(q)
        left, right = HT[tile], HTS[tile]
        hold = kept(q)
        if isinstance(q, int):
            ry_copy(q - 4).wait_send()
        for n in range(8):
            grad = mm(left, D[n].reshape(depth, 256), NN) + mm(right, DS[n].reshape(depth, 256), NN)
            hold[n] = grad[:64]
            SY[q % 4, n] = grad[64:].astype(BF)
        ry_copy(q).start()

    def add_y(q):
        ry_copy(q).wait_recv()
        hold = kept(q)
        hold[...] = hold[...] + RY[q].astype(F32)

    @pl.loop(0, 4)
    def _(i):
        make_tile(3 - i)

    def pass_on(k):
        add_y(k)
        SM[k] = kept(k)[...].astype(BF)
        rm_copy(k).start()

    for s in range(2):
        backward(0, s, False, True)
        input_side(0, s)

    leader = jnp.logical_and(x == 0, a == 0)
    high_row = lax.broadcasted_iota(jnp.int32, (8, VPAD), 0)
    loss = jnp.sum(LV[...], axis=0, keepdims=True)
    loss = jnp.concatenate([loss] * (VPAD // 128), axis=1)
    extra = jnp.where(high_row == 0, BD[...], jnp.where(high_row == 1, loss, 0.0))
    out_small[0 : SMALL - 8] = EMBT[0 : SMALL - 8]
    out_small[SMALL - 8 : SMALL] = jnp.where(leader, extra, 0.0)

    small_to = (sib, ydev, mir, kdev(1), kdev(2))

    def sm_copy(n):
        return rc(out_small, RSM.at[n], s_sm.at[n], r_sm.at[n], small_to[n])

    def sm_next(n):
        sm_copy(n).wait()
        out_small[...] = out_small[...] + RSM[n]
        if n < 4:
            sm_copy(n + 1).start()

    sm_copy(0).start()

    live = pl.ds(0, 104)

    def gi_s():
        return rc(DWI.at[:, :, 1 - c, live], IS, s_gi.at[0], r_gi.at[0], sib)

    def gi_y():
        return rc(DWI.at[:, 1 - y, c, live], IY, s_gi.at[1], r_gi.at[1], ydev)

    def gi_m():
        return rc(DWI.at[1 - zh, y, c, live], IM, s_gi.at[2], r_gi.at[2], mir)

    def gi_p():
        return rc(DWI.at[zh, y, c, live], out_in, s_gi.at[3], r_gi.at[3], back)

    gi_s().start()
    pass_on(3)
    gi_s().wait_recv()
    DWI[:, :, c, 0:104] = DWI[:, :, c, 0:104] + IS[...]
    gi_y().start()
    sm_next(0)
    make_tile(7)
    pass_on(2)
    make_tile(6)
    pass_on(1)
    make_tile(5)
    pass_on(0)
    make_tile(4)
    gi_y().wait_recv()
    DWI[:, y, c, 0:104] = DWI[:, y, c, 0:104] + IY[...]
    gi_m().start()
    sm_next(1)

    def finish(k):
        add_y(4 + k)
        rm_copy(k).wait_recv()
        hold = kept(4 + k)
        hold[...] = hold[...] + RM[k].astype(F32)
        for j in (0, 1):
            if k == 0:
                ra_own(j).start()
            else:
                ra_copy(k, j, 0).start()

    finish(3)
    sm_next(2)
    gi_m().wait_recv()
    DWI[zh, y, c, 0:104] = DWI[zh, y, c, 0:104] + IM[...]

    @pl.when(moved)
    def _():
        gi_p().start()

    @pl.when(stays)
    def _():
        out_in[...] = DWI[zh, y, c, 0:104]

    finish(2)
    sm_next(3)
    finish(1)
    sm_next(4)
    finish(0)

    for k in (1, 2, 3):
        for j in (0, 1):
            ra_copy(k, j, k).wait_recv()
            ra_copy(k, j, 0).wait_send()
            wa(k, j, me).wait_send()
            for s in range(2):
                pr_copy(1, s, k, j).wait_send()
        ids_copy(k, member(0)).wait_send()
        da(k, me).wait_send()
    ra_own(0).wait()
    ra_own(1).wait()

    @pl.when(moved)
    def _():
        gi_p().wait()
        win_perm(x, z // 2, z % 2).wait_send()

    win_mir(zh).wait_send()
    win_y(y).wait_send()
    win_s(c).wait_send()
    for copy in (gd_s, gd_y, gd_m, gi_s, gi_y, gi_m):
        copy().wait_send()
    for s in range(2):
        ht_copy(last - 1, s, s).wait_send()

    @pl.loop(0, 4)
    def _(k):
        to_mir(k).wait_send()
        dec_mir(k, 0).wait_send()
        rm_copy(k).wait_send()

    @pl.loop(0, 8)
    def _(i):
        to_y(i).wait_send()
        dec_y(i, y).wait_send()

    @pl.loop(4, 8)
    def _(q):
        ry_copy(q).wait_send()

    @pl.loop(0, 16)
    def _(i):
        to_s(i).wait_send()
        dec_s(i, c).wait_send()

    @pl.loop(2 * (steps - RING + 1), 2 * steps)
    def _(i):
        released(i // 2, i % 2)

    @pl.loop(0, 2 * (steps - 1))
    def _(i):
        d_copy(1 + i // 2, i % 2).wait_send()


def fused(chars, resets, targets, embed, w_in, bias_in, w_rec, w_dec, bias_dec):
    micro, count, steps = chars.shape
    own_rows, gate_cols = w_rec.shape
    vocab, emb = embed.shape
    width = gate_cols // 4
    members = 4
    rows = count * members
    w_rec4 = w_rec.reshape(own_rows, 4, 8, 256).transpose(2, 1, 0, 3)
    w_in_e = jnp.zeros((EPAD, 256), BF).at[:emb].set(w_in).at[emb].set(bias_in)
    w_dec_e = jnp.pad(w_dec, ((0, 0), (0, VPAD - vocab)))
    emb_t = jnp.zeros((EPAD, VPAD), BF).at[:emb, :vocab].set(embed.T).at[emb, :].set(1.0)
    bias_e = jnp.full((8, VPAD), -1e30, F32).at[:, :vocab].set(bias_dec.astype(F32)[None, :])

    def six(v):
        return jnp.pad(v, ((0, 0), (0, 0), (0, 8 - steps)))

    ids = jnp.concatenate([six(chars), six(resets), six(targets)], axis=2)
    ids = jnp.pad(ids, ((0, 0), (0, 0), (0, 128 - 24)))

    vm = pl.BlockSpec(memory_space=pltpu.VMEM)
    hbm = pl.BlockSpec(memory_space=pl.ANY)
    dma = pltpu.SemaphoreType.DMA
    n = steps - 1
    scratch = [
        pltpu.VMEM((8, width, 256), BF),
        pltpu.VMEM((2, 2, 2, EPAD, 256), BF),
        pltpu.VMEM((width, VPAD), BF),
        pltpu.VMEM((micro, members, count, 128), jnp.int32),
        pltpu.VMEM((RING, micro, rows, width), BF),
        pltpu.VMEM((8, 128, 2 * n * rows), BF),
        pltpu.VMEM((8, 128, 2 * n * rows), BF),
        pltpu.VMEM((2, 8, 128, rows), BF),
        pltpu.VMEM((steps, micro, 8, rows, 256), F32),
        pltpu.VMEM((steps, micro, 2, rows, 256), F32),
        pltpu.VMEM((8, n, micro, rows, 256), BF),
        pltpu.VMEM((8, n, micro, rows, 256), BF),
        pltpu.VMEM((8, rows, 256), BF),
        pltpu.VMEM((steps, micro, rows, VPAD), BF),
        pltpu.VMEM((2, micro, 3, 2, rows, 256), BF),
        pltpu.VMEM((micro, 3, 2, rows, 256), BF),
        pltpu.VMEM((micro, 2, rows, 256), F32),
        pltpu.VMEM((micro, 2, rows, 256), F32),
        pltpu.VMEM((4, 8, 64, 256), BF),
        pltpu.VMEM((8, 8, 64, 256), BF),
        pltpu.VMEM((4, 8, 64, 256), BF),
        pltpu.VMEM((4, 8, 64, 256), BF),
        pltpu.VMEM((EPAD, VPAD), F32),
        pltpu.VMEM((rows, 128), F32),
        pltpu.VMEM((8, VPAD), F32),
        pltpu.VMEM((2, 2, 2, 64, VPAD), F32),
        pltpu.VMEM((2, 2, 64, VPAD), F32),
        pltpu.VMEM((2, 64, VPAD), F32),
        pltpu.VMEM((64, VPAD), F32),
        pltpu.VMEM((2, 2, 2, EPAD, 256), F32),
        pltpu.VMEM((2, 2, 104, 256), F32),
        pltpu.VMEM((2, 104, 256), F32),
        pltpu.VMEM((104, 256), F32),
        pltpu.VMEM((5, SMALL, VPAD), F32),
    ]
    shapes = [
        (3,), (4,), (3, 2), (4,), (8,), (16,), (3,), (4,), (8,), (16,),
        (steps, 2, 3, 2), (n, 2), (steps, 2), (steps, 2, 3, 2), (3,), (4,), (5,), (8,), (4,), (3, 2),
    ]
    for shape in shapes:
        scratch += [dma(shape), dma(shape)]
    scratch += [dma((6,)), dma((steps, 2))]
    out_rec, out_in, out_dec, out_hid, out_small = pl.pallas_call(
        functools.partial(lstm_kernel, steps, rows),
        out_shape=(
            jax.ShapeDtypeStruct((8, 4, own_rows, 256), F32),
            jax.ShapeDtypeStruct((104, 256), F32),
            jax.ShapeDtypeStruct((own_rows, VPAD), F32),
            jax.ShapeDtypeStruct((micro, steps, count, width), BF),
            jax.ShapeDtypeStruct((SMALL, VPAD), F32),
        ),
        in_specs=[hbm, vm, vm, vm, vm, vm],
        out_specs=(hbm, vm, vm, hbm, vm),
        scratch_shapes=scratch,
        compiler_params=pltpu.CompilerParams(
            collective_id=0, has_side_effects=True, vmem_limit_bytes=66 * 1000 * 1000
        ),
    )(w_rec4, w_in_e, w_dec_e, emb_t, bias_e, ids)
    everyone = lax.axis_size(("dp", "fsdp"))
    loss = out_small[SMALL - 7, 0] / (micro * count * steps * everyone)
    hidden = out_hid.transpose(0, 2, 1, 3)
    grad_embed = out_small[:emb, :vocab].T
    grad_rec = out_rec.transpose(2, 1, 0, 3).reshape(own_rows, gate_cols)
    return (
        loss,
        hidden,
        grad_embed,
        out_in[:emb],
        out_in[emb],
        grad_rec,
        out_dec[:, :vocab],
        out_small[SMALL - 8, :vocab],
    )


def dot_plain(left, right):
    return jnp.dot(left, right, preferred_element_type=jnp.float32)


def dot_right_t(left, right):
    return lax.dot_general(
        left, right, (((1,), (1,)), ((), ())), preferred_element_type=jnp.float32
    )


def dot_left_t(left, right):
    return lax.dot_general(
        left, right, (((0,), (0,)), ((), ())), preferred_element_type=jnp.float32
    )


def lstm_forward(weights, embed, bias_dec, ids, marks, goals):
    w_rec, w_dec, w_in, bias_in = weights
    count, steps = ids.shape
    width = w_rec.shape[0]
    letters = jnp.arange(embed.shape[0], dtype=jnp.int32)
    onehot = (ids.T.reshape(-1)[:, None] == letters[None, :]).astype(jnp.bfloat16)
    feature = dot_plain(onehot, embed).astype(jnp.bfloat16)
    drives = (dot_plain(feature, w_in) + bias_in.astype(jnp.float32)).reshape(steps, count, -1)
    keeps = (1 - marks.T).astype(jnp.float32)[:, :, None]

    def advance(state, slot):
        hidden_now, cell = state
        drive, keep_now = slot
        prev_hidden = hidden_now * keep_now.astype(jnp.bfloat16)
        prev_cell = cell * keep_now
        pre = drive + dot_plain(prev_hidden, w_rec)
        gin, gforget, gcand, gout = jnp.split(pre, 4, axis=1)
        cell_new = jax.nn.sigmoid(gforget) * prev_cell + jax.nn.sigmoid(gin) * jnp.tanh(gcand)
        hid_new = (jax.nn.sigmoid(gout) * jnp.tanh(cell_new)).astype(jnp.bfloat16)
        return ((hid_new, cell_new), (pre, prev_hidden, prev_cell, cell_new, hid_new))

    start = (jnp.zeros((count, width), jnp.bfloat16), jnp.zeros((count, width), jnp.float32))
    state, saved = lax.scan(advance, start, (drives, keeps))
    pres, prev_hiddens, prev_cells, cells, hiddens = saved
    flat_hidden = hiddens.reshape(steps * count, width)
    logits = dot_plain(flat_hidden, w_dec) + bias_dec.astype(jnp.float32)
    top = jnp.max(logits, axis=1, keepdims=True)
    shifted = jnp.exp(logits - top)
    summed = jnp.sum(shifted, axis=1, keepdims=True)
    goal_hot = (goals.T.reshape(-1)[:, None] == letters[None, :]).astype(jnp.float32)
    loss_part = jnp.sum(top[:, 0] + jnp.log(summed[:, 0])) - jnp.sum(goal_hot * logits)
    d_logits = (shifted / summed - goal_hot).astype(jnp.bfloat16)
    kept = (pres, prev_hiddens, prev_cells, cells, keeps, flat_hidden, d_logits, feature, onehot)
    return (kept, loss_part, jnp.transpose(hiddens, (1, 0, 2)))


def lstm_backward(weights, kept):
    w_rec, w_dec, w_in, bias_in = weights
    pres, prev_hiddens, prev_cells, cells, keeps, flat_hidden, d_logits, feature, onehot = kept
    steps, count, width = cells.shape
    from_dec = dot_right_t(d_logits, w_dec).reshape(steps, count, width)

    def retreat(carry, slot):
        grad_h, grad_c = carry
        pre, prev_cell, cell, extra, keep_now = slot
        gin, gforget, gcand, gout = jnp.split(pre, 4, axis=1)
        sig_in = jax.nn.sigmoid(gin)
        sig_forget = jax.nn.sigmoid(gforget)
        sig_out = jax.nn.sigmoid(gout)
        tan_cand = jnp.tanh(gcand)
        tan_cell = jnp.tanh(cell)
        grad_hid = extra + grad_h
        grad_out = grad_hid * tan_cell
        grad_cell = grad_c + grad_hid * sig_out * (1.0 - tan_cell * tan_cell)
        d_pre = jnp.concatenate(
            [
                grad_cell * tan_cand * sig_in * (1.0 - sig_in),
                grad_cell * prev_cell * sig_forget * (1.0 - sig_forget),
                grad_cell * sig_in * (1.0 - tan_cand * tan_cand),
                grad_out * sig_out * (1.0 - sig_out),
            ],
            axis=1,
        ).astype(jnp.bfloat16)
        back_h = dot_right_t(d_pre, w_rec) * keep_now
        back_c = grad_cell * sig_forget * keep_now
        return ((back_h, back_c), d_pre)

    start = (jnp.zeros((count, width), jnp.float32), jnp.zeros((count, width), jnp.float32))
    state, d_pres = lax.scan(
        retreat, start, (pres, prev_cells, cells, from_dec, keeps), reverse=True
    )
    flat_pre = d_pres.reshape(steps * count, -1)
    grad_dec = dot_left_t(flat_hidden, d_logits)
    grad_in = dot_left_t(feature, flat_pre)
    grad_bias = jnp.sum(flat_pre.astype(jnp.float32), axis=0)
    grad_feature = dot_right_t(flat_pre, w_in)
    grad_table = lax.dot_general(
        onehot.astype(jnp.float32),
        grad_feature,
        (((0,), (0,)), ((), ())),
        precision=lax.Precision.HIGHEST,
        preferred_element_type=jnp.float32,
    )
    grad_bias_out = jnp.sum(d_logits.astype(jnp.float32), axis=0)
    flat_prev = prev_hiddens.reshape(steps * count, width)
    return (grad_dec, grad_in, grad_bias, grad_table, grad_bias_out, flat_prev, flat_pre)


def general(chars, resets, targets, embed, w_in, bias_in, w_rec, w_dec, bias_dec):
    micro, count, steps = chars.shape
    everyone = lax.axis_size(("dp", "fsdp"))
    sums = None
    prev_list = []
    pre_list = []
    hidden_list = []
    for index in range(micro):
        forward_set = (
            lax.all_gather(w_rec, ("dp", "fsdp"), axis=0, tiled=True),
            lax.all_gather(w_dec, ("dp", "fsdp"), axis=0, tiled=True),
            lax.all_gather(w_in, ("dp", "fsdp"), axis=1, tiled=True),
            lax.all_gather(bias_in, ("dp", "fsdp"), axis=0, tiled=True),
        )
        kept, loss_part, hiddens = lstm_forward(
            forward_set, embed, bias_dec, chars[index], resets[index], targets[index]
        )
        backward_set = (
            lax.all_gather(w_rec, ("dp", "fsdp"), axis=0, tiled=True),
            lax.all_gather(w_dec, ("dp", "fsdp"), axis=0, tiled=True),
            lax.all_gather(w_in, ("dp", "fsdp"), axis=1, tiled=True),
            lax.all_gather(bias_in, ("dp", "fsdp"), axis=0, tiled=True),
        )
        grad_dec, grad_in, grad_bias, grad_table, grad_bias_out, flat_prev, flat_pre = (
            lstm_backward(backward_set, kept)
        )
        pieces = (grad_dec, grad_in, grad_bias, grad_table, grad_bias_out, loss_part)
        if sums is None:
            sums = pieces
        else:
            sums = tuple((first + second for first, second in zip(sums, pieces)))
        prev_list.append(flat_prev)
        pre_list.append(flat_pre)
        hidden_list.append(hiddens)
    prev_all = jnp.concatenate(prev_list, axis=0)
    pre_all = jnp.concatenate(pre_list, axis=0)
    grad_w_rec = lax.psum_scatter(
        dot_left_t(prev_all, pre_all), ("dp", "fsdp"), scatter_dimension=0, tiled=True
    )
    grad_w_dec, grad_w_in, grad_bias_in = (
        lax.psum_scatter(sums[0], ("dp", "fsdp"), scatter_dimension=0, tiled=True),
        lax.psum_scatter(sums[1], ("dp", "fsdp"), scatter_dimension=1, tiled=True),
        lax.psum_scatter(sums[2], ("dp", "fsdp"), scatter_dimension=0, tiled=True),
    )
    grad_embed, grad_bias_dec, total = lax.psum((sums[3], sums[4], sums[5]), ("dp", "fsdp"))
    loss = total / (micro * count * steps * everyone)
    hidden = jnp.stack(hidden_list, axis=0)
    return (
        loss,
        hidden,
        grad_embed,
        grad_w_in,
        grad_bias_in,
        grad_w_rec,
        grad_w_dec,
        grad_bias_dec,
    )


def solution(mesh):
    per_device = fused if (mesh.shape["dp"], mesh.shape["fsdp"]) == (8, 4) else general
    return jax.shard_map(
        per_device,
        mesh=mesh,
        in_specs=(
            P(None, ("dp", "fsdp"), None),
            P(None, ("dp", "fsdp"), None),
            P(None, ("dp", "fsdp"), None),
            P(),
            P(None, ("dp", "fsdp")),
            P(("dp", "fsdp")),
            P(("dp", "fsdp"), None),
            P(("dp", "fsdp"), None),
            P(),
        ),
        out_specs=(
            P(),
            P(None, ("dp", "fsdp"), None, None),
            P(),
            P(None, ("dp", "fsdp")),
            P(("dp", "fsdp")),
            P(("dp", "fsdp"), None),
            P(("dp", "fsdp"), None),
            P(),
        ),
        check_vma=False,
    )
```

```python
import functools

import jax
import jax.numpy as jnp
from jax import lax
from jax.experimental import pallas as pl
from jax.experimental.pallas import tpu as pltpu
from jax.sharding import PartitionSpec as P

MESH = pl.DeviceIdType.MESH
NN = ((1,), (0,))
NT = ((1,), (1,))
TN = ((0,), (0,))
F32 = jnp.float32
BF = jnp.bfloat16

VPAD = 384
EPAD = 128
RING = 4
SMALL = 112


def mm(left, right, dims):
    return lax.dot_general(left, right, (dims, ((), ())), preferred_element_type=F32)


def sigmoid(v):
    return 0.5 * jnp.tanh(0.5 * v) + 0.5


def lstm_kernel(
    steps, rows,
    w_rec, w_in_raw, b_in_raw, w_dec_raw, emb_raw, bias_raw, chars_in, resets_in, targets_in,
    out_own, out_recv, out_in, out_dec, out_hid, out_small,
    W, WIN, WDEC, IDS, H, HT, HTS, HSEND, A, C, D, DS, DRAW, DL,
    ids_in, w_in, emb_t, emb_p, w_dec, bias_dec, PR, STG, OWN, DCN, SY, RY, SM, RM, EMBT, LV, BD, GWD, GS, GY, GM, DWI, IS, IY, IM, RS1, RS2, RS3, RS4, RS5, PIECE, TOTAL,
    s_ids, r_ids, s_win, r_win, s_wa, r_wa, s_wm, r_wm, s_wy, r_wy, s_ws, r_ws,
    s_da, r_da, s_dm, r_dm, s_dy, r_dy, s_ds, r_ds, s_h, r_h, s_ht, r_ht, s_d, r_d,
    s_pr, r_pr, s_gd, r_gd, s_gi, r_gi, s_sm, r_sm, s_ry, r_ry, s_rm, r_rm, s_ra, r_ra,
    l_sem, hid_sem,
):
    last = steps - 1
    dp, fs = lax.axis_index("dp"), lax.axis_index("fsdp")
    z, x, y, c = dp // 2, dp % 2, fs // 2, fs % 2
    zh = z // 2
    a = z + zh * (3 - 2 * z)

    def dev(zz, xx, yy, cc):
        return (zz * 2 + xx, yy * 2 + cc)

    def block(zz, xx, yy, cc):
        return zz * 8 + xx * 4 + yy * 2 + cc

    def kx(k):
        return x + (k % 2) * (1 - 2 * x)

    def kz(k):
        return z + (k // 2) * (1 - 2 * (z % 2))

    def ka(k):
        return a + (k // 2) * (1 - 2 * a)

    def kdev(k):
        return dev(kz(k), kx(k), y, c)

    def member(k):
        return 2 * kx(k) + ka(k)

    def unit_block(k, j):
        return 2 * (ka(k) + j * (3 - 2 * ka(k))) + kx(k)

    def lanes(ub):
        return pl.ds(pl.multiple_of(256 * ub, 256), 256)

    mir, ydev, sib = dev(3 - z, x, y, c), dev(z, x, 1 - y, c), dev(z, x, y, 1 - c)
    cross = dev(3 - z, x, 1 - y, c)
    perm = dev(2 * x + y, c, z // 2, z % 2)
    back = dev(2 * y + c, z // 2, z % 2, x)
    stays = jnp.logical_and(perm[0] == dp, perm[1] == fs)
    moved = jnp.logical_not(stays)

    def rc(src, dst, ss, rs, to):
        return pltpu.make_async_remote_copy(
            src_ref=src, dst_ref=dst, send_sem=ss, recv_sem=rs, device_id=to, device_id_type=MESH
        )

    emb, vocab = emb_raw.shape[1], emb_raw.shape[0]
    w_in[...] = jnp.zeros_like(w_in)
    w_in[0:emb, :] = w_in_raw[...]
    tail = emb // 16 * 16
    part = w_in[tail : tail + 16, :].astype(F32)
    bias_row = b_in_raw[...].astype(F32).reshape(1, 256)
    part = jnp.where(lax.broadcasted_iota(jnp.int32, (16, 256), 0) == emb - tail, bias_row, part)
    w_in[tail : tail + 16, :] = part.astype(BF)
    for s in range(2):
        stack = jnp.concatenate(
            [v for ref in (chars_in, resets_in, targets_in) for v in (ref[:, s, :], jnp.zeros((8 - steps, 32), jnp.int32))],
            axis=0,
        ).astype(F32)
        wide_stack = jnp.concatenate([stack, jnp.zeros((24, 96), F32)], axis=1)
        ids_in[s] = wide_stack.T[:32, :].astype(jnp.int32)
    barrier = pltpu.get_barrier_semaphore()

    def greet(to):
        pl.semaphore_signal(barrier, inc=1, device_id=to, device_id_type=MESH)

    for k in (1, 2, 3):
        greet(kdev(k))
    for to in (mir, ydev, sib, cross):
        greet(to)

    @pl.when(moved)
    def _():
        greet(perm)
        greet(back)

    pl.semaphore_wait(barrier, 7 + 2 * moved.astype(jnp.int32))

    me = block(z, x, y, c)

    def d_slot(b):
        return WDEC.at[pl.ds(pl.multiple_of(64 * b, 64), 64), :]

    def w_cols(ub, g):
        return w_rec.at[:, lanes(8 * g + ub)]

    def w_part(j, g, b):
        return W.at[4 * j + g, pl.ds(pl.multiple_of(64 * b, 64), 64), :]

    def wa_start(k):
        for j in (0, 1):
            for g in range(4):
                rc(w_cols(unit_block(k, j), g), w_part(j, g, me), s_wa.at[k - 1, j], r_wa.at[k - 1, j], kdev(k)).start()

    def wa(k, j, b):
        part = W.at[pl.ds(4 * j, 4), pl.ds(pl.multiple_of(64 * b, 64), 64), :]
        return rc(part, part, s_wa.at[k - 1, j], r_wa.at[k - 1, j], kdev(k))

    def ids_copy(k, mem):
        return rc(ids_in, IDS.at[:, mem], s_ids.at[k - 1], r_ids.at[k - 1], kdev(k))

    def own_w(j, g):
        return pltpu.make_async_copy(w_cols(unit_block(0, j), g), w_part(j, g, me), l_sem.at[4 * j + g])

    for j in (0, 1):
        for g in range(4):
            own_w(j, g).start()
    for k in (1, 2, 3):
        ids_copy(k, member(0)).start()

    def win_perm(jj, gy, gc):
        return rc(w_in, WIN.at[jj, gy, gc], s_win.at[0], r_win.at[0], perm)

    def win_local():
        return pltpu.make_async_copy(w_in, WIN.at[x, z // 2, z % 2], l_sem.at[8])

    @pl.when(moved)
    def _():
        win_perm(x, z // 2, z % 2).start()

    @pl.when(stays)
    def _():
        win_local().start()

    for k in (1, 2, 3):
        wa_start(k)

    def w_half(j, b):
        return W.at[pl.ds(4 * j, 4), pl.ds(pl.multiple_of(64 * b, 64), 64), :]

    def to_mir(k, j):
        b = block(kz(k), kx(k), y, c)
        return rc(w_half(j, b), w_half(j, b), s_wm.at[k, j], r_wm.at[k, j], mir)

    def from_mir(k, j):
        b = block(3 - kz(k), kx(k), y, c)
        return rc(w_half(j, b), w_half(j, b), s_wm.at[k, j], r_wm.at[k, j], mir)

    def group_block(i, yy, cc):
        k, far = i % 4, i // 4
        zz = kz(k)
        return block(zz + far * (3 - 2 * zz), kx(k), yy, cc)

    def to_y(i, j):
        b = group_block(i, y, c)
        return rc(w_half(j, b), w_half(j, b), s_wy.at[i, j], r_wy.at[i, j], ydev)

    def from_y(i, j):
        b = group_block(i, 1 - y, c)
        return rc(w_half(j, b), w_half(j, b), s_wy.at[i, j], r_wy.at[i, j], ydev)

    def to_s(i, j):
        b = group_block(i % 8, y + (i // 8) * (1 - 2 * y), c)
        return rc(w_half(j, b), w_half(j, b), s_ws.at[i, j], r_ws.at[i, j], sib)

    def from_s(i, j):
        b = group_block(i % 8, y + (i // 8) * (1 - 2 * y), 1 - c)
        return rc(w_half(j, b), w_half(j, b), s_ws.at[i, j], r_ws.at[i, j], sib)

    for j in (0, 1):
        for g in range(4):
            own_w(j, g).wait()
    inner = a == 1

    @pl.when(inner)
    def _():
        for j in (0, 1):
            to_mir(0, j).start()

    for j in (0, 1):
        to_y(0, j).start()
        to_s(0, j).start()

    def win_mir(jj):
        return rc(WIN.at[jj, y, c], WIN.at[jj, y, c], s_win.at[1], r_win.at[1], mir)

    def win_y(yy):
        return rc(WIN.at[:, yy, c], WIN.at[:, yy, c], s_win.at[2], r_win.at[2], ydev)

    def win_s(cc):
        return rc(WIN.at[:, :, cc], WIN.at[:, :, cc], s_win.at[3], r_win.at[3], sib)

    @pl.when(moved)
    def _():
        win_perm(zh, y, c).wait_recv()

    @pl.when(stays)
    def _():
        win_local().wait()

    win_mir(zh).start()


    IDS[:, member(0)] = ids_in[...]

    def own_blocks(k):
        for j in (0, 1):
            wa(k, j, block(kz(k), kx(k), y, c)).wait_recv()
            to_y(k, j).start()

            @pl.when(inner)
            def _(j=j):
                to_mir(k, j).start()

            to_s(k, j).start()

    own_blocks(1)
    own_blocks(2)
    own_blocks(3)

    def da(k, b):
        return rc(w_dec, d_slot(b), s_da.at[k - 1], r_da.at[k - 1], kdev(k))

    emb_p[...] = jnp.zeros_like(emb_p)
    emb_p[0:vocab, 0:emb] = emb_raw[...]
    unit = jnp.where(
        lax.broadcasted_iota(jnp.int32, (EPAD, EPAD), 0) == lax.broadcasted_iota(jnp.int32, (EPAD, EPAD), 1), 1.0, 0.0
    ).astype(BF)
    turned = mm(unit, emb_p[...], NT)
    emb_t[...] = jnp.where(lax.broadcasted_iota(jnp.int32, (EPAD, VPAD), 0) == emb, 1.0, turned).astype(BF)
    w_dec[...] = jnp.zeros_like(w_dec)
    w_dec[:, :vocab] = w_dec_raw[...]
    bias_dec[...] = jnp.full_like(bias_dec, -1e30)
    bias_dec[0:1, :vocab] = bias_raw[...].astype(F32).reshape(1, vocab)
    for k in (1, 2, 3):
        da(k, me).start()
    own_dec = pltpu.make_async_copy(w_dec, d_slot(me), l_sem.at[9])
    own_dec.start()

    for k in (1, 2, 3):
        ids_copy(k, member(k)).wait_recv()
    lane = lax.broadcasted_iota(jnp.int32, (rows, 24), 1)
    wide = lax.broadcasted_iota(jnp.int32, (rows, VPAD), 1).astype(F32)

    def column(at, s):
        packed = IDS[s].reshape(rows, 24)
        return jnp.sum(jnp.where(lane == at, packed, 0).astype(F32), axis=1, keepdims=True)

    def keep_of(t, s):
        return 1.0 - column(8 + t, s)

    def letter(t, s):
        return jnp.where(column(t, s) == wide, 1.0, 0.0).astype(BF)

    EMBT[...] = jnp.zeros_like(EMBT)
    LV[...] = jnp.zeros_like(LV)
    BD[...] = jnp.zeros_like(BD)
    GWD[...] = jnp.zeros_like(GWD)
    DWI[...] = jnp.zeros_like(DWI)
    DCN[...] = jnp.zeros_like(DCN)

    win_mir(1 - zh).wait_recv()

    win_y(y).start()
    def pass_y(i):
        for j in (0, 1):
            from_y(i, j).wait_recv()
            to_s(8 + i, j).start()

    def pass_mir(k):
        for j in (0, 1):
            from_mir(k, j).wait_recv()
            to_y(4 + k, j).start()
            to_s(4 + k, j).start()

    for i in range(3):
        pass_y(i)

    @pl.when(inner)
    def _():
        pass_mir(0)

    @pl.when(jnp.logical_not(inner))
    def _():
        for k in range(4):
            for j in (0, 1):
                to_mir(k, j).start()

    pass_y(3)
    win_y(1 - y).wait_recv()
    win_s(c).start()
    win_s(1 - c).wait_recv()

    def h_copy(t, s, k, j, ub):
        part = H.at[t % RING, s, :, lanes(ub)]
        return rc(part, part, s_h.at[t, s, k - 1, j], r_h.at[t, s, k - 1, j], kdev(k))

    def wait_h(t, s):
        for k in (1, 2, 3):
            for j in (0, 1):
                h_copy(t, s, k, j, unit_block(k, j)).wait_recv()

    def gates(t, s, first):
        keep = None if first else keep_of(t, s)
        feature = mm(letter(t, s), emb_t[...], NT).astype(BF)
        for j in (0, 1):
            pre = []
            for g in range(4):
                drive = mm(feature, WIN[j, g // 2, g % 2], NN)
                if not first:
                    drive = drive + keep * mm(H[(t - 1) % RING, s], W[4 * j + g], NN)
                pre.append(drive)
            s_i, s_f, t_g, s_o = sigmoid(pre[0]), sigmoid(pre[1]), jnp.tanh(pre[2]), sigmoid(pre[3])
            cell = s_i * t_g
            if not first:
                cell = s_f * (C[t - 1, s, j] * keep) + cell
            for g, v in enumerate((s_i, s_f, t_g, s_o)):
                A[t, s, 4 * j + g] = v
            C[t, s, j] = cell
            ub = unit_block(0, j)
            H[t % RING, s, :, lanes(ub)] = (s_o * jnp.tanh(cell)).astype(BF)
            for k in (3, 1, 2):
                h_copy(t, s, k, j, ub).start()

    gates(0, 0, True)
    gates(0, 1, True)

    @pl.when(jnp.logical_not(inner))
    def _():
        pass_mir(0)

    for k in (1, 2, 3):
        pass_mir(k)

    def dec_mir(k, far):
        zz = kz(k)
        b = block(zz + far * (3 - 2 * zz), kx(k), y, c)
        return rc(d_slot(b), d_slot(b), s_dm.at[k], r_dm.at[k], mir)

    def dec_y(i, yy):
        b = group_block(i, yy, c)
        return rc(d_slot(b), d_slot(b), s_dy.at[i], r_dy.at[i], ydev)

    def dec_s(i, cc):
        b = group_block(i % 8, y + (i // 8) * (1 - 2 * y), cc)
        return rc(d_slot(b), d_slot(b), s_ds.at[i], r_ds.at[i], sib)

    own_dec.wait()
    dec_mir(0, 0).start()
    dec_y(0, y).start()
    dec_s(0, c).start()
    for k in (1, 2, 3):
        da(k, block(kz(k), kx(k), y, c)).wait_recv()
        dec_mir(k, 0).start()
        dec_y(k, y).start()
        dec_s(k, c).start()

    for i in (4, 5, 6, 7):
        pass_y(i)

    @pl.loop(0, 16)
    def _(i):
        for j in (0, 1):
            from_s(i, j).wait_recv()

    def released(t, s):
        hid_copy(t, s).wait()
        for k in (1, 2, 3):
            for j in (0, 1):
                h_copy(t, s, k, j, unit_block(0, j)).wait_send()

    def forward(t, s):
        wait_h(t - 1, s)

        @pl.when(t >= RING - 1)
        def _():
            released(t - (RING - 1), s)

        gates(t, s, False)

    for s in range(2):
        wait_h(0, s)
        gates(1, s, False)

    for k in range(4):
        dec_mir(k, 1).wait_recv()
        dec_y(4 + k, y).start()
        dec_s(4 + k, c).start()

    row = lax.broadcasted_iota(jnp.int32, (128, 256), 0)
    col = lax.broadcasted_iota(jnp.int32, (128, 256), 1)

    def select(cc):
        yy = y + (row // 64) * (1 - 2 * y)
        return jnp.where(col == 64 * (2 * yy + cc) + row % 64, 1.0, 0.0).astype(BF)

    def lane_slot(t, s):
        return pl.ds(pl.multiple_of((2 * t + s) * rows, rows), rows)

    def ht_copy(t, s, slot):
        return rc(HSEND.at[slot], HTS.at[:, :, lane_slot(t, s)], s_ht.at[t, s], r_ht.at[t, s], sib)

    def hid_copy(t, s):
        mine = H.at[t % RING, s, pl.ds(pl.multiple_of(32 * member(0), 32), 32), :]
        return pltpu.make_async_copy(mine, out_hid.at[s * steps + t], hid_sem.at[t, s])

    def logits_of(t, s):
        scores = mm(H[t % RING, s], WDEC[...], NN) + bias_dec[0:1, :]
        top = jnp.max(scores, axis=1, keepdims=True)
        shifted = jnp.exp(scores - top)
        summed = jnp.sum(shifted, axis=1, keepdims=True)
        goal = jnp.where(column(16 + t, s) == wide, 1.0, 0.0)
        picked = jnp.sum(goal * scores, axis=1, keepdims=True)
        LV[...] += jnp.broadcast_to(top + jnp.log(summed) - picked, (rows, 128))
        DL[t, s] = (shifted / summed - goal).astype(BF)

    def decoder_side(t, s):
        hid_copy(t, s).start()
        grad = DL[t, s]
        BD[...] += mm(jnp.ones((8, rows), BF), grad, NN)
        for j in (0, 1):
            GWD[j] += mm(H[t % RING, s, :, lanes(unit_block(0, j))], grad, TN).reshape(2, 2, 64, VPAD)

    def transposed_side(t, s):
        slot = s
        mine, other = select(c), select(1 - c)

        @pl.when(t >= 1)
        def _():
            ht_copy(t - 1, s, slot).wait_send()

        for tile in range(8):
            part = H[t % RING, s, :, 256 * tile : 256 * (tile + 1)]
            HT[tile, :, lane_slot(t, s)] = mm(mine, part, NT).astype(BF)
            HSEND[slot, tile] = mm(other, part, NT).astype(BF)
        ht_copy(t, s, slot).start()

    for s in range(2):
        wait_h(1, s)
        gates(2, s, False)

    @pl.loop(0, 8)
    def _(i):
        k, j = i // 2, i % 2
        to_mir(k, j).wait_send()
        to_y(i, 0).wait_send()
        to_y(i, 1).wait_send()

    @pl.loop(0, 16)
    def _(i):
        to_s(i, 0).wait_send()
        to_s(i, 1).wait_send()

    for i in range(8):
        dec_y(i, 1 - y).wait_recv()
        dec_s(8 + i, c).start()

    @pl.loop(0, 16)
    def _(i):
        dec_s(i, 1 - c).wait_recv()

    @pl.loop(0, 2)
    def _(s):
        logits_of(0, s)
        decoder_side(0, s)
        transposed_side(0, s)

    @pl.loop(6, 2 * steps)
    def _(i):
        t, s = i // 2, i % 2
        forward(t, s)
        logits_of(t - 2, s)
        decoder_side(t - 2, s)
        transposed_side(t - 2, s)

    @pl.loop(0, 2)
    def _(s):
        logits_of(last - 1, s)
        decoder_side(last - 1, s)
        transposed_side(last - 1, s)

    def pr_copy(t, s, k, j):
        return rc(STG.at[s, k - 1, j], PR.at[t % 2, s, k - 1, j], s_pr.at[t, s, k - 1, j], r_pr.at[t, s, k - 1, j], kdev(k))

    def d_copy(t, s):
        return rc(D.at[:, t - 1, s], DS.at[:, t - 1, s], s_d.at[t, s], r_d.at[t, s], sib)

    def backward(t, s, newest, oldest):
        if not newest:
            for k in (1, 2, 3):
                for j in (0, 1):
                    pr_copy(t + 1, s, k, j).wait_recv()
        keep = keep_of(t, s)
        for j in (0, 1):
            up = WDEC[lanes(unit_block(0, j)), :]
            dh = mm(DL[t, s], up, NT)
            if not newest:
                rest = PR[(t + 1) % 2, s, 0, j].astype(F32) + PR[(t + 1) % 2, s, 1, j].astype(F32)
                rest = rest + PR[(t + 1) % 2, s, 2, j].astype(F32)
                dh = dh + (OWN[s, j] + rest)
            s_i, s_f, t_g, s_o = (A[t, s, 4 * j + g] for g in range(4))
            t_c = jnp.tanh(C[t, s, j])
            d_o = dh * t_c
            d_c = dh * s_o * (1.0 - t_c * t_c)
            if not newest:
                d_c = d_c + DCN[s, j]
            d_i = d_c * t_g * s_i * (1.0 - s_i)
            d_g = d_c * s_i * (1.0 - t_g * t_g)
            d_o = d_o * s_o * (1.0 - s_o)
            if oldest:
                d_f = jnp.zeros_like(d_i)
            else:
                d_f = d_c * (C[t - 1, s, j] * keep) * s_f * (1.0 - s_f)
                DCN[s, j] = keep * (d_c * s_f)
            for g, v in enumerate((d_i, d_f, d_g, d_o)):
                low = v.astype(BF)
                DRAW[4 * j + g] = low
                if not oldest:
                    D[4 * j + g, t - 1, s] = low * keep.astype(BF)
        if oldest:
            return
        d_copy(t, s).start()
        if not newest:
            for k in (1, 2, 3):
                for j in (0, 1):
                    pr_copy(t + 1, s, k, j).wait_send()
        left = jnp.concatenate([D[q, t - 1, s] for q in range(8)], axis=1)
        for k in (3, 1, 2, 0):
            for j in (0, 1):
                ub = unit_block(k, j)
                if newest and s == 0:
                    for q in range(8):
                        W[q, lanes(ub), :] = W[q, lanes(ub), :].T
                total = mm(left, W[:, lanes(ub), :].reshape(8 * 256, 256), NN)
                if k == 0:
                    OWN[s, j] = total
                else:
                    STG[s, k - 1, j] = total.astype(BF)
                    pr_copy(t, s, k, j).start()

    def input_side(t, s):
        onehot = letter(t, s)
        feat_t = mm(emb_t[...], onehot, NT).astype(BF)
        inputs = []
        for q in range(8):
            jj, gy, gc = q // 4, (q // 2) % 2, q % 2
            DWI[jj, gy, gc] += mm(feat_t, DRAW[q], NN)
            inputs.append(WIN[jj, gy, gc])
        grad_t = mm(jnp.concatenate(inputs, axis=1), jnp.concatenate([DRAW[q] for q in range(8)], axis=1), NT)
        high = grad_t.astype(BF)
        low = (grad_t - high.astype(F32)).astype(BF)
        EMBT[...] += mm(high, onehot, NN) + mm(low, onehot, NN)

    for s in range(2):
        wait_h(last, s)
        logits_of(last, s)
        backward(last, s, True, False)
        input_side(last, s)
    for s in range(2):
        decoder_side(last, s)

    def gd_s():
        return rc(GWD.at[:, :, 1 - c], GS, s_gd.at[0], r_gd.at[0], sib)

    def gd_y():
        return rc(GWD.at[:, 1 - y, c], GY, s_gd.at[1], r_gd.at[1], ydev)

    def gd_m():
        return rc(GWD.at[1 - zh, y, c], GM, s_gd.at[2], r_gd.at[2], mir)

    gd_s().start()

    @pl.loop(0, 2 * (steps - 2))
    def _(i):
        t, s = last - 1 - i // 2, i % 2
        backward(t, s, False, False)
        input_side(t, s)

        @pl.when(i == 1)
        def _():
            gd_s().wait_recv()
            GWD[:, :, c] += GS[...]
            gd_y().start()

        @pl.when(i == 3)
        def _():
            gd_y().wait_recv()
            GWD[:, y, c] += GY[...]
            gd_m().start()

        @pl.when(i == 5)
        def _():
            gd_m().wait_recv()
            out_dec[...] = GWD[zh, y, c] + GM[...]

    @pl.loop(0, 2 * (steps - 1))
    def _(i):
        ht_copy(i // 2, i % 2, 0).wait_recv()
        d_copy(1 + i // 2, i % 2).wait_recv()

    depth = 2 * (steps - 1) * rows

    def kept(q):
        return A.at[2 + q // 4, (q % 4) // 2, :, pl.ds(pl.multiple_of(64 * (q % 2), 64), 64), :]

    def tile_of(q):
        k, near = q % 4, q // 4
        zz = kz(k)
        return 2 * (3 - zz + near * (2 * zz - 3)) + kx(k)

    def ry_copy(p, q):
        return rc(SY.at[p % 4], RY.at[q], s_ry.at[p], r_ry.at[q], ydev)

    def rm_copy(k):
        return rc(SM.at[k], RM.at[k], s_rm.at[k], r_rm.at[k], mir)

    def ra_copy(k):
        return rc(SM.at[k], out_recv.at[k - 1], s_ra.at[k - 1], r_ra.at[k - 1], kdev(k))

    def order(p):
        return (3, 2, 1, 0, 7, 6, 5, 4)[p]

    def make_tile(p):
        q = order(p)
        tile = tile_of(q)
        left, right = HT[tile], HTS[tile]
        hold = kept(q)
        if p >= 4:
            ry_copy(p - 4, order(p - 4)).wait_send()
        for n in range(8):
            grad = mm(left, D[n].reshape(depth, 256), NN) + mm(right, DS[n].reshape(depth, 256), NN)
            hold[n] = grad[:64]
            SY[p % 4, n] = grad[64:].astype(BF)
        ry_copy(p, q).start()

    def add_y(q):
        ry_copy(0, q).wait_recv()
        hold = kept(q)
        hold[...] = hold[...] + RY[q].astype(F32)

    for p in range(3):
        make_tile(p)

    def pass_on(k):
        add_y(k)
        SM[k] = kept(k)[...].astype(BF)
        rm_copy(k).start()

    for s in range(2):
        backward(0, s, False, True)
        input_side(0, s)

    leader = jnp.logical_and(x == 0, a == 0)
    high_row = lax.broadcasted_iota(jnp.int32, (8, VPAD), 0)
    loss = jnp.sum(LV[...], axis=0, keepdims=True)
    loss = jnp.concatenate([loss] * (VPAD // 128), axis=1)
    extra = jnp.where(high_row == 0, BD[...], jnp.where(high_row == 1, loss, 0.0))
    out_small[...] = EMBT[...]
    out_small[SMALL - 8 : SMALL] = jnp.where(leader, extra, 0.0)

    def core_rows(cc):
        return pl.ds(pl.multiple_of(64 * cc, 64), 64)

    def piece_rows(k):
        return pl.ds(pl.multiple_of(64 * c + 16 * member(k), 16), 16)

    def sm_core():
        return rc(out_small.at[core_rows(1 - c)], RS1, s_sm.at[0], r_sm.at[0], sib)

    def sm_group(k):
        return rc(out_small.at[piece_rows(k)], RS2.at[k - 1], s_sm.at[k], r_sm.at[k], kdev(k))

    def sm_quarter(n):
        return rc(PIECE, RS3.at[n], s_sm.at[4 + n], r_sm.at[4 + n], (ydev, mir, cross)[n])

    def sm_spread(k):
        return rc(TOTAL, RS4.at[k - 1], s_sm.at[6 + k], r_sm.at[6 + k], kdev(k))

    def sm_last():
        return rc(out_small.at[core_rows(c)], RS5, s_sm.at[10], r_sm.at[10], sib)

    def sm_step1():
        sm_core().wait_recv()
        out_small[core_rows(c)] = out_small[core_rows(c)] + RS1[...]
        for k in (1, 2, 3):
            sm_group(k).start()

    def sm_step2():
        for k in (1, 2, 3):
            sm_group(k).wait_recv()
        PIECE[...] = (out_small[piece_rows(0)] + RS2[0]) + (RS2[1] + RS2[2])
        for n in range(3):
            sm_quarter(n).start()

    def sm_step3():
        for n in range(3):
            sm_quarter(n).wait_recv()
        TOTAL[...] = (PIECE[...] + RS3[0]) + (RS3[1] + RS3[2])
        for k in (1, 2, 3):
            sm_spread(k).start()

    def sm_step4():
        sm_core().wait_send()
        for k in (1, 2, 3):
            sm_group(k).wait_send()
            sm_spread(k).wait_recv()
            out_small[piece_rows(k)] = RS4[k - 1]
        out_small[piece_rows(0)] = TOTAL[...]
        sm_last().start()

    def sm_step5():
        sm_last().wait_recv()
        out_small[core_rows(1 - c)] = RS5[...]

    sm_core().start()

    live = pl.ds(0, 104)

    def gi_s():
        return rc(DWI.at[:, :, 1 - c, live], IS, s_gi.at[0], r_gi.at[0], sib)

    def gi_y():
        return rc(DWI.at[:, 1 - y, c, live], IY, s_gi.at[1], r_gi.at[1], ydev)

    def gi_m():
        return rc(DWI.at[1 - zh, y, c, live], IM, s_gi.at[2], r_gi.at[2], mir)

    def gi_p():
        return rc(DWI.at[zh, y, c, live], out_in, s_gi.at[3], r_gi.at[3], back)

    gi_s().start()

    def finish(k):
        add_y(4 + k)
        rm_copy(k).wait_recv()
        total = kept(4 + k)[...] + RM[k].astype(F32)
        if k == 0:
            out_own[...] = total
        else:
            rm_copy(k).wait_send()
            SM[k] = total.astype(BF)
            ra_copy(k).start()

    def settle(p):
        q = order(p)
        pass_on(q) if q < 4 else finish(q - 4)

    make_tile(3)
    sm_step1()
    gi_s().wait_recv()
    DWI[:, :, c, 0:104] = DWI[:, :, c, 0:104] + IS[...]
    gi_y().start()
    settle(0)
    make_tile(4)
    sm_step2()
    settle(1)
    make_tile(5)
    settle(2)
    make_tile(6)
    gi_y().wait_recv()
    DWI[:, y, c, 0:104] = DWI[:, y, c, 0:104] + IY[...]
    gi_m().start()
    settle(3)
    make_tile(7)
    sm_step3()
    settle(4)
    settle(5)
    sm_step4()
    settle(6)
    gi_m().wait_recv()
    DWI[zh, y, c, 0:104] = DWI[zh, y, c, 0:104] + IM[...]

    @pl.when(moved)
    def _():
        gi_p().start()

    @pl.when(stays)
    def _():
        out_in[...] = DWI[zh, y, c, 0:104]

    settle(7)
    sm_step5()

    for k in (1, 2, 3):
        for j in (0, 1):
            wa(k, j, me).wait_send()
            for s in range(2):
                pr_copy(1, s, k, j).wait_send()
        ids_copy(k, member(0)).wait_send()
        da(k, me).wait_send()
        ra_copy(k).wait()
    rm_copy(0).wait_send()

    @pl.when(moved)
    def _():
        gi_p().wait()
        win_perm(x, z // 2, z % 2).wait_send()

    win_mir(zh).wait_send()
    win_y(y).wait_send()
    win_s(c).wait_send()
    for k in (1, 2, 3):
        sm_quarter(k - 1).wait_send()
        sm_spread(k).wait_send()
    for copy in (gd_s, gd_y, gd_m, gi_s, gi_y, gi_m, sm_last):
        copy().wait_send()
    for s in range(2):
        ht_copy(last - 1, s, s).wait_send()

    @pl.loop(0, 4)
    def _(k):
        dec_mir(k, 0).wait_send()

    @pl.loop(0, 8)
    def _(i):
        dec_y(i, y).wait_send()

    for p in range(4, 8):
        ry_copy(p, order(p)).wait_send()

    @pl.loop(0, 16)
    def _(i):
        dec_s(i, c).wait_send()

    @pl.loop(2 * (steps - RING + 1), 2 * steps)
    def _(i):
        released(i // 2, i % 2)

    @pl.loop(0, 2 * (steps - 1))
    def _(i):
        d_copy(1 + i // 2, i % 2).wait_send()


def output_kernel(
    scale, own, recv, g_in, g_dec, hid_in, small, hid, table, o_in, o_bias, o_rec, o_dec, o_bias_dec, loss,
    h_buf, own_buf, recv_buf, rec_buf, in_sem, out_sem,
):
    dp = lax.axis_index("dp")
    z, x = dp // 2, dp % 2
    a = z + (z // 2) * (3 - 2 * z)
    parts = hid_in.shape[0]

    def hid_load(i):
        return pltpu.make_async_copy(hid_in.at[i], h_buf.at[i], in_sem.at[i])

    def hid_store(i):
        return pltpu.make_async_copy(h_buf.at[i], hid.at[i], out_sem.at[i])

    def rec_load(k):
        if k == 0:
            return pltpu.make_async_copy(own, own_buf, in_sem.at[parts])
        return pltpu.make_async_copy(recv.at[k - 1], recv_buf.at[k - 1], in_sem.at[parts + k])

    def cols(k, j, g):
        xk, ak = x + (k % 2) * (1 - 2 * x), a + (k // 2) * (1 - 2 * a)
        ub = 2 * (ak + j * (3 - 2 * ak)) + xk
        return pl.ds(pl.multiple_of(256 * (8 * g + ub), 256), 256)

    for k in range(4):
        rec_load(k).start()
    for i in range(parts):
        hid_load(i).start()
    vocab, emb = table.shape
    table[...] = small[0:SMALL, :].T[:vocab, :emb]
    o_in[...] = g_in[0:emb, :]
    o_bias[...] = g_in[emb, :]
    o_dec[...] = g_dec[:, :vocab]
    o_bias_dec[...] = small[SMALL - 8, :vocab]
    loss[...] = small[SMALL - 7 : SMALL - 6, 0:1] * scale
    for k in range(4):
        rec_load(k).wait()
        for j in (0, 1):
            for g in range(4):
                part = own_buf[4 * j + g] if k == 0 else recv_buf[k - 1, 4 * j + g].astype(F32)
                rec_buf[:, cols(k, j, g)] = part
    rec_store = pltpu.make_async_copy(rec_buf, o_rec, out_sem.at[parts])
    rec_store.start()
    for i in range(parts):
        hid_load(i).wait()
        hid_store(i).start()
    for i in range(parts):
        hid_store(i).wait()
    rec_store.wait()


def fused(chars, resets, targets, embed, w_in, bias_in, w_rec, w_dec, bias_dec):
    micro, count, steps = chars.shape
    own_rows, gate_cols = w_rec.shape
    vocab, emb = embed.shape
    width = gate_cols // 4
    members = 4
    rows = count * members
    vm = pl.BlockSpec(memory_space=pltpu.VMEM)
    hbm = pl.BlockSpec(memory_space=pl.ANY)
    dma = pltpu.SemaphoreType.DMA
    n = steps - 1
    scratch = [
        pltpu.VMEM((8, width, 256), BF),
        pltpu.VMEM((2, 2, 2, EPAD, 256), BF),
        pltpu.VMEM((width, VPAD), BF),
        pltpu.VMEM((micro, members, count, 24), jnp.int32),
        pltpu.VMEM((RING, micro, rows, width), BF),
        pltpu.VMEM((8, 128, 2 * n * rows), BF),
        pltpu.VMEM((8, 128, 2 * n * rows), BF),
        pltpu.VMEM((2, 8, 128, rows), BF),
        pltpu.VMEM((steps, micro, 8, rows, 256), F32),
        pltpu.VMEM((steps, micro, 2, rows, 256), F32),
        pltpu.VMEM((8, n, micro, rows, 256), BF),
        pltpu.VMEM((8, n, micro, rows, 256), BF),
        pltpu.VMEM((8, rows, 256), BF),
        pltpu.VMEM((steps, micro, rows, VPAD), BF),
        pltpu.VMEM((micro, count, 24), jnp.int32),
        pltpu.VMEM((EPAD, 256), BF),
        pltpu.VMEM((EPAD, VPAD), BF),
        pltpu.VMEM((VPAD, EPAD), BF),
        pltpu.VMEM((own_rows, VPAD), BF),
        pltpu.VMEM((8, VPAD), F32),
        pltpu.VMEM((2, micro, 3, 2, rows, 256), BF),
        pltpu.VMEM((micro, 3, 2, rows, 256), BF),
        pltpu.VMEM((micro, 2, rows, 256), F32),
        pltpu.VMEM((micro, 2, rows, 256), F32),
        pltpu.VMEM((4, 8, 64, 256), BF),
        pltpu.VMEM((8, 8, 64, 256), BF),
        pltpu.VMEM((4, 8, 64, 256), BF),
        pltpu.VMEM((4, 8, 64, 256), BF),
        pltpu.VMEM((EPAD, VPAD), F32),
        pltpu.VMEM((rows, 128), F32),
        pltpu.VMEM((8, VPAD), F32),
        pltpu.VMEM((2, 2, 2, 64, VPAD), F32),
        pltpu.VMEM((2, 2, 64, VPAD), F32),
        pltpu.VMEM((2, 64, VPAD), F32),
        pltpu.VMEM((64, VPAD), F32),
        pltpu.VMEM((2, 2, 2, EPAD, 256), F32),
        pltpu.VMEM((2, 2, 104, 256), F32),
        pltpu.VMEM((2, 104, 256), F32),
        pltpu.VMEM((104, 256), F32),
        pltpu.VMEM((64, VPAD), F32),
        pltpu.VMEM((3, 16, VPAD), F32),
        pltpu.VMEM((3, 16, VPAD), F32),
        pltpu.VMEM((3, 16, VPAD), F32),
        pltpu.VMEM((64, VPAD), F32),
        pltpu.VMEM((16, VPAD), F32),
        pltpu.VMEM((16, VPAD), F32),
    ]
    shapes = [
        (3,), (4,), (3, 2), (4, 2), (8, 2), (16, 2), (3,), (4,), (8,), (16,),
        (steps, 2, 3, 2), (n, 2), (steps, 2), (steps, 2, 3, 2), (3,), (4,), (11,), (8,), (4,), (3,),
    ]
    for shape in shapes:
        scratch += [dma(shape), dma(shape)]
    scratch += [dma((12,)), dma((steps, 2))]
    out_own, out_recv, out_in, out_dec, out_hid, out_small = pl.pallas_call(
        functools.partial(lstm_kernel, steps, rows),
        out_shape=(
            jax.ShapeDtypeStruct((8, own_rows, 256), F32),
            jax.ShapeDtypeStruct((3, 8, own_rows, 256), BF),
            jax.ShapeDtypeStruct((104, 256), F32),
            jax.ShapeDtypeStruct((own_rows, VPAD), F32),
            jax.ShapeDtypeStruct((micro * steps, count, width), BF),
            jax.ShapeDtypeStruct((EPAD, VPAD), F32),
        ),
        in_specs=[hbm] + [vm] * 8,
        out_specs=(vm, hbm, vm, vm, hbm, vm),
        scratch_shapes=scratch,
        compiler_params=pltpu.CompilerParams(
            collective_id=0, has_side_effects=True, vmem_limit_bytes=66 * 1000 * 1000
        ),
    )(
        w_rec, w_in, bias_in, w_dec, embed, bias_dec,
        chars.transpose(2, 0, 1), resets.transpose(2, 0, 1), targets.transpose(2, 0, 1),
    )
    everyone = lax.axis_size(("dp", "fsdp"))
    hid, table, g_in, g_bias, g_rec, g_dec, g_bias_dec, loss = pl.pallas_call(
        functools.partial(output_kernel, 1.0 / (micro * count * steps * everyone)),
        out_shape=(
            jax.ShapeDtypeStruct((micro * steps, count, width), BF),
            jax.ShapeDtypeStruct((vocab, emb), F32),
            jax.ShapeDtypeStruct((emb, 256), F32),
            jax.ShapeDtypeStruct((256,), F32),
            jax.ShapeDtypeStruct((own_rows, gate_cols), F32),
            jax.ShapeDtypeStruct((own_rows, vocab), F32),
            jax.ShapeDtypeStruct((vocab,), F32),
            jax.ShapeDtypeStruct((1, 1), F32),
        ),
        in_specs=[hbm, hbm, vm, vm, hbm, vm],
        out_specs=(hbm, vm, vm, vm, hbm, vm, vm, vm),
        scratch_shapes=[
            pltpu.VMEM((micro * steps, count, width), BF),
            pltpu.VMEM((8, own_rows, 256), F32),
            pltpu.VMEM((3, 8, own_rows, 256), BF),
            pltpu.VMEM((own_rows, gate_cols), F32),
            dma((micro * steps + 4,)),
            dma((micro * steps + 1,)),
        ],
    )(out_own, out_recv, out_in, out_dec, out_hid, out_small)
    return (
        loss.reshape(()),
        hid.reshape(micro, steps, count, width).transpose(0, 2, 1, 3),
        table,
        g_in,
        g_bias,
        g_rec,
        g_dec,
        g_bias_dec,
    )


def dot_plain(left, right):
    return jnp.dot(left, right, preferred_element_type=jnp.float32)


def dot_right_t(left, right):
    return lax.dot_general(
        left, right, (((1,), (1,)), ((), ())), preferred_element_type=jnp.float32
    )


def dot_left_t(left, right):
    return lax.dot_general(
        left, right, (((0,), (0,)), ((), ())), preferred_element_type=jnp.float32
    )


def lstm_forward(weights, embed, bias_dec, ids, marks, goals):
    w_rec, w_dec, w_in, bias_in = weights
    count, steps = ids.shape
    width = w_rec.shape[0]
    letters = jnp.arange(embed.shape[0], dtype=jnp.int32)
    onehot = (ids.T.reshape(-1)[:, None] == letters[None, :]).astype(jnp.bfloat16)
    feature = dot_plain(onehot, embed).astype(jnp.bfloat16)
    drives = (dot_plain(feature, w_in) + bias_in.astype(jnp.float32)).reshape(steps, count, -1)
    keeps = (1 - marks.T).astype(jnp.float32)[:, :, None]

    def advance(state, slot):
        hidden_now, cell = state
        drive, keep_now = slot
        prev_hidden = hidden_now * keep_now.astype(jnp.bfloat16)
        prev_cell = cell * keep_now
        pre = drive + dot_plain(prev_hidden, w_rec)
        gin, gforget, gcand, gout = jnp.split(pre, 4, axis=1)
        cell_new = jax.nn.sigmoid(gforget) * prev_cell + jax.nn.sigmoid(gin) * jnp.tanh(gcand)
        hid_new = (jax.nn.sigmoid(gout) * jnp.tanh(cell_new)).astype(jnp.bfloat16)
        return ((hid_new, cell_new), (pre, prev_hidden, prev_cell, cell_new, hid_new))

    start = (jnp.zeros((count, width), jnp.bfloat16), jnp.zeros((count, width), jnp.float32))
    state, saved = lax.scan(advance, start, (drives, keeps))
    pres, prev_hiddens, prev_cells, cells, hiddens = saved
    flat_hidden = hiddens.reshape(steps * count, width)
    logits = dot_plain(flat_hidden, w_dec) + bias_dec.astype(jnp.float32)
    top = jnp.max(logits, axis=1, keepdims=True)
    shifted = jnp.exp(logits - top)
    summed = jnp.sum(shifted, axis=1, keepdims=True)
    goal_hot = (goals.T.reshape(-1)[:, None] == letters[None, :]).astype(jnp.float32)
    loss_part = jnp.sum(top[:, 0] + jnp.log(summed[:, 0])) - jnp.sum(goal_hot * logits)
    d_logits = (shifted / summed - goal_hot).astype(jnp.bfloat16)
    kept = (pres, prev_hiddens, prev_cells, cells, keeps, flat_hidden, d_logits, feature, onehot)
    return (kept, loss_part, jnp.transpose(hiddens, (1, 0, 2)))


def lstm_backward(weights, kept):
    w_rec, w_dec, w_in, bias_in = weights
    pres, prev_hiddens, prev_cells, cells, keeps, flat_hidden, d_logits, feature, onehot = kept
    steps, count, width = cells.shape
    from_dec = dot_right_t(d_logits, w_dec).reshape(steps, count, width)

    def retreat(carry, slot):
        grad_h, grad_c = carry
        pre, prev_cell, cell, extra, keep_now = slot
        gin, gforget, gcand, gout = jnp.split(pre, 4, axis=1)
        sig_in = jax.nn.sigmoid(gin)
        sig_forget = jax.nn.sigmoid(gforget)
        sig_out = jax.nn.sigmoid(gout)
        tan_cand = jnp.tanh(gcand)
        tan_cell = jnp.tanh(cell)
        grad_hid = extra + grad_h
        grad_out = grad_hid * tan_cell
        grad_cell = grad_c + grad_hid * sig_out * (1.0 - tan_cell * tan_cell)
        d_pre = jnp.concatenate(
            [
                grad_cell * tan_cand * sig_in * (1.0 - sig_in),
                grad_cell * prev_cell * sig_forget * (1.0 - sig_forget),
                grad_cell * sig_in * (1.0 - tan_cand * tan_cand),
                grad_out * sig_out * (1.0 - sig_out),
            ],
            axis=1,
        ).astype(jnp.bfloat16)
        back_h = dot_right_t(d_pre, w_rec) * keep_now
        back_c = grad_cell * sig_forget * keep_now
        return ((back_h, back_c), d_pre)

    start = (jnp.zeros((count, width), jnp.float32), jnp.zeros((count, width), jnp.float32))
    state, d_pres = lax.scan(
        retreat, start, (pres, prev_cells, cells, from_dec, keeps), reverse=True
    )
    flat_pre = d_pres.reshape(steps * count, -1)
    grad_dec = dot_left_t(flat_hidden, d_logits)
    grad_in = dot_left_t(feature, flat_pre)
    grad_bias = jnp.sum(flat_pre.astype(jnp.float32), axis=0)
    grad_feature = dot_right_t(flat_pre, w_in)
    grad_table = lax.dot_general(
        onehot.astype(jnp.float32),
        grad_feature,
        (((0,), (0,)), ((), ())),
        precision=lax.Precision.HIGHEST,
        preferred_element_type=jnp.float32,
    )
    grad_bias_out = jnp.sum(d_logits.astype(jnp.float32), axis=0)
    flat_prev = prev_hiddens.reshape(steps * count, width)
    return (grad_dec, grad_in, grad_bias, grad_table, grad_bias_out, flat_prev, flat_pre)


def general(chars, resets, targets, embed, w_in, bias_in, w_rec, w_dec, bias_dec):
    micro, count, steps = chars.shape
    everyone = lax.axis_size(("dp", "fsdp"))
    sums = None
    prev_list = []
    pre_list = []
    hidden_list = []
    for index in range(micro):
        forward_set = (
            lax.all_gather(w_rec, ("dp", "fsdp"), axis=0, tiled=True),
            lax.all_gather(w_dec, ("dp", "fsdp"), axis=0, tiled=True),
            lax.all_gather(w_in, ("dp", "fsdp"), axis=1, tiled=True),
            lax.all_gather(bias_in, ("dp", "fsdp"), axis=0, tiled=True),
        )
        kept, loss_part, hiddens = lstm_forward(
            forward_set, embed, bias_dec, chars[index], resets[index], targets[index]
        )
        backward_set = (
            lax.all_gather(w_rec, ("dp", "fsdp"), axis=0, tiled=True),
            lax.all_gather(w_dec, ("dp", "fsdp"), axis=0, tiled=True),
            lax.all_gather(w_in, ("dp", "fsdp"), axis=1, tiled=True),
            lax.all_gather(bias_in, ("dp", "fsdp"), axis=0, tiled=True),
        )
        grad_dec, grad_in, grad_bias, grad_table, grad_bias_out, flat_prev, flat_pre = (
            lstm_backward(backward_set, kept)
        )
        pieces = (grad_dec, grad_in, grad_bias, grad_table, grad_bias_out, loss_part)
        if sums is None:
            sums = pieces
        else:
            sums = tuple((first + second for first, second in zip(sums, pieces)))
        prev_list.append(flat_prev)
        pre_list.append(flat_pre)
        hidden_list.append(hiddens)
    prev_all = jnp.concatenate(prev_list, axis=0)
    pre_all = jnp.concatenate(pre_list, axis=0)
    grad_w_rec = lax.psum_scatter(
        dot_left_t(prev_all, pre_all), ("dp", "fsdp"), scatter_dimension=0, tiled=True
    )
    grad_w_dec, grad_w_in, grad_bias_in = (
        lax.psum_scatter(sums[0], ("dp", "fsdp"), scatter_dimension=0, tiled=True),
        lax.psum_scatter(sums[1], ("dp", "fsdp"), scatter_dimension=1, tiled=True),
        lax.psum_scatter(sums[2], ("dp", "fsdp"), scatter_dimension=0, tiled=True),
    )
    grad_embed, grad_bias_dec, total = lax.psum((sums[3], sums[4], sums[5]), ("dp", "fsdp"))
    loss = total / (micro * count * steps * everyone)
    hidden = jnp.stack(hidden_list, axis=0)
    return (
        loss,
        hidden,
        grad_embed,
        grad_w_in,
        grad_bias_in,
        grad_w_rec,
        grad_w_dec,
        grad_bias_dec,
    )


def solution(mesh):
    per_device = fused if (mesh.shape["dp"], mesh.shape["fsdp"]) == (8, 4) else general
    return jax.shard_map(
        per_device,
        mesh=mesh,
        in_specs=(
            P(None, ("dp", "fsdp"), None),
            P(None, ("dp", "fsdp"), None),
            P(None, ("dp", "fsdp"), None),
            P(),
            P(None, ("dp", "fsdp")),
            P(("dp", "fsdp")),
            P(("dp", "fsdp"), None),
            P(("dp", "fsdp"), None),
            P(),
        ),
        out_specs=(
            P(),
            P(None, ("dp", "fsdp"), None, None),
            P(),
            P(None, ("dp", "fsdp")),
            P(("dp", "fsdp")),
            P(("dp", "fsdp"), None),
            P(("dp", "fsdp"), None),
            P(),
        ),
        check_vma=False,
    )
```

```python
import functools

import jax
import jax.numpy as jnp
from jax import lax
from jax.experimental import pallas as pl
from jax.experimental.pallas import tpu as pltpu
from jax.sharding import PartitionSpec as P

MESH = pl.DeviceIdType.MESH
NN = ((1,), (0,))
NT = ((1,), (1,))
TN = ((0,), (0,))
F32 = jnp.float32
BF = jnp.bfloat16

VPAD = 384
EPAD = 128
RING = 4
SMALL = 112


def mm(left, right, dims):
    return lax.dot_general(left, right, (dims, ((), ())), preferred_element_type=F32)


def sigmoid(v):
    return 0.5 * jnp.tanh(0.5 * v) + 0.5


def lstm_kernel(
    steps, rows,
    w_rec, w_in_raw, b_in_raw, w_dec_raw, emb_raw, bias_raw, chars_in, resets_in, targets_in,
    out_own, out_recv, out_in, out_dec, out_hid, out_small,
    W, WIN, WDEC, IDS, H, HT, HTS, HSEND, A, C, D, DS, DRAW, DL,
    ids_in, w_in, emb_t, w_dec, bias_dec, PR, STG, OWN, DCN, SY, RY, SM, RM, EMBT, LV, BD, GWD, GIS, GY, GM, DWI, IY, SIM, IM, RS1, RS2, RS3, RS4, RS5, PIECE, TOTAL,
    s_ids, r_ids, s_win, r_win, s_wa, r_wa, s_wm, r_wm, s_wy, r_wy, s_ws, r_ws,
    s_da, r_da, s_dm, r_dm, s_dy, r_dy, s_ds, r_ds, s_h, r_h, s_ht, r_ht, s_d, r_d,
    s_pr, r_pr, s_gd, r_gd, s_gi, r_gi, s_sm, r_sm, s_ry, r_ry, s_rm, r_rm, s_ra, r_ra,
    l_sem, hid_sem,
):
    last = steps - 1
    dp, fs = lax.axis_index("dp"), lax.axis_index("fsdp")
    z, x, y, c = dp // 2, dp % 2, fs // 2, fs % 2
    zh = z // 2
    a = z + zh * (3 - 2 * z)

    def dev(zz, xx, yy, cc):
        return (zz * 2 + xx, yy * 2 + cc)

    def kx(k):
        return x + (k % 2) * (1 - 2 * x)

    def kz(k):
        return z + (k // 2) * (1 - 2 * (z % 2))

    def ka(k):
        return a + (k // 2) * (1 - 2 * a)

    def kdev(k):
        return dev(kz(k), kx(k), y, c)

    def member(k):
        return 2 * kx(k) + ka(k)

    def unit_block(k, j):
        return 2 * (ka(k) + j * (3 - 2 * ka(k))) + kx(k)

    def lanes(ub):
        return pl.ds(pl.multiple_of(256 * ub, 256), 256)

    def place(k, far, yy, cc):
        return 4 * (2 * k + zh + far * (1 - 2 * zh)) + 2 * yy + cc

    def span(k, j):
        return slice(256 * (2 * k + j), 256 * (2 * k + j + 1))

    mir, ydev, sib = dev(3 - z, x, y, c), dev(z, x, 1 - y, c), dev(z, x, y, 1 - c)
    cross = dev(3 - z, x, 1 - y, c)
    perm = dev(2 * x + y, c, z // 2, z % 2)
    back = dev(2 * y + c, z // 2, z % 2, x)
    stays = jnp.logical_and(perm[0] == dp, perm[1] == fs)
    moved = jnp.logical_not(stays)

    def rc(src, dst, ss, rs, to):
        return pltpu.make_async_remote_copy(
            src_ref=src, dst_ref=dst, send_sem=ss, recv_sem=rs, device_id=to, device_id_type=MESH
        )

    emb, vocab = emb_raw.shape[1], emb_raw.shape[0]
    w_in[...] = jnp.zeros_like(w_in)
    w_in[0:emb, :] = w_in_raw[...]
    tail = emb // 16 * 16
    part = w_in[tail : tail + 16, :].astype(F32)
    bias_row = b_in_raw[...].astype(F32).reshape(1, 256)
    part = jnp.where(lax.broadcasted_iota(jnp.int32, (16, 256), 0) == emb - tail, bias_row, part)
    w_in[tail : tail + 16, :] = part.astype(BF)
    for s in range(2):
        stack = jnp.concatenate(
            [v for ref in (chars_in, resets_in, targets_in) for v in (ref[:, s, :], jnp.zeros((8 - steps, 32), jnp.int32))],
            axis=0,
        ).astype(F32)
        wide_stack = jnp.concatenate([stack, jnp.zeros((24, 96), F32)], axis=1)
        ids_in[s] = wide_stack.T[:32, :].astype(jnp.int32)
    barrier = pltpu.get_barrier_semaphore()

    def greet(to):
        pl.semaphore_signal(barrier, inc=1, device_id=to, device_id_type=MESH)

    for k in (1, 2, 3):
        greet(kdev(k))
    for to in (mir, ydev, sib, cross):
        greet(to)

    @pl.when(moved)
    def _():
        greet(perm)
        greet(back)

    pl.semaphore_wait(barrier, 7 + 2 * moved.astype(jnp.int32))


    def d_slot(b):
        return WDEC.at[pl.ds(pl.multiple_of(64 * b, 64), 64), :]

    def w_cols(ub, g):
        return w_rec.at[:, lanes(8 * g + ub)]

    def w_part(j, g, b):
        return W.at[4 * j + g, pl.ds(pl.multiple_of(64 * b, 64), 64), :]

    def wa_start(k):
        for j in (0, 1):
            for g in range(4):
                rc(w_cols(unit_block(k, j), g), w_part(j, g, place(k, 0, y, c)), s_wa.at[k - 1, j], r_wa.at[k - 1, j], kdev(k)).start()

    def wa(k, j):
        b = place(k, 0, y, c)
        part = W.at[pl.ds(4 * j, 4), pl.ds(pl.multiple_of(64 * b, 64), 64), :]
        return rc(part, part, s_wa.at[k - 1, j], r_wa.at[k - 1, j], kdev(k))

    def ids_copy(k, mem):
        return rc(ids_in, IDS.at[:, mem], s_ids.at[k - 1], r_ids.at[k - 1], kdev(k))

    def own_w(j, g):
        return pltpu.make_async_copy(w_cols(unit_block(0, j), g), w_part(j, g, place(0, 0, y, c)), l_sem.at[4 * j + g])

    for j in (0, 1):
        for g in range(4):
            own_w(j, g).start()
    for k in (1, 2, 3):
        ids_copy(k, member(0)).start()

    def win_perm(jj, gy, gc):
        return rc(w_in, WIN.at[jj, gy, gc], s_win.at[0], r_win.at[0], perm)

    def win_local():
        return pltpu.make_async_copy(w_in, WIN.at[x, z // 2, z % 2], l_sem.at[8])

    @pl.when(moved)
    def _():
        win_perm(x, z // 2, z % 2).start()

    @pl.when(stays)
    def _():
        win_local().start()

    for k in (1, 2, 3):
        wa_start(k)

    def w_half(j, b):
        return W.at[pl.ds(4 * j, 4), pl.ds(pl.multiple_of(64 * b, 64), 64), :]

    def to_mir(k, j):
        b = place(k, 0, y, c)
        return rc(w_half(j, b), w_half(j, b), s_wm.at[k, j], r_wm.at[k, j], mir)

    def from_mir(k, j):
        b = place(k, 1, y, c)
        return rc(w_half(j, b), w_half(j, b), s_wm.at[k, j], r_wm.at[k, j], mir)

    def group_block(i, yy, cc):
        return place(i % 4, i // 4, yy, cc)

    def to_y(i, j):
        b = group_block(i, y, c)
        return rc(w_half(j, b), w_half(j, b), s_wy.at[i, j], r_wy.at[i, j], ydev)

    def from_y(i, j):
        b = group_block(i, 1 - y, c)
        return rc(w_half(j, b), w_half(j, b), s_wy.at[i, j], r_wy.at[i, j], ydev)

    def to_s(i, j):
        b = group_block(i % 8, y + (i // 8) * (1 - 2 * y), c)
        return rc(w_half(j, b), w_half(j, b), s_ws.at[i, j], r_ws.at[i, j], sib)

    def from_s(i, j):
        b = group_block(i % 8, y + (i // 8) * (1 - 2 * y), 1 - c)
        return rc(w_half(j, b), w_half(j, b), s_ws.at[i, j], r_ws.at[i, j], sib)

    for j in (0, 1):
        for g in range(4):
            own_w(j, g).wait()
    inner = a == 1

    @pl.when(inner)
    def _():
        for j in (0, 1):
            to_mir(0, j).start()

    for j in (0, 1):
        to_y(0, j).start()
        to_s(0, j).start()

    def win_mir(jj):
        return rc(WIN.at[jj, y, c], WIN.at[jj, y, c], s_win.at[1], r_win.at[1], mir)

    def win_y(yy):
        return rc(WIN.at[:, yy, c], WIN.at[:, yy, c], s_win.at[2], r_win.at[2], ydev)

    def win_s(cc):
        return rc(WIN.at[:, :, cc], WIN.at[:, :, cc], s_win.at[3], r_win.at[3], sib)

    @pl.when(moved)
    def _():
        win_perm(zh, y, c).wait_recv()

    @pl.when(stays)
    def _():
        win_local().wait()

    win_mir(zh).start()


    IDS[:, member(0)] = ids_in[...]

    def own_blocks(k):
        for j in (0, 1):
            wa(k, j).wait_recv()
            to_y(k, j).start()

            @pl.when(inner)
            def _(j=j):
                to_mir(k, j).start()

            to_s(k, j).start()

    own_blocks(1)
    own_blocks(2)
    own_blocks(3)

    def da(k):
        return rc(w_dec, d_slot(place(k, 0, y, c)), s_da.at[k - 1], r_da.at[k - 1], kdev(k))

    HSEND[0, 0 : VPAD // 128] = jnp.zeros((VPAD // 128, 128, rows), BF)
    for n in range(VPAD // 128):
        held = min(128, vocab - 128 * n)
        HSEND[0, n, 0:held, 0:emb] = emb_raw[128 * n : 128 * n + held, :]
    unit = jnp.where(
        lax.broadcasted_iota(jnp.int32, (EPAD, EPAD), 0) == lax.broadcasted_iota(jnp.int32, (EPAD, EPAD), 1), 1.0, 0.0
    ).astype(BF)
    turned = mm(unit, HSEND[0, 0 : VPAD // 128].reshape(VPAD, EPAD), NT)
    emb_t[...] = jnp.where(lax.broadcasted_iota(jnp.int32, (EPAD, VPAD), 0) == emb, 1.0, turned).astype(BF)
    w_dec[...] = jnp.zeros_like(w_dec)
    w_dec[:, :vocab] = w_dec_raw[...]
    bias_dec[...] = jnp.full_like(bias_dec, -1e30)
    bias_dec[0:1, :vocab] = bias_raw[...].astype(F32).reshape(1, vocab)
    for k in (1, 2, 3):
        da(k).start()
    own_dec = pltpu.make_async_copy(w_dec, d_slot(place(0, 0, y, c)), l_sem.at[9])
    own_dec.start()

    for k in (1, 2, 3):
        ids_copy(k, member(k)).wait_recv()
    lane = lax.broadcasted_iota(jnp.int32, (rows, 24), 1)
    wide = lax.broadcasted_iota(jnp.int32, (rows, VPAD), 1).astype(F32)

    def column(at, s):
        packed = IDS[s].reshape(rows, 24)
        return jnp.sum(jnp.where(lane == at, packed, 0).astype(F32), axis=1, keepdims=True)

    def keep_of(t, s):
        return 1.0 - column(8 + t, s)

    def letter(t, s):
        return jnp.where(column(t, s) == wide, 1.0, 0.0).astype(BF)

    EMBT[...] = jnp.zeros_like(EMBT)
    LV[...] = jnp.zeros_like(LV)
    BD[...] = jnp.zeros_like(BD)
    GWD[...] = jnp.zeros_like(GWD)
    DWI[...] = jnp.zeros_like(DWI)
    DCN[...] = jnp.zeros_like(DCN)
    OWN[...] = jnp.zeros_like(OWN)
    PR[0] = jnp.zeros(PR.shape[1:], BF)

    win_mir(1 - zh).wait_recv()

    win_y(y).start()
    def pass_y(i):
        for j in (0, 1):
            from_y(i, j).wait_recv()
            to_s(8 + i, j).start()

    def pass_mir(k):
        for j in (0, 1):
            from_mir(k, j).wait_recv()
            to_y(4 + k, j).start()
            to_s(4 + k, j).start()

    for i in range(3):
        pass_y(i)

    @pl.when(inner)
    def _():
        pass_mir(0)

    @pl.when(jnp.logical_not(inner))
    def _():
        for k in range(4):
            for j in (0, 1):
                to_mir(k, j).start()

    pass_y(3)
    win_y(1 - y).wait_recv()
    win_s(c).start()
    win_s(1 - c).wait_recv()

    def h_copy(t, s, k, j):
        src, dst = H.at[t % RING, s, :, span(0, j)], H.at[t % RING, s, :, span(k, j)]
        return rc(src, dst, s_h.at[t, s, k - 1, j], r_h.at[t, s, k - 1, j], kdev(k))

    def wait_h(t, s):
        for k in (1, 2, 3):
            for j in (0, 1):
                h_copy(t, s, k, j).wait_recv()

    def gates(t, s, first):
        keep = None if first else keep_of(t, s)
        feature = mm(letter(t, s), emb_t[...], NT).astype(BF)
        for j in (0, 1):
            pre = []
            for g in range(4):
                drive = mm(feature, WIN[j, g // 2, g % 2], NN)
                if not first:
                    drive = drive + keep * mm(H[(t - 1) % RING, s], W[4 * j + g], NN)
                pre.append(drive)
            s_i, s_f, t_g, s_o = sigmoid(pre[0]), sigmoid(pre[1]), jnp.tanh(pre[2]), sigmoid(pre[3])
            cell = s_i * t_g
            if not first:
                cell = s_f * (C[t - 1, s, j] * keep) + cell
            for g, v in enumerate((s_i, s_f, t_g, s_o)):
                A[t, s, 4 * j + g] = v
            C[t, s, j] = cell
            H[t % RING, s, :, span(0, j)] = (s_o * jnp.tanh(cell)).astype(BF)
            for k in (3, 1, 2):
                h_copy(t, s, k, j).start()

    @pl.loop(0, 2)
    def _(s):
        gates(0, s, True)

    @pl.when(jnp.logical_not(inner))
    def _():
        pass_mir(0)

    for k in (1, 2, 3):
        pass_mir(k)

    def dec_mir(k, far):
        b = place(k, far, y, c)
        return rc(d_slot(b), d_slot(b), s_dm.at[k], r_dm.at[k], mir)

    def dec_y(i, yy):
        b = group_block(i, yy, c)
        return rc(d_slot(b), d_slot(b), s_dy.at[i], r_dy.at[i], ydev)

    def dec_s(i, cc):
        b = group_block(i % 8, y + (i // 8) * (1 - 2 * y), cc)
        return rc(d_slot(b), d_slot(b), s_ds.at[i], r_ds.at[i], sib)

    own_dec.wait()
    dec_mir(0, 0).start()
    dec_y(0, y).start()
    dec_s(0, c).start()
    for k in (1, 2, 3):
        da(k).wait_recv()
        dec_mir(k, 0).start()
        dec_y(k, y).start()
        dec_s(k, c).start()

    for i in (4, 5, 6, 7):
        pass_y(i)

    @pl.loop(0, 16)
    def _(i):
        for j in (0, 1):
            from_s(i, j).wait_recv()

    def released(t, s):
        hid_copy(t, s).wait()
        for k in (1, 2, 3):
            for j in (0, 1):
                h_copy(t, s, k, j).wait_send()

    def forward(t, s):
        wait_h(t - 1, s)

        @pl.when(t >= RING - 1)
        def _():
            released(t - (RING - 1), s)

        gates(t, s, False)

    row = lax.broadcasted_iota(jnp.int32, (128, 256), 0)
    col = lax.broadcasted_iota(jnp.int32, (128, 256), 1)

    def select(cc):
        yy = y + (row // 64) * (1 - 2 * y)
        return jnp.where(col == 64 * (2 * yy + cc) + row % 64, 1.0, 0.0).astype(BF)

    def lane_slot(t, s):
        return pl.ds(pl.multiple_of((2 * t + s) * rows, rows), rows)

    def ht_copy(t, s, slot):
        return rc(HSEND.at[slot], HTS.at[:, :, lane_slot(t, s)], s_ht.at[t, s], r_ht.at[t, s], sib)

    def hid_copy(t, s):
        mine = H.at[t % RING, s, pl.ds(pl.multiple_of(32 * member(0), 32), 32), :]
        return pltpu.make_async_copy(mine, out_hid.at[s * steps + t], hid_sem.at[t, s])

    def logits_of(t, s):
        scores = mm(H[t % RING, s], WDEC[...], NN) + bias_dec[0:1, :]
        top = jnp.max(scores, axis=1, keepdims=True)
        shifted = jnp.exp(scores - top)
        summed = jnp.sum(shifted, axis=1, keepdims=True)
        goal = jnp.where(column(16 + t, s) == wide, 1.0, 0.0)
        picked = jnp.sum(goal * scores, axis=1, keepdims=True)
        LV[...] += jnp.broadcast_to(top + jnp.log(summed) - picked, (rows, 128))
        DL[t, s] = (shifted / summed - goal).astype(BF)

    def decoder_side(t, s):
        hid_copy(t, s).start()
        grad = DL[t, s]
        BD[...] += mm(jnp.ones((8, rows), BF), grad, NN)
        for j in (0, 1):
            GWD[j] += mm(H[t % RING, s, :, span(0, j)], grad, TN).reshape(2, 2, 64, VPAD)

    def transposed_side(t, s):
        slot = s
        mine, other = select(c), select(1 - c)

        @pl.when(t >= 1)
        def _():
            ht_copy(t - 1, s, slot).wait_send()

        for tile in range(8):
            part = H[t % RING, s, :, 256 * tile : 256 * (tile + 1)]
            HT[tile, :, lane_slot(t, s)] = mm(mine, part, NT).astype(BF)
            HSEND[slot, tile] = mm(other, part, NT).astype(BF)
        ht_copy(t, s, slot).start()

    def decoder_mirror():
        @pl.loop(0, 4)
        def _(k):
            dec_mir(k, 1).wait_recv()
            dec_y(4 + k, y).start()
            dec_s(4 + k, c).start()

    def decoder_rest():
        @pl.loop(0, 8)
        def _(i):
            k, j = i // 2, i % 2
            to_mir(k, j).wait_send()
            to_y(i, 0).wait_send()
            to_y(i, 1).wait_send()

        @pl.loop(0, 16)
        def _(i):
            to_s(i, 0).wait_send()
            to_s(i, 1).wait_send()

        @pl.loop(0, 8)
        def _(i):
            dec_y(i, 1 - y).wait_recv()
            dec_s(8 + i, c).start()

        @pl.loop(0, 16)
        def _(i):
            dec_s(i, 1 - c).wait_recv()

    def aside(t, s):
        logits_of(t, s)
        decoder_side(t, s)
        transposed_side(t, s)

    @pl.loop(2, 2 * steps)
    def _(i):
        t, s = i // 2, i % 2
        forward(t, s)

        @pl.when(i == 3)
        def _():
            decoder_mirror()

        @pl.when(i == 5)
        def _():
            decoder_rest()

        @pl.when(i >= 5)
        def _():
            @pl.loop(i - 4 - (13 - i) // 8, i - 3)
            def _(n):
                aside(n // 2, n % 2)

    def pr_copy(t, s, k, j):
        return rc(STG.at[s, k - 1, j], PR.at[t % 2, s, k - 1, j], s_pr.at[t, s, k - 1, j], r_pr.at[t, s, k - 1, j], kdev(k))

    def d_copy(t, s):
        return rc(D.at[:, t - 1, s], DS.at[:, t - 1, s], s_d.at[t, s], r_d.at[t, s], sib)

    def turn():
        def rows_of(q):
            return pl.ds(pl.multiple_of(256 * q, 256), 256)

        def swap(p, q):
            upper, lower = W[p, rows_of(q), :].T, W[q, rows_of(p), :].T
            W[p, rows_of(q), :] = lower
            W[q, rows_of(p), :] = upper

        @pl.loop(0, 8)
        def _(p):
            W[p, rows_of(p), :] = W[p, rows_of(p), :].T
            for step in (1, 2, 3):
                swap(p, (p + step) % 8)

        @pl.loop(0, 4)
        def _(p):
            swap(p, p + 4)

    def cell_back(t, s, oldest):
        keep = keep_of(t, s)
        for j in (0, 1):
            up = WDEC[span(0, j), :]
            dh = mm(DL[t, s], up, NT)
            rest = PR[(t + 1) % 2, s, 0, j].astype(F32) + PR[(t + 1) % 2, s, 1, j].astype(F32)
            rest = rest + PR[(t + 1) % 2, s, 2, j].astype(F32)
            dh = dh + (OWN[s, j] + rest)
            s_i, s_f, t_g, s_o = (A[t, s, 4 * j + g] for g in range(4))
            t_c = jnp.tanh(C[t, s, j])
            d_o = dh * t_c
            d_c = dh * s_o * (1.0 - t_c * t_c) + DCN[s, j]
            d_i = d_c * t_g * s_i * (1.0 - s_i)
            d_g = d_c * s_i * (1.0 - t_g * t_g)
            d_o = d_o * s_o * (1.0 - s_o)
            if oldest:
                d_f = jnp.zeros_like(d_i)
            else:
                d_f = d_c * (C[t - 1, s, j] * keep) * s_f * (1.0 - s_f)
                DCN[s, j] = keep * (d_c * s_f)
            for g, v in enumerate((d_i, d_f, d_g, d_o)):
                low = v.astype(BF)
                DRAW[4 * j + g] = low
                if not oldest:
                    D[4 * j + g, t - 1, s] = low * keep.astype(BF)

    def pr_each(act):
        for k in (3, 1, 2):
            for j in (0, 1):
                act(k, j)

    def product_back(t, s):
        left = jnp.concatenate([D[q, t - 1, s] for q in range(8)], axis=1)
        for k in (3, 1, 2, 0):
            for j in (0, 1):
                total = mm(left, W[2 * k + j], NN)
                if k == 0:
                    OWN[s, j] = total
                else:
                    STG[s, k - 1, j] = total.astype(BF)
        pr_each(lambda k, j: pr_copy(t, s, k, j).start())

    def input_side(t, s):
        onehot = letter(t, s)
        feat_t = mm(emb_t[...], onehot, NT).astype(BF)
        inputs = []
        for q in range(8):
            jj, gy, gc = q // 4, (q // 2) % 2, q % 2
            DWI[jj, gy, gc] += mm(feat_t, DRAW[q], NN)
            inputs.append(WIN[jj, gy, gc])
        grad_t = mm(jnp.concatenate(inputs, axis=1), jnp.concatenate([DRAW[q] for q in range(8)], axis=1), NT)
        high = grad_t.astype(BF)
        low = (grad_t - high.astype(F32)).astype(BF)
        EMBT[...] += mm(high, onehot, NN) + mm(low, onehot, NN)

    def gd_s():
        return rc(GWD.at[:, :, 1 - c], GIS.at[:, :, 0:64], s_gd.at[0], r_gd.at[0], sib)

    def gd_y():
        return rc(GWD.at[:, 1 - y, c], GY, s_gd.at[1], r_gd.at[1], ydev)

    def gd_m():
        return rc(GWD.at[1 - zh, y, c], GM, s_gd.at[2], r_gd.at[2], mir)

    @pl.loop(0, 2 * (steps - 1))
    def _(i):
        t, s = last - i // 2, i % 2

        @pl.when(i < 2)
        def _():
            wait_h(last, s)
            logits_of(last, s)

        @pl.when(i >= 2)
        def _():
            pr_each(lambda k, j: pr_copy(t + 1, s, k, j).wait_recv())

        cell_back(t, s, False)
        d_copy(t, s).start()

        @pl.when(i >= 2)
        def _():
            pr_each(lambda k, j: pr_copy(t + 1, s, k, j).wait_send())

        @pl.when(i == 0)
        def _():
            turn()

        product_back(t, s)
        input_side(t, s)

        @pl.when(i < 2)
        def _():
            aside(last - 1, s)

        @pl.when(i == 3)
        def _():
            @pl.loop(0, 2)
            def _(n):
                decoder_side(last, n)

            gd_s().start()

        @pl.when(i == 4)
        def _():
            gd_s().wait_recv()
            GWD[:, :, c] += GIS[:, :, 0:64]
            gd_y().start()

        @pl.when(i == 6)
        def _():
            gd_y().wait_recv()
            GWD[:, y, c] += GY[...]
            gd_m().start()

        @pl.when(i == 8)
        def _():
            gd_m().wait_recv()
            out_dec[...] = GWD[zh, y, c] + GM[...]

    @pl.loop(0, 2 * (steps - 1))
    def _(i):
        ht_copy(i // 2, i % 2, 0).wait_recv()
        d_copy(1 + i // 2, i % 2).wait_recv()

    depth = 2 * (steps - 1) * rows

    def kept(q):
        return A.at[2 + q // 4, (q % 4) // 2, :, pl.ds(pl.multiple_of(64 * (q % 2), 64), 64), :]

    def tile_of(q):
        k, near = q % 4, q // 4
        return 2 * k + 1 - zh + near * (2 * zh - 1)

    def ry_copy(p, q):
        return rc(SY.at[p % 4], RY.at[q], s_ry.at[p], r_ry.at[q], ydev)

    def rm_copy(k):
        return rc(SM.at[k], RM.at[k], s_rm.at[k], r_rm.at[k], mir)

    def half(h):
        return pl.ds(4 * h, 4)

    def ry_half(h):
        return rc(SY.at[0, half(h)], RY.at[3, half(h)], s_ry.at[8 + h], r_ry.at[8 + h], ydev)

    def rm_half(h):
        return rc(SM.at[3, half(h)], RM.at[3, half(h)], s_rm.at[4 + h], r_rm.at[4 + h], mir)

    def ry_sent(p):
        @pl.when(p == 0)
        def _():
            ry_half(0).wait_send()
            ry_half(1).wait_send()

        @pl.when(p > 0)
        def _():
            ry_copy(p, order(p)).wait_send()

    def rm_sent(k):
        if k == 3:
            rm_half(0).wait_send()
            rm_half(1).wait_send()
        else:
            rm_copy(k).wait_send()

    def ra_copy(k):
        return rc(SM.at[k], out_recv.at[k - 1], s_ra.at[k - 1], r_ra.at[k - 1], kdev(k))

    def order(p):
        return 3 - p + 8 * (p // 4)

    def make_tile(p):
        q = order(p)
        tile = tile_of(q)
        left, right = HT[tile], HTS[tile]
        hold = kept(q)

        @pl.when(p >= 4)
        def _():
            ry_sent(p - 4)

        for n in range(8):
            grad = mm(left, D[n].reshape(depth, 256), NN) + mm(right, DS[n].reshape(depth, 256), NN)
            hold[n] = grad[:64]
            SY[p % 4, n] = grad[64:].astype(BF)
            if n % 4 == 3:
                @pl.when(p == 0)
                def _(n=n):
                    ry_half(n // 4).start()

        @pl.when(p > 0)
        def _():
            ry_copy(p, q).start()

    def add_y(q):
        ry_copy(0, q).wait_recv()
        hold = kept(q)
        hold[...] = hold[...] + RY[q].astype(F32)

    def pass_on(k):
        if k == 3:
            hold = kept(k)
            for h in (0, 1):
                ry_half(h).wait_recv()
                SM[3, half(h)] = (hold[half(h)] + RY[3, half(h)].astype(F32)).astype(BF)
                rm_half(h).start()
            return
        add_y(k)
        SM[k] = kept(k)[...].astype(BF)
        rm_copy(k).start()

    def finish(k):
        add_y(4 + k)
        if k == 3:
            rm_half(0).wait_recv()
            rm_half(1).wait_recv()
        else:
            rm_copy(k).wait_recv()
        total = kept(4 + k)[...] + RM[k].astype(F32)
        if k == 0:
            out_own[...] = total
        else:
            rm_sent(k)
            SM[k] = total.astype(BF)
            ra_copy(k).start()

    def settle(p):
        q = order(p)
        pass_on(q) if q < 4 else finish(q - 4)

    outer = jnp.logical_not(inner)

    def core_rows(cc):
        return pl.ds(pl.multiple_of(64 * cc, 64), 64)

    def piece_rows(xx):
        return pl.ds(pl.multiple_of(64 * c + 32 * xx, 32), 32)

    def sm_core():
        return rc(out_small.at[core_rows(1 - c)], RS1, s_sm.at[0], r_sm.at[0], sib)

    def sm_group(k):
        xx = kx(k)
        return rc(out_small.at[piece_rows(xx)], RS2.at[k - 1], s_sm.at[k], r_sm.at[k], kdev(k))

    def sm_quarter(n):
        return rc(PIECE, RS3.at[n], s_sm.at[4 + n], r_sm.at[4 + n], (ydev, mir, cross)[n])

    def sm_spread(k):
        return rc(TOTAL, RS4.at[k - 1], s_sm.at[6 + k], r_sm.at[6 + k], kdev(k))

    def sm_last():
        return rc(out_small.at[core_rows(c)], RS5, s_sm.at[10], r_sm.at[10], sib)

    def sm_step1():
        sm_core().wait_recv()
        out_small[core_rows(c)] = out_small[core_rows(c)] + RS1[...]

        @pl.when(outer)
        def _():
            sm_group(1).start()

        @pl.when(inner)
        def _():
            sm_group(2).start()
            sm_group(3).start()

    def sm_step2():
        @pl.when(outer)
        def _():
            for k in (1, 2, 3):
                sm_group(k).wait_recv()
            PIECE[...] = (out_small[piece_rows(x)] + RS2[0]) + (RS2[1] + RS2[2])
            for n in range(3):
                sm_quarter(n).start()

    def sm_step3():
        @pl.when(outer)
        def _():
            for n in range(3):
                sm_quarter(n).wait_recv()
            TOTAL[...] = (PIECE[...] + RS3[0]) + (RS3[1] + RS3[2])
            for k in (1, 2, 3):
                sm_spread(k).start()

    def sm_step4():
        sm_core().wait_send()

        @pl.when(outer)
        def _():
            sm_group(1).wait_send()
            sm_spread(1).wait_recv()
            out_small[piece_rows(1 - x)] = RS4[0]
            out_small[piece_rows(x)] = TOTAL[...]

        @pl.when(inner)
        def _():
            for k in (2, 3):
                sm_group(k).wait_send()
                sm_spread(k).wait_recv()
                out_small[piece_rows(kx(k))] = RS4[k - 1]

        sm_last().start()

    def sm_step5():
        sm_last().wait_recv()
        out_small[core_rows(1 - c)] = RS5[...]

    live = pl.ds(0, 104)

    def gi_s():
        return rc(DWI.at[:, :, 1 - c, live], GIS.at[:, :, :, 0:256], s_gi.at[0], r_gi.at[0], sib)

    def gi_y():
        return rc(DWI.at[:, 1 - y, c, live], IY, s_gi.at[1], r_gi.at[1], ydev)

    def gi_m():
        return rc(SIM, IM, s_gi.at[2], r_gi.at[2], mir)

    def gi_p():
        return rc(DWI.at[zh, y, c, live], out_in, s_gi.at[3], r_gi.at[3], back)

    def first_position():
        @pl.loop(0, 2)
        def _(s):
            pr_each(lambda k, j: pr_copy(1, s, k, j).wait_recv())
            cell_back(0, s, True)
            input_side(0, s)

        leader = jnp.logical_and(x == 0, a == 0)
        high_row = lax.broadcasted_iota(jnp.int32, (8, VPAD), 0)
        loss = jnp.sum(LV[...], axis=0, keepdims=True)
        loss = jnp.concatenate([loss] * (VPAD // 128), axis=1)
        extra = jnp.where(high_row == 0, BD[...], jnp.where(high_row == 1, loss, 0.0))
        out_small[...] = EMBT[...]
        out_small[SMALL - 8 : SMALL] = jnp.where(leader, extra, 0.0)
        sm_core().start()
        gi_s().start()

    @pl.loop(0, 8)
    def _(p):
        make_tile(p)

        @pl.when(p == 1)
        def _():
            @pl.when(inner)
            def _():
                settle(0)

            first_position()
            sm_step1()
            gi_s().wait_recv()
            DWI[:, :, c, 0:104] = DWI[:, :, c, 0:104] + GIS[:, :, :, 0:256]
            gi_y().start()

            @pl.when(outer)
            def _():
                settle(0)

        @pl.when(p == 2)
        def _():
            settle(1)

        @pl.when(p == 3)
        def _():
            gi_y().wait_recv()
            DWI[:, y, c, 0:104] = DWI[:, y, c, 0:104] + IY[...]
            SIM[...] = DWI[1 - zh, y, c, 0:112].astype(BF)
            gi_m().start()

        @pl.when(p == 4)
        def _():
            settle(2)

        @pl.when(p == 5)
        def _():
            settle(3)

    sm_step2()
    settle(4)
    settle(5)
    settle(6)
    sm_step3()
    gi_m().wait_recv()
    DWI[zh, y, c, 0:104] = DWI[zh, y, c, 0:104] + IM[...].astype(F32)[0:104]

    @pl.when(moved)
    def _():
        gi_p().start()

    @pl.when(stays)
    def _():
        out_in[...] = DWI[zh, y, c, 0:104]

    sm_step4()
    settle(7)
    sm_step5()

    for k in (1, 2, 3):
        for j in (0, 1):
            wa(k, j).wait_send()
            for s in range(2):
                pr_copy(1, s, k, j).wait_send()
        ids_copy(k, member(0)).wait_send()
        da(k).wait_send()
        ra_copy(k).wait()
    rm_copy(0).wait_send()

    @pl.when(moved)
    def _():
        gi_p().wait()
        win_perm(x, z // 2, z % 2).wait_send()

    win_mir(zh).wait_send()
    win_y(y).wait_send()
    win_s(c).wait_send()
    @pl.when(outer)
    def _():
        for k in (1, 2, 3):
            sm_quarter(k - 1).wait_send()
            sm_spread(k).wait_send()

    for copy in (gd_s, gd_y, gd_m, gi_s, gi_y, gi_m, sm_last):
        copy().wait_send()
    for s in range(2):
        ht_copy(last - 1, s, s).wait_send()

    @pl.loop(0, 4)
    def _(k):
        dec_mir(k, 0).wait_send()

    @pl.loop(0, 8)
    def _(i):
        dec_y(i, y).wait_send()

    for p in range(4, 8):
        ry_copy(p, order(p)).wait_send()

    @pl.loop(0, 16)
    def _(i):
        dec_s(i, c).wait_send()

    @pl.loop(2 * (steps - RING + 1), 2 * steps)
    def _(i):
        released(i // 2, i % 2)

    @pl.loop(0, 2 * (steps - 1))
    def _(i):
        d_copy(1 + i // 2, i % 2).wait_send()


def output_kernel(
    own, recv, g_in, g_dec, hid_in, small, hid, table, o_in, o_bias, o_rec, o_dec, o_bias_dec, loss,
    h_buf, own_buf, recv_buf, rec_buf, in_sem, out_sem,
):
    dp = lax.axis_index("dp")
    z, x = dp // 2, dp % 2
    a = z + (z // 2) * (3 - 2 * z)
    parts = 8

    def cols(k, j, g):
        xk, ak = x + (k % 2) * (1 - 2 * x), a + (k // 2) * (1 - 2 * a)
        ub = 2 * (ak + j * (3 - 2 * ak)) + xk
        return pl.ds(pl.multiple_of(256 * (8 * g + ub), 256), 256)

    def hid_load(p):
        return pltpu.make_async_copy(hid_in.at[:, :, 256 * p : 256 * (p + 1)], h_buf.at[:, :, cols(p // 2, p % 2, 0)], in_sem.at[p])

    def hid_store():
        return pltpu.make_async_copy(h_buf, hid, out_sem.at[1])

    def rec_load(k):
        if k == 0:
            return pltpu.make_async_copy(own, own_buf, in_sem.at[parts])
        return pltpu.make_async_copy(recv.at[k - 1], recv_buf.at[k - 1], in_sem.at[parts + k])

    for p in range(parts):
        hid_load(p).start()
    for k in range(4):
        rec_load(k).start()
    for p in range(parts):
        hid_load(p).wait()
    hid_store().start()
    vocab, emb = table.shape
    table[...] = small[0:SMALL, :].T[:vocab, :emb]
    o_in[...] = g_in[0:emb, :]
    o_bias[...] = g_in[emb, :]
    o_dec[...] = g_dec[:, :vocab]
    o_bias_dec[...] = small[SMALL - 8, :vocab]
    loss[...] = small[SMALL - 7 : SMALL - 6, 0:1]
    for k in range(4):
        rec_load(k).wait()
        for j in (0, 1):
            for g in range(4):
                part = own_buf[4 * j + g] if k == 0 else recv_buf[k - 1, 4 * j + g].astype(F32)
                rec_buf[:, cols(k, j, g)] = part
    rec_store = pltpu.make_async_copy(rec_buf, o_rec, out_sem.at[0])
    rec_store.start()
    rec_store.wait()
    hid_store().wait()


def fused(chars, resets, targets, embed, w_in, bias_in, w_rec, w_dec, bias_dec):
    micro, count, steps = chars.shape
    own_rows, gate_cols = w_rec.shape
    vocab, emb = embed.shape
    width = gate_cols // 4
    members = 4
    rows = count * members
    vm = pl.BlockSpec(memory_space=pltpu.VMEM)
    hbm = pl.BlockSpec(memory_space=pl.ANY)
    dma = pltpu.SemaphoreType.DMA
    n = steps - 1
    scratch = [
        pltpu.VMEM((8, width, 256), BF),
        pltpu.VMEM((2, 2, 2, EPAD, 256), BF),
        pltpu.VMEM((width, VPAD), BF),
        pltpu.VMEM((micro, members, count, 24), jnp.int32),
        pltpu.VMEM((RING, micro, rows, width), BF),
        pltpu.VMEM((8, 128, 2 * n * rows), BF),
        pltpu.VMEM((8, 128, 2 * n * rows), BF),
        pltpu.VMEM((2, 8, 128, rows), BF),
        pltpu.VMEM((steps, micro, 8, rows, 256), F32),
        pltpu.VMEM((steps, micro, 2, rows, 256), F32),
        pltpu.VMEM((8, n, micro, rows, 256), BF),
        pltpu.VMEM((8, n, micro, rows, 256), BF),
        pltpu.VMEM((8, rows, 256), BF),
        pltpu.VMEM((steps, micro, rows, VPAD), BF),
        pltpu.VMEM((micro, count, 24), jnp.int32),
        pltpu.VMEM((EPAD, 256), BF),
        pltpu.VMEM((EPAD, VPAD), BF),
        pltpu.VMEM((own_rows, VPAD), BF),
        pltpu.VMEM((8, VPAD), F32),
        pltpu.VMEM((2, micro, 3, 2, rows, 256), BF),
        pltpu.VMEM((micro, 3, 2, rows, 256), BF),
        pltpu.VMEM((micro, 2, rows, 256), F32),
        pltpu.VMEM((micro, 2, rows, 256), F32),
        pltpu.VMEM((4, 8, 64, 256), BF),
        pltpu.VMEM((8, 8, 64, 256), BF),
        pltpu.VMEM((4, 8, 64, 256), BF),
        pltpu.VMEM((4, 8, 64, 256), BF),
        pltpu.VMEM((EPAD, VPAD), F32),
        pltpu.VMEM((rows, 128), F32),
        pltpu.VMEM((8, VPAD), F32),
        pltpu.VMEM((2, 2, 2, 64, VPAD), F32),
        pltpu.VMEM((2, 2, 104, VPAD), F32),
        pltpu.VMEM((2, 64, VPAD), F32),
        pltpu.VMEM((64, VPAD), F32),
        pltpu.VMEM((2, 2, 2, EPAD, 256), F32),
        pltpu.VMEM((2, 104, 256), F32),
        pltpu.VMEM((112, 256), BF),
        pltpu.VMEM((112, 256), BF),
        pltpu.VMEM((64, VPAD), F32),
        pltpu.VMEM((3, 32, VPAD), F32),
        pltpu.VMEM((3, 32, VPAD), F32),
        pltpu.VMEM((3, 32, VPAD), F32),
        pltpu.VMEM((64, VPAD), F32),
        pltpu.VMEM((32, VPAD), F32),
        pltpu.VMEM((32, VPAD), F32),
    ]
    shapes = [
        (3,), (4,), (3, 2), (4, 2), (8, 2), (16, 2), (3,), (4,), (8,), (16,),
        (steps, 2, 3, 2), (n, 2), (steps, 2), (steps, 2, 3, 2), (3,), (4,), (11,), (10,), (6,), (3,),
    ]
    for shape in shapes:
        scratch += [dma(shape), dma(shape)]
    scratch += [dma((12,)), dma((steps, 2))]
    out_own, out_recv, out_in, out_dec, out_hid, out_small = pl.pallas_call(
        functools.partial(lstm_kernel, steps, rows),
        out_shape=(
            jax.ShapeDtypeStruct((8, own_rows, 256), F32),
            jax.ShapeDtypeStruct((3, 8, own_rows, 256), BF),
            jax.ShapeDtypeStruct((104, 256), F32),
            jax.ShapeDtypeStruct((own_rows, VPAD), F32),
            jax.ShapeDtypeStruct((micro * steps, count, width), BF),
            jax.ShapeDtypeStruct((EPAD, VPAD), F32),
        ),
        in_specs=[hbm] + [vm] * 8,
        out_specs=(vm, hbm, vm, vm, hbm, vm),
        scratch_shapes=scratch,
        compiler_params=pltpu.CompilerParams(
            collective_id=0, has_side_effects=True, vmem_limit_bytes=66 * 1000 * 1000
        ),
    )(
        w_rec, w_in, bias_in, w_dec, embed, bias_dec,
        chars.transpose(2, 0, 1), resets.transpose(2, 0, 1), targets.transpose(2, 0, 1),
    )
    everyone = lax.axis_size(("dp", "fsdp"))
    hid, table, g_in, g_bias, g_rec, g_dec, g_bias_dec, loss = pl.pallas_call(
        output_kernel,
        out_shape=(
            jax.ShapeDtypeStruct((micro * steps, count, width), BF),
            jax.ShapeDtypeStruct((vocab, emb), F32),
            jax.ShapeDtypeStruct((emb, 256), F32),
            jax.ShapeDtypeStruct((256,), F32),
            jax.ShapeDtypeStruct((own_rows, gate_cols), F32),
            jax.ShapeDtypeStruct((own_rows, vocab), F32),
            jax.ShapeDtypeStruct((vocab,), F32),
            jax.ShapeDtypeStruct((1, 1), F32),
        ),
        in_specs=[hbm, hbm, vm, vm, hbm, vm],
        out_specs=(hbm, vm, vm, vm, hbm, vm, vm, vm),
        scratch_shapes=[
            pltpu.VMEM((micro * steps, count, width), BF),
            pltpu.VMEM((8, own_rows, 256), F32),
            pltpu.VMEM((3, 8, own_rows, 256), BF),
            pltpu.VMEM((own_rows, gate_cols), F32),
            dma((12,)),
            dma((2,)),
        ],
    )(out_own, out_recv, out_in, out_dec, out_hid, out_small)
    return (
        loss[0, 0] / (micro * count * steps * everyone),
        hid.reshape(micro, steps, count, width).transpose(0, 2, 1, 3),
        table,
        g_in,
        g_bias,
        g_rec,
        g_dec,
        g_bias_dec,
    )


def dot_plain(left, right):
    return jnp.dot(left, right, preferred_element_type=jnp.float32)


def dot_right_t(left, right):
    return lax.dot_general(
        left, right, (((1,), (1,)), ((), ())), preferred_element_type=jnp.float32
    )


def dot_left_t(left, right):
    return lax.dot_general(
        left, right, (((0,), (0,)), ((), ())), preferred_element_type=jnp.float32
    )


def lstm_forward(weights, embed, bias_dec, ids, marks, goals):
    w_rec, w_dec, w_in, bias_in = weights
    count, steps = ids.shape
    width = w_rec.shape[0]
    letters = jnp.arange(embed.shape[0], dtype=jnp.int32)
    onehot = (ids.T.reshape(-1)[:, None] == letters[None, :]).astype(jnp.bfloat16)
    feature = dot_plain(onehot, embed).astype(jnp.bfloat16)
    drives = (dot_plain(feature, w_in) + bias_in.astype(jnp.float32)).reshape(steps, count, -1)
    keeps = (1 - marks.T).astype(jnp.float32)[:, :, None]

    def advance(state, slot):
        hidden_now, cell = state
        drive, keep_now = slot
        prev_hidden = hidden_now * keep_now.astype(jnp.bfloat16)
        prev_cell = cell * keep_now
        pre = drive + dot_plain(prev_hidden, w_rec)
        gin, gforget, gcand, gout = jnp.split(pre, 4, axis=1)
        cell_new = jax.nn.sigmoid(gforget) * prev_cell + jax.nn.sigmoid(gin) * jnp.tanh(gcand)
        hid_new = (jax.nn.sigmoid(gout) * jnp.tanh(cell_new)).astype(jnp.bfloat16)
        return ((hid_new, cell_new), (pre, prev_hidden, prev_cell, cell_new, hid_new))

    start = (jnp.zeros((count, width), jnp.bfloat16), jnp.zeros((count, width), jnp.float32))
    state, saved = lax.scan(advance, start, (drives, keeps))
    pres, prev_hiddens, prev_cells, cells, hiddens = saved
    flat_hidden = hiddens.reshape(steps * count, width)
    logits = dot_plain(flat_hidden, w_dec) + bias_dec.astype(jnp.float32)
    top = jnp.max(logits, axis=1, keepdims=True)
    shifted = jnp.exp(logits - top)
    summed = jnp.sum(shifted, axis=1, keepdims=True)
    goal_hot = (goals.T.reshape(-1)[:, None] == letters[None, :]).astype(jnp.float32)
    loss_part = jnp.sum(top[:, 0] + jnp.log(summed[:, 0])) - jnp.sum(goal_hot * logits)
    d_logits = (shifted / summed - goal_hot).astype(jnp.bfloat16)
    kept = (pres, prev_hiddens, prev_cells, cells, keeps, flat_hidden, d_logits, feature, onehot)
    return (kept, loss_part, jnp.transpose(hiddens, (1, 0, 2)))


def lstm_backward(weights, kept):
    w_rec, w_dec, w_in, bias_in = weights
    pres, prev_hiddens, prev_cells, cells, keeps, flat_hidden, d_logits, feature, onehot = kept
    steps, count, width = cells.shape
    from_dec = dot_right_t(d_logits, w_dec).reshape(steps, count, width)

    def retreat(carry, slot):
        grad_h, grad_c = carry
        pre, prev_cell, cell, extra, keep_now = slot
        gin, gforget, gcand, gout = jnp.split(pre, 4, axis=1)
        sig_in = jax.nn.sigmoid(gin)
        sig_forget = jax.nn.sigmoid(gforget)
        sig_out = jax.nn.sigmoid(gout)
        tan_cand = jnp.tanh(gcand)
        tan_cell = jnp.tanh(cell)
        grad_hid = extra + grad_h
        grad_out = grad_hid * tan_cell
        grad_cell = grad_c + grad_hid * sig_out * (1.0 - tan_cell * tan_cell)
        d_pre = jnp.concatenate(
            [
                grad_cell * tan_cand * sig_in * (1.0 - sig_in),
                grad_cell * prev_cell * sig_forget * (1.0 - sig_forget),
                grad_cell * sig_in * (1.0 - tan_cand * tan_cand),
                grad_out * sig_out * (1.0 - sig_out),
            ],
            axis=1,
        ).astype(jnp.bfloat16)
        back_h = dot_right_t(d_pre, w_rec) * keep_now
        back_c = grad_cell * sig_forget * keep_now
        return ((back_h, back_c), d_pre)

    start = (jnp.zeros((count, width), jnp.float32), jnp.zeros((count, width), jnp.float32))
    state, d_pres = lax.scan(
        retreat, start, (pres, prev_cells, cells, from_dec, keeps), reverse=True
    )
    flat_pre = d_pres.reshape(steps * count, -1)
    grad_dec = dot_left_t(flat_hidden, d_logits)
    grad_in = dot_left_t(feature, flat_pre)
    grad_bias = jnp.sum(flat_pre.astype(jnp.float32), axis=0)
    grad_feature = dot_right_t(flat_pre, w_in)
    grad_table = lax.dot_general(
        onehot.astype(jnp.float32),
        grad_feature,
        (((0,), (0,)), ((), ())),
        precision=lax.Precision.HIGHEST,
        preferred_element_type=jnp.float32,
    )
    grad_bias_out = jnp.sum(d_logits.astype(jnp.float32), axis=0)
    flat_prev = prev_hiddens.reshape(steps * count, width)
    return (grad_dec, grad_in, grad_bias, grad_table, grad_bias_out, flat_prev, flat_pre)


def general(chars, resets, targets, embed, w_in, bias_in, w_rec, w_dec, bias_dec):
    micro, count, steps = chars.shape
    everyone = lax.axis_size(("dp", "fsdp"))
    sums = None
    prev_list = []
    pre_list = []
    hidden_list = []
    for index in range(micro):
        forward_set = (
            lax.all_gather(w_rec, ("dp", "fsdp"), axis=0, tiled=True),
            lax.all_gather(w_dec, ("dp", "fsdp"), axis=0, tiled=True),
            lax.all_gather(w_in, ("dp", "fsdp"), axis=1, tiled=True),
            lax.all_gather(bias_in, ("dp", "fsdp"), axis=0, tiled=True),
        )
        kept, loss_part, hiddens = lstm_forward(
            forward_set, embed, bias_dec, chars[index], resets[index], targets[index]
        )
        backward_set = (
            lax.all_gather(w_rec, ("dp", "fsdp"), axis=0, tiled=True),
            lax.all_gather(w_dec, ("dp", "fsdp"), axis=0, tiled=True),
            lax.all_gather(w_in, ("dp", "fsdp"), axis=1, tiled=True),
            lax.all_gather(bias_in, ("dp", "fsdp"), axis=0, tiled=True),
        )
        grad_dec, grad_in, grad_bias, grad_table, grad_bias_out, flat_prev, flat_pre = (
            lstm_backward(backward_set, kept)
        )
        pieces = (grad_dec, grad_in, grad_bias, grad_table, grad_bias_out, loss_part)
        if sums is None:
            sums = pieces
        else:
            sums = tuple((first + second for first, second in zip(sums, pieces)))
        prev_list.append(flat_prev)
        pre_list.append(flat_pre)
        hidden_list.append(hiddens)
    prev_all = jnp.concatenate(prev_list, axis=0)
    pre_all = jnp.concatenate(pre_list, axis=0)
    grad_w_rec = lax.psum_scatter(
        dot_left_t(prev_all, pre_all), ("dp", "fsdp"), scatter_dimension=0, tiled=True
    )
    grad_w_dec, grad_w_in, grad_bias_in = (
        lax.psum_scatter(sums[0], ("dp", "fsdp"), scatter_dimension=0, tiled=True),
        lax.psum_scatter(sums[1], ("dp", "fsdp"), scatter_dimension=1, tiled=True),
        lax.psum_scatter(sums[2], ("dp", "fsdp"), scatter_dimension=0, tiled=True),
    )
    grad_embed, grad_bias_dec, total = lax.psum((sums[3], sums[4], sums[5]), ("dp", "fsdp"))
    loss = total / (micro * count * steps * everyone)
    hidden = jnp.stack(hidden_list, axis=0)
    return (
        loss,
        hidden,
        grad_embed,
        grad_w_in,
        grad_bias_in,
        grad_w_rec,
        grad_w_dec,
        grad_bias_dec,
    )


def solution(mesh):
    per_device = fused if (mesh.shape["dp"], mesh.shape["fsdp"]) == (8, 4) else general
    return jax.shard_map(
        per_device,
        mesh=mesh,
        in_specs=(
            P(None, ("dp", "fsdp"), None),
            P(None, ("dp", "fsdp"), None),
            P(None, ("dp", "fsdp"), None),
            P(),
            P(None, ("dp", "fsdp")),
            P(("dp", "fsdp")),
            P(("dp", "fsdp"), None),
            P(("dp", "fsdp"), None),
            P(),
        ),
        out_specs=(
            P(),
            P(None, ("dp", "fsdp"), None, None),
            P(),
            P(None, ("dp", "fsdp")),
            P(("dp", "fsdp")),
            P(("dp", "fsdp"), None),
            P(("dp", "fsdp"), None),
            P(),
        ),
        check_vma=False,
    )
```

```python
import functools

import jax
import jax.numpy as jnp
from jax import lax
from jax.experimental import pallas as pl
from jax.experimental.pallas import tpu as pltpu
from jax.sharding import PartitionSpec as P

MESH = pl.DeviceIdType.MESH
NN = ((1,), (0,))
NT = ((1,), (1,))
TN = ((0,), (0,))
F32 = jnp.float32
BF = jnp.bfloat16

VPAD = 384
EPAD = 128
RING = 4
SMALL = 112


def mm(left, right, dims):
    return lax.dot_general(left, right, (dims, ((), ())), preferred_element_type=F32)


def sigmoid(v):
    return 0.5 * jnp.tanh(0.5 * v) + 0.5


def lstm_kernel(
    steps, rows,
    w_rec, w_in_raw, b_in_raw, w_dec_raw, emb_raw, bias_raw, chars_in, resets_in, targets_in,
    out_own, out_recv, out_in, out_dec, out_hid, out_small,
    W, WIN, WDEC, IDS, H, HT, HTS, HSEND, A, C, D, DS, DRAW, DL,
    ids_in, w_in, emb_t, w_dec, bias_dec, PR, STG, CB, PEND, OWN, DCN, SY, RY, SM, RM, EMBT, LV, BD, GWD, GIS, GY, GM, DWI, SIY, IY, SIM, IM, RS1, RS2, RS3, RS4, RS5, PIECE, TOTAL,
    s_ids, r_ids, s_win, r_win, s_wa, r_wa, s_wm, r_wm, s_wy, r_wy, s_ws, r_ws,
    s_da, r_da, s_dm, r_dm, s_dy, r_dy, s_ds, r_ds, s_h, r_h, s_ht, r_ht, s_d, r_d,
    s_pr, r_pr, s_ph, r_ph, s_cb, r_cb, s_gd, r_gd, s_gi, r_gi, s_sm, r_sm, s_ry, r_ry, s_rm, r_rm, s_ra, r_ra,
    l_sem, hid_sem,
):
    last = steps - 1
    dp, fs = lax.axis_index("dp"), lax.axis_index("fsdp")
    z, x, y, c = dp // 2, dp % 2, fs // 2, fs % 2
    zh = z // 2
    a = z + zh * (3 - 2 * z)

    def dev(zz, xx, yy, cc):
        return (zz * 2 + xx, yy * 2 + cc)

    def kx(k):
        return x + (k % 2) * (1 - 2 * x)

    def kz(k):
        return z + (k // 2) * (1 - 2 * (z % 2))

    def ka(k):
        return a + (k // 2) * (1 - 2 * a)

    def kdev(k):
        return dev(kz(k), kx(k), y, c)

    def member(k):
        return 2 * kx(k) + ka(k)

    def unit_block(k, j):
        return 2 * (ka(k) + j * (3 - 2 * ka(k))) + kx(k)

    def lanes(ub):
        return pl.ds(pl.multiple_of(256 * ub, 256), 256)

    def place(k, far, yy, cc):
        return 4 * (2 * k + zh + far * (1 - 2 * zh)) + 2 * yy + cc

    def span(k, j):
        return slice(256 * (2 * k + j), 256 * (2 * k + j + 1))

    mir, ydev, sib = dev(3 - z, x, y, c), dev(z, x, 1 - y, c), dev(z, x, y, 1 - c)
    cross = dev(3 - z, x, 1 - y, c)
    perm = dev(2 * x + y, c, z // 2, z % 2)
    back = dev(2 * y + c, z // 2, z % 2, x)
    stays = jnp.logical_and(perm[0] == dp, perm[1] == fs)
    moved = jnp.logical_not(stays)

    def rc(src, dst, ss, rs, to):
        return pltpu.make_async_remote_copy(
            src_ref=src, dst_ref=dst, send_sem=ss, recv_sem=rs, device_id=to, device_id_type=MESH
        )

    emb, vocab = emb_raw.shape[1], emb_raw.shape[0]
    w_in[...] = jnp.zeros_like(w_in)
    w_in[0:emb, :] = w_in_raw[...]
    tail = emb // 16 * 16
    part = w_in[tail : tail + 16, :].astype(F32)
    bias_row = b_in_raw[...].astype(F32).reshape(1, 256)
    part = jnp.where(lax.broadcasted_iota(jnp.int32, (16, 256), 0) == emb - tail, bias_row, part)
    w_in[tail : tail + 16, :] = part.astype(BF)
    for s in range(2):
        stack = jnp.concatenate(
            [v for ref in (chars_in, resets_in, targets_in) for v in (ref[:, s, :], jnp.zeros((8 - steps, 32), jnp.int32))],
            axis=0,
        ).astype(F32)
        wide_stack = jnp.concatenate([stack, jnp.zeros((24, 96), F32)], axis=1)
        ids_in[s] = wide_stack.T[:32, :].astype(jnp.int32)
    barrier = pltpu.get_barrier_semaphore()

    def greet(to):
        pl.semaphore_signal(barrier, inc=1, device_id=to, device_id_type=MESH)

    for k in (1, 2, 3):
        greet(kdev(k))
    for to in (mir, ydev, sib, cross):
        greet(to)

    @pl.when(moved)
    def _():
        greet(perm)
        greet(back)

    pl.semaphore_wait(barrier, 7 + 2 * moved.astype(jnp.int32))


    def d_slot(b):
        return WDEC.at[pl.ds(pl.multiple_of(64 * b, 64), 64), :]

    def w_cols(ub, g):
        return w_rec.at[:, lanes(8 * g + ub)]

    def w_part(j, g, b):
        return W.at[4 * j + g, pl.ds(pl.multiple_of(64 * b, 64), 64), :]

    def wa_start(k):
        for j in (0, 1):
            for g in range(4):
                rc(w_cols(unit_block(k, j), g), w_part(j, g, place(k, 0, y, c)), s_wa.at[k - 1, j], r_wa.at[k - 1, j], kdev(k)).start()

    def wa(k, j):
        b = place(k, 0, y, c)
        part = W.at[pl.ds(4 * j, 4), pl.ds(pl.multiple_of(64 * b, 64), 64), :]
        return rc(part, part, s_wa.at[k - 1, j], r_wa.at[k - 1, j], kdev(k))

    def ids_copy(k, mem):
        return rc(ids_in, IDS.at[:, mem], s_ids.at[k - 1], r_ids.at[k - 1], kdev(k))

    def own_w(j, g):
        return pltpu.make_async_copy(w_cols(unit_block(0, j), g), w_part(j, g, place(0, 0, y, c)), l_sem.at[4 * j + g])

    for j in (0, 1):
        for g in range(4):
            own_w(j, g).start()
    for k in (1, 2, 3):
        ids_copy(k, member(0)).start()

    def win_perm(jj, gy, gc):
        return rc(w_in, WIN.at[jj, gy, gc], s_win.at[0], r_win.at[0], perm)

    def win_local():
        return pltpu.make_async_copy(w_in, WIN.at[x, z // 2, z % 2], l_sem.at[8])

    @pl.when(moved)
    def _():
        win_perm(x, z // 2, z % 2).start()

    @pl.when(stays)
    def _():
        win_local().start()

    for k in (1, 2, 3):
        wa_start(k)

    def w_half(j, b):
        return W.at[pl.ds(4 * j, 4), pl.ds(pl.multiple_of(64 * b, 64), 64), :]

    def to_mir(k, j):
        b = place(k, 0, y, c)
        return rc(w_half(j, b), w_half(j, b), s_wm.at[k, j], r_wm.at[k, j], mir)

    def from_mir(k, j):
        b = place(k, 1, y, c)
        return rc(w_half(j, b), w_half(j, b), s_wm.at[k, j], r_wm.at[k, j], mir)

    def group_block(i, yy, cc):
        return place(i % 4, i // 4, yy, cc)

    def to_y(i, j):
        b = group_block(i, y, c)
        return rc(w_half(j, b), w_half(j, b), s_wy.at[i, j], r_wy.at[i, j], ydev)

    def from_y(i, j):
        b = group_block(i, 1 - y, c)
        return rc(w_half(j, b), w_half(j, b), s_wy.at[i, j], r_wy.at[i, j], ydev)

    def to_s(i, j):
        b = group_block(i % 8, y + (i // 8) * (1 - 2 * y), c)
        return rc(w_half(j, b), w_half(j, b), s_ws.at[i, j], r_ws.at[i, j], sib)

    def from_s(i, j):
        b = group_block(i % 8, y + (i // 8) * (1 - 2 * y), 1 - c)
        return rc(w_half(j, b), w_half(j, b), s_ws.at[i, j], r_ws.at[i, j], sib)

    for j in (0, 1):
        for g in range(4):
            own_w(j, g).wait()
    inner = a == 1

    @pl.when(inner)
    def _():
        for j in (0, 1):
            to_mir(0, j).start()

    for j in (0, 1):
        to_y(0, j).start()
        to_s(0, j).start()

    def win_mir(jj):
        return rc(WIN.at[jj, y, c], WIN.at[jj, y, c], s_win.at[1], r_win.at[1], mir)

    def win_y(yy):
        return rc(WIN.at[:, yy, c], WIN.at[:, yy, c], s_win.at[2], r_win.at[2], ydev)

    def win_s(cc):
        return rc(WIN.at[:, :, cc], WIN.at[:, :, cc], s_win.at[3], r_win.at[3], sib)

    @pl.when(moved)
    def _():
        win_perm(zh, y, c).wait_recv()

    @pl.when(stays)
    def _():
        win_local().wait()

    win_mir(zh).start()


    IDS[:, member(0)] = ids_in[...]

    def own_blocks(k):
        for j in (0, 1):
            wa(k, j).wait_recv()
            to_y(k, j).start()

            @pl.when(inner)
            def _(j=j):
                to_mir(k, j).start()

            to_s(k, j).start()

    own_blocks(1)
    own_blocks(2)
    own_blocks(3)

    def da(k):
        return rc(w_dec, d_slot(place(k, 0, y, c)), s_da.at[k - 1], r_da.at[k - 1], kdev(k))

    HSEND[0, 0 : VPAD // 128] = jnp.zeros((VPAD // 128, 128, rows), BF)
    for n in range(VPAD // 128):
        held = min(128, vocab - 128 * n)
        HSEND[0, n, 0:held, 0:emb] = emb_raw[128 * n : 128 * n + held, :]
    unit = jnp.where(
        lax.broadcasted_iota(jnp.int32, (EPAD, EPAD), 0) == lax.broadcasted_iota(jnp.int32, (EPAD, EPAD), 1), 1.0, 0.0
    ).astype(BF)
    turned = mm(unit, HSEND[0, 0 : VPAD // 128].reshape(VPAD, EPAD), NT)
    emb_t[...] = jnp.where(lax.broadcasted_iota(jnp.int32, (EPAD, VPAD), 0) == emb, 1.0, turned).astype(BF)
    w_dec[...] = jnp.zeros_like(w_dec)
    w_dec[:, :vocab] = w_dec_raw[...]
    bias_dec[...] = jnp.full_like(bias_dec, -1e30)
    bias_dec[0:1, :vocab] = bias_raw[...].astype(F32).reshape(1, vocab)
    for k in (1, 2, 3):
        da(k).start()
    own_dec = pltpu.make_async_copy(w_dec, d_slot(place(0, 0, y, c)), l_sem.at[9])
    own_dec.start()

    for k in (1, 2, 3):
        ids_copy(k, member(k)).wait_recv()
    lane = lax.broadcasted_iota(jnp.int32, (rows, 24), 1)
    wide = lax.broadcasted_iota(jnp.int32, (rows, VPAD), 1).astype(F32)

    def column(at, s):
        packed = IDS[s].reshape(rows, 24)
        return jnp.sum(jnp.where(lane == at, packed, 0).astype(F32), axis=1, keepdims=True)

    def keep_of(t, s):
        return 1.0 - column(8 + t, s)

    def letter(t, s):
        return jnp.where(column(t, s) == wide, 1.0, 0.0).astype(BF)

    EMBT[...] = jnp.zeros_like(EMBT)
    LV[...] = jnp.zeros_like(LV)
    BD[...] = jnp.zeros_like(BD)
    GWD[...] = jnp.zeros_like(GWD)
    DWI[...] = jnp.zeros_like(DWI)
    DCN[...] = jnp.zeros_like(DCN)
    OWN[...] = jnp.zeros_like(OWN)
    PR[0] = jnp.zeros(PR.shape[1:], BF)

    win_mir(1 - zh).wait_recv()

    win_y(y).start()
    def pass_y(i):
        for j in (0, 1):
            from_y(i, j).wait_recv()
            to_s(8 + i, j).start()

    def pass_mir(k):
        for j in (0, 1):
            from_mir(k, j).wait_recv()
            to_y(4 + k, j).start()
            to_s(4 + k, j).start()

    for i in range(3):
        pass_y(i)

    @pl.when(inner)
    def _():
        pass_mir(0)

    @pl.when(jnp.logical_not(inner))
    def _():
        for k in range(4):
            for j in (0, 1):
                to_mir(k, j).start()

    pass_y(3)
    win_y(1 - y).wait_recv()
    win_s(c).start()
    win_s(1 - c).wait_recv()

    def h_copy(t, s, k, j):
        src, dst = H.at[t % RING, s, :, span(0, j)], H.at[t % RING, s, :, span(k, j)]
        return rc(src, dst, s_h.at[t, s, k - 1, j], r_h.at[t, s, k - 1, j], kdev(k))

    def wait_h(t, s):
        for k in (1, 2, 3):
            for j in (0, 1):
                h_copy(t, s, k, j).wait_recv()

    def gates(t, s, first):
        keep = None if first else keep_of(t, s)
        feature = mm(letter(t, s), emb_t[...], NT).astype(BF)
        for j in (0, 1):
            pre = []
            for g in range(4):
                drive = mm(feature, WIN[j, g // 2, g % 2], NN)
                if not first:
                    drive = drive + keep * mm(H[(t - 1) % RING, s], W[4 * j + g], NN)
                pre.append(drive)
            s_i, s_f, t_g, s_o = sigmoid(pre[0]), sigmoid(pre[1]), jnp.tanh(pre[2]), sigmoid(pre[3])
            cell = s_i * t_g
            if not first:
                cell = s_f * (C[t - 1, s, j] * keep) + cell
            for g, v in enumerate((s_i, s_f, t_g, s_o)):
                A[t, s, 4 * j + g] = v
            C[t, s, j] = cell
            H[t % RING, s, :, span(0, j)] = (s_o * jnp.tanh(cell)).astype(BF)
            for k in (3, 1, 2):
                h_copy(t, s, k, j).start()

    @pl.loop(0, 2)
    def _(s):
        gates(0, s, True)

    @pl.when(jnp.logical_not(inner))
    def _():
        pass_mir(0)

    for k in (1, 2, 3):
        pass_mir(k)

    def dec_mir(k, far):
        b = place(k, far, y, c)
        return rc(d_slot(b), d_slot(b), s_dm.at[k], r_dm.at[k], mir)

    def dec_y(i, yy):
        b = group_block(i, yy, c)
        return rc(d_slot(b), d_slot(b), s_dy.at[i], r_dy.at[i], ydev)

    def dec_s(i, cc):
        b = group_block(i % 8, y + (i // 8) * (1 - 2 * y), cc)
        return rc(d_slot(b), d_slot(b), s_ds.at[i], r_ds.at[i], sib)

    own_dec.wait()
    dec_mir(0, 0).start()
    dec_y(0, y).start()
    dec_s(0, c).start()
    for k in (1, 2, 3):
        da(k).wait_recv()
        dec_mir(k, 0).start()
        dec_y(k, y).start()
        dec_s(k, c).start()

    for i in (4, 5, 6, 7):
        pass_y(i)

    @pl.loop(0, 16)
    def _(i):
        for j in (0, 1):
            from_s(i, j).wait_recv()

    def released(t, s):
        hid_copy(t, s).wait()
        for k in (1, 2, 3):
            for j in (0, 1):
                h_copy(t, s, k, j).wait_send()

    def forward(t, s):
        wait_h(t - 1, s)

        @pl.when(t >= RING - 1)
        def _():
            released(t - (RING - 1), s)

        gates(t, s, False)

    row = lax.broadcasted_iota(jnp.int32, (128, 256), 0)
    col = lax.broadcasted_iota(jnp.int32, (128, 256), 1)

    def select(cc):
        yy = y + (row // 64) * (1 - 2 * y)
        return jnp.where(col == 64 * (2 * yy + cc) + row % 64, 1.0, 0.0).astype(BF)

    def lane_slot(t, s):
        return pl.ds(pl.multiple_of((2 * t + s) * rows, rows), rows)

    def ht_copy(t, s, slot):
        return rc(HSEND.at[slot], HTS.at[:, :, lane_slot(t, s)], s_ht.at[t, s], r_ht.at[t, s], sib)

    def hid_copy(t, s):
        mine = H.at[t % RING, s, pl.ds(pl.multiple_of(32 * member(0), 32), 32), :]
        return pltpu.make_async_copy(mine, out_hid.at[s * steps + t], hid_sem.at[t, s])

    def logits_of(t, s):
        scores = mm(H[t % RING, s], WDEC[...], NN) + bias_dec[0:1, :]
        top = jnp.max(scores, axis=1, keepdims=True)
        shifted = jnp.exp(scores - top)
        summed = jnp.sum(shifted, axis=1, keepdims=True)
        goal = jnp.where(column(16 + t, s) == wide, 1.0, 0.0)
        picked = jnp.sum(goal * scores, axis=1, keepdims=True)
        LV[...] += jnp.broadcast_to(top + jnp.log(summed) - picked, (rows, 128))
        DL[t, s] = (shifted / summed - goal).astype(BF)

    def decoder_side(t, s):
        hid_copy(t, s).start()
        grad = DL[t, s]
        BD[...] += mm(jnp.ones((8, rows), BF), grad, NN)
        for j in (0, 1):
            GWD[j] += mm(H[t % RING, s, :, span(0, j)], grad, TN).reshape(2, 2, 64, VPAD)

    def transposed_side(t, s):
        slot = s
        mine, other = select(c), select(1 - c)

        @pl.when(t >= 1)
        def _():
            ht_copy(t - 1, s, slot).wait_send()

        for tile in range(8):
            part = H[t % RING, s, :, 256 * tile : 256 * (tile + 1)]
            HT[tile, :, lane_slot(t, s)] = mm(mine, part, NT).astype(BF)
            HSEND[slot, tile] = mm(other, part, NT).astype(BF)
        ht_copy(t, s, slot).start()

    def decoder_mirror():
        @pl.loop(0, 4)
        def _(k):
            dec_mir(k, 1).wait_recv()
            dec_y(4 + k, y).start()
            dec_s(4 + k, c).start()

    def decoder_rest():
        @pl.loop(0, 8)
        def _(i):
            k, j = i // 2, i % 2
            to_mir(k, j).wait_send()
            to_y(i, 0).wait_send()
            to_y(i, 1).wait_send()

        @pl.loop(0, 16)
        def _(i):
            to_s(i, 0).wait_send()
            to_s(i, 1).wait_send()

        @pl.loop(0, 8)
        def _(i):
            dec_y(i, 1 - y).wait_recv()
            dec_s(8 + i, c).start()

        @pl.loop(0, 16)
        def _(i):
            dec_s(i, 1 - c).wait_recv()

    def aside(t, s):
        logits_of(t, s)
        decoder_side(t, s)
        transposed_side(t, s)

    @pl.loop(2, 2 * steps)
    def _(i):
        t, s = i // 2, i % 2
        forward(t, s)

        @pl.when(i == 3)
        def _():
            decoder_mirror()

        @pl.when(i == 5)
        def _():
            decoder_rest()

        @pl.when(i >= 5)
        def _():
            @pl.loop(i - 4 - (13 - i) // 8, i - 3)
            def _(n):
                aside(n // 2, n % 2)


    def pr_copy(t, s, k, j):
        return rc(STG.at[s, k - 1, j], PR.at[t % 2, s, k - 1, j], s_pr.at[t, s, k - 1, j], r_pr.at[t, s, k - 1, j], kdev(k))

    def d_copy(t, s):
        return rc(D.at[:, t - 1, s], DS.at[:, t - 1, s], s_d.at[t, s], r_d.at[t, s], sib)

    def turn():
        def rows_of(q):
            return slice(256 * q, 256 * (q + 1))

        def swap(p, q):
            upper, lower = W[p, rows_of(q), :].T, W[q, rows_of(p), :].T
            W[p, rows_of(q), :] = lower
            W[q, rows_of(p), :] = upper

        for p in range(8):
            W[p, rows_of(p), :] = W[p, rows_of(p), :].T
            for q in range(p):
                swap(p, q)

    def cell_back(t, s, oldest):
        keep = keep_of(t, s)
        for j in (0, 1):
            up = WDEC[span(0, j), :]
            dh = mm(DL[t, s], up, NT)
            rest = PR[(t + 1) % 2, s, 0, j].astype(F32) + PR[(t + 1) % 2, s, 1, j].astype(F32)
            if j == 1:
                rest = rest + PR[(t + 1) % 2, s, 2, j].astype(F32)
            dh = dh + (OWN[s, j] + rest)
            s_i, s_f, t_g, s_o = (A[t, s, 4 * j + g] for g in range(4))
            t_c = jnp.tanh(C[t, s, j])
            d_o = dh * t_c
            d_c = dh * s_o * (1.0 - t_c * t_c) + DCN[s, j]
            d_i = d_c * t_g * s_i * (1.0 - s_i)
            d_g = d_c * s_i * (1.0 - t_g * t_g)
            d_o = d_o * s_o * (1.0 - s_o)
            if oldest:
                d_f = jnp.zeros_like(d_i)
            else:
                d_f = d_c * (C[t - 1, s, j] * keep) * s_f * (1.0 - s_f)
                DCN[s, j] = keep * (d_c * s_f)
            for g, v in enumerate((d_i, d_f, d_g, d_o)):
                low = v.astype(BF)
                DRAW[4 * j + g] = low
                if not oldest:
                    D[4 * j + g, t - 1, s] = low * keep.astype(BF)

    def part_rows(h):
        return slice(64 * h, 64 * (h + 1))

    def pr_half(t, s, k, h):
        src, dst = STG.at[s, k - 1, 0, part_rows(h)], PR.at[t % 2, s, k - 1, 0, part_rows(h)]
        return rc(src, dst, s_ph.at[t, s, k - 1, h], r_ph.at[t, s, k - 1, h], kdev(k))

    def owed_copy(t, s, n):
        return rc(STG.at[s, 2, 0, part_rows(n)], CB.at[s, n], s_cb.at[t, s, n], r_cb.at[t, s, n], kdev(1 + n))

    def pr_arrived(t, s):
        for k in (1, 2, 3):
            pr_copy(t, s, k, 1).wait_recv()
        for k in (1, 2):
            for h in (0, 1):
                pr_half(t, s, k, h).wait_recv()

    def pr_left(t, s):
        for k in (1, 2, 3):
            pr_copy(t, s, k, 1).wait_send()
        for k in (1, 2):
            for h in (0, 1):
                pr_half(t, s, k, h).wait_send()
        for n in (0, 1):
            owed_copy(t, s, n).wait_send()

    def product_back(t, s):
        left = jnp.concatenate([D[q, t - 1, s] for q in range(8)], axis=1)
        for k, j in ((3, 0), (3, 1), (1, 0), (1, 1), (2, 0), (2, 1), (0, 0), (0, 1)):
            total = mm(left, W[2 * k + j], NN)
            if k == 0:
                OWN[s, j] = total
                continue
            STG[s, k - 1, j] = total.astype(BF)
            if k == 3 and j == 0:
                owed_copy(t, s, 0).start()
                owed_copy(t, s, 1).start()
            elif j == 0:
                PEND[k - 1] = total[part_rows(2 - k)]
        pr_copy(t, s, 3, 1).start()
        for k in (1, 2):
            pr_half(t, s, k, k - 1).start()
            pr_copy(t, s, k, 1).start()

    def add_owed(t, s):
        for k in (2, 1):
            h = 2 - k
            owed_copy(t, s, h).wait_recv()
            STG[s, k - 1, 0, part_rows(h)] = (PEND[k - 1] + CB[s, h].astype(F32)).astype(BF)
            pr_half(t, s, k, h).start()

    def input_side(t, s):
        onehot = letter(t, s)
        feat_t = mm(emb_t[...], onehot, NT).astype(BF)
        inputs = []
        for q in range(8):
            jj, gy, gc = q // 4, (q // 2) % 2, q % 2
            DWI[jj, gy, gc] += mm(feat_t, DRAW[q], NN)
            inputs.append(WIN[jj, gy, gc])
        grad_t = mm(jnp.concatenate(inputs, axis=1), jnp.concatenate([DRAW[q] for q in range(8)], axis=1), NT)
        high = grad_t.astype(BF)
        low = (grad_t - high.astype(F32)).astype(BF)
        EMBT[...] += mm(high, onehot, NN) + mm(low, onehot, NN)

    def gd_s():
        return rc(GWD.at[:, :, 1 - c], GIS.at[:, :, 0:64], s_gd.at[0], r_gd.at[0], sib)

    def gd_y():
        return rc(GWD.at[:, 1 - y, c], GY, s_gd.at[1], r_gd.at[1], ydev)

    def gd_m():
        return rc(GWD.at[1 - zh, y, c], GM, s_gd.at[2], r_gd.at[2], mir)

    turn()

    @pl.loop(0, 2 * (steps - 1))
    def _(i):
        t, s = last - i // 2, i % 2

        @pl.when(i < 2)
        def _():
            wait_h(t, s)
            logits_of(last, s)

        @pl.when(i >= 2)
        def _():
            pr_arrived(t + 1, s)

        cell_back(t, s, False)

        @pl.when(i >= 1)
        def _():
            add_owed(t + 1 - s, 1 - s)

        d_copy(t, s).start()

        @pl.when(i >= 2)
        def _():
            pr_left(t + 1, s)

        product_back(t, s)
        input_side(t, s)

        @pl.when(i < 2)
        def _():
            logits_of(last - 1, s)

        @pl.when(jnp.logical_and(i >= 2, i < 4))
        def _():
            decoder_side(last - 1, s)
            transposed_side(last - 1, s)

        @pl.when(i == 4)
        def _():
            @pl.loop(0, 2)
            def _(n):
                decoder_side(last, n)

            gd_s().start()

        @pl.when(i == 5)
        def _():
            gd_s().wait_recv()
            GWD[:, :, c] += GIS[:, :, 0:64]
            gd_y().start()

        @pl.when(i == 7)
        def _():
            gd_y().wait_recv()
            GWD[:, y, c] += GY[...]
            gd_m().start()

        @pl.when(i == 9)
        def _():
            gd_m().wait_recv()
            out_dec[...] = GWD[zh, y, c] + GM[...]

    @pl.loop(0, 2 * (steps - 1))
    def _(i):
        ht_copy(i // 2, i % 2, 0).wait_recv()
        d_copy(1 + i // 2, i % 2).wait_recv()

    depth = 2 * (steps - 1) * rows

    def kept(q):
        return A.at[2 + q // 4, (q % 4) // 2, :, pl.ds(pl.multiple_of(64 * (q % 2), 64), 64), :]

    def tile_of(q):
        k, near = q % 4, q // 4
        return 2 * k + 1 - zh + near * (2 * zh - 1)

    def ry_copy(p, q):
        return rc(SY.at[p % 4], RY.at[q], s_ry.at[p], r_ry.at[q], ydev)

    def rm_copy(k):
        return rc(SM.at[k], RM.at[k], s_rm.at[k], r_rm.at[k], mir)

    def half(h):
        return pl.ds(4 * h, 4)

    def ry_half(h):
        return rc(SY.at[0, half(h)], RY.at[3, half(h)], s_ry.at[8 + h], r_ry.at[8 + h], ydev)

    def rm_half(h):
        return rc(SM.at[3, half(h)], RM.at[3, half(h)], s_rm.at[4 + h], r_rm.at[4 + h], mir)

    def ry_sent(p):
        @pl.when(p == 0)
        def _():
            ry_half(0).wait_send()
            ry_half(1).wait_send()

        @pl.when(p > 0)
        def _():
            ry_copy(p, order(p)).wait_send()

    def rm_sent(k):
        if k == 3:
            rm_half(0).wait_send()
            rm_half(1).wait_send()
        else:
            rm_copy(k).wait_send()

    def ra_copy(k):
        return rc(SM.at[k], out_recv.at[k - 1], s_ra.at[k - 1], r_ra.at[k - 1], kdev(k))

    def order(p):
        return 3 - p + 8 * (p // 4)

    def make_tile(p):
        q = order(p)
        tile = tile_of(q)
        left, right = HT[tile], HTS[tile]
        hold = kept(q)

        @pl.when(p >= 4)
        def _():
            ry_sent(p - 4)

        for n in range(8):
            grad = mm(left, D[n].reshape(depth, 256), NN) + mm(right, DS[n].reshape(depth, 256), NN)
            hold[n] = grad[:64]
            SY[p % 4, n] = grad[64:].astype(BF)
            if n % 4 == 3:
                @pl.when(p == 0)
                def _(n=n):
                    ry_half(n // 4).start()

        @pl.when(p > 0)
        def _():
            ry_copy(p, q).start()

    def add_y(q):
        ry_copy(0, q).wait_recv()
        hold = kept(q)
        hold[...] = hold[...] + RY[q].astype(F32)

    def pass_on(k):
        if k == 3:
            for h in (0, 1):
                pass_half(h)
            return
        add_y(k)
        SM[k] = kept(k)[...].astype(BF)
        rm_copy(k).start()

    def finish(k):
        add_y(4 + k)
        if k == 3:
            rm_half(0).wait_recv()
            rm_half(1).wait_recv()
        else:
            rm_copy(k).wait_recv()
        total = kept(4 + k)[...] + RM[k].astype(F32)
        if k == 0:
            out_own[...] = total
        else:
            rm_sent(k)
            SM[k] = total.astype(BF)
            ra_copy(k).start()

    def settle(p):
        q = order(p)
        pass_on(q) if q < 4 else finish(q - 4)

    outer = jnp.logical_not(inner)

    def core_rows(cc):
        return pl.ds(pl.multiple_of(64 * cc, 64), 64)

    def piece_rows(xx):
        return pl.ds(pl.multiple_of(64 * c + 32 * xx, 32), 32)

    def sm_core():
        return rc(out_small.at[core_rows(1 - c)], RS1, s_sm.at[0], r_sm.at[0], sib)

    def sm_group(k):
        xx = kx(k)
        return rc(out_small.at[piece_rows(xx)], RS2.at[k - 1], s_sm.at[k], r_sm.at[k], kdev(k))

    def sm_quarter(n):
        return rc(PIECE, RS3.at[n], s_sm.at[4 + n], r_sm.at[4 + n], (ydev, mir, cross)[n])

    def sm_spread(k):
        return rc(TOTAL, RS4.at[k - 1], s_sm.at[6 + k], r_sm.at[6 + k], kdev(k))

    def sm_last():
        return rc(out_small.at[core_rows(c)], RS5, s_sm.at[10], r_sm.at[10], sib)

    def sm_step1():
        sm_core().wait_recv()
        out_small[core_rows(c)] = out_small[core_rows(c)] + RS1[...]

        @pl.when(outer)
        def _():
            sm_group(1).start()

        @pl.when(inner)
        def _():
            sm_group(2).start()
            sm_group(3).start()

    def sm_step2():
        @pl.when(outer)
        def _():
            for k in (1, 2, 3):
                sm_group(k).wait_recv()
            PIECE[...] = (out_small[piece_rows(x)] + RS2[0]) + (RS2[1] + RS2[2])
            for n in range(3):
                sm_quarter(n).start()

    def sm_step3():
        @pl.when(outer)
        def _():
            for n in range(3):
                sm_quarter(n).wait_recv()
            TOTAL[...] = (PIECE[...] + RS3[0]) + (RS3[1] + RS3[2])
            for k in (1, 2, 3):
                sm_spread(k).start()

    def sm_step4():
        sm_core().wait_send()

        @pl.when(outer)
        def _():
            sm_group(1).wait_send()
            sm_spread(1).wait_recv()
            out_small[piece_rows(1 - x)] = RS4[0]
            out_small[piece_rows(x)] = TOTAL[...]

        @pl.when(inner)
        def _():
            for k in (2, 3):
                sm_group(k).wait_send()
                sm_spread(k).wait_recv()
                out_small[piece_rows(kx(k))] = RS4[k - 1]

        sm_last().start()

    def sm_step5():
        sm_last().wait_recv()
        out_small[core_rows(1 - c)] = RS5[...]

    live = pl.ds(0, 104)

    def gi_s():
        return rc(DWI.at[:, :, 1 - c, live], GIS.at[:, :, :, 0:256], s_gi.at[0], r_gi.at[0], sib)

    def gi_y():
        return rc(SIY, IY, s_gi.at[1], r_gi.at[1], ydev)

    def gi_m():
        return rc(SIM, IM, s_gi.at[2], r_gi.at[2], mir)

    def gi_p():
        return rc(DWI.at[zh, y, c, live], out_in, s_gi.at[3], r_gi.at[3], back)

    def pass_half(h):
        ry_half(h).wait_recv()
        SM[3, half(h)] = (kept(3)[half(h)] + RY[3, half(h)].astype(F32)).astype(BF)
        rm_half(h).start()

    def first_position():
        @pl.loop(0, 2)
        def _(s):
            pr_arrived(1, s)
            cell_back(0, s, True)
            input_side(0, s)

            @pl.when(jnp.logical_and(inner, s == 0))
            def _():
                pass_half(0)

        leader = jnp.logical_and(x == 0, a == 0)
        high_row = lax.broadcasted_iota(jnp.int32, (8, VPAD), 0)
        loss = jnp.sum(LV[...], axis=0, keepdims=True)
        loss = jnp.concatenate([loss] * (VPAD // 128), axis=1)
        extra = jnp.where(high_row == 0, BD[...], jnp.where(high_row == 1, loss, 0.0))
        out_small[...] = EMBT[...]
        out_small[SMALL - 8 : SMALL] = jnp.where(leader, extra, 0.0)
        sm_core().start()
        gi_s().start()

    @pl.loop(0, 8)
    def _(p):
        make_tile(p)

        @pl.when(p == 0)
        def _():
            add_owed(1, 1)

        @pl.when(p == 1)
        def _():
            first_position()
            sm_step1()
            @pl.when(inner)
            def _():
                pass_half(1)

            gi_s().wait_recv()
            DWI[:, :, c, 0:104] = DWI[:, :, c, 0:104] + GIS[:, :, :, 0:256]
            sm_step2()
            SIY[...] = DWI[:, 1 - y, c, 0:112].astype(BF)
            gi_y().start()

            @pl.when(outer)
            def _():
                settle(0)

        @pl.when(p == 2)
        def _():
            settle(1)

        @pl.when(p == 3)
        def _():
            gi_y().wait_recv()
            DWI[:, y, c, 0:104] = DWI[:, y, c, 0:104] + IY[...].astype(F32)[:, 0:104]
            SIM[...] = DWI[1 - zh, y, c, 0:112].astype(BF)
            gi_m().start()

        @pl.when(p == 4)
        def _():
            settle(2)
            sm_step3()

        @pl.when(p == 5)
        def _():
            settle(3)

    settle(4)
    settle(5)
    sm_step4()
    settle(6)
    gi_m().wait_recv()
    DWI[zh, y, c, 0:104] = DWI[zh, y, c, 0:104] + IM[...].astype(F32)[0:104]

    @pl.when(moved)
    def _():
        gi_p().start()

    @pl.when(stays)
    def _():
        out_in[...] = DWI[zh, y, c, 0:104]

    sm_step5()
    settle(7)

    for k in (1, 2, 3):
        for j in (0, 1):
            wa(k, j).wait_send()
        ids_copy(k, member(0)).wait_send()
        da(k).wait_send()
        ra_copy(k).wait()
    rm_copy(0).wait_send()

    @pl.when(moved)
    def _():
        gi_p().wait()
        win_perm(x, z // 2, z % 2).wait_send()

    for s in range(2):
        pr_left(1, s)
    win_mir(zh).wait_send()
    win_y(y).wait_send()
    win_s(c).wait_send()
    @pl.when(outer)
    def _():
        for k in (1, 2, 3):
            sm_quarter(k - 1).wait_send()
            sm_spread(k).wait_send()

    for copy in (gd_s, gd_y, gd_m, gi_s, gi_y, gi_m, sm_last):
        copy().wait_send()
    for s in range(2):
        ht_copy(last - 1, s, s).wait_send()

    @pl.loop(0, 4)
    def _(k):
        dec_mir(k, 0).wait_send()

    @pl.loop(0, 8)
    def _(i):
        dec_y(i, y).wait_send()

    for p in range(4, 8):
        ry_copy(p, order(p)).wait_send()

    @pl.loop(0, 16)
    def _(i):
        dec_s(i, c).wait_send()

    @pl.loop(2 * (steps - RING + 1), 2 * steps)
    def _(i):
        released(i // 2, i % 2)

    @pl.loop(0, 2 * (steps - 1))
    def _(i):
        d_copy(1 + i // 2, i % 2).wait_send()


def output_kernel(
    own, recv, g_in, g_dec, hid_in, small, hid, table, o_in, o_bias, o_rec, o_dec, o_bias_dec, loss,
    h_buf, own_buf, recv_buf, rec_buf, in_buf, dec_buf, small_buf, t_buf, i_buf, b_buf, d_buf, bd_buf, l_buf, in_sem, out_sem,
):
    dp = lax.axis_index("dp")
    z, x = dp // 2, dp % 2
    a = z + (z // 2) * (3 - 2 * z)

    def cols(k, j, g):
        xk, ak = x + (k % 2) * (1 - 2 * x), a + (k // 2) * (1 - 2 * a)
        ub = 2 * (ak + j * (3 - 2 * ak)) + xk
        return pl.ds(pl.multiple_of(256 * (8 * g + ub), 256), 256)

    def load(n, src, dst):
        copy = pltpu.make_async_copy(src, dst, in_sem.at[n])
        copy.start()
        return copy

    def store(n, src, dst):
        copy = pltpu.make_async_copy(src, dst, out_sem.at[n])
        copy.start()
        return copy

    hid_loads = [
        load(p, hid_in.at[:, :, 256 * p : 256 * (p + 1)], h_buf.at[:, :, cols(p // 2, p % 2, 0)]) for p in range(8)
    ]
    rec_loads = [load(8, own, own_buf), load(9, recv, recv_buf)]
    small_loads = [load(10, small, small_buf), load(11, g_in, in_buf), load(12, g_dec, dec_buf)]
    for copy in hid_loads:
        copy.wait()
    stores = [store(0, h_buf, hid)]
    for copy in rec_loads:
        copy.wait()
    for k in range(4):
        for j in (0, 1):
            for g in range(4):
                part = own_buf[4 * j + g] if k == 0 else recv_buf[k - 1, 4 * j + g].astype(F32)
                rec_buf[:, cols(k, j, g)] = part
    stores.append(store(1, rec_buf, o_rec))
    for copy in small_loads:
        copy.wait()
    vocab, emb = table.shape
    t_buf[...] = small_buf[0:SMALL, :].T[:vocab, :emb]
    i_buf[...] = in_buf[0:emb, :]
    b_buf[...] = in_buf[emb, :]
    d_buf[...] = dec_buf[:, :vocab]
    bd_buf[...] = small_buf[SMALL - 8, :vocab]
    l_buf[...] = small_buf[SMALL - 7 : SMALL - 6, 0:1]
    pairs = ((t_buf, table), (i_buf, o_in), (b_buf, o_bias), (d_buf, o_dec), (bd_buf, o_bias_dec), (l_buf, loss))
    for n, (src, dst) in enumerate(pairs):
        stores.append(store(2 + n, src, dst))
    for copy in stores:
        copy.wait()


def fused(chars, resets, targets, embed, w_in, bias_in, w_rec, w_dec, bias_dec):
    micro, count, steps = chars.shape
    own_rows, gate_cols = w_rec.shape
    vocab, emb = embed.shape
    width = gate_cols // 4
    members = 4
    rows = count * members
    vm = pl.BlockSpec(memory_space=pltpu.VMEM)
    hbm = pl.BlockSpec(memory_space=pl.ANY)
    dma = pltpu.SemaphoreType.DMA
    n = steps - 1
    scratch = [
        pltpu.VMEM((8, width, 256), BF),
        pltpu.VMEM((2, 2, 2, EPAD, 256), BF),
        pltpu.VMEM((width, VPAD), BF),
        pltpu.VMEM((micro, members, count, 24), jnp.int32),
        pltpu.VMEM((RING, micro, rows, width), BF),
        pltpu.VMEM((8, 128, 2 * n * rows), BF),
        pltpu.VMEM((8, 128, 2 * n * rows), BF),
        pltpu.VMEM((2, 8, 128, rows), BF),
        pltpu.VMEM((steps, micro, 8, rows, 256), F32),
        pltpu.VMEM((steps, micro, 2, rows, 256), F32),
        pltpu.VMEM((8, n, micro, rows, 256), BF),
        pltpu.VMEM((8, n, micro, rows, 256), BF),
        pltpu.VMEM((8, rows, 256), BF),
        pltpu.VMEM((steps, micro, rows, VPAD), BF),
        pltpu.VMEM((micro, count, 24), jnp.int32),
        pltpu.VMEM((EPAD, 256), BF),
        pltpu.VMEM((EPAD, VPAD), BF),
        pltpu.VMEM((own_rows, VPAD), BF),
        pltpu.VMEM((8, VPAD), F32),
        pltpu.VMEM((2, micro, 3, 2, rows, 256), BF),
        pltpu.VMEM((micro, 3, 2, rows, 256), BF),
        pltpu.VMEM((micro, 2, rows // 2, 256), BF),
        pltpu.VMEM((2, rows // 2, 256), F32),
        pltpu.VMEM((micro, 2, rows, 256), F32),
        pltpu.VMEM((micro, 2, rows, 256), F32),
        pltpu.VMEM((4, 8, 64, 256), BF),
        pltpu.VMEM((8, 8, 64, 256), BF),
        pltpu.VMEM((4, 8, 64, 256), BF),
        pltpu.VMEM((4, 8, 64, 256), BF),
        pltpu.VMEM((EPAD, VPAD), F32),
        pltpu.VMEM((rows, 128), F32),
        pltpu.VMEM((8, VPAD), F32),
        pltpu.VMEM((2, 2, 2, 64, VPAD), F32),
        pltpu.VMEM((2, 2, 104, VPAD), F32),
        pltpu.VMEM((2, 64, VPAD), F32),
        pltpu.VMEM((64, VPAD), F32),
        pltpu.VMEM((2, 2, 2, EPAD, 256), F32),
        pltpu.VMEM((2, 112, 256), BF),
        pltpu.VMEM((2, 112, 256), BF),
        pltpu.VMEM((112, 256), BF),
        pltpu.VMEM((112, 256), BF),
        pltpu.VMEM((64, VPAD), F32),
        pltpu.VMEM((3, 32, VPAD), F32),
        pltpu.VMEM((3, 32, VPAD), F32),
        pltpu.VMEM((3, 32, VPAD), F32),
        pltpu.VMEM((64, VPAD), F32),
        pltpu.VMEM((32, VPAD), F32),
        pltpu.VMEM((32, VPAD), F32),
    ]
    shapes = [
        (3,), (4,), (3, 2), (4, 2), (8, 2), (16, 2), (3,), (4,), (8,), (16,),
        (steps, 2, 3, 2), (n, 2), (steps, 2), (steps, 2, 3, 2),
        (steps, 2, 2, 2), (steps, 2, 2), (3,), (4,), (11,), (10,), (6,), (3,),
    ]
    for shape in shapes:
        scratch += [dma(shape), dma(shape)]
    scratch += [dma((12,)), dma((steps, 2))]
    out_own, out_recv, out_in, out_dec, out_hid, out_small = pl.pallas_call(
        functools.partial(lstm_kernel, steps, rows),
        out_shape=(
            jax.ShapeDtypeStruct((8, own_rows, 256), F32),
            jax.ShapeDtypeStruct((3, 8, own_rows, 256), BF),
            jax.ShapeDtypeStruct((104, 256), F32),
            jax.ShapeDtypeStruct((own_rows, VPAD), F32),
            jax.ShapeDtypeStruct((micro * steps, count, width), BF),
            jax.ShapeDtypeStruct((EPAD, VPAD), F32),
        ),
        in_specs=[hbm] + [vm] * 8,
        out_specs=(vm, hbm, vm, vm, hbm, vm),
        scratch_shapes=scratch,
        compiler_params=pltpu.CompilerParams(
            collective_id=0, has_side_effects=True, vmem_limit_bytes=66 * 1000 * 1000
        ),
    )(
        w_rec, w_in, bias_in, w_dec, embed, bias_dec,
        chars.transpose(2, 0, 1), resets.transpose(2, 0, 1), targets.transpose(2, 0, 1),
    )
    everyone = lax.axis_size(("dp", "fsdp"))
    hid, table, g_in, g_bias, g_rec, g_dec, g_bias_dec, loss = pl.pallas_call(
        output_kernel,
        out_shape=(
            jax.ShapeDtypeStruct((micro * steps, count, width), BF),
            jax.ShapeDtypeStruct((vocab, emb), F32),
            jax.ShapeDtypeStruct((emb, 256), F32),
            jax.ShapeDtypeStruct((256,), F32),
            jax.ShapeDtypeStruct((own_rows, gate_cols), F32),
            jax.ShapeDtypeStruct((own_rows, vocab), F32),
            jax.ShapeDtypeStruct((vocab,), F32),
            jax.ShapeDtypeStruct((1, 1), F32),
        ),
        in_specs=[hbm] * 6,
        out_specs=(hbm,) * 8,
        scratch_shapes=[
            pltpu.VMEM((micro * steps, count, width), BF),
            pltpu.VMEM((8, own_rows, 256), F32),
            pltpu.VMEM((3, 8, own_rows, 256), BF),
            pltpu.VMEM((own_rows, gate_cols), F32),
            pltpu.VMEM((104, 256), F32),
            pltpu.VMEM((own_rows, VPAD), F32),
            pltpu.VMEM((EPAD, VPAD), F32),
            pltpu.VMEM((vocab, emb), F32),
            pltpu.VMEM((emb, 256), F32),
            pltpu.VMEM((256,), F32),
            pltpu.VMEM((own_rows, vocab), F32),
            pltpu.VMEM((vocab,), F32),
            pltpu.VMEM((1, 1), F32),
            dma((13,)),
            dma((8,)),
        ],
    )(out_own, out_recv, out_in, out_dec, out_hid, out_small)
    return (
        loss[0, 0] / (micro * count * steps * everyone),
        hid.reshape(micro, steps, count, width).transpose(0, 2, 1, 3),
        table,
        g_in,
        g_bias,
        g_rec,
        g_dec,
        g_bias_dec,
    )


def dot_plain(left, right):
    return jnp.dot(left, right, preferred_element_type=jnp.float32)


def dot_right_t(left, right):
    return lax.dot_general(
        left, right, (((1,), (1,)), ((), ())), preferred_element_type=jnp.float32
    )


def dot_left_t(left, right):
    return lax.dot_general(
        left, right, (((0,), (0,)), ((), ())), preferred_element_type=jnp.float32
    )


def lstm_forward(weights, embed, bias_dec, ids, marks, goals):
    w_rec, w_dec, w_in, bias_in = weights
    count, steps = ids.shape
    width = w_rec.shape[0]
    letters = jnp.arange(embed.shape[0], dtype=jnp.int32)
    onehot = (ids.T.reshape(-1)[:, None] == letters[None, :]).astype(jnp.bfloat16)
    feature = dot_plain(onehot, embed).astype(jnp.bfloat16)
    drives = (dot_plain(feature, w_in) + bias_in.astype(jnp.float32)).reshape(steps, count, -1)
    keeps = (1 - marks.T).astype(jnp.float32)[:, :, None]

    def advance(state, slot):
        hidden_now, cell = state
        drive, keep_now = slot
        prev_hidden = hidden_now * keep_now.astype(jnp.bfloat16)
        prev_cell = cell * keep_now
        pre = drive + dot_plain(prev_hidden, w_rec)
        gin, gforget, gcand, gout = jnp.split(pre, 4, axis=1)
        cell_new = jax.nn.sigmoid(gforget) * prev_cell + jax.nn.sigmoid(gin) * jnp.tanh(gcand)
        hid_new = (jax.nn.sigmoid(gout) * jnp.tanh(cell_new)).astype(jnp.bfloat16)
        return ((hid_new, cell_new), (pre, prev_hidden, prev_cell, cell_new, hid_new))

    start = (jnp.zeros((count, width), jnp.bfloat16), jnp.zeros((count, width), jnp.float32))
    state, saved = lax.scan(advance, start, (drives, keeps))
    pres, prev_hiddens, prev_cells, cells, hiddens = saved
    flat_hidden = hiddens.reshape(steps * count, width)
    logits = dot_plain(flat_hidden, w_dec) + bias_dec.astype(jnp.float32)
    top = jnp.max(logits, axis=1, keepdims=True)
    shifted = jnp.exp(logits - top)
    summed = jnp.sum(shifted, axis=1, keepdims=True)
    goal_hot = (goals.T.reshape(-1)[:, None] == letters[None, :]).astype(jnp.float32)
    loss_part = jnp.sum(top[:, 0] + jnp.log(summed[:, 0])) - jnp.sum(goal_hot * logits)
    d_logits = (shifted / summed - goal_hot).astype(jnp.bfloat16)
    kept = (pres, prev_hiddens, prev_cells, cells, keeps, flat_hidden, d_logits, feature, onehot)
    return (kept, loss_part, jnp.transpose(hiddens, (1, 0, 2)))


def lstm_backward(weights, kept):
    w_rec, w_dec, w_in, bias_in = weights
    pres, prev_hiddens, prev_cells, cells, keeps, flat_hidden, d_logits, feature, onehot = kept
    steps, count, width = cells.shape
    from_dec = dot_right_t(d_logits, w_dec).reshape(steps, count, width)

    def retreat(carry, slot):
        grad_h, grad_c = carry
        pre, prev_cell, cell, extra, keep_now = slot
        gin, gforget, gcand, gout = jnp.split(pre, 4, axis=1)
        sig_in = jax.nn.sigmoid(gin)
        sig_forget = jax.nn.sigmoid(gforget)
        sig_out = jax.nn.sigmoid(gout)
        tan_cand = jnp.tanh(gcand)
        tan_cell = jnp.tanh(cell)
        grad_hid = extra + grad_h
        grad_out = grad_hid * tan_cell
        grad_cell = grad_c + grad_hid * sig_out * (1.0 - tan_cell * tan_cell)
        d_pre = jnp.concatenate(
            [
                grad_cell * tan_cand * sig_in * (1.0 - sig_in),
                grad_cell * prev_cell * sig_forget * (1.0 - sig_forget),
                grad_cell * sig_in * (1.0 - tan_cand * tan_cand),
                grad_out * sig_out * (1.0 - sig_out),
            ],
            axis=1,
        ).astype(jnp.bfloat16)
        back_h = dot_right_t(d_pre, w_rec) * keep_now
        back_c = grad_cell * sig_forget * keep_now
        return ((back_h, back_c), d_pre)

    start = (jnp.zeros((count, width), jnp.float32), jnp.zeros((count, width), jnp.float32))
    state, d_pres = lax.scan(
        retreat, start, (pres, prev_cells, cells, from_dec, keeps), reverse=True
    )
    flat_pre = d_pres.reshape(steps * count, -1)
    grad_dec = dot_left_t(flat_hidden, d_logits)
    grad_in = dot_left_t(feature, flat_pre)
    grad_bias = jnp.sum(flat_pre.astype(jnp.float32), axis=0)
    grad_feature = dot_right_t(flat_pre, w_in)
    grad_table = lax.dot_general(
        onehot.astype(jnp.float32),
        grad_feature,
        (((0,), (0,)), ((), ())),
        precision=lax.Precision.HIGHEST,
        preferred_element_type=jnp.float32,
    )
    grad_bias_out = jnp.sum(d_logits.astype(jnp.float32), axis=0)
    flat_prev = prev_hiddens.reshape(steps * count, width)
    return (grad_dec, grad_in, grad_bias, grad_table, grad_bias_out, flat_prev, flat_pre)


def general(chars, resets, targets, embed, w_in, bias_in, w_rec, w_dec, bias_dec):
    micro, count, steps = chars.shape
    everyone = lax.axis_size(("dp", "fsdp"))
    sums = None
    prev_list = []
    pre_list = []
    hidden_list = []
    for index in range(micro):
        forward_set = (
            lax.all_gather(w_rec, ("dp", "fsdp"), axis=0, tiled=True),
            lax.all_gather(w_dec, ("dp", "fsdp"), axis=0, tiled=True),
            lax.all_gather(w_in, ("dp", "fsdp"), axis=1, tiled=True),
            lax.all_gather(bias_in, ("dp", "fsdp"), axis=0, tiled=True),
        )
        kept, loss_part, hiddens = lstm_forward(
            forward_set, embed, bias_dec, chars[index], resets[index], targets[index]
        )
        backward_set = (
            lax.all_gather(w_rec, ("dp", "fsdp"), axis=0, tiled=True),
            lax.all_gather(w_dec, ("dp", "fsdp"), axis=0, tiled=True),
            lax.all_gather(w_in, ("dp", "fsdp"), axis=1, tiled=True),
            lax.all_gather(bias_in, ("dp", "fsdp"), axis=0, tiled=True),
        )
        grad_dec, grad_in, grad_bias, grad_table, grad_bias_out, flat_prev, flat_pre = (
            lstm_backward(backward_set, kept)
        )
        pieces = (grad_dec, grad_in, grad_bias, grad_table, grad_bias_out, loss_part)
        if sums is None:
            sums = pieces
        else:
            sums = tuple((first + second for first, second in zip(sums, pieces)))
        prev_list.append(flat_prev)
        pre_list.append(flat_pre)
        hidden_list.append(hiddens)
    prev_all = jnp.concatenate(prev_list, axis=0)
    pre_all = jnp.concatenate(pre_list, axis=0)
    grad_w_rec = lax.psum_scatter(
        dot_left_t(prev_all, pre_all), ("dp", "fsdp"), scatter_dimension=0, tiled=True
    )
    grad_w_dec, grad_w_in, grad_bias_in = (
        lax.psum_scatter(sums[0], ("dp", "fsdp"), scatter_dimension=0, tiled=True),
        lax.psum_scatter(sums[1], ("dp", "fsdp"), scatter_dimension=1, tiled=True),
        lax.psum_scatter(sums[2], ("dp", "fsdp"), scatter_dimension=0, tiled=True),
    )
    grad_embed, grad_bias_dec, total = lax.psum((sums[3], sums[4], sums[5]), ("dp", "fsdp"))
    loss = total / (micro * count * steps * everyone)
    hidden = jnp.stack(hidden_list, axis=0)
    return (
        loss,
        hidden,
        grad_embed,
        grad_w_in,
        grad_bias_in,
        grad_w_rec,
        grad_w_dec,
        grad_bias_dec,
    )


def solution(mesh):
    per_device = fused if (mesh.shape["dp"], mesh.shape["fsdp"]) == (8, 4) else general
    return jax.shard_map(
        per_device,
        mesh=mesh,
        in_specs=(
            P(None, ("dp", "fsdp"), None),
            P(None, ("dp", "fsdp"), None),
            P(None, ("dp", "fsdp"), None),
            P(),
            P(None, ("dp", "fsdp")),
            P(("dp", "fsdp")),
            P(("dp", "fsdp"), None),
            P(("dp", "fsdp"), None),
            P(),
        ),
        out_specs=(
            P(),
            P(None, ("dp", "fsdp"), None, None),
            P(),
            P(None, ("dp", "fsdp")),
            P(("dp", "fsdp")),
            P(("dp", "fsdp"), None),
            P(("dp", "fsdp"), None),
            P(),
        ),
        check_vma=False,
    )
```

```python
import functools

import jax
import jax.numpy as jnp
from jax import lax
from jax.experimental import pallas as pl
from jax.experimental.pallas import tpu as pltpu
from jax.sharding import PartitionSpec as P

MESH = pl.DeviceIdType.MESH
NN = ((1,), (0,))
NT = ((1,), (1,))
TN = ((0,), (0,))
F32 = jnp.float32
BF = jnp.bfloat16

VPAD = 384
EPAD = 128
RING = 4
SMALL = 112


def mm(left, right, dims):
    return lax.dot_general(left, right, (dims, ((), ())), preferred_element_type=F32)


def sigmoid(v):
    return 0.5 * jnp.tanh(0.5 * v) + 0.5


def lstm_kernel(
    steps, rows,
    w_rec, w_in_raw, b_in_raw, w_dec_raw, emb_raw, bias_raw, chars_in, resets_in, targets_in,
    out_own, out_recv, out_in, out_dec, out_hid, out_small,
    W, WIN, WDEC, IDS, H, HT, HTS, HSEND, A, C, D, DS, DRAW, DL,
    ids_in, w_in, emb_t, w_dec, bias_dec, PR, STG, CB, PEND, OWN, DCN, SY, RY, SM, RM, EMBT, LV, BD, GWD, GIS, GY, GM, DWI, SIY, IY, SIM, IM, RS1, RS2, RS3, RS4, RS5, PIECE, PAIR, TOTAL,
    s_ids, r_ids, s_win, r_win, s_wa, r_wa, s_wm, r_wm, s_wy, r_wy, s_ws, r_ws,
    s_da, r_da, s_dm, r_dm, s_dy, r_dy, s_ds, r_ds, s_h, r_h, s_ht, r_ht, s_d, r_d,
    s_ph, r_ph, s_cb, r_cb, s_gd, r_gd, s_gi, r_gi, s_sm, r_sm, s_ry, r_ry, s_rm, r_rm, s_ra, r_ra,
    l_sem, hid_sem,
):
    last = steps - 1
    dp, fs = lax.axis_index("dp"), lax.axis_index("fsdp")
    z, x, y, c = dp // 2, dp % 2, fs // 2, fs % 2
    zh = z // 2
    a = z + zh * (3 - 2 * z)

    def dev(zz, xx, yy, cc):
        return (zz * 2 + xx, yy * 2 + cc)

    def kx(k):
        return x + (k % 2) * (1 - 2 * x)

    def kz(k):
        return z + (k // 2) * (1 - 2 * (z % 2))

    def ka(k):
        return a + (k // 2) * (1 - 2 * a)

    def kdev(k):
        return dev(kz(k), kx(k), y, c)

    def member(k):
        return 2 * kx(k) + ka(k)

    def unit_block(k, j):
        return 2 * (ka(k) + j * (3 - 2 * ka(k))) + kx(k)

    def lanes(ub):
        return pl.ds(pl.multiple_of(256 * ub, 256), 256)

    def place(k, far, yy, cc):
        return 4 * (2 * k + zh + far * (1 - 2 * zh)) + 2 * yy + cc

    def span(k, j):
        return slice(256 * (2 * k + j), 256 * (2 * k + j + 1))

    mir, ydev, sib = dev(3 - z, x, y, c), dev(z, x, 1 - y, c), dev(z, x, y, 1 - c)
    side = x + y - 2 * x * y
    perm = dev(side + zh * (3 - 2 * side), c, x, z % 2)
    back = dev(2 * zh + c, y, a + y - 2 * a * y, x)
    stays = jnp.logical_and(perm[0] == dp, perm[1] == fs)
    moved = jnp.logical_not(stays)

    def rc(src, dst, ss, rs, to):
        return pltpu.make_async_remote_copy(
            src_ref=src, dst_ref=dst, send_sem=ss, recv_sem=rs, device_id=to, device_id_type=MESH
        )

    emb, vocab = emb_raw.shape[1], emb_raw.shape[0]
    w_in[...] = jnp.zeros_like(w_in)
    w_in[0:emb, :] = w_in_raw[...]
    tail = emb // 16 * 16
    part = w_in[tail : tail + 16, :].astype(F32)
    bias_row = b_in_raw[...].astype(F32).reshape(1, 256)
    part = jnp.where(lax.broadcasted_iota(jnp.int32, (16, 256), 0) == emb - tail, bias_row, part)
    w_in[tail : tail + 16, :] = part.astype(BF)
    for s in range(2):
        stack = jnp.concatenate(
            [v for ref in (chars_in, resets_in, targets_in) for v in (ref[:, s, :], jnp.zeros((8 - steps, 32), jnp.int32))],
            axis=0,
        ).astype(F32)
        wide_stack = jnp.concatenate([stack, jnp.zeros((24, 96), F32)], axis=1)
        ids_in[s] = wide_stack.T[:32, :].astype(jnp.int32)
    barrier = pltpu.get_barrier_semaphore()

    def greet(to):
        pl.semaphore_signal(barrier, inc=1, device_id=to, device_id_type=MESH)

    for k in (1, 2, 3):
        greet(kdev(k))
    for to in (mir, ydev, sib):
        greet(to)

    @pl.when(moved)
    def _():
        greet(perm)
        greet(back)

    pl.semaphore_wait(barrier, 6 + 2 * moved.astype(jnp.int32))


    def d_slot(b):
        return WDEC.at[pl.ds(pl.multiple_of(64 * b, 64), 64), :]

    def w_cols(ub, g):
        return w_rec.at[:, lanes(8 * g + ub)]

    def w_part(j, g, b):
        return W.at[4 * j + g, pl.ds(pl.multiple_of(64 * b, 64), 64), :]

    def wa_start(k):
        for j in (0, 1):
            for g in range(4):
                rc(w_cols(unit_block(k, j), g), w_part(j, g, place(k, 0, y, c)), s_wa.at[k - 1, j], r_wa.at[k - 1, j], kdev(k)).start()

    def wa(k, j):
        b = place(k, 0, y, c)
        part = W.at[pl.ds(4 * j, 4), pl.ds(pl.multiple_of(64 * b, 64), 64), :]
        return rc(part, part, s_wa.at[k - 1, j], r_wa.at[k - 1, j], kdev(k))

    def ids_copy(k, mem):
        return rc(ids_in, IDS.at[:, mem], s_ids.at[k - 1], r_ids.at[k - 1], kdev(k))

    def own_w(j, g):
        return pltpu.make_async_copy(w_cols(unit_block(0, j), g), w_part(j, g, place(0, 0, y, c)), l_sem.at[4 * j + g])

    for j in (0, 1):
        for g in range(4):
            own_w(j, g).start()
    for k in (1, 2, 3):
        ids_copy(k, member(0)).start()

    def win_perm(jj, gy, gc):
        return rc(w_in, WIN.at[jj, gy, gc], s_win.at[0], r_win.at[0], perm)

    def win_local():
        return pltpu.make_async_copy(w_in, WIN.at[x, z // 2, z % 2], l_sem.at[8])

    @pl.when(moved)
    def _():
        win_perm(x, z // 2, z % 2).start()

    @pl.when(stays)
    def _():
        win_local().start()

    for k in (1, 2, 3):
        wa_start(k)

    def w_half(j, b):
        return W.at[pl.ds(4 * j, 4), pl.ds(pl.multiple_of(64 * b, 64), 64), :]

    def to_mir(k, j):
        b = place(k, 0, y, c)
        return rc(w_half(j, b), w_half(j, b), s_wm.at[k, j], r_wm.at[k, j], mir)

    def from_mir(k, j):
        b = place(k, 1, y, c)
        return rc(w_half(j, b), w_half(j, b), s_wm.at[k, j], r_wm.at[k, j], mir)

    def group_block(i, yy, cc):
        return place(i % 4, i // 4, yy, cc)

    def to_y(i, j):
        b = group_block(i, y, c)
        return rc(w_half(j, b), w_half(j, b), s_wy.at[i, j], r_wy.at[i, j], ydev)

    def from_y(i, j):
        b = group_block(i, 1 - y, c)
        return rc(w_half(j, b), w_half(j, b), s_wy.at[i, j], r_wy.at[i, j], ydev)

    def to_s(i, j):
        b = group_block(i % 8, y + (i // 8) * (1 - 2 * y), c)
        return rc(w_half(j, b), w_half(j, b), s_ws.at[i, j], r_ws.at[i, j], sib)

    def from_s(i, j):
        b = group_block(i % 8, y + (i // 8) * (1 - 2 * y), 1 - c)
        return rc(w_half(j, b), w_half(j, b), s_ws.at[i, j], r_ws.at[i, j], sib)

    for j in (0, 1):
        for g in range(4):
            own_w(j, g).wait()
    inner = a == 1

    @pl.when(inner)
    def _():
        for j in (0, 1):
            to_mir(0, j).start()

    for j in (0, 1):
        to_y(0, j).start()
        to_s(0, j).start()

    def win_mir(jj):
        return rc(WIN.at[y, jj, c], WIN.at[y, jj, c], s_win.at[1], r_win.at[1], mir)

    def win_y(yy):
        return rc(WIN.at[yy, :, c], WIN.at[yy, :, c], s_win.at[2], r_win.at[2], ydev)

    def win_s(cc):
        return rc(WIN.at[:, :, cc], WIN.at[:, :, cc], s_win.at[3], r_win.at[3], sib)

    @pl.when(moved)
    def _():
        win_perm(y, zh, c).wait_recv()

    @pl.when(stays)
    def _():
        win_local().wait()

    win_mir(zh).start()


    IDS[:, member(0)] = ids_in[...]

    def own_blocks(k):
        for j in (0, 1):
            wa(k, j).wait_recv()
            to_y(k, j).start()

            @pl.when(inner)
            def _(j=j):
                to_mir(k, j).start()

            to_s(k, j).start()

    own_blocks(1)
    own_blocks(2)
    own_blocks(3)

    def da(k):
        return rc(w_dec, d_slot(place(k, 0, y, c)), s_da.at[k - 1], r_da.at[k - 1], kdev(k))

    HSEND[0, 0 : VPAD // 128] = jnp.zeros((VPAD // 128, 128, rows), BF)
    for n in range(VPAD // 128):
        held = min(128, vocab - 128 * n)
        HSEND[0, n, 0:held, 0:emb] = emb_raw[128 * n : 128 * n + held, :]
    unit = jnp.where(
        lax.broadcasted_iota(jnp.int32, (EPAD, EPAD), 0) == lax.broadcasted_iota(jnp.int32, (EPAD, EPAD), 1), 1.0, 0.0
    ).astype(BF)
    turned = mm(unit, HSEND[0, 0 : VPAD // 128].reshape(VPAD, EPAD), NT)
    emb_t[...] = jnp.where(lax.broadcasted_iota(jnp.int32, (EPAD, VPAD), 0) == emb, 1.0, turned).astype(BF)
    w_dec[...] = jnp.zeros_like(w_dec)
    w_dec[:, :vocab] = w_dec_raw[...]
    bias_dec[...] = jnp.full_like(bias_dec, -1e30)
    bias_dec[0:1, :vocab] = bias_raw[...].astype(F32).reshape(1, vocab)
    for k in (1, 2, 3):
        da(k).start()
    own_dec = pltpu.make_async_copy(w_dec, d_slot(place(0, 0, y, c)), l_sem.at[9])
    own_dec.start()

    for k in (1, 2, 3):
        ids_copy(k, member(k)).wait_recv()
    lane = lax.broadcasted_iota(jnp.int32, (rows, 24), 1)
    wide = lax.broadcasted_iota(jnp.int32, (rows, VPAD), 1).astype(F32)

    def column(at, s):
        packed = IDS[s].reshape(rows, 24)
        return jnp.sum(jnp.where(lane == at, packed, 0).astype(F32), axis=1, keepdims=True)

    def keep_of(t, s):
        return 1.0 - column(8 + t, s)

    def letter(t, s):
        return jnp.where(column(t, s) == wide, 1.0, 0.0).astype(BF)

    EMBT[...] = jnp.zeros_like(EMBT)
    LV[...] = jnp.zeros_like(LV)
    BD[...] = jnp.zeros_like(BD)
    GWD[...] = jnp.zeros_like(GWD)
    DWI[...] = jnp.zeros_like(DWI)
    DCN[...] = jnp.zeros_like(DCN)
    OWN[...] = jnp.zeros_like(OWN)
    PR[0] = jnp.zeros(PR.shape[1:], BF)

    win_mir(1 - zh).wait_recv()

    win_y(y).start()
    def pass_y(i):
        for j in (0, 1):
            from_y(i, j).wait_recv()
            to_s(8 + i, j).start()

    def pass_mir(k):
        for j in (0, 1):
            from_mir(k, j).wait_recv()
            to_y(4 + k, j).start()
            to_s(4 + k, j).start()

    for i in range(3):
        pass_y(i)

    @pl.when(inner)
    def _():
        pass_mir(0)

    @pl.when(jnp.logical_not(inner))
    def _():
        for k in range(4):
            for j in (0, 1):
                to_mir(k, j).start()

    pass_y(3)
    win_y(1 - y).wait_recv()
    win_s(c).start()
    win_s(1 - c).wait_recv()

    def h_copy(t, s, k, j):
        src, dst = H.at[t % RING, s, :, span(0, j)], H.at[t % RING, s, :, span(k, j)]
        return rc(src, dst, s_h.at[t, s, k - 1, j], r_h.at[t, s, k - 1, j], kdev(k))

    def wait_h(t, s):
        for k in (1, 2, 3):
            for j in (0, 1):
                h_copy(t, s, k, j).wait_recv()

    def gates(t, s, first):
        keep = None if first else keep_of(t, s)
        feature = mm(letter(t, s), emb_t[...], NT).astype(BF)
        for j in (0, 1):
            pre = []
            for g in range(4):
                drive = mm(feature, WIN[j, g // 2, g % 2], NN)
                if not first:
                    drive = drive + keep * mm(H[(t - 1) % RING, s], W[4 * j + g], NN)
                pre.append(drive)
            s_i, s_f, t_g, s_o = sigmoid(pre[0]), sigmoid(pre[1]), jnp.tanh(pre[2]), sigmoid(pre[3])
            cell = s_i * t_g
            if not first:
                cell = s_f * (C[t - 1, s, j] * keep) + cell
            for g, v in enumerate((s_i, s_f, t_g, s_o)):
                A[t, s, 4 * j + g] = v
            C[t, s, j] = cell
            H[t % RING, s, :, span(0, j)] = (s_o * jnp.tanh(cell)).astype(BF)
            for k in (3, 1, 2):
                h_copy(t, s, k, j).start()

    @pl.loop(0, 2)
    def _(s):
        gates(0, s, True)

    @pl.when(jnp.logical_not(inner))
    def _():
        pass_mir(0)

    for k in (1, 2, 3):
        pass_mir(k)

    def dec_mir(k, far):
        b = place(k, far, y, c)
        return rc(d_slot(b), d_slot(b), s_dm.at[k], r_dm.at[k], mir)

    def dec_y(i, yy):
        b = group_block(i, yy, c)
        return rc(d_slot(b), d_slot(b), s_dy.at[i], r_dy.at[i], ydev)

    def dec_s(i, cc):
        b = group_block(i % 8, y + (i // 8) * (1 - 2 * y), cc)
        return rc(d_slot(b), d_slot(b), s_ds.at[i], r_ds.at[i], sib)

    own_dec.wait()
    dec_mir(0, 0).start()
    dec_y(0, y).start()
    dec_s(0, c).start()
    for k in (1, 2, 3):
        da(k).wait_recv()
        dec_mir(k, 0).start()
        dec_y(k, y).start()
        dec_s(k, c).start()

    for i in (4, 5, 6, 7):
        pass_y(i)

    @pl.loop(0, 16)
    def _(i):
        for j in (0, 1):
            from_s(i, j).wait_recv()

    def released(t, s):
        hid_copy(t, s).wait()
        for k in (1, 2, 3):
            for j in (0, 1):
                h_copy(t, s, k, j).wait_send()

    def forward(t, s):
        wait_h(t - 1, s)

        @pl.when(t >= RING - 1)
        def _():
            released(t - (RING - 1), s)

        gates(t, s, False)

    row = lax.broadcasted_iota(jnp.int32, (128, 256), 0)
    col = lax.broadcasted_iota(jnp.int32, (128, 256), 1)

    def select(cc):
        yy = y + (row // 64) * (1 - 2 * y)
        return jnp.where(col == 64 * (2 * yy + cc) + row % 64, 1.0, 0.0).astype(BF)

    def lane_slot(t, s):
        return pl.ds(pl.multiple_of((2 * t + s) * rows, rows), rows)

    def ht_copy(t, s, slot):
        return rc(HSEND.at[slot], HTS.at[:, :, lane_slot(t, s)], s_ht.at[t, s], r_ht.at[t, s], sib)

    def hid_copy(t, s):
        mine = H.at[t % RING, s, pl.ds(pl.multiple_of(32 * member(0), 32), 32), :]
        return pltpu.make_async_copy(mine, out_hid.at[s * steps + t], hid_sem.at[t, s])

    def logits_of(t, s):
        scores = mm(H[t % RING, s], WDEC[...], NN) + bias_dec[0:1, :]
        top = jnp.max(scores, axis=1, keepdims=True)
        shifted = jnp.exp(scores - top)
        summed = jnp.sum(shifted, axis=1, keepdims=True)
        goal = jnp.where(column(16 + t, s) == wide, 1.0, 0.0)
        picked = jnp.sum(goal * scores, axis=1, keepdims=True)
        LV[...] += jnp.broadcast_to(top + jnp.log(summed) - picked, (rows, 128))
        DL[t, s] = (shifted / summed - goal).astype(BF)

    def decoder_side(t, s):
        hid_copy(t, s).start()
        grad = DL[t, s]
        BD[...] += mm(jnp.ones((8, rows), BF), grad, NN)
        for j in (0, 1):
            GWD[j] += mm(H[t % RING, s, :, span(0, j)], grad, TN).reshape(2, 2, 64, VPAD)

    def transposed_side(t, s):
        slot = s
        mine, other = select(c), select(1 - c)

        @pl.when(t >= 1)
        def _():
            ht_copy(t - 1, s, slot).wait_send()

        for tile in range(8):
            part = H[t % RING, s, :, 256 * tile : 256 * (tile + 1)]
            HT[tile, :, lane_slot(t, s)] = mm(mine, part, NT).astype(BF)
            HSEND[slot, tile] = mm(other, part, NT).astype(BF)
        ht_copy(t, s, slot).start()

    def decoder_mirror():
        @pl.loop(0, 4)
        def _(k):
            dec_mir(k, 1).wait_recv()
            dec_y(4 + k, y).start()
            dec_s(4 + k, c).start()

    def decoder_rest():
        @pl.loop(0, 8)
        def _(i):
            k, j = i // 2, i % 2
            to_mir(k, j).wait_send()
            to_y(i, 0).wait_send()
            to_y(i, 1).wait_send()

        @pl.loop(0, 16)
        def _(i):
            to_s(i, 0).wait_send()
            to_s(i, 1).wait_send()

        @pl.loop(0, 8)
        def _(i):
            dec_y(i, 1 - y).wait_recv()
            dec_s(8 + i, c).start()

        @pl.loop(0, 16)
        def _(i):
            dec_s(i, 1 - c).wait_recv()

    def aside(t, s):
        logits_of(t, s)
        decoder_side(t, s)
        transposed_side(t, s)

    @pl.loop(2, 2 * steps)
    def _(i):
        t, s = i // 2, i % 2
        forward(t, s)

        @pl.when(i == 3)
        def _():
            decoder_mirror()

        @pl.when(i == 5)
        def _():
            decoder_rest()

        @pl.when(i >= 5)
        def _():
            @pl.loop(i - 4 - (13 - i) // 8, i - 3)
            def _(n):
                aside(n // 2, n % 2)


    def d_copy(t, s):
        return rc(D.at[:, t - 1, s], DS.at[:, t - 1, s], s_d.at[t, s], r_d.at[t, s], sib)

    def turn():
        def rows_of(q):
            return slice(256 * q, 256 * (q + 1))

        def swap(p, q):
            upper, lower = W[p, rows_of(q), :].T, W[q, rows_of(p), :].T
            W[p, rows_of(q), :] = lower
            W[q, rows_of(p), :] = upper

        for p in range(8):
            W[p, rows_of(p), :] = W[p, rows_of(p), :].T
            for q in range(p):
                swap(p, q)

    def cell_back(t, s, oldest):
        keep = keep_of(t, s)
        for j in (0, 1):
            up = WDEC[span(0, j), :]
            dh = mm(DL[t, s], up, NT)
            rest = PR[(t + 1) % 2, s, 0, j].astype(F32) + PR[(t + 1) % 2, s, 1, j].astype(F32)
            dh = dh + (OWN[s, j] + rest)
            s_i, s_f, t_g, s_o = (A[t, s, 4 * j + g] for g in range(4))
            t_c = jnp.tanh(C[t, s, j])
            d_o = dh * t_c
            d_c = dh * s_o * (1.0 - t_c * t_c) + DCN[s, j]
            d_i = d_c * t_g * s_i * (1.0 - s_i)
            d_g = d_c * s_i * (1.0 - t_g * t_g)
            d_o = d_o * s_o * (1.0 - s_o)
            if oldest:
                d_f = jnp.zeros_like(d_i)
            else:
                d_f = d_c * (C[t - 1, s, j] * keep) * s_f * (1.0 - s_f)
                DCN[s, j] = keep * (d_c * s_f)
            for g, v in enumerate((d_i, d_f, d_g, d_o)):
                low = v.astype(BF)
                DRAW[4 * j + g] = low
                if not oldest:
                    D[4 * j + g, t - 1, s] = low * keep.astype(BF)

    def part_rows(h):
        return slice(64 * h, 64 * (h + 1))

    def pr_half(t, s, k, h):
        src, dst = STG.at[s, k - 1, :, part_rows(h)], PR.at[t % 2, s, k - 1, :, part_rows(h)]
        return rc(src, dst, s_ph.at[t, s, k - 1, h], r_ph.at[t, s, k - 1, h], kdev(k))

    def owed_copy(t, s, n):
        return rc(STG.at[s, 2, :, part_rows(n)], CB.at[s, n], s_cb.at[t, s, n], r_cb.at[t, s, n], kdev(1 + n))

    def pr_each(act):
        for k in (1, 2):
            for h in (0, 1):
                act(k, h)

    def pr_arrived(t, s):
        pr_each(lambda k, h: pr_half(t, s, k, h).wait_recv())

    def pr_left(t, s):
        pr_each(lambda k, h: pr_half(t, s, k, h).wait_send())
        for n in (0, 1):
            owed_copy(t, s, n).wait_send()

    def product_back(t, s):
        left = jnp.concatenate([D[q, t - 1, s] for q in range(8)], axis=1)
        for k, j in ((3, 0), (3, 1), (1, 0), (1, 1), (2, 0), (2, 1), (0, 0), (0, 1)):
            total = mm(left, W[2 * k + j], NN)
            if k == 0:
                OWN[s, j] = total
                continue
            STG[s, k - 1, j] = total.astype(BF)
            if k < 3:
                PEND[k - 1, j] = total[part_rows(2 - k)]
            elif j == 1:
                owed_copy(t, s, 0).start()
                owed_copy(t, s, 1).start()
        for k in (1, 2):
            pr_half(t, s, k, k - 1).start()

    def add_owed(t, s):
        for k in (2, 1):
            h = 2 - k
            owed_copy(t, s, h).wait_recv()
            STG[s, k - 1, :, part_rows(h)] = (PEND[k - 1] + CB[s, h].astype(F32)).astype(BF)
            pr_half(t, s, k, h).start()

    def input_side(t, s):
        onehot = letter(t, s)
        feat_t = mm(emb_t[...], onehot, NT).astype(BF)
        inputs = []
        for q in range(8):
            jj, gy, gc = q // 4, (q // 2) % 2, q % 2
            DWI[jj, gy, gc] += mm(feat_t, DRAW[q], NN)
            inputs.append(WIN[jj, gy, gc])
        grad_t = mm(jnp.concatenate(inputs, axis=1), jnp.concatenate([DRAW[q] for q in range(8)], axis=1), NT)
        high = grad_t.astype(BF)
        low = (grad_t - high.astype(F32)).astype(BF)
        EMBT[...] += mm(high, onehot, NN) + mm(low, onehot, NN)

    def gd_s():
        return rc(GWD.at[:, :, 1 - c], GIS.at[:, :, 0:64], s_gd.at[0], r_gd.at[0], sib)

    def gd_y():
        return rc(GWD.at[:, 1 - y, c], GY, s_gd.at[1], r_gd.at[1], ydev)

    def gd_m():
        return rc(GWD.at[1 - zh, y, c], GM, s_gd.at[2], r_gd.at[2], mir)

    turn()

    @pl.loop(0, 2 * (steps - 1))
    def _(i):
        t, s = last - i // 2, i % 2

        @pl.when(i < 2)
        def _():
            wait_h(t, s)
            logits_of(last, s)

        @pl.when(i >= 2)
        def _():
            pr_arrived(t + 1, s)

        cell_back(t, s, False)

        @pl.when(i >= 1)
        def _():
            add_owed(t + 1 - s, 1 - s)

        d_copy(t, s).start()

        @pl.when(i >= 2)
        def _():
            pr_left(t + 1, s)

        product_back(t, s)

        @pl.when(i < 2 * (steps - 1) - 1)
        def _():
            input_side(t, s)

        @pl.when(i < 2)
        def _():
            logits_of(last - 1, s)

        @pl.when(jnp.logical_and(i >= 2, i < 4))
        def _():
            decoder_side(last - 1, s)
            transposed_side(last - 1, s)

        @pl.when(i == 4)
        def _():
            @pl.loop(0, 2)
            def _(n):
                decoder_side(last, n)

            gd_s().start()

        @pl.when(i == 5)
        def _():
            gd_s().wait_recv()
            GWD[:, :, c] += GIS[:, :, 0:64]
            gd_y().start()

        @pl.when(i == 7)
        def _():
            gd_y().wait_recv()
            GWD[:, y, c] += GY[...]
            gd_m().start()

        @pl.when(i == 9)
        def _():
            gd_m().wait_recv()
            out_dec[...] = GWD[zh, y, c] + GM[...]

    @pl.loop(0, 2 * (steps - 1))
    def _(i):
        ht_copy(i // 2, i % 2, 0).wait_recv()
        d_copy(1 + i // 2, i % 2).wait_recv()

    depth = 2 * (steps - 1) * rows

    def kept(q):
        return A.at[2 + q // 4, (q % 4) // 2, :, pl.ds(pl.multiple_of(64 * (q % 2), 64), 64), :]

    def tile_of(q):
        k, near = q % 4, q // 4
        return 2 * k + 1 - zh + near * (2 * zh - 1)

    def ry_copy(p, q):
        return rc(SY.at[p % 4], RY.at[q], s_ry.at[p], r_ry.at[q], ydev)

    def rm_copy(k):
        return rc(SM.at[k], RM.at[k], s_rm.at[k], r_rm.at[k], mir)

    def half(h):
        return pl.ds(4 * h, 4)

    def ry_half(h):
        return rc(SY.at[0, half(h)], RY.at[3, half(h)], s_ry.at[8 + h], r_ry.at[8 + h], ydev)

    def rm_half(h):
        return rc(SM.at[3, half(h)], RM.at[3, half(h)], s_rm.at[4 + h], r_rm.at[4 + h], mir)

    def ry_sent(p):
        @pl.when(p == 0)
        def _():
            ry_half(0).wait_send()
            ry_half(1).wait_send()

        @pl.when(p > 0)
        def _():
            ry_copy(p, order(p)).wait_send()

    def rm_sent(k):
        if k == 3:
            rm_half(0).wait_send()
            rm_half(1).wait_send()
        else:
            rm_copy(k).wait_send()

    def ra_copy(k):
        return rc(SM.at[k], out_recv.at[k - 1], s_ra.at[k - 1], r_ra.at[k - 1], kdev(k))

    def order(p):
        return 3 - p + 8 * (p // 4)

    def make_tile(p):
        q = order(p)
        tile = tile_of(q)
        left, right = HT[tile], HTS[tile]
        hold = kept(q)

        @pl.when(p >= 4)
        def _():
            ry_sent(p - 4)

        for n in range(8):
            grad = mm(left, D[n].reshape(depth, 256), NN) + mm(right, DS[n].reshape(depth, 256), NN)
            hold[n] = grad[:64]
            SY[p % 4, n] = grad[64:].astype(BF)
            if n % 4 == 3:
                @pl.when(p == 0)
                def _(n=n):
                    ry_half(n // 4).start()

        @pl.when(p > 0)
        def _():
            ry_copy(p, q).start()

    def add_y(q):
        ry_copy(0, q).wait_recv()
        hold = kept(q)
        hold[...] = hold[...] + RY[q].astype(F32)

    def pass_on(k):
        if k == 3:
            for h in (0, 1):
                pass_half(h)
            return
        add_y(k)
        SM[k] = kept(k)[...].astype(BF)
        rm_copy(k).start()

    def finish(k):
        add_y(4 + k)
        if k == 3:
            rm_half(0).wait_recv()
            rm_half(1).wait_recv()
        else:
            rm_copy(k).wait_recv()
        total = kept(4 + k)[...] + RM[k].astype(F32)
        if k == 0:
            out_own[...] = total
        else:
            rm_sent(k)
            SM[k] = total.astype(BF)
            ra_copy(k).start()

    def settle(p):
        q = order(p)
        pass_on(q) if q < 4 else finish(q - 4)

    outer = jnp.logical_not(inner)

    def core_rows(cc):
        return pl.ds(pl.multiple_of(64 * cc, 64), 64)

    def piece_rows(xx):
        return pl.ds(pl.multiple_of(64 * c + 32 * xx, 32), 32)

    def sm_core():
        return rc(out_small.at[core_rows(1 - c)], RS1, s_sm.at[0], r_sm.at[0], sib)

    def sm_group(k):
        xx = kx(k)
        return rc(out_small.at[piece_rows(xx)], RS2.at[k - 1], s_sm.at[k], r_sm.at[k], kdev(k))

    def sm_quarter(n):
        return rc(PIECE if n == 0 else PAIR, RS3.at[n], s_sm.at[4 + n], r_sm.at[4 + n], (ydev, mir)[n])

    def sm_spread(k):
        return rc(TOTAL, RS4.at[k - 1], s_sm.at[6 + k], r_sm.at[6 + k], kdev(k))

    def sm_last():
        return rc(out_small.at[core_rows(c)], RS5, s_sm.at[10], r_sm.at[10], sib)

    def sm_step1():
        sm_core().wait_recv()
        out_small[core_rows(c)] = out_small[core_rows(c)] + RS1[...]

        @pl.when(outer)
        def _():
            sm_group(1).start()

        @pl.when(inner)
        def _():
            sm_group(2).start()
            sm_group(3).start()

    def sm_step2():
        @pl.when(outer)
        def _():
            for k in (1, 2, 3):
                sm_group(k).wait_recv()
            PIECE[...] = (out_small[piece_rows(x)] + RS2[0]) + (RS2[1] + RS2[2])
            sm_quarter(0).start()

    def sm_step_mir():
        @pl.when(outer)
        def _():
            sm_quarter(0).wait_recv()
            PAIR[...] = PIECE[...] + RS3[0]
            sm_quarter(1).start()

    def sm_step3():
        @pl.when(outer)
        def _():
            sm_quarter(1).wait_recv()
            TOTAL[...] = PAIR[...] + RS3[1]
            for k in (1, 2, 3):
                sm_spread(k).start()

    def sm_step4():
        sm_core().wait_send()

        @pl.when(outer)
        def _():
            sm_group(1).wait_send()
            sm_spread(1).wait_recv()
            out_small[piece_rows(1 - x)] = RS4[0]
            out_small[piece_rows(x)] = TOTAL[...]

        @pl.when(inner)
        def _():
            for k in (2, 3):
                sm_group(k).wait_send()
                sm_spread(k).wait_recv()
                out_small[piece_rows(kx(k))] = RS4[k - 1]

        sm_last().start()

    def sm_step5():
        sm_last().wait_recv()
        out_small[core_rows(1 - c)] = RS5[...]

    live = pl.ds(0, 104)

    def gi_s():
        return rc(DWI.at[:, :, 1 - c, live], GIS.at[:, :, :, 0:256], s_gi.at[0], r_gi.at[0], sib)

    def gi_y():
        return rc(SIY, IY, s_gi.at[1], r_gi.at[1], ydev)

    def gi_m():
        return rc(SIM, IM, s_gi.at[2], r_gi.at[2], mir)

    def gi_p():
        return rc(DWI.at[y, zh, c, live], out_in, s_gi.at[3], r_gi.at[3], back)

    def pass_half(h):
        ry_half(h).wait_recv()
        SM[3, half(h)] = (kept(3)[half(h)] + RY[3, half(h)].astype(F32)).astype(BF)
        rm_half(h).start()

    def first_position():
        @pl.loop(0, 2)
        def _(s):
            pr_arrived(1, s)
            cell_back(0, s, True)
            input_side(0, s)

            @pl.when(jnp.logical_and(inner, s == 0))
            def _():
                pass_half(0)

        leader = jnp.logical_and(x == 0, a == 0)
        high_row = lax.broadcasted_iota(jnp.int32, (8, VPAD), 0)
        loss = jnp.sum(LV[...], axis=0, keepdims=True)
        loss = jnp.concatenate([loss] * (VPAD // 128), axis=1)
        extra = jnp.where(high_row == 0, BD[...], jnp.where(high_row == 1, loss, 0.0))
        out_small[...] = EMBT[...]
        out_small[SMALL - 8 : SMALL] = jnp.where(leader, extra, 0.0)
        sm_core().start()
        gi_s().start()

    @pl.loop(0, 8)
    def _(p):
        make_tile(p)

        @pl.when(p == 0)
        def _():
            add_owed(1, 1)

        @pl.when(p == 1)
        def _():
            input_side(1, 1)
            first_position()
            sm_step1()
            @pl.when(inner)
            def _():
                pass_half(1)
                settle(1)

            gi_s().wait_recv()
            DWI[:, :, c, 0:104] = DWI[:, :, c, 0:104] + GIS[:, :, :, 0:256]
            sm_step2()
            SIY[...] = DWI[1 - y, :, c, 0:112].astype(BF)
            gi_y().start()

            @pl.when(outer)
            def _():
                settle(0)

        @pl.when(p == 2)
        def _():
            @pl.when(outer)
            def _():
                settle(1)

            sm_step_mir()

        @pl.when(p == 3)
        def _():
            gi_y().wait_recv()
            DWI[y, :, c, 0:104] = DWI[y, :, c, 0:104] + IY[...].astype(F32)[:, 0:104]
            SIM[...] = DWI[y, 1 - zh, c, 0:112].astype(BF)
            gi_m().start()

        @pl.when(p == 4)
        def _():
            settle(2)
            sm_step3()

        @pl.when(p == 5)
        def _():
            settle(3)

    settle(4)
    settle(5)
    sm_step4()
    settle(6)
    gi_m().wait_recv()
    DWI[y, zh, c, 0:104] = DWI[y, zh, c, 0:104] + IM[...].astype(F32)[0:104]

    @pl.when(moved)
    def _():
        gi_p().start()

    @pl.when(stays)
    def _():
        out_in[...] = DWI[y, zh, c, 0:104]

    sm_step5()
    settle(7)

    for k in (1, 2, 3):
        for j in (0, 1):
            wa(k, j).wait_send()
        ids_copy(k, member(0)).wait_send()
        da(k).wait_send()
        ra_copy(k).wait()
    rm_copy(0).wait_send()

    @pl.when(moved)
    def _():
        gi_p().wait()
        win_perm(x, z // 2, z % 2).wait_send()

    for s in range(2):
        pr_left(1, s)
    win_mir(zh).wait_send()
    win_y(y).wait_send()
    win_s(c).wait_send()
    @pl.when(outer)
    def _():
        sm_quarter(0).wait_send()
        sm_quarter(1).wait_send()
        for k in (1, 2, 3):
            sm_spread(k).wait_send()

    for copy in (gd_s, gd_y, gd_m, gi_s, gi_y, gi_m, sm_last):
        copy().wait_send()
    for s in range(2):
        ht_copy(last - 1, s, s).wait_send()

    @pl.loop(0, 4)
    def _(k):
        dec_mir(k, 0).wait_send()

    @pl.loop(0, 8)
    def _(i):
        dec_y(i, y).wait_send()

    for p in range(4, 8):
        ry_copy(p, order(p)).wait_send()

    @pl.loop(0, 16)
    def _(i):
        dec_s(i, c).wait_send()

    @pl.loop(2 * (steps - RING + 1), 2 * steps)
    def _(i):
        released(i // 2, i % 2)

    @pl.loop(0, 2 * (steps - 1))
    def _(i):
        d_copy(1 + i // 2, i % 2).wait_send()


def output_kernel(
    own, recv, g_in, g_dec, hid_in, small, hid, table, o_in, o_bias, o_rec, o_dec, o_bias_dec, loss,
    h_buf, own_buf, recv_buf, rec_buf, in_buf, dec_buf, small_buf, t_buf, i_buf, b_buf, d_buf, bd_buf, l_buf, in_sem, out_sem,
):
    dp = lax.axis_index("dp")
    z, x = dp // 2, dp % 2
    a = z + (z // 2) * (3 - 2 * z)

    def cols(k, j, g):
        xk, ak = x + (k % 2) * (1 - 2 * x), a + (k // 2) * (1 - 2 * a)
        ub = 2 * (ak + j * (3 - 2 * ak)) + xk
        return pl.ds(pl.multiple_of(256 * (8 * g + ub), 256), 256)

    def load(n, src, dst):
        copy = pltpu.make_async_copy(src, dst, in_sem.at[n])
        copy.start()
        return copy

    def store(n, src, dst):
        copy = pltpu.make_async_copy(src, dst, out_sem.at[n])
        copy.start()
        return copy

    hid_loads = [
        load(p, hid_in.at[:, :, 256 * p : 256 * (p + 1)], h_buf.at[:, :, cols(p // 2, p % 2, 0)]) for p in range(8)
    ]
    rec_loads = [load(8, own, own_buf), load(9, recv, recv_buf)]
    small_loads = [load(10, small, small_buf), load(11, g_in, in_buf), load(12, g_dec, dec_buf)]
    for copy in hid_loads:
        copy.wait()
    stores = [store(0, h_buf, hid)]
    for copy in rec_loads:
        copy.wait()
    for k in range(4):
        for j in (0, 1):
            for g in range(4):
                part = own_buf[4 * j + g] if k == 0 else recv_buf[k - 1, 4 * j + g].astype(F32)
                rec_buf[:, cols(k, j, g)] = part
    stores.append(store(1, rec_buf, o_rec))
    for copy in small_loads:
        copy.wait()
    vocab, emb = table.shape
    t_buf[...] = small_buf[0:SMALL, :].T[:vocab, :emb]
    i_buf[...] = in_buf[0:emb, :]
    b_buf[...] = in_buf[emb, :]
    d_buf[...] = dec_buf[:, :vocab]
    bd_buf[...] = small_buf[SMALL - 8, :vocab]
    l_buf[...] = small_buf[SMALL - 7 : SMALL - 6, 0:1]
    pairs = ((t_buf, table), (i_buf, o_in), (b_buf, o_bias), (d_buf, o_dec), (bd_buf, o_bias_dec), (l_buf, loss))
    for n, (src, dst) in enumerate(pairs):
        stores.append(store(2 + n, src, dst))
    for copy in stores:
        copy.wait()


def fused(chars, resets, targets, embed, w_in, bias_in, w_rec, w_dec, bias_dec):
    micro, count, steps = chars.shape
    own_rows, gate_cols = w_rec.shape
    vocab, emb = embed.shape
    width = gate_cols // 4
    members = 4
    rows = count * members
    vm = pl.BlockSpec(memory_space=pltpu.VMEM)
    hbm = pl.BlockSpec(memory_space=pl.ANY)
    dma = pltpu.SemaphoreType.DMA
    n = steps - 1
    scratch = [
        pltpu.VMEM((8, width, 256), BF),
        pltpu.VMEM((2, 2, 2, EPAD, 256), BF),
        pltpu.VMEM((width, VPAD), BF),
        pltpu.VMEM((micro, members, count, 24), jnp.int32),
        pltpu.VMEM((RING, micro, rows, width), BF),
        pltpu.VMEM((8, 128, 2 * n * rows), BF),
        pltpu.VMEM((8, 128, 2 * n * rows), BF),
        pltpu.VMEM((2, 8, 128, rows), BF),
        pltpu.VMEM((steps, micro, 8, rows, 256), F32),
        pltpu.VMEM((steps, micro, 2, rows, 256), F32),
        pltpu.VMEM((8, n, micro, rows, 256), BF),
        pltpu.VMEM((8, n, micro, rows, 256), BF),
        pltpu.VMEM((8, rows, 256), BF),
        pltpu.VMEM((steps, micro, rows, VPAD), BF),
        pltpu.VMEM((micro, count, 24), jnp.int32),
        pltpu.VMEM((EPAD, 256), BF),
        pltpu.VMEM((EPAD, VPAD), BF),
        pltpu.VMEM((own_rows, VPAD), BF),
        pltpu.VMEM((8, VPAD), F32),
        pltpu.VMEM((2, micro, 2, 2, rows, 256), BF),
        pltpu.VMEM((micro, 3, 2, rows, 256), BF),
        pltpu.VMEM((micro, 2, 2, rows // 2, 256), BF),
        pltpu.VMEM((2, 2, rows // 2, 256), F32),
        pltpu.VMEM((micro, 2, rows, 256), F32),
        pltpu.VMEM((micro, 2, rows, 256), F32),
        pltpu.VMEM((4, 8, 64, 256), BF),
        pltpu.VMEM((8, 8, 64, 256), BF),
        pltpu.VMEM((4, 8, 64, 256), BF),
        pltpu.VMEM((4, 8, 64, 256), BF),
        pltpu.VMEM((EPAD, VPAD), F32),
        pltpu.VMEM((rows, 128), F32),
        pltpu.VMEM((8, VPAD), F32),
        pltpu.VMEM((2, 2, 2, 64, VPAD), F32),
        pltpu.VMEM((2, 2, 104, VPAD), F32),
        pltpu.VMEM((2, 64, VPAD), F32),
        pltpu.VMEM((64, VPAD), F32),
        pltpu.VMEM((2, 2, 2, EPAD, 256), F32),
        pltpu.VMEM((2, 112, 256), BF),
        pltpu.VMEM((2, 112, 256), BF),
        pltpu.VMEM((112, 256), BF),
        pltpu.VMEM((112, 256), BF),
        pltpu.VMEM((64, VPAD), F32),
        pltpu.VMEM((3, 32, VPAD), F32),
        pltpu.VMEM((2, 32, VPAD), F32),
        pltpu.VMEM((3, 32, VPAD), F32),
        pltpu.VMEM((64, VPAD), F32),
        pltpu.VMEM((32, VPAD), F32),
        pltpu.VMEM((32, VPAD), F32),
        pltpu.VMEM((32, VPAD), F32),
    ]
    shapes = [
        (3,), (4,), (3, 2), (4, 2), (8, 2), (16, 2), (3,), (4,), (8,), (16,),
        (steps, 2, 3, 2), (n, 2), (steps, 2),
        (steps, 2, 2, 2), (steps, 2, 2), (3,), (4,), (11,), (10,), (6,), (3,),
    ]
    for shape in shapes:
        scratch += [dma(shape), dma(shape)]
    scratch += [dma((12,)), dma((steps, 2))]
    out_own, out_recv, out_in, out_dec, out_hid, out_small = pl.pallas_call(
        functools.partial(lstm_kernel, steps, rows),
        out_shape=(
            jax.ShapeDtypeStruct((8, own_rows, 256), F32),
            jax.ShapeDtypeStruct((3, 8, own_rows, 256), BF),
            jax.ShapeDtypeStruct((104, 256), F32),
            jax.ShapeDtypeStruct((own_rows, VPAD), F32),
            jax.ShapeDtypeStruct((micro * steps, count, width), BF),
            jax.ShapeDtypeStruct((EPAD, VPAD), F32),
        ),
        in_specs=[hbm] + [vm] * 8,
        out_specs=(vm, hbm, vm, vm, hbm, vm),
        scratch_shapes=scratch,
        compiler_params=pltpu.CompilerParams(
            collective_id=0, has_side_effects=True, vmem_limit_bytes=66 * 1000 * 1000
        ),
    )(
        w_rec, w_in, bias_in, w_dec, embed, bias_dec,
        chars.transpose(2, 0, 1), resets.transpose(2, 0, 1), targets.transpose(2, 0, 1),
    )
    everyone = lax.axis_size(("dp", "fsdp"))
    hid, table, g_in, g_bias, g_rec, g_dec, g_bias_dec, loss = pl.pallas_call(
        output_kernel,
        out_shape=(
            jax.ShapeDtypeStruct((micro * steps, count, width), BF),
            jax.ShapeDtypeStruct((vocab, emb), F32),
            jax.ShapeDtypeStruct((emb, 256), F32),
            jax.ShapeDtypeStruct((256,), F32),
            jax.ShapeDtypeStruct((own_rows, gate_cols), F32),
            jax.ShapeDtypeStruct((own_rows, vocab), F32),
            jax.ShapeDtypeStruct((vocab,), F32),
            jax.ShapeDtypeStruct((1, 1), F32),
        ),
        in_specs=[hbm] * 6,
        out_specs=(hbm,) * 8,
        scratch_shapes=[
            pltpu.VMEM((micro * steps, count, width), BF),
            pltpu.VMEM((8, own_rows, 256), F32),
            pltpu.VMEM((3, 8, own_rows, 256), BF),
            pltpu.VMEM((own_rows, gate_cols), F32),
            pltpu.VMEM((104, 256), F32),
            pltpu.VMEM((own_rows, VPAD), F32),
            pltpu.VMEM((EPAD, VPAD), F32),
            pltpu.VMEM((vocab, emb), F32),
            pltpu.VMEM((emb, 256), F32),
            pltpu.VMEM((256,), F32),
            pltpu.VMEM((own_rows, vocab), F32),
            pltpu.VMEM((vocab,), F32),
            pltpu.VMEM((1, 1), F32),
            dma((13,)),
            dma((8,)),
        ],
    )(out_own, out_recv, out_in, out_dec, out_hid, out_small)
    return (
        loss[0, 0] / (micro * count * steps * everyone),
        hid.reshape(micro, steps, count, width).transpose(0, 2, 1, 3),
        table,
        g_in,
        g_bias,
        g_rec,
        g_dec,
        g_bias_dec,
    )


def dot_plain(left, right):
    return jnp.dot(left, right, preferred_element_type=jnp.float32)


def dot_right_t(left, right):
    return lax.dot_general(
        left, right, (((1,), (1,)), ((), ())), preferred_element_type=jnp.float32
    )


def dot_left_t(left, right):
    return lax.dot_general(
        left, right, (((0,), (0,)), ((), ())), preferred_element_type=jnp.float32
    )


def lstm_forward(weights, embed, bias_dec, ids, marks, goals):
    w_rec, w_dec, w_in, bias_in = weights
    count, steps = ids.shape
    width = w_rec.shape[0]
    letters = jnp.arange(embed.shape[0], dtype=jnp.int32)
    onehot = (ids.T.reshape(-1)[:, None] == letters[None, :]).astype(jnp.bfloat16)
    feature = dot_plain(onehot, embed).astype(jnp.bfloat16)
    drives = (dot_plain(feature, w_in) + bias_in.astype(jnp.float32)).reshape(steps, count, -1)
    keeps = (1 - marks.T).astype(jnp.float32)[:, :, None]

    def advance(state, slot):
        hidden_now, cell = state
        drive, keep_now = slot
        prev_hidden = hidden_now * keep_now.astype(jnp.bfloat16)
        prev_cell = cell * keep_now
        pre = drive + dot_plain(prev_hidden, w_rec)
        gin, gforget, gcand, gout = jnp.split(pre, 4, axis=1)
        cell_new = jax.nn.sigmoid(gforget) * prev_cell + jax.nn.sigmoid(gin) * jnp.tanh(gcand)
        hid_new = (jax.nn.sigmoid(gout) * jnp.tanh(cell_new)).astype(jnp.bfloat16)
        return ((hid_new, cell_new), (pre, prev_hidden, prev_cell, cell_new, hid_new))

    start = (jnp.zeros((count, width), jnp.bfloat16), jnp.zeros((count, width), jnp.float32))
    state, saved = lax.scan(advance, start, (drives, keeps))
    pres, prev_hiddens, prev_cells, cells, hiddens = saved
    flat_hidden = hiddens.reshape(steps * count, width)
    logits = dot_plain(flat_hidden, w_dec) + bias_dec.astype(jnp.float32)
    top = jnp.max(logits, axis=1, keepdims=True)
    shifted = jnp.exp(logits - top)
    summed = jnp.sum(shifted, axis=1, keepdims=True)
    goal_hot = (goals.T.reshape(-1)[:, None] == letters[None, :]).astype(jnp.float32)
    loss_part = jnp.sum(top[:, 0] + jnp.log(summed[:, 0])) - jnp.sum(goal_hot * logits)
    d_logits = (shifted / summed - goal_hot).astype(jnp.bfloat16)
    kept = (pres, prev_hiddens, prev_cells, cells, keeps, flat_hidden, d_logits, feature, onehot)
    return (kept, loss_part, jnp.transpose(hiddens, (1, 0, 2)))


def lstm_backward(weights, kept):
    w_rec, w_dec, w_in, bias_in = weights
    pres, prev_hiddens, prev_cells, cells, keeps, flat_hidden, d_logits, feature, onehot = kept
    steps, count, width = cells.shape
    from_dec = dot_right_t(d_logits, w_dec).reshape(steps, count, width)

    def retreat(carry, slot):
        grad_h, grad_c = carry
        pre, prev_cell, cell, extra, keep_now = slot
        gin, gforget, gcand, gout = jnp.split(pre, 4, axis=1)
        sig_in = jax.nn.sigmoid(gin)
        sig_forget = jax.nn.sigmoid(gforget)
        sig_out = jax.nn.sigmoid(gout)
        tan_cand = jnp.tanh(gcand)
        tan_cell = jnp.tanh(cell)
        grad_hid = extra + grad_h
        grad_out = grad_hid * tan_cell
        grad_cell = grad_c + grad_hid * sig_out * (1.0 - tan_cell * tan_cell)
        d_pre = jnp.concatenate(
            [
                grad_cell * tan_cand * sig_in * (1.0 - sig_in),
                grad_cell * prev_cell * sig_forget * (1.0 - sig_forget),
                grad_cell * sig_in * (1.0 - tan_cand * tan_cand),
                grad_out * sig_out * (1.0 - sig_out),
            ],
            axis=1,
        ).astype(jnp.bfloat16)
        back_h = dot_right_t(d_pre, w_rec) * keep_now
        back_c = grad_cell * sig_forget * keep_now
        return ((back_h, back_c), d_pre)

    start = (jnp.zeros((count, width), jnp.float32), jnp.zeros((count, width), jnp.float32))
    state, d_pres = lax.scan(
        retreat, start, (pres, prev_cells, cells, from_dec, keeps), reverse=True
    )
    flat_pre = d_pres.reshape(steps * count, -1)
    grad_dec = dot_left_t(flat_hidden, d_logits)
    grad_in = dot_left_t(feature, flat_pre)
    grad_bias = jnp.sum(flat_pre.astype(jnp.float32), axis=0)
    grad_feature = dot_right_t(flat_pre, w_in)
    grad_table = lax.dot_general(
        onehot.astype(jnp.float32),
        grad_feature,
        (((0,), (0,)), ((), ())),
        precision=lax.Precision.HIGHEST,
        preferred_element_type=jnp.float32,
    )
    grad_bias_out = jnp.sum(d_logits.astype(jnp.float32), axis=0)
    flat_prev = prev_hiddens.reshape(steps * count, width)
    return (grad_dec, grad_in, grad_bias, grad_table, grad_bias_out, flat_prev, flat_pre)


def general(chars, resets, targets, embed, w_in, bias_in, w_rec, w_dec, bias_dec):
    micro, count, steps = chars.shape
    everyone = lax.axis_size(("dp", "fsdp"))
    sums = None
    prev_list = []
    pre_list = []
    hidden_list = []
    for index in range(micro):
        forward_set = (
            lax.all_gather(w_rec, ("dp", "fsdp"), axis=0, tiled=True),
            lax.all_gather(w_dec, ("dp", "fsdp"), axis=0, tiled=True),
            lax.all_gather(w_in, ("dp", "fsdp"), axis=1, tiled=True),
            lax.all_gather(bias_in, ("dp", "fsdp"), axis=0, tiled=True),
        )
        kept, loss_part, hiddens = lstm_forward(
            forward_set, embed, bias_dec, chars[index], resets[index], targets[index]
        )
        backward_set = (
            lax.all_gather(w_rec, ("dp", "fsdp"), axis=0, tiled=True),
            lax.all_gather(w_dec, ("dp", "fsdp"), axis=0, tiled=True),
            lax.all_gather(w_in, ("dp", "fsdp"), axis=1, tiled=True),
            lax.all_gather(bias_in, ("dp", "fsdp"), axis=0, tiled=True),
        )
        grad_dec, grad_in, grad_bias, grad_table, grad_bias_out, flat_prev, flat_pre = (
            lstm_backward(backward_set, kept)
        )
        pieces = (grad_dec, grad_in, grad_bias, grad_table, grad_bias_out, loss_part)
        if sums is None:
            sums = pieces
        else:
            sums = tuple((first + second for first, second in zip(sums, pieces)))
        prev_list.append(flat_prev)
        pre_list.append(flat_pre)
        hidden_list.append(hiddens)
    prev_all = jnp.concatenate(prev_list, axis=0)
    pre_all = jnp.concatenate(pre_list, axis=0)
    grad_w_rec = lax.psum_scatter(
        dot_left_t(prev_all, pre_all), ("dp", "fsdp"), scatter_dimension=0, tiled=True
    )
    grad_w_dec, grad_w_in, grad_bias_in = (
        lax.psum_scatter(sums[0], ("dp", "fsdp"), scatter_dimension=0, tiled=True),
        lax.psum_scatter(sums[1], ("dp", "fsdp"), scatter_dimension=1, tiled=True),
        lax.psum_scatter(sums[2], ("dp", "fsdp"), scatter_dimension=0, tiled=True),
    )
    grad_embed, grad_bias_dec, total = lax.psum((sums[3], sums[4], sums[5]), ("dp", "fsdp"))
    loss = total / (micro * count * steps * everyone)
    hidden = jnp.stack(hidden_list, axis=0)
    return (
        loss,
        hidden,
        grad_embed,
        grad_w_in,
        grad_bias_in,
        grad_w_rec,
        grad_w_dec,
        grad_bias_dec,
    )


def solution(mesh):
    per_device = fused if (mesh.shape["dp"], mesh.shape["fsdp"]) == (8, 4) else general
    return jax.shard_map(
        per_device,
        mesh=mesh,
        in_specs=(
            P(None, ("dp", "fsdp"), None),
            P(None, ("dp", "fsdp"), None),
            P(None, ("dp", "fsdp"), None),
            P(),
            P(None, ("dp", "fsdp")),
            P(("dp", "fsdp")),
            P(("dp", "fsdp"), None),
            P(("dp", "fsdp"), None),
            P(),
        ),
        out_specs=(
            P(),
            P(None, ("dp", "fsdp"), None, None),
            P(),
            P(None, ("dp", "fsdp")),
            P(("dp", "fsdp")),
            P(("dp", "fsdp"), None),
            P(("dp", "fsdp"), None),
            P(),
        ),
        check_vma=False,
    )
```

```python
import functools

import jax
import jax.numpy as jnp
from jax import lax
from jax.experimental import pallas as pl
from jax.experimental.pallas import tpu as pltpu
from jax.sharding import PartitionSpec as P

MESH = pl.DeviceIdType.MESH
NN = ((1,), (0,))
NT = ((1,), (1,))
TN = ((0,), (0,))
F32 = jnp.float32
BF = jnp.bfloat16

VPAD = 384
EPAD = 128
RING = 4
SMALL = 112


def mm(left, right, dims):
    return lax.dot_general(left, right, (dims, ((), ())), preferred_element_type=F32)


def sigmoid(v):
    return 0.5 * jnp.tanh(0.5 * v) + 0.5


def lstm_kernel(
    steps, rows,
    w_rec, w_in_hbm, b_in_hbm, w_dec_hbm, emb_hbm, bias_hbm, chars_hbm, resets_hbm, targets_hbm,
    out_own, out_recv, out_in, out_dec, out_hid, out_small,
    W, WIN, WDEC, IDS, H, HT, HTS, HSEND, A, C, D, DS, DRAW, DL,
    w_in_raw, b_in_raw, w_dec_raw, emb_raw, bias_raw, chars_in, resets_in, targets_in, load_sem, ids_in, w_in, emb_t, w_dec, bias_dec, PR, STG, CB, PEND, OWN, DCN, SY, RY, SM, RM, EMBT, LV, BD, GWD, GIS, GY, SGM, GM, DWI, SIY, IY, SIM, IM, RS1, RS2, RS3, RS4, RS5, PIECE, PAIR, TOTAL,
    s_ids, r_ids, s_win, r_win, s_wa, r_wa, s_wm, r_wm, s_wy, r_wy, s_ws, r_ws,
    s_da, r_da, s_dm, r_dm, s_dy, r_dy, s_ds, r_ds, s_h, r_h, s_ht, r_ht, s_d, r_d,
    s_ph, r_ph, s_cb, r_cb, s_gd, r_gd, s_gi, r_gi, s_sm, r_sm, s_ry, r_ry, s_rm, r_rm, s_ra, r_ra,
    l_sem, hid_sem,
):
    last = steps - 1
    dp, fs = lax.axis_index("dp"), lax.axis_index("fsdp")
    z, x, y, c = dp // 2, dp % 2, fs // 2, fs % 2
    zh = z // 2
    a = z + zh * (3 - 2 * z)

    def dev(zz, xx, yy, cc):
        return (zz * 2 + xx, yy * 2 + cc)

    def kx(k):
        return x + (k % 2) * (1 - 2 * x)

    def kz(k):
        return z + (k // 2) * (1 - 2 * (z % 2))

    def ka(k):
        return a + (k // 2) * (1 - 2 * a)

    def kdev(k):
        return dev(kz(k), kx(k), y, c)

    def member(k):
        return 2 * kx(k) + ka(k)

    def unit_block(k, j):
        return 2 * (ka(k) + j * (3 - 2 * ka(k))) + kx(k)

    def lanes(ub):
        return pl.ds(pl.multiple_of(256 * ub, 256), 256)

    def place(k, far, yy, cc):
        return 4 * (2 * k + zh + far * (1 - 2 * zh)) + 2 * yy + cc

    def span(k, j):
        return slice(256 * (2 * k + j), 256 * (2 * k + j + 1))

    mir, ydev, sib = dev(3 - z, x, y, c), dev(z, x, 1 - y, c), dev(z, x, y, 1 - c)
    side = x + y - 2 * x * y
    perm = dev(side + zh * (3 - 2 * side), c, x, z % 2)
    back = dev(2 * zh + c, y, a + y - 2 * a * y, x)
    stays = jnp.logical_and(perm[0] == dp, perm[1] == fs)
    moved = jnp.logical_not(stays)

    def rc(src, dst, ss, rs, to):
        return pltpu.make_async_remote_copy(
            src_ref=src, dst_ref=dst, send_sem=ss, recv_sem=rs, device_id=to, device_id_type=MESH
        )

    barrier = pltpu.get_barrier_semaphore()

    def greet(to):
        pl.semaphore_signal(barrier, inc=1, device_id=to, device_id_type=MESH)

    for k in (1, 2, 3):
        greet(kdev(k))
    for to in (mir, ydev, sib):
        greet(to)

    @pl.when(moved)
    def _():
        greet(perm)
        greet(back)

    pairs = (
        (w_in_hbm, w_in_raw), (b_in_hbm, b_in_raw), (w_dec_hbm, w_dec_raw), (emb_hbm, emb_raw), (bias_hbm, bias_raw),
        (chars_hbm, chars_in), (resets_hbm, resets_in), (targets_hbm, targets_in),
    )
    loads = [pltpu.make_async_copy(src, dst, load_sem.at[n]) for n, (src, dst) in enumerate(pairs)]
    for load in loads:
        load.start()
    for load in loads:
        load.wait()
    emb, vocab = emb_raw.shape[1], emb_raw.shape[0]
    w_in[...] = jnp.zeros_like(w_in)
    w_in[0:emb, :] = w_in_raw[...]
    tail = emb // 16 * 16
    part = w_in[tail : tail + 16, :].astype(F32)
    bias_row = b_in_raw[...].astype(F32).reshape(1, 256)
    part = jnp.where(lax.broadcasted_iota(jnp.int32, (16, 256), 0) == emb - tail, bias_row, part)
    w_in[tail : tail + 16, :] = part.astype(BF)
    for s in range(2):
        stack = jnp.concatenate(
            [v for ref in (chars_in, resets_in, targets_in) for v in (ref[:, s, :], jnp.zeros((8 - steps, 32), jnp.int32))],
            axis=0,
        ).astype(F32)
        wide_stack = jnp.concatenate([stack, jnp.zeros((24, 96), F32)], axis=1)
        ids_in[s] = wide_stack.T[:32, :].astype(jnp.int32)
    pl.semaphore_wait(barrier, 6 + 2 * moved.astype(jnp.int32))


    def d_slot(b):
        return WDEC.at[pl.ds(pl.multiple_of(64 * b, 64), 64), :]

    def w_cols(ub, g):
        return w_rec.at[:, lanes(8 * g + ub)]

    def w_part(j, g, b):
        return W.at[4 * j + g, pl.ds(pl.multiple_of(64 * b, 64), 64), :]

    def wa_start(k):
        for j in (0, 1):
            for g in range(4):
                rc(w_cols(unit_block(k, j), g), w_part(j, g, place(k, 0, y, c)), s_wa.at[k - 1, j], r_wa.at[k - 1, j], kdev(k)).start()

    def wa(k, j):
        b = place(k, 0, y, c)
        part = W.at[pl.ds(4 * j, 4), pl.ds(pl.multiple_of(64 * b, 64), 64), :]
        return rc(part, part, s_wa.at[k - 1, j], r_wa.at[k - 1, j], kdev(k))

    def ids_copy(k, mem):
        return rc(ids_in, IDS.at[:, mem], s_ids.at[k - 1], r_ids.at[k - 1], kdev(k))

    def own_w(j, g):
        return pltpu.make_async_copy(w_cols(unit_block(0, j), g), w_part(j, g, place(0, 0, y, c)), l_sem.at[4 * j + g])

    for j in (0, 1):
        for g in range(4):
            own_w(j, g).start()
    for k in (1, 2, 3):
        ids_copy(k, member(0)).start()

    def win_perm(jj, gy, gc):
        return rc(w_in, WIN.at[jj, gy, gc], s_win.at[0], r_win.at[0], perm)

    def win_local():
        return pltpu.make_async_copy(w_in, WIN.at[x, z // 2, z % 2], l_sem.at[8])

    @pl.when(moved)
    def _():
        win_perm(x, z // 2, z % 2).start()

    @pl.when(stays)
    def _():
        win_local().start()

    for k in (1, 2, 3):
        wa_start(k)

    def w_half(j, b):
        return W.at[pl.ds(4 * j, 4), pl.ds(pl.multiple_of(64 * b, 64), 64), :]

    def to_mir(k, j):
        b = place(k, 0, y, c)
        return rc(w_half(j, b), w_half(j, b), s_wm.at[k, j], r_wm.at[k, j], mir)

    def from_mir(k, j):
        b = place(k, 1, y, c)
        return rc(w_half(j, b), w_half(j, b), s_wm.at[k, j], r_wm.at[k, j], mir)

    def group_block(i, yy, cc):
        return place(i % 4, i // 4, yy, cc)

    def to_y(i, j):
        b = group_block(i, y, c)
        return rc(w_half(j, b), w_half(j, b), s_wy.at[i, j], r_wy.at[i, j], ydev)

    def from_y(i, j):
        b = group_block(i, 1 - y, c)
        return rc(w_half(j, b), w_half(j, b), s_wy.at[i, j], r_wy.at[i, j], ydev)

    def to_s(i, j):
        b = group_block(i % 8, y + (i // 8) * (1 - 2 * y), c)
        return rc(w_half(j, b), w_half(j, b), s_ws.at[i, j], r_ws.at[i, j], sib)

    def from_s(i, j):
        b = group_block(i % 8, y + (i // 8) * (1 - 2 * y), 1 - c)
        return rc(w_half(j, b), w_half(j, b), s_ws.at[i, j], r_ws.at[i, j], sib)

    for j in (0, 1):
        for g in range(4):
            own_w(j, g).wait()
    inner = a == 1

    @pl.when(inner)
    def _():
        for j in (0, 1):
            to_mir(0, j).start()

    for j in (0, 1):
        to_y(0, j).start()
        to_s(0, j).start()

    def win_mir(jj):
        return rc(WIN.at[y, jj, c], WIN.at[y, jj, c], s_win.at[1], r_win.at[1], mir)

    def win_y(yy):
        return rc(WIN.at[yy, :, c], WIN.at[yy, :, c], s_win.at[2], r_win.at[2], ydev)

    def win_s(cc):
        return rc(WIN.at[:, :, cc], WIN.at[:, :, cc], s_win.at[3], r_win.at[3], sib)

    @pl.when(moved)
    def _():
        win_perm(y, zh, c).wait_recv()

    @pl.when(stays)
    def _():
        win_local().wait()

    win_mir(zh).start()


    IDS[:, member(0)] = ids_in[...]

    def own_blocks(k):
        for j in (0, 1):
            wa(k, j).wait_recv()
            to_y(k, j).start()

            @pl.when(inner)
            def _(j=j):
                to_mir(k, j).start()

            to_s(k, j).start()

    own_blocks(1)
    own_blocks(2)
    own_blocks(3)

    def da(k):
        return rc(w_dec, d_slot(place(k, 0, y, c)), s_da.at[k - 1], r_da.at[k - 1], kdev(k))

    HSEND[0, 0 : VPAD // 128] = jnp.zeros((VPAD // 128, 128, rows), BF)
    for n in range(VPAD // 128):
        held = min(128, vocab - 128 * n)
        HSEND[0, n, 0:held, 0:emb] = emb_raw[128 * n : 128 * n + held, :]
    unit = jnp.where(
        lax.broadcasted_iota(jnp.int32, (EPAD, EPAD), 0) == lax.broadcasted_iota(jnp.int32, (EPAD, EPAD), 1), 1.0, 0.0
    ).astype(BF)
    turned = mm(unit, HSEND[0, 0 : VPAD // 128].reshape(VPAD, EPAD), NT)
    emb_t[...] = jnp.where(lax.broadcasted_iota(jnp.int32, (EPAD, VPAD), 0) == emb, 1.0, turned).astype(BF)
    w_dec[...] = jnp.zeros_like(w_dec)
    w_dec[:, :vocab] = w_dec_raw[...]
    bias_dec[...] = jnp.full_like(bias_dec, -1e30)
    bias_dec[0:1, :vocab] = bias_raw[...].astype(F32).reshape(1, vocab)
    for k in (1, 2, 3):
        da(k).start()
    own_dec = pltpu.make_async_copy(w_dec, d_slot(place(0, 0, y, c)), l_sem.at[9])
    own_dec.start()

    for k in (1, 2, 3):
        ids_copy(k, member(k)).wait_recv()
    lane = lax.broadcasted_iota(jnp.int32, (rows, 24), 1)
    wide = lax.broadcasted_iota(jnp.int32, (rows, VPAD), 1).astype(F32)

    def column(at, s):
        packed = IDS[s].reshape(rows, 24)
        return jnp.sum(jnp.where(lane == at, packed, 0).astype(F32), axis=1, keepdims=True)

    def keep_of(t, s):
        return 1.0 - column(8 + t, s)

    def letter(t, s):
        return jnp.where(column(t, s) == wide, 1.0, 0.0).astype(BF)

    EMBT[...] = jnp.zeros_like(EMBT)
    LV[...] = jnp.zeros_like(LV)
    BD[...] = jnp.zeros_like(BD)
    GWD[...] = jnp.zeros_like(GWD)
    DWI[...] = jnp.zeros_like(DWI)
    DCN[...] = jnp.zeros_like(DCN)
    OWN[...] = jnp.zeros_like(OWN)
    PR[0] = jnp.zeros(PR.shape[1:], BF)

    win_mir(1 - zh).wait_recv()

    win_y(y).start()
    def pass_y(i):
        for j in (0, 1):
            from_y(i, j).wait_recv()
            to_s(8 + i, j).start()

    def pass_mir(k):
        for j in (0, 1):
            from_mir(k, j).wait_recv()
            to_y(4 + k, j).start()
            to_s(4 + k, j).start()

    for i in range(3):
        pass_y(i)

    @pl.when(inner)
    def _():
        pass_mir(0)

    @pl.when(jnp.logical_not(inner))
    def _():
        for k in range(4):
            for j in (0, 1):
                to_mir(k, j).start()

    pass_y(3)
    win_y(1 - y).wait_recv()
    win_s(c).start()
    win_s(1 - c).wait_recv()

    def h_copy(t, s, k, j):
        src, dst = H.at[t % RING, s, :, span(0, j)], H.at[t % RING, s, :, span(k, j)]
        return rc(src, dst, s_h.at[t, s, k - 1, j], r_h.at[t, s, k - 1, j], kdev(k))

    def wait_h(t, s):
        for k in (1, 2, 3):
            for j in (0, 1):
                h_copy(t, s, k, j).wait_recv()

    def gates(t, s, first):
        keep = None if first else keep_of(t, s)
        feature = mm(letter(t, s), emb_t[...], NT).astype(BF)
        for j in (0, 1):
            pre = []
            for g in range(4):
                drive = mm(feature, WIN[j, g // 2, g % 2], NN)
                if not first:
                    drive = drive + keep * mm(H[(t - 1) % RING, s], W[4 * j + g], NN)
                pre.append(drive)
            s_i, s_f, t_g, s_o = sigmoid(pre[0]), sigmoid(pre[1]), jnp.tanh(pre[2]), sigmoid(pre[3])
            cell = s_i * t_g
            if not first:
                cell = s_f * (C[t - 1, s, j] * keep) + cell
            for g, v in enumerate((s_i, s_f, t_g, s_o)):
                A[t, s, 4 * j + g] = v
            C[t, s, j] = cell
            H[t % RING, s, :, span(0, j)] = (s_o * jnp.tanh(cell)).astype(BF)
            for k in (3, 1, 2):
                h_copy(t, s, k, j).start()

    @pl.loop(0, 2)
    def _(s):
        gates(0, s, True)

    @pl.when(jnp.logical_not(inner))
    def _():
        pass_mir(0)

    for k in (1, 2, 3):
        pass_mir(k)

    def dec_mir(k, far):
        b = place(k, far, y, c)
        return rc(d_slot(b), d_slot(b), s_dm.at[k], r_dm.at[k], mir)

    def dec_y(i, yy):
        b = group_block(i, yy, c)
        return rc(d_slot(b), d_slot(b), s_dy.at[i], r_dy.at[i], ydev)

    def dec_s(i, cc):
        b = group_block(i % 8, y + (i // 8) * (1 - 2 * y), cc)
        return rc(d_slot(b), d_slot(b), s_ds.at[i], r_ds.at[i], sib)

    own_dec.wait()
    dec_mir(0, 0).start()
    dec_y(0, y).start()
    dec_s(0, c).start()
    for k in (1, 2, 3):
        da(k).wait_recv()
        dec_mir(k, 0).start()
        dec_y(k, y).start()
        dec_s(k, c).start()

    for i in (4, 5, 6, 7):
        pass_y(i)

    @pl.loop(0, 16)
    def _(i):
        for j in (0, 1):
            from_s(i, j).wait_recv()

    def released(t, s):
        hid_copy(t, s).wait()
        for k in (1, 2, 3):
            for j in (0, 1):
                h_copy(t, s, k, j).wait_send()

    def forward(t, s):
        wait_h(t - 1, s)

        @pl.when(t >= RING - 1)
        def _():
            released(t - (RING - 1), s)

        gates(t, s, False)

    row = lax.broadcasted_iota(jnp.int32, (128, 256), 0)
    col = lax.broadcasted_iota(jnp.int32, (128, 256), 1)

    def select(cc):
        yy = y + (row // 64) * (1 - 2 * y)
        return jnp.where(col == 64 * (2 * yy + cc) + row % 64, 1.0, 0.0).astype(BF)

    def lane_slot(t, s):
        return pl.ds(pl.multiple_of((2 * t + s) * rows, rows), rows)

    def ht_copy(t, s, slot):
        return rc(HSEND.at[slot], HTS.at[:, :, lane_slot(t, s)], s_ht.at[t, s], r_ht.at[t, s], sib)

    def hid_copy(t, s):
        mine = H.at[t % RING, s, pl.ds(pl.multiple_of(32 * member(0), 32), 32), :]
        return pltpu.make_async_copy(mine, out_hid.at[s * steps + t], hid_sem.at[t, s])

    def logits_of(t, s):
        scores = mm(H[t % RING, s], WDEC[...], NN) + bias_dec[0:1, :]
        top = jnp.max(scores, axis=1, keepdims=True)
        shifted = jnp.exp(scores - top)
        summed = jnp.sum(shifted, axis=1, keepdims=True)
        goal = jnp.where(column(16 + t, s) == wide, 1.0, 0.0)
        picked = jnp.sum(goal * scores, axis=1, keepdims=True)
        LV[...] += jnp.broadcast_to(top + jnp.log(summed) - picked, (rows, 128))
        DL[t, s] = (shifted / summed - goal).astype(BF)

    def decoder_side(t, s):
        hid_copy(t, s).start()
        grad = DL[t, s]
        BD[...] += mm(jnp.ones((8, rows), BF), grad, NN)
        for j in (0, 1):
            GWD[j] += mm(H[t % RING, s, :, span(0, j)], grad, TN).reshape(2, 2, 64, VPAD)

    def transposed_side(t, s):
        slot = s
        mine, other = select(c), select(1 - c)

        @pl.when(t >= 1)
        def _():
            ht_copy(t - 1, s, slot).wait_send()

        for tile in range(8):
            part = H[t % RING, s, :, 256 * tile : 256 * (tile + 1)]
            HT[tile, :, lane_slot(t, s)] = mm(mine, part, NT).astype(BF)
            HSEND[slot, tile] = mm(other, part, NT).astype(BF)
        ht_copy(t, s, slot).start()

    def decoder_mirror():
        @pl.loop(0, 4)
        def _(k):
            dec_mir(k, 1).wait_recv()
            dec_y(4 + k, y).start()
            dec_s(4 + k, c).start()

    def decoder_rest():
        @pl.loop(0, 8)
        def _(i):
            k, j = i // 2, i % 2
            to_mir(k, j).wait_send()
            to_y(i, 0).wait_send()
            to_y(i, 1).wait_send()

        @pl.loop(0, 16)
        def _(i):
            to_s(i, 0).wait_send()
            to_s(i, 1).wait_send()

        @pl.loop(0, 8)
        def _(i):
            dec_y(i, 1 - y).wait_recv()
            dec_s(8 + i, c).start()

        @pl.loop(0, 16)
        def _(i):
            dec_s(i, 1 - c).wait_recv()

    def aside(t, s):
        logits_of(t, s)
        decoder_side(t, s)
        transposed_side(t, s)

    @pl.loop(2, 2 * steps)
    def _(i):
        t, s = i // 2, i % 2
        forward(t, s)

        @pl.when(i == 3)
        def _():
            decoder_mirror()

        @pl.when(i == 5)
        def _():
            decoder_rest()

        @pl.when(i >= 5)
        def _():
            @pl.loop(i - 4 - (13 - i) // 8, i - 3)
            def _(n):
                aside(n // 2, n % 2)


    def d_copy(t, s):
        return rc(D.at[:, t - 1, s], DS.at[:, t - 1, s], s_d.at[t, s], r_d.at[t, s], sib)

    def turn():
        def rows_of(q):
            return slice(256 * q, 256 * (q + 1))

        def swap(p, q):
            upper, lower = W[p, rows_of(q), :].T, W[q, rows_of(p), :].T
            W[p, rows_of(q), :] = lower
            W[q, rows_of(p), :] = upper

        for p in range(8):
            W[p, rows_of(p), :] = W[p, rows_of(p), :].T
            for q in range(p):
                swap(p, q)

    def cell_back(t, s, oldest):
        keep = keep_of(t, s)
        for j in (0, 1):
            up = WDEC[span(0, j), :]
            dh = mm(DL[t, s], up, NT)
            rest = PR[(t + 1) % 2, s, 0, j].astype(F32) + PR[(t + 1) % 2, s, 1, j].astype(F32)
            dh = dh + (OWN[s, j] + rest)
            s_i, s_f, t_g, s_o = (A[t, s, 4 * j + g] for g in range(4))
            t_c = jnp.tanh(C[t, s, j])
            d_o = dh * t_c
            d_c = dh * s_o * (1.0 - t_c * t_c) + DCN[s, j]
            d_i = d_c * t_g * s_i * (1.0 - s_i)
            d_g = d_c * s_i * (1.0 - t_g * t_g)
            d_o = d_o * s_o * (1.0 - s_o)
            if oldest:
                d_f = jnp.zeros_like(d_i)
            else:
                d_f = d_c * (C[t - 1, s, j] * keep) * s_f * (1.0 - s_f)
                DCN[s, j] = keep * (d_c * s_f)
            for g, v in enumerate((d_i, d_f, d_g, d_o)):
                low = v.astype(BF)
                DRAW[4 * j + g] = low
                if not oldest:
                    D[4 * j + g, t - 1, s] = low * keep.astype(BF)

    def part_rows(h):
        return slice(64 * h, 64 * (h + 1))

    def pr_half(t, s, k, h):
        src, dst = STG.at[s, k - 1, :, part_rows(h)], PR.at[t % 2, s, k - 1, :, part_rows(h)]
        return rc(src, dst, s_ph.at[t, s, k - 1, h], r_ph.at[t, s, k - 1, h], kdev(k))

    def owed_copy(t, s, n):
        return rc(STG.at[s, 2, :, part_rows(n)], CB.at[s, n], s_cb.at[t, s, n], r_cb.at[t, s, n], kdev(1 + n))

    def pr_each(act):
        for k in (1, 2):
            for h in (0, 1):
                act(k, h)

    def pr_arrived(t, s):
        pr_each(lambda k, h: pr_half(t, s, k, h).wait_recv())

    def pr_left(t, s):
        pr_each(lambda k, h: pr_half(t, s, k, h).wait_send())
        for n in (0, 1):
            owed_copy(t, s, n).wait_send()

    def product_back(t, s):
        left = jnp.concatenate([D[q, t - 1, s] for q in range(8)], axis=1)
        for k, j in ((3, 0), (3, 1), (1, 0), (1, 1), (2, 0), (2, 1), (0, 0), (0, 1)):
            total = mm(left, W[2 * k + j], NN)
            if k == 0:
                OWN[s, j] = total
                continue
            STG[s, k - 1, j] = total.astype(BF)
            if k < 3:
                PEND[k - 1, j] = total[part_rows(2 - k)]
            elif j == 1:
                owed_copy(t, s, 0).start()
                owed_copy(t, s, 1).start()
        for k in (1, 2):
            pr_half(t, s, k, k - 1).start()

    def add_owed(t, s):
        for k in (2, 1):
            h = 2 - k
            owed_copy(t, s, h).wait_recv()
            STG[s, k - 1, :, part_rows(h)] = (PEND[k - 1] + CB[s, h].astype(F32)).astype(BF)
            pr_half(t, s, k, h).start()

    def input_side(t, s):
        onehot = letter(t, s)
        feat_t = mm(emb_t[...], onehot, NT).astype(BF)
        inputs = []
        for q in range(8):
            jj, gy, gc = q // 4, (q // 2) % 2, q % 2
            DWI[jj, gy, gc] += mm(feat_t, DRAW[q], NN)
            inputs.append(WIN[jj, gy, gc])
        grad_t = mm(jnp.concatenate(inputs, axis=1), jnp.concatenate([DRAW[q] for q in range(8)], axis=1), NT)
        high = grad_t.astype(BF)
        low = (grad_t - high.astype(F32)).astype(BF)
        EMBT[...] += mm(high, onehot, NN) + mm(low, onehot, NN)

    def gd_s():
        return rc(GWD.at[:, :, 1 - c], GIS.at[:, :, 0:64], s_gd.at[0], r_gd.at[0], sib)

    def gd_y():
        return rc(GWD.at[:, 1 - y, c], GY, s_gd.at[1], r_gd.at[1], ydev)

    def gd_m():
        return rc(SGM, GM, s_gd.at[2], r_gd.at[2], mir)

    turn()

    @pl.loop(0, 2 * (steps - 1))
    def _(i):
        t, s = last - i // 2, i % 2

        @pl.when(i < 2)
        def _():
            wait_h(t, s)
            logits_of(last, s)

        @pl.when(i >= 2)
        def _():
            pr_arrived(t + 1, s)

        cell_back(t, s, False)

        @pl.when(i >= 1)
        def _():
            add_owed(t + 1 - s, 1 - s)

        @pl.when(i >= 2)
        def _():
            pr_left(t + 1, s)

        product_back(t, s)
        d_copy(t, s).start()

        @pl.when(i < 2 * (steps - 1) - 1)
        def _():
            input_side(t, s)

        @pl.when(i < 2)
        def _():
            logits_of(last - 1, s)

        @pl.when(jnp.logical_and(i >= 2, i < 4))
        def _():
            decoder_side(last - 1, s)
            transposed_side(last - 1, s)

        @pl.when(i == 4)
        def _():
            @pl.loop(0, 2)
            def _(n):
                decoder_side(last, n)

            gd_s().start()

        @pl.when(i == 5)
        def _():
            gd_s().wait_recv()
            GWD[:, :, c] += GIS[:, :, 0:64]
            gd_y().start()

        @pl.when(i == 7)
        def _():
            gd_y().wait_recv()
            GWD[:, y, c] += GY[...]
            SGM[...] = GWD[1 - zh, y, c].astype(BF)
            gd_m().start()

        @pl.when(i == 9)
        def _():
            gd_m().wait_recv()
            out_dec[...] = GWD[zh, y, c] + GM[...].astype(F32)

    @pl.loop(0, 2 * (steps - 1))
    def _(i):
        ht_copy(i // 2, i % 2, 0).wait_recv()
        d_copy(1 + i // 2, i % 2).wait_recv()

    depth = 2 * (steps - 1) * rows

    def kept(q):
        return A.at[2 + q // 4, (q % 4) // 2, :, pl.ds(pl.multiple_of(64 * (q % 2), 64), 64), :]

    def tile_of(q):
        k, near = q % 4, q // 4
        return 2 * k + 1 - zh + near * (2 * zh - 1)

    def ry_copy(p, q):
        return rc(SY.at[p % 4], RY.at[q], s_ry.at[p], r_ry.at[q], ydev)

    def pieces(k):
        return (1, 2, 1, 4)[k]

    def piece(k, n):
        size = 8 // pieces(k)
        return slice(size * n, size * (n + 1))

    def rm_copy(k, n):
        at = (0, 2, 1, 4)[k] + n
        return rc(SM.at[k, piece(k, n)], RM.at[k, piece(k, n)], s_rm.at[at], r_rm.at[at], mir)

    def ry_first(n):
        return rc(SY.at[0, piece(3, n)], RY.at[3, piece(3, n)], s_ry.at[8 + n], r_ry.at[8 + n], ydev)

    def ry_sent(p):
        @pl.when(p == 0)
        def _():
            for n in range(4):
                ry_first(n).wait_send()

        @pl.when(p > 0)
        def _():
            ry_copy(p, order(p)).wait_send()

    def ra_copy(k, n):
        at = (0, 0, 2, 3)[k] + n
        rows_of_q = piece(k, n) if k == 1 else slice(0, 8)
        return rc(SM.at[k, rows_of_q], out_recv.at[k - 1, rows_of_q], s_ra.at[at], r_ra.at[at], kdev(k))

    def ra_pieces(k):
        return 2 if k == 1 else 1

    def order(p):
        return 3 - p + 8 * (p // 4)

    def make_tile(p):
        q = order(p)
        tile = tile_of(q)
        left, right = HT[tile], HTS[tile]
        hold = kept(q)

        @pl.when(p >= 4)
        def _():
            ry_sent(p - 4)

        for n in range(8):
            grad = mm(left, D[n].reshape(depth, 256), NN) + mm(right, DS[n].reshape(depth, 256), NN)
            hold[n] = grad[:64]
            SY[p % 4, n] = grad[64:].astype(BF)
            if n % 2 == 1:
                @pl.when(p == 0)
                def _(n=n):
                    ry_first(n // 2).start()

        @pl.when(p > 0)
        def _():
            ry_copy(p, q).start()

    def add_y(q):
        ry_copy(0, q).wait_recv()
        hold = kept(q)
        hold[...] = hold[...] + RY[q].astype(F32)

    def pass_first(n):
        ry_first(n).wait_recv()
        SM[3, piece(3, n)] = (kept(3)[piece(3, n)] + RY[3, piece(3, n)].astype(F32)).astype(BF)
        rm_copy(3, n).start()

    def pass_on(k):
        if k == 3:
            for n in range(4):
                pass_first(n)
            return
        add_y(k)
        for n in range(pieces(k)):
            SM[k, piece(k, n)] = kept(k)[piece(k, n)].astype(BF)
            rm_copy(k, n).start()

    def finish(k):
        add_y(4 + k)
        if k != 1:
            for n in range(pieces(k)):
                rm_copy(k, n).wait_recv()
        if k == 0:
            out_own[...] = kept(4)[...] + RM[0].astype(F32)
            return
        for n in range(ra_pieces(k)):
            part = piece(1, n) if k == 1 else slice(0, 8)
            if k == 1:
                rm_copy(k, n).wait_recv()
                rm_copy(k, n).wait_send()
            else:
                for m in range(pieces(k)):
                    rm_copy(k, m).wait_send()
            SM[k, part] = (kept(4 + k)[part] + RM[k, part].astype(F32)).astype(BF)
            ra_copy(k, n).start()

    def settle(p):
        q = order(p)
        pass_on(q) if q < 4 else finish(q - 4)

    outer = jnp.logical_not(inner)

    def core_rows(cc):
        return pl.ds(pl.multiple_of(64 * cc, 64), 64)

    def piece_rows(xx):
        return pl.ds(pl.multiple_of(64 * c + 32 * xx, 32), 32)

    def sm_core():
        return rc(out_small.at[core_rows(1 - c)], RS1, s_sm.at[0], r_sm.at[0], sib)

    def sm_group(k):
        xx = kx(k)
        return rc(out_small.at[piece_rows(xx)], RS2.at[k - 1], s_sm.at[k], r_sm.at[k], kdev(k))

    def sm_quarter(n):
        return rc(PIECE if n == 0 else PAIR, RS3.at[n], s_sm.at[4 + n], r_sm.at[4 + n], (ydev, mir)[n])

    def sm_spread(k):
        return rc(TOTAL, RS4.at[k - 1], s_sm.at[6 + k], r_sm.at[6 + k], kdev(k))

    def sm_last():
        return rc(out_small.at[core_rows(c)], RS5, s_sm.at[10], r_sm.at[10], sib)

    def sm_step1():
        sm_core().wait_recv()
        out_small[core_rows(c)] = out_small[core_rows(c)] + RS1[...]

        @pl.when(outer)
        def _():
            sm_group(1).start()

        @pl.when(inner)
        def _():
            sm_group(2).start()
            sm_group(3).start()

    def sm_step2():
        @pl.when(outer)
        def _():
            for k in (1, 2, 3):
                sm_group(k).wait_recv()
            PIECE[...] = (out_small[piece_rows(x)] + RS2[0]) + (RS2[1] + RS2[2])
            sm_quarter(0).start()

    def sm_step_mir():
        @pl.when(outer)
        def _():
            sm_quarter(0).wait_recv()
            PAIR[...] = PIECE[...] + RS3[0]
            sm_quarter(1).start()

    def sm_step3():
        @pl.when(outer)
        def _():
            sm_quarter(1).wait_recv()
            TOTAL[...] = PAIR[...] + RS3[1]
            for k in (1, 2, 3):
                sm_spread(k).start()

    def sm_step4():
        sm_core().wait_send()

        @pl.when(outer)
        def _():
            sm_group(1).wait_send()
            sm_spread(1).wait_recv()
            out_small[piece_rows(1 - x)] = RS4[0]
            out_small[piece_rows(x)] = TOTAL[...]

        @pl.when(inner)
        def _():
            for k in (2, 3):
                sm_group(k).wait_send()
                sm_spread(k).wait_recv()
                out_small[piece_rows(kx(k))] = RS4[k - 1]

        sm_last().start()

    def sm_step5():
        sm_last().wait_recv()
        out_small[core_rows(1 - c)] = RS5[...]

    live = pl.ds(0, 104)

    def gi_s():
        return rc(DWI.at[:, :, 1 - c, live], GIS.at[:, :, :, 0:256], s_gi.at[0], r_gi.at[0], sib)

    def gi_y():
        return rc(SIY, IY, s_gi.at[1], r_gi.at[1], ydev)

    def gi_m():
        return rc(SIM, IM, s_gi.at[2], r_gi.at[2], mir)

    def gi_p():
        return rc(DWI.at[y, zh, c, live], out_in, s_gi.at[3], r_gi.at[3], back)

    def first_position():
        @pl.loop(0, 2)
        def _(s):
            pr_arrived(1, s)
            cell_back(0, s, True)
            input_side(0, s)

            @pl.when(jnp.logical_and(inner, s == 0))
            def _():
                pass_first(2)

        leader = jnp.logical_and(x == 0, a == 0)
        high_row = lax.broadcasted_iota(jnp.int32, (8, VPAD), 0)
        loss = jnp.sum(LV[...], axis=0, keepdims=True)
        loss = jnp.concatenate([loss] * (VPAD // 128), axis=1)
        extra = jnp.where(high_row == 0, BD[...], jnp.where(high_row == 1, loss, 0.0))
        out_small[...] = EMBT[...]
        out_small[SMALL - 8 : SMALL] = jnp.where(leader, extra, 0.0)
        sm_core().start()
        gi_s().start()

    @pl.loop(0, 8)
    def _(p):
        make_tile(p)

        @pl.when(p == 0)
        def _():
            add_owed(1, 1)

        @pl.when(p == 1)
        def _():
            @pl.when(inner)
            def _():
                pass_first(0)

            input_side(1, 1)

            @pl.when(inner)
            def _():
                pass_first(1)

            first_position()
            sm_step1()
            @pl.when(inner)
            def _():
                pass_first(3)
                settle(1)

            gi_s().wait_recv()
            DWI[:, :, c, 0:104] = DWI[:, :, c, 0:104] + GIS[:, :, :, 0:256]
            sm_step2()
            SIY[...] = DWI[1 - y, :, c, 0:112].astype(BF)
            gi_y().start()

            @pl.when(outer)
            def _():
                settle(0)

        @pl.when(p == 2)
        def _():
            @pl.when(outer)
            def _():
                settle(1)

            sm_step_mir()

        @pl.when(p == 3)
        def _():
            gi_y().wait_recv()
            DWI[y, :, c, 0:104] = DWI[y, :, c, 0:104] + IY[...].astype(F32)[:, 0:104]
            SIM[...] = DWI[y, 1 - zh, c, 0:112].astype(BF)
            gi_m().start()

        @pl.when(p == 4)
        def _():
            settle(2)
            sm_step3()

        @pl.when(p == 5)
        def _():
            settle(3)

    settle(4)
    settle(5)
    sm_step4()
    settle(6)
    gi_m().wait_recv()
    DWI[y, zh, c, 0:104] = DWI[y, zh, c, 0:104] + IM[...].astype(F32)[0:104]

    @pl.when(moved)
    def _():
        gi_p().start()

    @pl.when(stays)
    def _():
        out_in[...] = DWI[y, zh, c, 0:104]

    sm_step5()
    settle(7)

    for k in (1, 2, 3):
        for j in (0, 1):
            wa(k, j).wait_send()
        ids_copy(k, member(0)).wait_send()
        da(k).wait_send()
        for n in range(ra_pieces(k)):
            ra_copy(k, n).wait()
    rm_copy(0, 0).wait_send()

    @pl.when(moved)
    def _():
        gi_p().wait()
        win_perm(x, z // 2, z % 2).wait_send()

    for s in range(2):
        pr_left(1, s)
    win_mir(zh).wait_send()
    win_y(y).wait_send()
    win_s(c).wait_send()
    @pl.when(outer)
    def _():
        sm_quarter(0).wait_send()
        sm_quarter(1).wait_send()
        for k in (1, 2, 3):
            sm_spread(k).wait_send()

    for copy in (gd_s, gd_y, gd_m, gi_s, gi_y, gi_m, sm_last):
        copy().wait_send()
    for s in range(2):
        ht_copy(last - 1, s, s).wait_send()

    @pl.loop(0, 4)
    def _(k):
        dec_mir(k, 0).wait_send()

    @pl.loop(0, 8)
    def _(i):
        dec_y(i, y).wait_send()

    for p in range(4, 8):
        ry_copy(p, order(p)).wait_send()

    @pl.loop(0, 16)
    def _(i):
        dec_s(i, c).wait_send()

    @pl.loop(2 * (steps - RING + 1), 2 * steps)
    def _(i):
        released(i // 2, i % 2)

    @pl.loop(0, 2 * (steps - 1))
    def _(i):
        d_copy(1 + i // 2, i % 2).wait_send()


def output_kernel(
    own, recv, g_in, g_dec, hid_in, small, hid, table, o_in, o_bias, o_rec, o_dec, o_bias_dec, loss,
    h_buf, own_buf, recv_buf, rec_buf, in_buf, dec_buf, small_buf, t_buf, i_buf, b_buf, d_buf, bd_buf, l_buf, in_sem, out_sem,
):
    dp = lax.axis_index("dp")
    z, x = dp // 2, dp % 2
    a = z + (z // 2) * (3 - 2 * z)

    def cols(k, j, g):
        xk, ak = x + (k % 2) * (1 - 2 * x), a + (k // 2) * (1 - 2 * a)
        ub = 2 * (ak + j * (3 - 2 * ak)) + xk
        return pl.ds(pl.multiple_of(256 * (8 * g + ub), 256), 256)

    def load(n, src, dst):
        copy = pltpu.make_async_copy(src, dst, in_sem.at[n])
        copy.start()
        return copy

    def store(n, src, dst):
        copy = pltpu.make_async_copy(src, dst, out_sem.at[n])
        copy.start()
        return copy

    hid_loads = [
        load(p, hid_in.at[:, :, 256 * p : 256 * (p + 1)], h_buf.at[:, :, cols(p // 2, p % 2, 0)]) for p in range(8)
    ]
    rec_loads = [load(8, own, own_buf), load(9, recv, recv_buf)]
    small_loads = [load(10, small, small_buf), load(11, g_in, in_buf), load(12, g_dec, dec_buf)]
    for copy in hid_loads:
        copy.wait()
    stores = [store(0, h_buf, hid)]
    for copy in rec_loads:
        copy.wait()
    for k in range(4):
        for j in (0, 1):
            for g in range(4):
                part = own_buf[4 * j + g] if k == 0 else recv_buf[k - 1, 4 * j + g].astype(F32)
                rec_buf[:, cols(k, j, g)] = part
    stores.append(store(1, rec_buf, o_rec))
    for copy in small_loads:
        copy.wait()
    vocab, emb = table.shape
    t_buf[...] = small_buf[0:SMALL, :].T[:vocab, :emb]
    i_buf[...] = in_buf[0:emb, :]
    b_buf[...] = in_buf[emb, :]
    d_buf[...] = dec_buf[:, :vocab]
    bd_buf[...] = small_buf[SMALL - 8, :vocab]
    l_buf[...] = small_buf[SMALL - 7 : SMALL - 6, 0:1]
    pairs = ((t_buf, table), (i_buf, o_in), (b_buf, o_bias), (d_buf, o_dec), (bd_buf, o_bias_dec), (l_buf, loss))
    for n, (src, dst) in enumerate(pairs):
        stores.append(store(2 + n, src, dst))
    for copy in stores:
        copy.wait()


def fused(chars, resets, targets, embed, w_in, bias_in, w_rec, w_dec, bias_dec):
    micro, count, steps = chars.shape
    own_rows, gate_cols = w_rec.shape
    vocab, emb = embed.shape
    width = gate_cols // 4
    members = 4
    rows = count * members
    vm = pl.BlockSpec(memory_space=pltpu.VMEM)
    hbm = pl.BlockSpec(memory_space=pl.ANY)
    dma = pltpu.SemaphoreType.DMA
    n = steps - 1
    scratch = [
        pltpu.VMEM((8, width, 256), BF),
        pltpu.VMEM((2, 2, 2, EPAD, 256), BF),
        pltpu.VMEM((width, VPAD), BF),
        pltpu.VMEM((micro, members, count, 24), jnp.int32),
        pltpu.VMEM((RING, micro, rows, width), BF),
        pltpu.VMEM((8, 128, 2 * n * rows), BF),
        pltpu.VMEM((8, 128, 2 * n * rows), BF),
        pltpu.VMEM((2, 8, 128, rows), BF),
        pltpu.VMEM((steps, micro, 8, rows, 256), F32),
        pltpu.VMEM((steps, micro, 2, rows, 256), F32),
        pltpu.VMEM((8, n, micro, rows, 256), BF),
        pltpu.VMEM((8, n, micro, rows, 256), BF),
        pltpu.VMEM((8, rows, 256), BF),
        pltpu.VMEM((steps, micro, rows, VPAD), BF),
        pltpu.VMEM(w_in.shape, BF),
        pltpu.VMEM(bias_in.shape, BF),
        pltpu.VMEM(w_dec.shape, BF),
        pltpu.VMEM(embed.shape, BF),
        pltpu.VMEM(bias_dec.shape, BF),
        pltpu.VMEM((steps, micro, count), jnp.int32),
        pltpu.VMEM((steps, micro, count), jnp.int32),
        pltpu.VMEM((steps, micro, count), jnp.int32),
        dma((8,)),
        pltpu.VMEM((micro, count, 24), jnp.int32),
        pltpu.VMEM((EPAD, 256), BF),
        pltpu.VMEM((EPAD, VPAD), BF),
        pltpu.VMEM((own_rows, VPAD), BF),
        pltpu.VMEM((8, VPAD), F32),
        pltpu.VMEM((2, micro, 2, 2, rows, 256), BF),
        pltpu.VMEM((micro, 3, 2, rows, 256), BF),
        pltpu.VMEM((micro, 2, 2, rows // 2, 256), BF),
        pltpu.VMEM((2, 2, rows // 2, 256), F32),
        pltpu.VMEM((micro, 2, rows, 256), F32),
        pltpu.VMEM((micro, 2, rows, 256), F32),
        pltpu.VMEM((4, 8, 64, 256), BF),
        pltpu.VMEM((8, 8, 64, 256), BF),
        pltpu.VMEM((4, 8, 64, 256), BF),
        pltpu.VMEM((4, 8, 64, 256), BF),
        pltpu.VMEM((EPAD, VPAD), F32),
        pltpu.VMEM((rows, 128), F32),
        pltpu.VMEM((8, VPAD), F32),
        pltpu.VMEM((2, 2, 2, 64, VPAD), F32),
        pltpu.VMEM((2, 2, 104, VPAD), F32),
        pltpu.VMEM((2, 64, VPAD), F32),
        pltpu.VMEM((64, VPAD), BF),
        pltpu.VMEM((64, VPAD), BF),
        pltpu.VMEM((2, 2, 2, EPAD, 256), F32),
        pltpu.VMEM((2, 112, 256), BF),
        pltpu.VMEM((2, 112, 256), BF),
        pltpu.VMEM((112, 256), BF),
        pltpu.VMEM((112, 256), BF),
        pltpu.VMEM((64, VPAD), F32),
        pltpu.VMEM((3, 32, VPAD), F32),
        pltpu.VMEM((2, 32, VPAD), F32),
        pltpu.VMEM((3, 32, VPAD), F32),
        pltpu.VMEM((64, VPAD), F32),
        pltpu.VMEM((32, VPAD), F32),
        pltpu.VMEM((32, VPAD), F32),
        pltpu.VMEM((32, VPAD), F32),
    ]
    shapes = [
        (3,), (4,), (3, 2), (4, 2), (8, 2), (16, 2), (3,), (4,), (8,), (16,),
        (steps, 2, 3, 2), (n, 2), (steps, 2),
        (steps, 2, 2, 2), (steps, 2, 2), (3,), (4,), (11,), (12,), (8,), (4,),
    ]
    for shape in shapes:
        scratch += [dma(shape), dma(shape)]
    scratch += [dma((12,)), dma((steps, 2))]
    out_own, out_recv, out_in, out_dec, out_hid, out_small = pl.pallas_call(
        functools.partial(lstm_kernel, steps, rows),
        out_shape=(
            jax.ShapeDtypeStruct((8, own_rows, 256), F32),
            jax.ShapeDtypeStruct((3, 8, own_rows, 256), BF),
            jax.ShapeDtypeStruct((104, 256), F32),
            jax.ShapeDtypeStruct((own_rows, VPAD), F32),
            jax.ShapeDtypeStruct((micro * steps, count, width), BF),
            jax.ShapeDtypeStruct((EPAD, VPAD), F32),
        ),
        in_specs=[hbm] * 9,
        out_specs=(vm, hbm, vm, vm, hbm, vm),
        scratch_shapes=scratch,
        compiler_params=pltpu.CompilerParams(
            collective_id=0, has_side_effects=True, vmem_limit_bytes=66 * 1000 * 1000
        ),
    )(
        w_rec, w_in, bias_in, w_dec, embed, bias_dec,
        chars.transpose(2, 0, 1), resets.transpose(2, 0, 1), targets.transpose(2, 0, 1),
    )
    everyone = lax.axis_size(("dp", "fsdp"))
    hid, table, g_in, g_bias, g_rec, g_dec, g_bias_dec, loss = pl.pallas_call(
        output_kernel,
        out_shape=(
            jax.ShapeDtypeStruct((micro * steps, count, width), BF),
            jax.ShapeDtypeStruct((vocab, emb), F32),
            jax.ShapeDtypeStruct((emb, 256), F32),
            jax.ShapeDtypeStruct((256,), F32),
            jax.ShapeDtypeStruct((own_rows, gate_cols), F32),
            jax.ShapeDtypeStruct((own_rows, vocab), F32),
            jax.ShapeDtypeStruct((vocab,), F32),
            jax.ShapeDtypeStruct((1, 1), F32),
        ),
        in_specs=[hbm] * 6,
        out_specs=(hbm,) * 8,
        scratch_shapes=[
            pltpu.VMEM((micro * steps, count, width), BF),
            pltpu.VMEM((8, own_rows, 256), F32),
            pltpu.VMEM((3, 8, own_rows, 256), BF),
            pltpu.VMEM((own_rows, gate_cols), F32),
            pltpu.VMEM((104, 256), F32),
            pltpu.VMEM((own_rows, VPAD), F32),
            pltpu.VMEM((EPAD, VPAD), F32),
            pltpu.VMEM((vocab, emb), F32),
            pltpu.VMEM((emb, 256), F32),
            pltpu.VMEM((256,), F32),
            pltpu.VMEM((own_rows, vocab), F32),
            pltpu.VMEM((vocab,), F32),
            pltpu.VMEM((1, 1), F32),
            dma((13,)),
            dma((8,)),
        ],
    )(out_own, out_recv, out_in, out_dec, out_hid, out_small)
    return (
        loss[0, 0] / (micro * count * steps * everyone),
        hid.reshape(micro, steps, count, width).transpose(0, 2, 1, 3),
        table,
        g_in,
        g_bias,
        g_rec,
        g_dec,
        g_bias_dec,
    )


def dot_plain(left, right):
    return jnp.dot(left, right, preferred_element_type=jnp.float32)


def dot_right_t(left, right):
    return lax.dot_general(
        left, right, (((1,), (1,)), ((), ())), preferred_element_type=jnp.float32
    )


def dot_left_t(left, right):
    return lax.dot_general(
        left, right, (((0,), (0,)), ((), ())), preferred_element_type=jnp.float32
    )


def lstm_forward(weights, embed, bias_dec, ids, marks, goals):
    w_rec, w_dec, w_in, bias_in = weights
    count, steps = ids.shape
    width = w_rec.shape[0]
    letters = jnp.arange(embed.shape[0], dtype=jnp.int32)
    onehot = (ids.T.reshape(-1)[:, None] == letters[None, :]).astype(jnp.bfloat16)
    feature = dot_plain(onehot, embed).astype(jnp.bfloat16)
    drives = (dot_plain(feature, w_in) + bias_in.astype(jnp.float32)).reshape(steps, count, -1)
    keeps = (1 - marks.T).astype(jnp.float32)[:, :, None]

    def advance(state, slot):
        hidden_now, cell = state
        drive, keep_now = slot
        prev_hidden = hidden_now * keep_now.astype(jnp.bfloat16)
        prev_cell = cell * keep_now
        pre = drive + dot_plain(prev_hidden, w_rec)
        gin, gforget, gcand, gout = jnp.split(pre, 4, axis=1)
        cell_new = jax.nn.sigmoid(gforget) * prev_cell + jax.nn.sigmoid(gin) * jnp.tanh(gcand)
        hid_new = (jax.nn.sigmoid(gout) * jnp.tanh(cell_new)).astype(jnp.bfloat16)
        return ((hid_new, cell_new), (pre, prev_hidden, prev_cell, cell_new, hid_new))

    start = (jnp.zeros((count, width), jnp.bfloat16), jnp.zeros((count, width), jnp.float32))
    state, saved = lax.scan(advance, start, (drives, keeps))
    pres, prev_hiddens, prev_cells, cells, hiddens = saved
    flat_hidden = hiddens.reshape(steps * count, width)
    logits = dot_plain(flat_hidden, w_dec) + bias_dec.astype(jnp.float32)
    top = jnp.max(logits, axis=1, keepdims=True)
    shifted = jnp.exp(logits - top)
    summed = jnp.sum(shifted, axis=1, keepdims=True)
    goal_hot = (goals.T.reshape(-1)[:, None] == letters[None, :]).astype(jnp.float32)
    loss_part = jnp.sum(top[:, 0] + jnp.log(summed[:, 0])) - jnp.sum(goal_hot * logits)
    d_logits = (shifted / summed - goal_hot).astype(jnp.bfloat16)
    kept = (pres, prev_hiddens, prev_cells, cells, keeps, flat_hidden, d_logits, feature, onehot)
    return (kept, loss_part, jnp.transpose(hiddens, (1, 0, 2)))


def lstm_backward(weights, kept):
    w_rec, w_dec, w_in, bias_in = weights
    pres, prev_hiddens, prev_cells, cells, keeps, flat_hidden, d_logits, feature, onehot = kept
    steps, count, width = cells.shape
    from_dec = dot_right_t(d_logits, w_dec).reshape(steps, count, width)

    def retreat(carry, slot):
        grad_h, grad_c = carry
        pre, prev_cell, cell, extra, keep_now = slot
        gin, gforget, gcand, gout = jnp.split(pre, 4, axis=1)
        sig_in = jax.nn.sigmoid(gin)
        sig_forget = jax.nn.sigmoid(gforget)
        sig_out = jax.nn.sigmoid(gout)
        tan_cand = jnp.tanh(gcand)
        tan_cell = jnp.tanh(cell)
        grad_hid = extra + grad_h
        grad_out = grad_hid * tan_cell
        grad_cell = grad_c + grad_hid * sig_out * (1.0 - tan_cell * tan_cell)
        d_pre = jnp.concatenate(
            [
                grad_cell * tan_cand * sig_in * (1.0 - sig_in),
                grad_cell * prev_cell * sig_forget * (1.0 - sig_forget),
                grad_cell * sig_in * (1.0 - tan_cand * tan_cand),
                grad_out * sig_out * (1.0 - sig_out),
            ],
            axis=1,
        ).astype(jnp.bfloat16)
        back_h = dot_right_t(d_pre, w_rec) * keep_now
        back_c = grad_cell * sig_forget * keep_now
        return ((back_h, back_c), d_pre)

    start = (jnp.zeros((count, width), jnp.float32), jnp.zeros((count, width), jnp.float32))
    state, d_pres = lax.scan(
        retreat, start, (pres, prev_cells, cells, from_dec, keeps), reverse=True
    )
    flat_pre = d_pres.reshape(steps * count, -1)
    grad_dec = dot_left_t(flat_hidden, d_logits)
    grad_in = dot_left_t(feature, flat_pre)
    grad_bias = jnp.sum(flat_pre.astype(jnp.float32), axis=0)
    grad_feature = dot_right_t(flat_pre, w_in)
    grad_table = lax.dot_general(
        onehot.astype(jnp.float32),
        grad_feature,
        (((0,), (0,)), ((), ())),
        precision=lax.Precision.HIGHEST,
        preferred_element_type=jnp.float32,
    )
    grad_bias_out = jnp.sum(d_logits.astype(jnp.float32), axis=0)
    flat_prev = prev_hiddens.reshape(steps * count, width)
    return (grad_dec, grad_in, grad_bias, grad_table, grad_bias_out, flat_prev, flat_pre)


def general(chars, resets, targets, embed, w_in, bias_in, w_rec, w_dec, bias_dec):
    micro, count, steps = chars.shape
    everyone = lax.axis_size(("dp", "fsdp"))
    sums = None
    prev_list = []
    pre_list = []
    hidden_list = []
    for index in range(micro):
        forward_set = (
            lax.all_gather(w_rec, ("dp", "fsdp"), axis=0, tiled=True),
            lax.all_gather(w_dec, ("dp", "fsdp"), axis=0, tiled=True),
            lax.all_gather(w_in, ("dp", "fsdp"), axis=1, tiled=True),
            lax.all_gather(bias_in, ("dp", "fsdp"), axis=0, tiled=True),
        )
        kept, loss_part, hiddens = lstm_forward(
            forward_set, embed, bias_dec, chars[index], resets[index], targets[index]
        )
        backward_set = (
            lax.all_gather(w_rec, ("dp", "fsdp"), axis=0, tiled=True),
            lax.all_gather(w_dec, ("dp", "fsdp"), axis=0, tiled=True),
            lax.all_gather(w_in, ("dp", "fsdp"), axis=1, tiled=True),
            lax.all_gather(bias_in, ("dp", "fsdp"), axis=0, tiled=True),
        )
        grad_dec, grad_in, grad_bias, grad_table, grad_bias_out, flat_prev, flat_pre = (
            lstm_backward(backward_set, kept)
        )
        pieces = (grad_dec, grad_in, grad_bias, grad_table, grad_bias_out, loss_part)
        if sums is None:
            sums = pieces
        else:
            sums = tuple((first + second for first, second in zip(sums, pieces)))
        prev_list.append(flat_prev)
        pre_list.append(flat_pre)
        hidden_list.append(hiddens)
    prev_all = jnp.concatenate(prev_list, axis=0)
    pre_all = jnp.concatenate(pre_list, axis=0)
    grad_w_rec = lax.psum_scatter(
        dot_left_t(prev_all, pre_all), ("dp", "fsdp"), scatter_dimension=0, tiled=True
    )
    grad_w_dec, grad_w_in, grad_bias_in = (
        lax.psum_scatter(sums[0], ("dp", "fsdp"), scatter_dimension=0, tiled=True),
        lax.psum_scatter(sums[1], ("dp", "fsdp"), scatter_dimension=1, tiled=True),
        lax.psum_scatter(sums[2], ("dp", "fsdp"), scatter_dimension=0, tiled=True),
    )
    grad_embed, grad_bias_dec, total = lax.psum((sums[3], sums[4], sums[5]), ("dp", "fsdp"))
    loss = total / (micro * count * steps * everyone)
    hidden = jnp.stack(hidden_list, axis=0)
    return (
        loss,
        hidden,
        grad_embed,
        grad_w_in,
        grad_bias_in,
        grad_w_rec,
        grad_w_dec,
        grad_bias_dec,
    )


def solution(mesh):
    per_device = fused if (mesh.shape["dp"], mesh.shape["fsdp"]) == (8, 4) else general
    return jax.shard_map(
        per_device,
        mesh=mesh,
        in_specs=(
            P(None, ("dp", "fsdp"), None),
            P(None, ("dp", "fsdp"), None),
            P(None, ("dp", "fsdp"), None),
            P(),
            P(None, ("dp", "fsdp")),
            P(("dp", "fsdp")),
            P(("dp", "fsdp"), None),
            P(("dp", "fsdp"), None),
            P(),
        ),
        out_specs=(
            P(),
            P(None, ("dp", "fsdp"), None, None),
            P(),
            P(None, ("dp", "fsdp")),
            P(("dp", "fsdp")),
            P(("dp", "fsdp"), None),
            P(("dp", "fsdp"), None),
            P(),
        ),
        check_vma=False,
    )
```

```python
import functools

import jax
import jax.numpy as jnp
from jax import lax
from jax.experimental import pallas as pl
from jax.experimental.pallas import tpu as pltpu
from jax.sharding import PartitionSpec as P

MESH = pl.DeviceIdType.MESH
NN = ((1,), (0,))
NT = ((1,), (1,))
TN = ((0,), (0,))
F32 = jnp.float32
BF = jnp.bfloat16

VPAD = 384
EPAD = 128
RING = 4
SMALL = 112


def mm(left, right, dims):
    return lax.dot_general(left, right, (dims, ((), ())), preferred_element_type=F32)


def sigmoid(v):
    return 0.5 * jnp.tanh(0.5 * v) + 0.5


def lstm_kernel(
    steps, rows,
    w_rec, w_in_hbm, b_in_hbm, w_dec_hbm, emb_hbm, bias_hbm, chars_hbm, resets_hbm, targets_hbm,
    out_own, out_recv, out_in, out_dec, out_hid, out_small,
    W, WIN, WDEC, IDS, H, HT, HTS, HSEND, A, C, D, DS, DRAW, DL,
    w_in_raw, b_in_raw, w_dec_raw, emb_raw, bias_raw, chars_in, resets_in, targets_in, load_sem, ids_in, w_in, emb_t, w_dec, bias_dec, PR, STG, CB, PEND, OWN, DCN, SY, RY, SM, RM, EMBT, LV, BD, GWD, GIS, GY, SGM, GM, DWI, SIY, IY, SIM, IM, RS1, RS2, RS3, RS4, RS5, PIECE, PAIR, TOTAL,
    s_ids, r_ids, s_win, r_win, s_wa, r_wa, s_wm, r_wm, s_wy, r_wy, s_ws, r_ws,
    s_da, r_da, s_dm, r_dm, s_dy, r_dy, s_ds, r_ds, s_h, r_h, s_ht, r_ht, s_d, r_d,
    s_ph, r_ph, s_cb, r_cb, s_gd, r_gd, s_gi, r_gi, s_sm, r_sm, s_ry, r_ry, s_rm, r_rm, s_ra, r_ra,
    l_sem, hid_sem,
):
    last = steps - 1
    dp, fs = lax.axis_index("dp"), lax.axis_index("fsdp")
    z, x, y, c = dp // 2, dp % 2, fs // 2, fs % 2
    zh = z // 2
    a = z + zh * (3 - 2 * z)

    def dev(zz, xx, yy, cc):
        return (zz * 2 + xx, yy * 2 + cc)

    def kx(k):
        return x + (k % 2) * (1 - 2 * x)

    def kz(k):
        return z + (k // 2) * (1 - 2 * (z % 2))

    def ka(k):
        return a + (k // 2) * (1 - 2 * a)

    def kdev(k):
        return dev(kz(k), kx(k), y, c)

    def member(k):
        return 2 * kx(k) + ka(k)

    def unit_block(k, j):
        return 2 * (ka(k) + j * (3 - 2 * ka(k))) + kx(k)

    def lanes(ub):
        return pl.ds(pl.multiple_of(256 * ub, 256), 256)

    def place(k, far, yy, cc):
        return 4 * (2 * k + zh + far * (1 - 2 * zh)) + 2 * yy + cc

    def span(k, j):
        return slice(256 * (2 * k + j), 256 * (2 * k + j + 1))

    mir, ydev, sib = dev(3 - z, x, y, c), dev(z, x, 1 - y, c), dev(z, x, y, 1 - c)
    side = x + y - 2 * x * y
    perm = dev(side + zh * (3 - 2 * side), c, x, z % 2)
    back = dev(2 * zh + c, y, a + y - 2 * a * y, x)
    stays = jnp.logical_and(perm[0] == dp, perm[1] == fs)
    moved = jnp.logical_not(stays)

    def rc(src, dst, ss, rs, to):
        return pltpu.make_async_remote_copy(
            src_ref=src, dst_ref=dst, send_sem=ss, recv_sem=rs, device_id=to, device_id_type=MESH
        )

    barrier = pltpu.get_barrier_semaphore()

    def greet(to):
        pl.semaphore_signal(barrier, inc=1, device_id=to, device_id_type=MESH)

    for k in (1, 2, 3):
        greet(kdev(k))
    for to in (mir, ydev, sib):
        greet(to)

    @pl.when(moved)
    def _():
        greet(perm)
        greet(back)

    pairs = (
        (w_in_hbm, w_in_raw), (b_in_hbm, b_in_raw), (w_dec_hbm, w_dec_raw), (emb_hbm, emb_raw), (bias_hbm, bias_raw),
        (chars_hbm, chars_in), (resets_hbm, resets_in), (targets_hbm, targets_in),
    )
    loads = [pltpu.make_async_copy(src, dst, load_sem.at[n]) for n, (src, dst) in enumerate(pairs)]
    for load in loads:
        load.start()
    for load in loads:
        load.wait()
    emb, vocab = emb_raw.shape[1], emb_raw.shape[0]
    w_in[...] = jnp.zeros_like(w_in)
    w_in[0:emb, :] = w_in_raw[...]
    tail = emb // 16 * 16
    part = w_in[tail : tail + 16, :].astype(F32)
    bias_row = b_in_raw[...].astype(F32).reshape(1, 256)
    part = jnp.where(lax.broadcasted_iota(jnp.int32, (16, 256), 0) == emb - tail, bias_row, part)
    w_in[tail : tail + 16, :] = part.astype(BF)
    for s in range(2):
        stack = jnp.concatenate(
            [v for ref in (chars_in, resets_in, targets_in) for v in (ref[:, s, :], jnp.zeros((8 - steps, 32), jnp.int32))],
            axis=0,
        ).astype(F32)
        wide_stack = jnp.concatenate([stack, jnp.zeros((24, 96), F32)], axis=1)
        ids_in[s] = wide_stack.T[:32, :].astype(jnp.int32)
    pl.semaphore_wait(barrier, 6 + 2 * moved.astype(jnp.int32))


    def d_slot(b):
        return WDEC.at[pl.ds(pl.multiple_of(64 * b, 64), 64), :]

    def w_cols(ub, g):
        return w_rec.at[:, lanes(8 * g + ub)]

    def w_part(j, g, b):
        return W.at[4 * j + g, pl.ds(pl.multiple_of(64 * b, 64), 64), :]

    def wa_start(k):
        for j in (0, 1):
            for g in range(4):
                rc(w_cols(unit_block(k, j), g), w_part(j, g, place(k, 0, y, c)), s_wa.at[k - 1, j], r_wa.at[k - 1, j], kdev(k)).start()

    def wa(k, j):
        b = place(k, 0, y, c)
        part = W.at[pl.ds(4 * j, 4), pl.ds(pl.multiple_of(64 * b, 64), 64), :]
        return rc(part, part, s_wa.at[k - 1, j], r_wa.at[k - 1, j], kdev(k))

    def ids_copy(k, mem):
        return rc(ids_in, IDS.at[:, mem], s_ids.at[k - 1], r_ids.at[k - 1], kdev(k))

    def own_w(j, g):
        return pltpu.make_async_copy(w_cols(unit_block(0, j), g), w_part(j, g, place(0, 0, y, c)), l_sem.at[4 * j + g])

    for j in (0, 1):
        for g in range(4):
            own_w(j, g).start()
    for k in (1, 2, 3):
        ids_copy(k, member(0)).start()

    def win_perm(jj, gy, gc):
        return rc(w_in, WIN.at[jj, gy, gc], s_win.at[0], r_win.at[0], perm)

    def win_local():
        return pltpu.make_async_copy(w_in, WIN.at[x, z // 2, z % 2], l_sem.at[8])

    @pl.when(moved)
    def _():
        win_perm(x, z // 2, z % 2).start()

    @pl.when(stays)
    def _():
        win_local().start()

    for k in (1, 2, 3):
        wa_start(k)

    def w_half(j, b):
        return W.at[pl.ds(4 * j, 4), pl.ds(pl.multiple_of(64 * b, 64), 64), :]

    def to_mir(k, j):
        b = place(k, 0, y, c)
        return rc(w_half(j, b), w_half(j, b), s_wm.at[k, j], r_wm.at[k, j], mir)

    def from_mir(k, j):
        b = place(k, 1, y, c)
        return rc(w_half(j, b), w_half(j, b), s_wm.at[k, j], r_wm.at[k, j], mir)

    def group_block(i, yy, cc):
        return place(i % 4, i // 4, yy, cc)

    def to_y(i, j):
        b = group_block(i, y, c)
        return rc(w_half(j, b), w_half(j, b), s_wy.at[i, j], r_wy.at[i, j], ydev)

    def from_y(i, j):
        b = group_block(i, 1 - y, c)
        return rc(w_half(j, b), w_half(j, b), s_wy.at[i, j], r_wy.at[i, j], ydev)

    def to_s(i, j):
        b = group_block(i % 8, y + (i // 8) * (1 - 2 * y), c)
        return rc(w_half(j, b), w_half(j, b), s_ws.at[i, j], r_ws.at[i, j], sib)

    def from_s(i, j):
        b = group_block(i % 8, y + (i // 8) * (1 - 2 * y), 1 - c)
        return rc(w_half(j, b), w_half(j, b), s_ws.at[i, j], r_ws.at[i, j], sib)

    for j in (0, 1):
        for g in range(4):
            own_w(j, g).wait()
    inner = a == 1

    @pl.when(inner)
    def _():
        for j in (0, 1):
            to_mir(0, j).start()

    for j in (0, 1):
        to_y(0, j).start()
        to_s(0, j).start()

    def win_mir(jj):
        return rc(WIN.at[y, jj, c], WIN.at[y, jj, c], s_win.at[1], r_win.at[1], mir)

    def win_y(yy):
        return rc(WIN.at[yy, :, c], WIN.at[yy, :, c], s_win.at[2], r_win.at[2], ydev)

    def win_s(cc):
        return rc(WIN.at[:, :, cc], WIN.at[:, :, cc], s_win.at[3], r_win.at[3], sib)

    @pl.when(moved)
    def _():
        win_perm(y, zh, c).wait_recv()

    @pl.when(stays)
    def _():
        win_local().wait()

    win_mir(zh).start()


    IDS[:, member(0)] = ids_in[...]

    def own_blocks(k):
        for j in (0, 1):
            wa(k, j).wait_recv()
            to_y(k, j).start()

            @pl.when(inner)
            def _(j=j):
                to_mir(k, j).start()

            to_s(k, j).start()

    own_blocks(1)
    own_blocks(2)
    own_blocks(3)

    def da(k):
        return rc(w_dec, d_slot(place(k, 0, y, c)), s_da.at[k - 1], r_da.at[k - 1], kdev(k))

    HSEND[0, 0 : VPAD // 128] = jnp.zeros((VPAD // 128, 128, rows), BF)
    for n in range(VPAD // 128):
        held = min(128, vocab - 128 * n)
        HSEND[0, n, 0:held, 0:emb] = emb_raw[128 * n : 128 * n + held, :]
    unit = jnp.where(
        lax.broadcasted_iota(jnp.int32, (EPAD, EPAD), 0) == lax.broadcasted_iota(jnp.int32, (EPAD, EPAD), 1), 1.0, 0.0
    ).astype(BF)
    turned = mm(unit, HSEND[0, 0 : VPAD // 128].reshape(VPAD, EPAD), NT)
    emb_t[...] = jnp.where(lax.broadcasted_iota(jnp.int32, (EPAD, VPAD), 0) == emb, 1.0, turned).astype(BF)
    w_dec[...] = jnp.zeros_like(w_dec)
    w_dec[:, :vocab] = w_dec_raw[...]
    bias_dec[...] = jnp.full_like(bias_dec, -1e30)
    bias_dec[0:1, :vocab] = bias_raw[...].astype(F32).reshape(1, vocab)
    for k in (1, 2, 3):
        da(k).start()
    own_dec = pltpu.make_async_copy(w_dec, d_slot(place(0, 0, y, c)), l_sem.at[9])
    own_dec.start()

    for k in (1, 2, 3):
        ids_copy(k, member(k)).wait_recv()
    lane = lax.broadcasted_iota(jnp.int32, (rows, 24), 1)
    wide = lax.broadcasted_iota(jnp.int32, (rows, VPAD), 1).astype(F32)

    def column(at, s):
        packed = IDS[s].reshape(rows, 24)
        return jnp.sum(jnp.where(lane == at, packed, 0).astype(F32), axis=1, keepdims=True)

    def keep_of(t, s):
        return 1.0 - column(8 + t, s)

    def letter(t, s):
        return jnp.where(column(t, s) == wide, 1.0, 0.0).astype(BF)

    EMBT[...] = jnp.zeros_like(EMBT)
    LV[...] = jnp.zeros_like(LV)
    BD[...] = jnp.zeros_like(BD)
    GWD[...] = jnp.zeros_like(GWD)
    DWI[...] = jnp.zeros_like(DWI)
    DCN[...] = jnp.zeros_like(DCN)
    OWN[...] = jnp.zeros_like(OWN)
    PR[0] = jnp.zeros(PR.shape[1:], BF)

    win_mir(1 - zh).wait_recv()

    win_y(y).start()
    def pass_y(i):
        for j in (0, 1):
            from_y(i, j).wait_recv()
            to_s(8 + i, j).start()

    def pass_mir(k):
        for j in (0, 1):
            from_mir(k, j).wait_recv()
            to_y(4 + k, j).start()
            to_s(4 + k, j).start()

    for i in range(3):
        pass_y(i)

    @pl.when(inner)
    def _():
        pass_mir(0)

    @pl.when(jnp.logical_not(inner))
    def _():
        for k in range(4):
            for j in (0, 1):
                to_mir(k, j).start()

    pass_y(3)
    win_y(1 - y).wait_recv()
    win_s(c).start()
    win_s(1 - c).wait_recv()

    def h_copy(t, s, k, j):
        src, dst = H.at[t % RING, s, :, span(0, j)], H.at[t % RING, s, :, span(k, j)]
        return rc(src, dst, s_h.at[t, s, k - 1, j], r_h.at[t, s, k - 1, j], kdev(k))

    def wait_h(t, s):
        for k in (1, 2, 3):
            for j in (0, 1):
                h_copy(t, s, k, j).wait_recv()

    def gates(t, s, first):
        keep = None if first else keep_of(t, s)
        feature = mm(letter(t, s), emb_t[...], NT).astype(BF)
        for j in (0, 1):
            pre = []
            for g in range(4):
                drive = mm(feature, WIN[j, g // 2, g % 2], NN)
                if not first:
                    drive = drive + keep * mm(H[(t - 1) % RING, s], W[4 * j + g], NN)
                pre.append(drive)
            s_i, s_f, t_g, s_o = sigmoid(pre[0]), sigmoid(pre[1]), jnp.tanh(pre[2]), sigmoid(pre[3])
            cell = s_i * t_g
            if not first:
                cell = s_f * (C[t - 1, s, j] * keep) + cell
            for g, v in enumerate((s_i, s_f, t_g, s_o)):
                A[t, s, 4 * j + g] = v
            C[t, s, j] = cell
            H[t % RING, s, :, span(0, j)] = (s_o * jnp.tanh(cell)).astype(BF)
            for k in (3, 1, 2):
                h_copy(t, s, k, j).start()

    @pl.loop(0, 2)
    def _(s):
        gates(0, s, True)

    @pl.when(jnp.logical_not(inner))
    def _():
        pass_mir(0)

    for k in (1, 2, 3):
        pass_mir(k)

    def dec_mir(k, far):
        b = place(k, far, y, c)
        return rc(d_slot(b), d_slot(b), s_dm.at[k], r_dm.at[k], mir)

    def dec_y(i, yy):
        b = group_block(i, yy, c)
        return rc(d_slot(b), d_slot(b), s_dy.at[i], r_dy.at[i], ydev)

    def dec_s(i, cc):
        b = group_block(i % 8, y + (i // 8) * (1 - 2 * y), cc)
        return rc(d_slot(b), d_slot(b), s_ds.at[i], r_ds.at[i], sib)

    own_dec.wait()
    dec_mir(0, 0).start()
    dec_y(0, y).start()
    dec_s(0, c).start()
    for k in (1, 2, 3):
        da(k).wait_recv()
        dec_mir(k, 0).start()
        dec_y(k, y).start()
        dec_s(k, c).start()

    for i in (4, 5, 6, 7):
        pass_y(i)

    @pl.loop(0, 16)
    def _(i):
        for j in (0, 1):
            from_s(i, j).wait_recv()

    def released(t, s):
        hid_copy(t, s).wait()
        for k in (1, 2, 3):
            for j in (0, 1):
                h_copy(t, s, k, j).wait_send()

    def forward(t, s):
        wait_h(t - 1, s)

        @pl.when(t >= RING - 1)
        def _():
            released(t - (RING - 1), s)

        gates(t, s, False)

    row = lax.broadcasted_iota(jnp.int32, (128, 256), 0)
    col = lax.broadcasted_iota(jnp.int32, (128, 256), 1)

    def select(cc):
        yy = y + (row // 64) * (1 - 2 * y)
        return jnp.where(col == 64 * (2 * yy + cc) + row % 64, 1.0, 0.0).astype(BF)

    def lane_slot(t, s):
        return pl.ds(pl.multiple_of((2 * t + s) * rows, rows), rows)

    def ht_copy(t, s, slot):
        return rc(HSEND.at[slot], HTS.at[:, :, lane_slot(t, s)], s_ht.at[t, s], r_ht.at[t, s], sib)

    def hid_copy(t, s):
        mine = H.at[t % RING, s, pl.ds(pl.multiple_of(32 * member(0), 32), 32), :]
        return pltpu.make_async_copy(mine, out_hid.at[s * steps + t], hid_sem.at[t, s])

    def logits_of(t, s):
        scores = mm(H[t % RING, s], WDEC[...], NN) + bias_dec[0:1, :]
        top = jnp.max(scores, axis=1, keepdims=True)
        shifted = jnp.exp(scores - top)
        summed = jnp.sum(shifted, axis=1, keepdims=True)
        goal = jnp.where(column(16 + t, s) == wide, 1.0, 0.0)
        picked = jnp.sum(goal * scores, axis=1, keepdims=True)
        LV[...] += jnp.broadcast_to(top + jnp.log(summed) - picked, (rows, 128))
        DL[t, s] = (shifted / summed - goal).astype(BF)

    def decoder_side(t, s):
        hid_copy(t, s).start()
        grad = DL[t, s]
        BD[...] += mm(jnp.ones((8, rows), BF), grad, NN)
        for j in (0, 1):
            GWD[j] += mm(H[t % RING, s, :, span(0, j)], grad, TN).reshape(2, 2, 64, VPAD)

    def transposed_side(t, s):
        slot = s
        mine, other = select(c), select(1 - c)

        @pl.when(t >= 1)
        def _():
            ht_copy(t - 1, s, slot).wait_send()

        for tile in range(8):
            part = H[t % RING, s, :, 256 * tile : 256 * (tile + 1)]
            HT[tile, :, lane_slot(t, s)] = mm(mine, part, NT).astype(BF)
            HSEND[slot, tile] = mm(other, part, NT).astype(BF)
        ht_copy(t, s, slot).start()

    def decoder_mirror():
        @pl.loop(0, 4)
        def _(k):
            dec_mir(k, 1).wait_recv()
            dec_y(4 + k, y).start()
            dec_s(4 + k, c).start()

    def decoder_rest():
        @pl.loop(0, 8)
        def _(i):
            k, j = i // 2, i % 2
            to_mir(k, j).wait_send()
            to_y(i, 0).wait_send()
            to_y(i, 1).wait_send()

        @pl.loop(0, 16)
        def _(i):
            to_s(i, 0).wait_send()
            to_s(i, 1).wait_send()

        @pl.loop(0, 8)
        def _(i):
            dec_y(i, 1 - y).wait_recv()
            dec_s(8 + i, c).start()

        @pl.loop(0, 16)
        def _(i):
            dec_s(i, 1 - c).wait_recv()

    def aside(t, s):
        logits_of(t, s)
        decoder_side(t, s)
        transposed_side(t, s)

    @pl.loop(2, 2 * steps)
    def _(i):
        t, s = i // 2, i % 2
        forward(t, s)

        @pl.when(i == 3)
        def _():
            decoder_mirror()

        @pl.when(i == 5)
        def _():
            decoder_rest()

        @pl.when(i >= 5)
        def _():
            @pl.loop(i - 4 - (13 - i) // 8, i - 3)
            def _(n):
                aside(n // 2, n % 2)


    def d_copy(t, s):
        return rc(D.at[:, t - 1, s], DS.at[:, t - 1, s], s_d.at[t, s], r_d.at[t, s], sib)

    def turn():
        def rows_of(q):
            return slice(256 * q, 256 * (q + 1))

        def swap(p, q):
            upper, lower = W[p, rows_of(q), :].T, W[q, rows_of(p), :].T
            W[p, rows_of(q), :] = lower
            W[q, rows_of(p), :] = upper

        for p in range(8):
            W[p, rows_of(p), :] = W[p, rows_of(p), :].T
            for q in range(p):
                swap(p, q)

    def cell_back(t, s, oldest):
        keep = keep_of(t, s)
        for j in (0, 1):
            up = WDEC[span(0, j), :]
            dh = mm(DL[t, s], up, NT)
            rest = PR[(t + 1) % 2, s, 0, j].astype(F32) + PR[(t + 1) % 2, s, 1, j].astype(F32)
            dh = dh + (OWN[s, j] + rest)
            s_i, s_f, t_g, s_o = (A[t, s, 4 * j + g] for g in range(4))
            t_c = jnp.tanh(C[t, s, j])
            d_o = dh * t_c
            d_c = dh * s_o * (1.0 - t_c * t_c) + DCN[s, j]
            d_i = d_c * t_g * s_i * (1.0 - s_i)
            d_g = d_c * s_i * (1.0 - t_g * t_g)
            d_o = d_o * s_o * (1.0 - s_o)
            if oldest:
                d_f = jnp.zeros_like(d_i)
            else:
                d_f = d_c * (C[t - 1, s, j] * keep) * s_f * (1.0 - s_f)
                DCN[s, j] = keep * (d_c * s_f)
            for g, v in enumerate((d_i, d_f, d_g, d_o)):
                low = v.astype(BF)
                DRAW[4 * j + g] = low
                if not oldest:
                    D[4 * j + g, t - 1, s] = low * keep.astype(BF)

    def part_rows(h):
        return slice(64 * h, 64 * (h + 1))

    def pr_half(t, s, k, h):
        src, dst = STG.at[s, k - 1, :, part_rows(h)], PR.at[t % 2, s, k - 1, :, part_rows(h)]
        return rc(src, dst, s_ph.at[t, s, k - 1, h], r_ph.at[t, s, k - 1, h], kdev(k))

    def owed_copy(t, s, n):
        return rc(STG.at[s, 2, :, part_rows(n)], CB.at[s, n], s_cb.at[t, s, n], r_cb.at[t, s, n], kdev(1 + n))

    def pr_each(act):
        for k in (1, 2):
            for h in (0, 1):
                act(k, h)

    def pr_arrived(t, s):
        pr_each(lambda k, h: pr_half(t, s, k, h).wait_recv())

    def pr_left(t, s):
        pr_each(lambda k, h: pr_half(t, s, k, h).wait_send())
        for n in (0, 1):
            owed_copy(t, s, n).wait_send()

    def product_back(t, s):
        left = jnp.concatenate([D[q, t - 1, s] for q in range(8)], axis=1)
        for k, j in ((3, 0), (3, 1), (1, 0), (1, 1), (2, 0), (2, 1), (0, 0), (0, 1)):
            total = mm(left, W[2 * k + j], NN)
            if k == 0:
                OWN[s, j] = total
                continue
            STG[s, k - 1, j] = total.astype(BF)
            if k < 3:
                PEND[k - 1, j] = total[part_rows(2 - k)]
            elif j == 1:
                owed_copy(t, s, 0).start()
                owed_copy(t, s, 1).start()
        for k in (1, 2):
            pr_half(t, s, k, k - 1).start()

    def add_owed(t, s):
        for k in (2, 1):
            h = 2 - k
            owed_copy(t, s, h).wait_recv()
            STG[s, k - 1, :, part_rows(h)] = (PEND[k - 1] + CB[s, h].astype(F32)).astype(BF)
            pr_half(t, s, k, h).start()

    def input_side(t, s):
        onehot = letter(t, s)
        feat_t = mm(emb_t[...], onehot, NT).astype(BF)
        inputs = []
        for q in range(8):
            jj, gy, gc = q // 4, (q // 2) % 2, q % 2
            DWI[jj, gy, gc] += mm(feat_t, DRAW[q], NN)
            inputs.append(WIN[jj, gy, gc])
        grad_t = mm(jnp.concatenate(inputs, axis=1), jnp.concatenate([DRAW[q] for q in range(8)], axis=1), NT)
        high = grad_t.astype(BF)
        low = (grad_t - high.astype(F32)).astype(BF)
        EMBT[...] += mm(high, onehot, NN) + mm(low, onehot, NN)

    def gd_s():
        return rc(GWD.at[:, :, 1 - c], GIS.at[:, :, 0:64], s_gd.at[0], r_gd.at[0], sib)

    def gd_y():
        return rc(GWD.at[:, 1 - y, c], GY, s_gd.at[1], r_gd.at[1], ydev)

    def gd_m():
        return rc(SGM, GM, s_gd.at[2], r_gd.at[2], mir)

    turn()

    @pl.loop(0, 2 * (steps - 1))
    def _(i):
        t, s = last - i // 2, i % 2

        @pl.when(i < 2)
        def _():
            wait_h(t, s)
            logits_of(last, s)

        @pl.when(i >= 2)
        def _():
            pr_arrived(t + 1, s)

        cell_back(t, s, False)

        @pl.when(i >= 1)
        def _():
            add_owed(t + 1 - s, 1 - s)

        @pl.when(i >= 2)
        def _():
            pr_left(t + 1, s)

        product_back(t, s)
        d_copy(t, s).start()

        @pl.when(i < 2 * (steps - 1) - 1)
        def _():
            input_side(t, s)

        @pl.when(i < 2)
        def _():
            logits_of(last - 1, s)

        @pl.when(jnp.logical_and(i >= 2, i < 4))
        def _():
            decoder_side(last - 1, s)
            transposed_side(last - 1, s)

        @pl.when(i == 4)
        def _():
            @pl.loop(0, 2)
            def _(n):
                decoder_side(last, n)

            gd_s().start()

        @pl.when(i == 5)
        def _():
            gd_s().wait_recv()
            GWD[:, :, c] += GIS[:, :, 0:64]
            gd_y().start()

        @pl.when(i == 7)
        def _():
            gd_y().wait_recv()
            GWD[:, y, c] += GY[...]
            SGM[...] = GWD[1 - zh, y, c].astype(BF)
            gd_m().start()

        @pl.when(i == 9)
        def _():
            gd_m().wait_recv()
            out_dec[...] = GWD[zh, y, c] + GM[...].astype(F32)

    @pl.loop(0, 2 * (steps - 1))
    def _(i):
        ht_copy(i // 2, i % 2, 0).wait_recv()
        d_copy(1 + i // 2, i % 2).wait_recv()

    depth = 2 * (steps - 1) * rows

    def kept(q):
        return A.at[2 + q // 4, (q % 4) // 2, :, pl.ds(pl.multiple_of(64 * (q % 2), 64), 64), :]

    def tile_of(q):
        k, near = q % 4, q // 4
        return 2 * k + 1 - zh + near * (2 * zh - 1)

    def ry_copy(p, q):
        return rc(SY.at[p % 4], RY.at[q], s_ry.at[p], r_ry.at[q], ydev)

    def pieces(k):
        return (1, 2, 2, 4)[k]

    def piece(k, n):
        size = 8 // pieces(k)
        return slice(size * n, size * (n + 1))

    def rm_copy(k, n):
        at = (0, 1, 3, 5)[k] + n
        return rc(SM.at[k, piece(k, n)], RM.at[k, piece(k, n)], s_rm.at[at], r_rm.at[at], mir)

    def ry_first(n):
        return rc(SY.at[0, piece(3, n)], RY.at[3, piece(3, n)], s_ry.at[8 + n], r_ry.at[8 + n], ydev)

    def ry_second(n):
        return rc(SY.at[1, piece(2, n)], RY.at[2, piece(2, n)], s_ry.at[12 + n], r_ry.at[12 + n], ydev)

    def ry_sent(p):
        @pl.when(p == 0)
        def _():
            for n in range(4):
                ry_first(n).wait_send()

        @pl.when(p == 1)
        def _():
            for n in range(2):
                ry_second(n).wait_send()

        @pl.when(p > 1)
        def _():
            ry_copy(p, order(p)).wait_send()

    def ra_copy(k, n):
        at = (0, 0, 2, 3)[k] + n
        rows_of_q = piece(k, n) if k == 1 else slice(0, 8)
        return rc(SM.at[k, rows_of_q], out_recv.at[k - 1, rows_of_q], s_ra.at[at], r_ra.at[at], kdev(k))

    def ra_pieces(k):
        return 2 if k == 1 else 1

    def order(p):
        return 3 - p + 8 * (p // 4)

    def make_tile(p):
        q = order(p)
        tile = tile_of(q)
        left, right = HT[tile], HTS[tile]
        hold = kept(q)

        @pl.when(p >= 4)
        def _():
            ry_sent(p - 4)

        for n in range(8):
            grad = mm(left, D[n].reshape(depth, 256), NN) + mm(right, DS[n].reshape(depth, 256), NN)
            hold[n] = grad[:64]
            SY[p % 4, n] = grad[64:].astype(BF)
            if n % 2 == 1:
                @pl.when(p == 0)
                def _(n=n):
                    ry_first(n // 2).start()

            if n % 4 == 3:
                @pl.when(p == 1)
                def _(n=n):
                    ry_second(n // 4).start()

        @pl.when(p > 1)
        def _():
            ry_copy(p, q).start()

    def add_y(q):
        ry_copy(0, q).wait_recv()
        hold = kept(q)
        hold[...] = hold[...] + RY[q].astype(F32)

    def pass_first(n):
        ry_first(n).wait_recv()
        SM[3, piece(3, n)] = (kept(3)[piece(3, n)] + RY[3, piece(3, n)].astype(F32)).astype(BF)
        rm_copy(3, n).start()

    def pass_on(k):
        if k == 3:
            for n in range(4):
                pass_first(n)
            return
        if k == 2:
            for n in range(2):
                ry_second(n).wait_recv()
                SM[2, piece(2, n)] = (kept(2)[piece(2, n)] + RY[2, piece(2, n)].astype(F32)).astype(BF)
                rm_copy(2, n).start()
            return
        add_y(k)
        for n in range(pieces(k)):
            SM[k, piece(k, n)] = kept(k)[piece(k, n)].astype(BF)
            rm_copy(k, n).start()

    def finish(k):
        add_y(4 + k)
        if k != 1:
            for n in range(pieces(k)):
                rm_copy(k, n).wait_recv()
        if k == 0:
            out_own[...] = kept(4)[...] + RM[0].astype(F32)
            return
        for n in range(ra_pieces(k)):
            part = piece(1, n) if k == 1 else slice(0, 8)
            if k == 1:
                rm_copy(k, n).wait_recv()
                rm_copy(k, n).wait_send()
            else:
                for m in range(pieces(k)):
                    rm_copy(k, m).wait_send()
            SM[k, part] = (kept(4 + k)[part] + RM[k, part].astype(F32)).astype(BF)
            ra_copy(k, n).start()

    def settle(p):
        q = order(p)
        pass_on(q) if q < 4 else finish(q - 4)

    outer = jnp.logical_not(inner)

    def core_rows(cc):
        return pl.ds(pl.multiple_of(64 * cc, 64), 64)

    def piece_rows(xx):
        return pl.ds(pl.multiple_of(64 * c + 32 * xx, 32), 32)

    def sm_core():
        return rc(out_small.at[core_rows(1 - c)], RS1, s_sm.at[0], r_sm.at[0], sib)

    def sm_group(k):
        xx = kx(k)
        return rc(out_small.at[piece_rows(xx)], RS2.at[k - 1], s_sm.at[k], r_sm.at[k], kdev(k))

    def sm_quarter(n):
        return rc(PIECE if n == 0 else PAIR, RS3.at[n], s_sm.at[4 + n], r_sm.at[4 + n], (ydev, mir)[n])

    def sm_spread(k):
        return rc(TOTAL, RS4.at[k - 1], s_sm.at[6 + k], r_sm.at[6 + k], kdev(k))

    def sm_last():
        return rc(out_small.at[core_rows(c)], RS5, s_sm.at[10], r_sm.at[10], sib)

    def sm_step1():
        sm_core().wait_recv()
        out_small[core_rows(c)] = out_small[core_rows(c)] + RS1[...]

        @pl.when(outer)
        def _():
            sm_group(1).start()

        @pl.when(inner)
        def _():
            sm_group(2).start()
            sm_group(3).start()

    def sm_step2():
        @pl.when(outer)
        def _():
            for k in (1, 2, 3):
                sm_group(k).wait_recv()
            PIECE[...] = (out_small[piece_rows(x)] + RS2[0]) + (RS2[1] + RS2[2])
            sm_quarter(0).start()

    def sm_step_mir():
        @pl.when(outer)
        def _():
            sm_quarter(0).wait_recv()
            PAIR[...] = PIECE[...] + RS3[0]
            sm_quarter(1).start()

    def sm_step3():
        @pl.when(outer)
        def _():
            sm_quarter(1).wait_recv()
            TOTAL[...] = PAIR[...] + RS3[1]
            for k in (1, 2, 3):
                sm_spread(k).start()

    def sm_step4():
        sm_core().wait_send()

        @pl.when(outer)
        def _():
            sm_group(1).wait_send()
            sm_spread(1).wait_recv()
            out_small[piece_rows(1 - x)] = RS4[0]
            out_small[piece_rows(x)] = TOTAL[...]

        @pl.when(inner)
        def _():
            for k in (2, 3):
                sm_group(k).wait_send()
                sm_spread(k).wait_recv()
                out_small[piece_rows(kx(k))] = RS4[k - 1]

        sm_last().start()

    def sm_step5():
        sm_last().wait_recv()
        out_small[core_rows(1 - c)] = RS5[...]

    live = pl.ds(0, 104)

    def gi_s():
        return rc(DWI.at[:, :, 1 - c, live], GIS.at[:, :, :, 0:256], s_gi.at[0], r_gi.at[0], sib)

    def gi_y():
        return rc(SIY, IY, s_gi.at[1], r_gi.at[1], ydev)

    def gi_m():
        return rc(SIM, IM, s_gi.at[2], r_gi.at[2], mir)

    def gi_p():
        return rc(DWI.at[y, zh, c, live], out_in, s_gi.at[3], r_gi.at[3], back)

    def first_position():
        @pl.loop(0, 2)
        def _(s):
            pr_arrived(1, s)
            cell_back(0, s, True)
            input_side(0, s)

            @pl.when(jnp.logical_and(inner, s == 0))
            def _():
                pass_first(2)

        leader = jnp.logical_and(x == 0, a == 0)
        high_row = lax.broadcasted_iota(jnp.int32, (8, VPAD), 0)
        loss = jnp.sum(LV[...], axis=0, keepdims=True)
        loss = jnp.concatenate([loss] * (VPAD // 128), axis=1)
        extra = jnp.where(high_row == 0, BD[...], jnp.where(high_row == 1, loss, 0.0))
        out_small[...] = EMBT[...]
        out_small[SMALL - 8 : SMALL] = jnp.where(leader, extra, 0.0)
        sm_core().start()
        gi_s().start()

    @pl.loop(0, 8)
    def _(p):
        make_tile(p)

        @pl.when(p == 0)
        def _():
            add_owed(1, 1)

        @pl.when(p == 1)
        def _():
            @pl.when(inner)
            def _():
                pass_first(0)

            input_side(1, 1)

            @pl.when(inner)
            def _():
                pass_first(1)

            first_position()
            sm_step1()
            @pl.when(inner)
            def _():
                pass_first(3)
                settle(1)

            gi_s().wait_recv()
            DWI[:, :, c, 0:104] = DWI[:, :, c, 0:104] + GIS[:, :, :, 0:256]
            sm_step2()
            SIY[...] = DWI[1 - y, :, c, 0:112].astype(BF)
            gi_y().start()

            @pl.when(outer)
            def _():
                settle(0)

        @pl.when(p == 2)
        def _():
            @pl.when(outer)
            def _():
                settle(1)

            sm_step_mir()

        @pl.when(p == 3)
        def _():
            gi_y().wait_recv()
            DWI[y, :, c, 0:104] = DWI[y, :, c, 0:104] + IY[...].astype(F32)[:, 0:104]
            SIM[...] = DWI[y, 1 - zh, c, 0:112].astype(BF)
            gi_m().start()

        @pl.when(p == 4)
        def _():
            settle(2)
            sm_step3()

        @pl.when(p == 5)
        def _():
            settle(3)

    settle(4)
    settle(5)
    sm_step4()
    settle(6)
    gi_m().wait_recv()
    DWI[y, zh, c, 0:104] = DWI[y, zh, c, 0:104] + IM[...].astype(F32)[0:104]

    @pl.when(moved)
    def _():
        gi_p().start()

    @pl.when(stays)
    def _():
        out_in[...] = DWI[y, zh, c, 0:104]

    sm_step5()
    settle(7)

    for k in (1, 2, 3):
        for j in (0, 1):
            wa(k, j).wait_send()
        ids_copy(k, member(0)).wait_send()
        da(k).wait_send()
        for n in range(ra_pieces(k)):
            ra_copy(k, n).wait()
    rm_copy(0, 0).wait_send()

    @pl.when(moved)
    def _():
        gi_p().wait()
        win_perm(x, z // 2, z % 2).wait_send()

    for s in range(2):
        pr_left(1, s)
    win_mir(zh).wait_send()
    win_y(y).wait_send()
    win_s(c).wait_send()
    @pl.when(outer)
    def _():
        sm_quarter(0).wait_send()
        sm_quarter(1).wait_send()
        for k in (1, 2, 3):
            sm_spread(k).wait_send()

    for copy in (gd_s, gd_y, gd_m, gi_s, gi_y, gi_m, sm_last):
        copy().wait_send()
    for s in range(2):
        ht_copy(last - 1, s, s).wait_send()

    @pl.loop(0, 4)
    def _(k):
        dec_mir(k, 0).wait_send()

    @pl.loop(0, 8)
    def _(i):
        dec_y(i, y).wait_send()

    for p in range(4, 8):
        ry_copy(p, order(p)).wait_send()

    @pl.loop(0, 16)
    def _(i):
        dec_s(i, c).wait_send()

    @pl.loop(2 * (steps - RING + 1), 2 * steps)
    def _(i):
        released(i // 2, i % 2)

    @pl.loop(0, 2 * (steps - 1))
    def _(i):
        d_copy(1 + i // 2, i % 2).wait_send()


def output_kernel(
    own, recv, g_in, g_dec, hid_in, small, hid, table, o_in, o_bias, o_rec, o_dec, o_bias_dec, loss,
    h_buf, own_buf, recv_buf, rec_buf, in_buf, dec_buf, small_buf, t_buf, i_buf, b_buf, d_buf, bd_buf, l_buf, in_sem, out_sem,
):
    dp = lax.axis_index("dp")
    z, x = dp // 2, dp % 2
    a = z + (z // 2) * (3 - 2 * z)

    def cols(k, j, g):
        xk, ak = x + (k % 2) * (1 - 2 * x), a + (k // 2) * (1 - 2 * a)
        ub = 2 * (ak + j * (3 - 2 * ak)) + xk
        return pl.ds(pl.multiple_of(256 * (8 * g + ub), 256), 256)

    def load(n, src, dst):
        copy = pltpu.make_async_copy(src, dst, in_sem.at[n])
        copy.start()
        return copy

    def store(n, src, dst):
        copy = pltpu.make_async_copy(src, dst, out_sem.at[n])
        copy.start()
        return copy

    hid_loads = [
        load(p, hid_in.at[:, :, 256 * p : 256 * (p + 1)], h_buf.at[:, :, cols(p // 2, p % 2, 0)]) for p in range(8)
    ]
    rec_loads = [load(8, own, own_buf), load(9, recv, recv_buf)]
    small_loads = [load(10, small, small_buf), load(11, g_in, in_buf), load(12, g_dec, dec_buf)]
    for copy in hid_loads:
        copy.wait()
    stores = [store(0, h_buf, hid)]
    for copy in rec_loads:
        copy.wait()
    for k in range(4):
        for j in (0, 1):
            for g in range(4):
                part = own_buf[4 * j + g] if k == 0 else recv_buf[k - 1, 4 * j + g].astype(F32)
                rec_buf[:, cols(k, j, g)] = part
    stores.append(store(1, rec_buf, o_rec))
    for copy in small_loads:
        copy.wait()
    vocab, emb = table.shape
    t_buf[...] = small_buf[0:SMALL, :].T[:vocab, :emb]
    i_buf[...] = in_buf[0:emb, :]
    b_buf[...] = in_buf[emb, :]
    d_buf[...] = dec_buf[:, :vocab]
    bd_buf[...] = small_buf[SMALL - 8, :vocab]
    l_buf[...] = small_buf[SMALL - 7 : SMALL - 6, 0:1]
    pairs = ((t_buf, table), (i_buf, o_in), (b_buf, o_bias), (d_buf, o_dec), (bd_buf, o_bias_dec), (l_buf, loss))
    for n, (src, dst) in enumerate(pairs):
        stores.append(store(2 + n, src, dst))
    for copy in stores:
        copy.wait()


def fused(chars, resets, targets, embed, w_in, bias_in, w_rec, w_dec, bias_dec):
    micro, count, steps = chars.shape
    own_rows, gate_cols = w_rec.shape
    vocab, emb = embed.shape
    width = gate_cols // 4
    members = 4
    rows = count * members
    vm = pl.BlockSpec(memory_space=pltpu.VMEM)
    hbm = pl.BlockSpec(memory_space=pl.ANY)
    dma = pltpu.SemaphoreType.DMA
    n = steps - 1
    scratch = [
        pltpu.VMEM((8, width, 256), BF),
        pltpu.VMEM((2, 2, 2, EPAD, 256), BF),
        pltpu.VMEM((width, VPAD), BF),
        pltpu.VMEM((micro, members, count, 24), jnp.int32),
        pltpu.VMEM((RING, micro, rows, width), BF),
        pltpu.VMEM((8, 128, 2 * n * rows), BF),
        pltpu.VMEM((8, 128, 2 * n * rows), BF),
        pltpu.VMEM((2, 8, 128, rows), BF),
        pltpu.VMEM((steps, micro, 8, rows, 256), F32),
        pltpu.VMEM((steps, micro, 2, rows, 256), F32),
        pltpu.VMEM((8, n, micro, rows, 256), BF),
        pltpu.VMEM((8, n, micro, rows, 256), BF),
        pltpu.VMEM((8, rows, 256), BF),
        pltpu.VMEM((steps, micro, rows, VPAD), BF),
        pltpu.VMEM(w_in.shape, BF),
        pltpu.VMEM(bias_in.shape, BF),
        pltpu.VMEM(w_dec.shape, BF),
        pltpu.VMEM(embed.shape, BF),
        pltpu.VMEM(bias_dec.shape, BF),
        pltpu.VMEM((steps, micro, count), jnp.int32),
        pltpu.VMEM((steps, micro, count), jnp.int32),
        pltpu.VMEM((steps, micro, count), jnp.int32),
        dma((8,)),
        pltpu.VMEM((micro, count, 24), jnp.int32),
        pltpu.VMEM((EPAD, 256), BF),
        pltpu.VMEM((EPAD, VPAD), BF),
        pltpu.VMEM((own_rows, VPAD), BF),
        pltpu.VMEM((8, VPAD), F32),
        pltpu.VMEM((2, micro, 2, 2, rows, 256), BF),
        pltpu.VMEM((micro, 3, 2, rows, 256), BF),
        pltpu.VMEM((micro, 2, 2, rows // 2, 256), BF),
        pltpu.VMEM((2, 2, rows // 2, 256), F32),
        pltpu.VMEM((micro, 2, rows, 256), F32),
        pltpu.VMEM((micro, 2, rows, 256), F32),
        pltpu.VMEM((4, 8, 64, 256), BF),
        pltpu.VMEM((8, 8, 64, 256), BF),
        pltpu.VMEM((4, 8, 64, 256), BF),
        pltpu.VMEM((4, 8, 64, 256), BF),
        pltpu.VMEM((EPAD, VPAD), F32),
        pltpu.VMEM((rows, 128), F32),
        pltpu.VMEM((8, VPAD), F32),
        pltpu.VMEM((2, 2, 2, 64, VPAD), F32),
        pltpu.VMEM((2, 2, 104, VPAD), F32),
        pltpu.VMEM((2, 64, VPAD), F32),
        pltpu.VMEM((64, VPAD), BF),
        pltpu.VMEM((64, VPAD), BF),
        pltpu.VMEM((2, 2, 2, EPAD, 256), F32),
        pltpu.VMEM((2, 112, 256), BF),
        pltpu.VMEM((2, 112, 256), BF),
        pltpu.VMEM((112, 256), BF),
        pltpu.VMEM((112, 256), BF),
        pltpu.VMEM((64, VPAD), F32),
        pltpu.VMEM((3, 32, VPAD), F32),
        pltpu.VMEM((2, 32, VPAD), F32),
        pltpu.VMEM((3, 32, VPAD), F32),
        pltpu.VMEM((64, VPAD), F32),
        pltpu.VMEM((32, VPAD), F32),
        pltpu.VMEM((32, VPAD), F32),
        pltpu.VMEM((32, VPAD), F32),
    ]
    shapes = [
        (3,), (4,), (3, 2), (4, 2), (8, 2), (16, 2), (3,), (4,), (8,), (16,),
        (steps, 2, 3, 2), (n, 2), (steps, 2),
        (steps, 2, 2, 2), (steps, 2, 2), (3,), (4,), (11,), (14,), (9,), (4,),
    ]
    for shape in shapes:
        scratch += [dma(shape), dma(shape)]
    scratch += [dma((12,)), dma((steps, 2))]
    out_own, out_recv, out_in, out_dec, out_hid, out_small = pl.pallas_call(
        functools.partial(lstm_kernel, steps, rows),
        out_shape=(
            jax.ShapeDtypeStruct((8, own_rows, 256), F32),
            jax.ShapeDtypeStruct((3, 8, own_rows, 256), BF),
            jax.ShapeDtypeStruct((104, 256), F32),
            jax.ShapeDtypeStruct((own_rows, VPAD), F32),
            jax.ShapeDtypeStruct((micro * steps, count, width), BF),
            jax.ShapeDtypeStruct((EPAD, VPAD), F32),
        ),
        in_specs=[hbm] * 9,
        out_specs=(vm, hbm, vm, vm, hbm, vm),
        scratch_shapes=scratch,
        compiler_params=pltpu.CompilerParams(
            collective_id=0, has_side_effects=True, vmem_limit_bytes=66 * 1000 * 1000
        ),
    )(
        w_rec, w_in, bias_in, w_dec, embed, bias_dec,
        chars.transpose(2, 0, 1), resets.transpose(2, 0, 1), targets.transpose(2, 0, 1),
    )
    everyone = lax.axis_size(("dp", "fsdp"))
    hid, table, g_in, g_bias, g_rec, g_dec, g_bias_dec, loss = pl.pallas_call(
        output_kernel,
        out_shape=(
            jax.ShapeDtypeStruct((micro * steps, count, width), BF),
            jax.ShapeDtypeStruct((vocab, emb), F32),
            jax.ShapeDtypeStruct((emb, 256), F32),
            jax.ShapeDtypeStruct((256,), F32),
            jax.ShapeDtypeStruct((own_rows, gate_cols), F32),
            jax.ShapeDtypeStruct((own_rows, vocab), F32),
            jax.ShapeDtypeStruct((vocab,), F32),
            jax.ShapeDtypeStruct((1, 1), F32),
        ),
        in_specs=[hbm] * 6,
        out_specs=(hbm,) * 8,
        scratch_shapes=[
            pltpu.VMEM((micro * steps, count, width), BF),
            pltpu.VMEM((8, own_rows, 256), F32),
            pltpu.VMEM((3, 8, own_rows, 256), BF),
            pltpu.VMEM((own_rows, gate_cols), F32),
            pltpu.VMEM((104, 256), F32),
            pltpu.VMEM((own_rows, VPAD), F32),
            pltpu.VMEM((EPAD, VPAD), F32),
            pltpu.VMEM((vocab, emb), F32),
            pltpu.VMEM((emb, 256), F32),
            pltpu.VMEM((256,), F32),
            pltpu.VMEM((own_rows, vocab), F32),
            pltpu.VMEM((vocab,), F32),
            pltpu.VMEM((1, 1), F32),
            dma((13,)),
            dma((8,)),
        ],
    )(out_own, out_recv, out_in, out_dec, out_hid, out_small)
    return (
        loss[0, 0] / (micro * count * steps * everyone),
        hid.reshape(micro, steps, count, width).transpose(0, 2, 1, 3),
        table,
        g_in,
        g_bias,
        g_rec,
        g_dec,
        g_bias_dec,
    )


def dot_plain(left, right):
    return jnp.dot(left, right, preferred_element_type=jnp.float32)


def dot_right_t(left, right):
    return lax.dot_general(
        left, right, (((1,), (1,)), ((), ())), preferred_element_type=jnp.float32
    )


def dot_left_t(left, right):
    return lax.dot_general(
        left, right, (((0,), (0,)), ((), ())), preferred_element_type=jnp.float32
    )


def lstm_forward(weights, embed, bias_dec, ids, marks, goals):
    w_rec, w_dec, w_in, bias_in = weights
    count, steps = ids.shape
    width = w_rec.shape[0]
    letters = jnp.arange(embed.shape[0], dtype=jnp.int32)
    onehot = (ids.T.reshape(-1)[:, None] == letters[None, :]).astype(jnp.bfloat16)
    feature = dot_plain(onehot, embed).astype(jnp.bfloat16)
    drives = (dot_plain(feature, w_in) + bias_in.astype(jnp.float32)).reshape(steps, count, -1)
    keeps = (1 - marks.T).astype(jnp.float32)[:, :, None]

    def advance(state, slot):
        hidden_now, cell = state
        drive, keep_now = slot
        prev_hidden = hidden_now * keep_now.astype(jnp.bfloat16)
        prev_cell = cell * keep_now
        pre = drive + dot_plain(prev_hidden, w_rec)
        gin, gforget, gcand, gout = jnp.split(pre, 4, axis=1)
        cell_new = jax.nn.sigmoid(gforget) * prev_cell + jax.nn.sigmoid(gin) * jnp.tanh(gcand)
        hid_new = (jax.nn.sigmoid(gout) * jnp.tanh(cell_new)).astype(jnp.bfloat16)
        return ((hid_new, cell_new), (pre, prev_hidden, prev_cell, cell_new, hid_new))

    start = (jnp.zeros((count, width), jnp.bfloat16), jnp.zeros((count, width), jnp.float32))
    state, saved = lax.scan(advance, start, (drives, keeps))
    pres, prev_hiddens, prev_cells, cells, hiddens = saved
    flat_hidden = hiddens.reshape(steps * count, width)
    logits = dot_plain(flat_hidden, w_dec) + bias_dec.astype(jnp.float32)
    top = jnp.max(logits, axis=1, keepdims=True)
    shifted = jnp.exp(logits - top)
    summed = jnp.sum(shifted, axis=1, keepdims=True)
    goal_hot = (goals.T.reshape(-1)[:, None] == letters[None, :]).astype(jnp.float32)
    loss_part = jnp.sum(top[:, 0] + jnp.log(summed[:, 0])) - jnp.sum(goal_hot * logits)
    d_logits = (shifted / summed - goal_hot).astype(jnp.bfloat16)
    kept = (pres, prev_hiddens, prev_cells, cells, keeps, flat_hidden, d_logits, feature, onehot)
    return (kept, loss_part, jnp.transpose(hiddens, (1, 0, 2)))


def lstm_backward(weights, kept):
    w_rec, w_dec, w_in, bias_in = weights
    pres, prev_hiddens, prev_cells, cells, keeps, flat_hidden, d_logits, feature, onehot = kept
    steps, count, width = cells.shape
    from_dec = dot_right_t(d_logits, w_dec).reshape(steps, count, width)

    def retreat(carry, slot):
        grad_h, grad_c = carry
        pre, prev_cell, cell, extra, keep_now = slot
        gin, gforget, gcand, gout = jnp.split(pre, 4, axis=1)
        sig_in = jax.nn.sigmoid(gin)
        sig_forget = jax.nn.sigmoid(gforget)
        sig_out = jax.nn.sigmoid(gout)
        tan_cand = jnp.tanh(gcand)
        tan_cell = jnp.tanh(cell)
        grad_hid = extra + grad_h
        grad_out = grad_hid * tan_cell
        grad_cell = grad_c + grad_hid * sig_out * (1.0 - tan_cell * tan_cell)
        d_pre = jnp.concatenate(
            [
                grad_cell * tan_cand * sig_in * (1.0 - sig_in),
                grad_cell * prev_cell * sig_forget * (1.0 - sig_forget),
                grad_cell * sig_in * (1.0 - tan_cand * tan_cand),
                grad_out * sig_out * (1.0 - sig_out),
            ],
            axis=1,
        ).astype(jnp.bfloat16)
        back_h = dot_right_t(d_pre, w_rec) * keep_now
        back_c = grad_cell * sig_forget * keep_now
        return ((back_h, back_c), d_pre)

    start = (jnp.zeros((count, width), jnp.float32), jnp.zeros((count, width), jnp.float32))
    state, d_pres = lax.scan(
        retreat, start, (pres, prev_cells, cells, from_dec, keeps), reverse=True
    )
    flat_pre = d_pres.reshape(steps * count, -1)
    grad_dec = dot_left_t(flat_hidden, d_logits)
    grad_in = dot_left_t(feature, flat_pre)
    grad_bias = jnp.sum(flat_pre.astype(jnp.float32), axis=0)
    grad_feature = dot_right_t(flat_pre, w_in)
    grad_table = lax.dot_general(
        onehot.astype(jnp.float32),
        grad_feature,
        (((0,), (0,)), ((), ())),
        precision=lax.Precision.HIGHEST,
        preferred_element_type=jnp.float32,
    )
    grad_bias_out = jnp.sum(d_logits.astype(jnp.float32), axis=0)
    flat_prev = prev_hiddens.reshape(steps * count, width)
    return (grad_dec, grad_in, grad_bias, grad_table, grad_bias_out, flat_prev, flat_pre)


def general(chars, resets, targets, embed, w_in, bias_in, w_rec, w_dec, bias_dec):
    micro, count, steps = chars.shape
    everyone = lax.axis_size(("dp", "fsdp"))
    sums = None
    prev_list = []
    pre_list = []
    hidden_list = []
    for index in range(micro):
        forward_set = (
            lax.all_gather(w_rec, ("dp", "fsdp"), axis=0, tiled=True),
            lax.all_gather(w_dec, ("dp", "fsdp"), axis=0, tiled=True),
            lax.all_gather(w_in, ("dp", "fsdp"), axis=1, tiled=True),
            lax.all_gather(bias_in, ("dp", "fsdp"), axis=0, tiled=True),
        )
        kept, loss_part, hiddens = lstm_forward(
            forward_set, embed, bias_dec, chars[index], resets[index], targets[index]
        )
        backward_set = (
            lax.all_gather(w_rec, ("dp", "fsdp"), axis=0, tiled=True),
            lax.all_gather(w_dec, ("dp", "fsdp"), axis=0, tiled=True),
            lax.all_gather(w_in, ("dp", "fsdp"), axis=1, tiled=True),
            lax.all_gather(bias_in, ("dp", "fsdp"), axis=0, tiled=True),
        )
        grad_dec, grad_in, grad_bias, grad_table, grad_bias_out, flat_prev, flat_pre = (
            lstm_backward(backward_set, kept)
        )
        pieces = (grad_dec, grad_in, grad_bias, grad_table, grad_bias_out, loss_part)
        if sums is None:
            sums = pieces
        else:
            sums = tuple((first + second for first, second in zip(sums, pieces)))
        prev_list.append(flat_prev)
        pre_list.append(flat_pre)
        hidden_list.append(hiddens)
    prev_all = jnp.concatenate(prev_list, axis=0)
    pre_all = jnp.concatenate(pre_list, axis=0)
    grad_w_rec = lax.psum_scatter(
        dot_left_t(prev_all, pre_all), ("dp", "fsdp"), scatter_dimension=0, tiled=True
    )
    grad_w_dec, grad_w_in, grad_bias_in = (
        lax.psum_scatter(sums[0], ("dp", "fsdp"), scatter_dimension=0, tiled=True),
        lax.psum_scatter(sums[1], ("dp", "fsdp"), scatter_dimension=1, tiled=True),
        lax.psum_scatter(sums[2], ("dp", "fsdp"), scatter_dimension=0, tiled=True),
    )
    grad_embed, grad_bias_dec, total = lax.psum((sums[3], sums[4], sums[5]), ("dp", "fsdp"))
    loss = total / (micro * count * steps * everyone)
    hidden = jnp.stack(hidden_list, axis=0)
    return (
        loss,
        hidden,
        grad_embed,
        grad_w_in,
        grad_bias_in,
        grad_w_rec,
        grad_w_dec,
        grad_bias_dec,
    )


def solution(mesh):
    per_device = fused if (mesh.shape["dp"], mesh.shape["fsdp"]) == (8, 4) else general
    return jax.shard_map(
        per_device,
        mesh=mesh,
        in_specs=(
            P(None, ("dp", "fsdp"), None),
            P(None, ("dp", "fsdp"), None),
            P(None, ("dp", "fsdp"), None),
            P(),
            P(None, ("dp", "fsdp")),
            P(("dp", "fsdp")),
            P(("dp", "fsdp"), None),
            P(("dp", "fsdp"), None),
            P(),
        ),
        out_specs=(
            P(),
            P(None, ("dp", "fsdp"), None, None),
            P(),
            P(None, ("dp", "fsdp")),
            P(("dp", "fsdp")),
            P(("dp", "fsdp"), None),
            P(("dp", "fsdp"), None),
            P(),
        ),
        check_vma=False,
    )
```

```python
import functools

import jax
import jax.numpy as jnp
from jax import lax
from jax.experimental import pallas as pl
from jax.experimental.pallas import tpu as pltpu
from jax.sharding import PartitionSpec as P

MESH = pl.DeviceIdType.MESH
NN = ((1,), (0,))
NT = ((1,), (1,))
TN = ((0,), (0,))
F32 = jnp.float32
BF = jnp.bfloat16

VPAD = 384
EPAD = 128
RING = 4
SMALL = 112


def mm(left, right, dims):
    return lax.dot_general(left, right, (dims, ((), ())), preferred_element_type=F32)


def sigmoid(v):
    return 0.5 * jnp.tanh(0.5 * v) + 0.5


def lstm_kernel(
    steps, rows,
    w_rec, w_in_hbm, b_in_hbm, w_dec_hbm, emb_hbm, bias_hbm, chars_hbm, resets_hbm, targets_hbm,
    out_own, out_recv, out_in, out_dec, out_hid, out_small,
    W, WIN, WDEC, IDS, H, HT, HTS, HSEND, A, C, D, DS, DRAW, DL,
    w_in_raw, b_in_raw, w_dec_raw, emb_raw, bias_raw, chars_in, resets_in, targets_in, load_sem, ids_in, w_in, emb_t, w_dec, bias_dec, PR, STG, CB, PEND, OWN, DCN, SY, RY, SM, RM, EMBT, LV, BD, GWD, GIS, GY, SGM, GM, DWI, SIY, IY, SIM, IM, RS1, RS2, RS3, RS4, RS5, PIECE, PAIR, TOTAL,
    s_ids, r_ids, s_win, r_win, s_wa, r_wa, s_wm, r_wm, s_wy, r_wy, s_ws, r_ws,
    s_da, r_da, s_dm, r_dm, s_dy, r_dy, s_ds, r_ds, s_h, r_h, s_ht, r_ht, s_d, r_d,
    s_ph, r_ph, s_cb, r_cb, s_gd, r_gd, s_gi, r_gi, s_sm, r_sm, s_ry, r_ry, s_rm, r_rm, s_ra, r_ra,
    l_sem, hid_sem,
):
    last = steps - 1
    dp, fs = lax.axis_index("dp"), lax.axis_index("fsdp")
    z, x, y, c = dp // 2, dp % 2, fs // 2, fs % 2
    zh = z // 2
    a = z + zh * (3 - 2 * z)

    def dev(zz, xx, yy, cc):
        return (zz * 2 + xx, yy * 2 + cc)

    def kx(k):
        return x + (k % 2) * (1 - 2 * x)

    def kz(k):
        return z + (k // 2) * (1 - 2 * (z % 2))

    def ka(k):
        return a + (k // 2) * (1 - 2 * a)

    def kdev(k):
        return dev(kz(k), kx(k), y, c)

    def member(k):
        return 2 * kx(k) + ka(k)

    def unit_block(k, j):
        return 2 * (ka(k) + j * (3 - 2 * ka(k))) + kx(k)

    def lanes(ub):
        return pl.ds(pl.multiple_of(256 * ub, 256), 256)

    def place(k, far, yy, cc):
        return 4 * (2 * k + zh + far * (1 - 2 * zh)) + 2 * yy + cc

    def span(k, j):
        return slice(256 * (2 * k + j), 256 * (2 * k + j + 1))

    mir, ydev, sib = dev(3 - z, x, y, c), dev(z, x, 1 - y, c), dev(z, x, y, 1 - c)
    side = x + y - 2 * x * y
    perm = dev(side + zh * (3 - 2 * side), c, x, z % 2)
    back = dev(2 * zh + c, y, a + y - 2 * a * y, x)
    stays = jnp.logical_and(perm[0] == dp, perm[1] == fs)
    moved = jnp.logical_not(stays)

    def rc(src, dst, ss, rs, to):
        return pltpu.make_async_remote_copy(
            src_ref=src, dst_ref=dst, send_sem=ss, recv_sem=rs, device_id=to, device_id_type=MESH
        )

    barrier = pltpu.get_barrier_semaphore()

    def greet(to):
        pl.semaphore_signal(barrier, inc=1, device_id=to, device_id_type=MESH)

    for k in (1, 2, 3):
        greet(kdev(k))
    for to in (mir, ydev, sib):
        greet(to)

    @pl.when(moved)
    def _():
        greet(perm)
        greet(back)

    pairs = (
        (w_in_hbm, w_in_raw), (b_in_hbm, b_in_raw), (w_dec_hbm, w_dec_raw), (emb_hbm, emb_raw), (bias_hbm, bias_raw),
        (chars_hbm, chars_in), (resets_hbm, resets_in), (targets_hbm, targets_in),
    )
    loads = [pltpu.make_async_copy(src, dst, load_sem.at[n]) for n, (src, dst) in enumerate(pairs)]
    for load in loads:
        load.start()
    for load in loads:
        load.wait()
    emb, vocab = emb_raw.shape[1], emb_raw.shape[0]
    w_in[...] = jnp.zeros_like(w_in)
    w_in[0:emb, :] = w_in_raw[...]
    tail = emb // 16 * 16
    part = w_in[tail : tail + 16, :].astype(F32)
    bias_row = b_in_raw[...].astype(F32).reshape(1, 256)
    part = jnp.where(lax.broadcasted_iota(jnp.int32, (16, 256), 0) == emb - tail, bias_row, part)
    w_in[tail : tail + 16, :] = part.astype(BF)
    for s in range(2):
        stack = jnp.concatenate(
            [v for ref in (chars_in, resets_in, targets_in) for v in (ref[:, s, :], jnp.zeros((8 - steps, 32), jnp.int32))],
            axis=0,
        ).astype(F32)
        wide_stack = jnp.concatenate([stack, jnp.zeros((24, 96), F32)], axis=1)
        ids_in[s] = wide_stack.T[:32, :].astype(jnp.int32)
    pl.semaphore_wait(barrier, 6 + 2 * moved.astype(jnp.int32))


    def d_slot(b):
        return WDEC.at[pl.ds(pl.multiple_of(64 * b, 64), 64), :]

    def w_cols(ub, g):
        return w_rec.at[:, lanes(8 * g + ub)]

    def w_part(j, g, b):
        return W.at[4 * j + g, pl.ds(pl.multiple_of(64 * b, 64), 64), :]

    def wa_start(k):
        for j in (0, 1):
            for g in range(4):
                rc(w_cols(unit_block(k, j), g), w_part(j, g, place(k, 0, y, c)), s_wa.at[k - 1, j], r_wa.at[k - 1, j], kdev(k)).start()

    def wa(k, j):
        b = place(k, 0, y, c)
        part = W.at[pl.ds(4 * j, 4), pl.ds(pl.multiple_of(64 * b, 64), 64), :]
        return rc(part, part, s_wa.at[k - 1, j], r_wa.at[k - 1, j], kdev(k))

    def ids_copy(k, mem):
        return rc(ids_in, IDS.at[:, mem], s_ids.at[k - 1], r_ids.at[k - 1], kdev(k))

    def own_w(j, g):
        return pltpu.make_async_copy(w_cols(unit_block(0, j), g), w_part(j, g, place(0, 0, y, c)), l_sem.at[4 * j + g])

    for j in (0, 1):
        for g in range(4):
            own_w(j, g).start()
    for k in (1, 2, 3):
        ids_copy(k, member(0)).start()

    def win_perm(jj, gy, gc):
        return rc(w_in, WIN.at[jj, gy, gc], s_win.at[0], r_win.at[0], perm)

    def win_local():
        return pltpu.make_async_copy(w_in, WIN.at[x, z // 2, z % 2], l_sem.at[8])

    @pl.when(moved)
    def _():
        win_perm(x, z // 2, z % 2).start()

    @pl.when(stays)
    def _():
        win_local().start()

    for k in (1, 2, 3):
        wa_start(k)

    def w_half(j, b):
        return W.at[pl.ds(4 * j, 4), pl.ds(pl.multiple_of(64 * b, 64), 64), :]

    def to_mir(k, j):
        b = place(k, 0, y, c)
        return rc(w_half(j, b), w_half(j, b), s_wm.at[k, j], r_wm.at[k, j], mir)

    def from_mir(k, j):
        b = place(k, 1, y, c)
        return rc(w_half(j, b), w_half(j, b), s_wm.at[k, j], r_wm.at[k, j], mir)

    def group_block(i, yy, cc):
        return place(i % 4, i // 4, yy, cc)

    def to_y(i, j):
        b = group_block(i, y, c)
        return rc(w_half(j, b), w_half(j, b), s_wy.at[i, j], r_wy.at[i, j], ydev)

    def from_y(i, j):
        b = group_block(i, 1 - y, c)
        return rc(w_half(j, b), w_half(j, b), s_wy.at[i, j], r_wy.at[i, j], ydev)

    def to_s(i, j):
        b = group_block(i % 8, y + (i // 8) * (1 - 2 * y), c)
        return rc(w_half(j, b), w_half(j, b), s_ws.at[i, j], r_ws.at[i, j], sib)

    def from_s(i, j):
        b = group_block(i % 8, y + (i // 8) * (1 - 2 * y), 1 - c)
        return rc(w_half(j, b), w_half(j, b), s_ws.at[i, j], r_ws.at[i, j], sib)

    for j in (0, 1):
        for g in range(4):
            own_w(j, g).wait()
    inner = a == 1

    @pl.when(inner)
    def _():
        for j in (0, 1):
            to_mir(0, j).start()

    for j in (0, 1):
        to_y(0, j).start()
        to_s(0, j).start()

    def win_mir(jj):
        return rc(WIN.at[y, jj, c], WIN.at[y, jj, c], s_win.at[1], r_win.at[1], mir)

    def win_y(yy):
        return rc(WIN.at[yy, :, c], WIN.at[yy, :, c], s_win.at[2], r_win.at[2], ydev)

    def win_s(cc):
        return rc(WIN.at[:, :, cc], WIN.at[:, :, cc], s_win.at[3], r_win.at[3], sib)

    @pl.when(moved)
    def _():
        win_perm(y, zh, c).wait_recv()

    @pl.when(stays)
    def _():
        win_local().wait()

    win_mir(zh).start()


    IDS[:, member(0)] = ids_in[...]

    def own_blocks(k):
        for j in (0, 1):
            wa(k, j).wait_recv()
            to_y(k, j).start()

            @pl.when(inner)
            def _(j=j):
                to_mir(k, j).start()

            to_s(k, j).start()

    own_blocks(1)
    own_blocks(2)
    own_blocks(3)

    def da(k):
        return rc(w_dec, d_slot(place(k, 0, y, c)), s_da.at[k - 1], r_da.at[k - 1], kdev(k))

    HSEND[0, 0 : VPAD // 128] = jnp.zeros((VPAD // 128, 128, rows), BF)
    for n in range(VPAD // 128):
        held = min(128, vocab - 128 * n)
        HSEND[0, n, 0:held, 0:emb] = emb_raw[128 * n : 128 * n + held, :]
    unit = jnp.where(
        lax.broadcasted_iota(jnp.int32, (EPAD, EPAD), 0) == lax.broadcasted_iota(jnp.int32, (EPAD, EPAD), 1), 1.0, 0.0
    ).astype(BF)
    turned = mm(unit, HSEND[0, 0 : VPAD // 128].reshape(VPAD, EPAD), NT)
    emb_t[...] = jnp.where(lax.broadcasted_iota(jnp.int32, (EPAD, VPAD), 0) == emb, 1.0, turned).astype(BF)
    w_dec[...] = jnp.zeros_like(w_dec)
    w_dec[:, :vocab] = w_dec_raw[...]
    bias_dec[...] = jnp.full_like(bias_dec, -1e30)
    bias_dec[0:1, :vocab] = bias_raw[...].astype(F32).reshape(1, vocab)
    for k in (1, 2, 3):
        da(k).start()
    own_dec = pltpu.make_async_copy(w_dec, d_slot(place(0, 0, y, c)), l_sem.at[9])
    own_dec.start()

    for k in (1, 2, 3):
        ids_copy(k, member(k)).wait_recv()
    lane = lax.broadcasted_iota(jnp.int32, (rows, 24), 1)
    wide = lax.broadcasted_iota(jnp.int32, (rows, VPAD), 1).astype(F32)

    def column(at, s):
        packed = IDS[s].reshape(rows, 24)
        return jnp.sum(jnp.where(lane == at, packed, 0).astype(F32), axis=1, keepdims=True)

    def keep_of(t, s):
        return 1.0 - column(8 + t, s)

    def letter(t, s):
        return jnp.where(column(t, s) == wide, 1.0, 0.0).astype(BF)

    EMBT[...] = jnp.zeros_like(EMBT)
    LV[...] = jnp.zeros_like(LV)
    BD[...] = jnp.zeros_like(BD)
    GWD[...] = jnp.zeros_like(GWD)
    DWI[...] = jnp.zeros_like(DWI)
    DCN[...] = jnp.zeros_like(DCN)
    OWN[...] = jnp.zeros_like(OWN)
    PR[0] = jnp.zeros(PR.shape[1:], BF)

    win_mir(1 - zh).wait_recv()

    win_y(y).start()
    def pass_y(i):
        for j in (0, 1):
            from_y(i, j).wait_recv()
            to_s(8 + i, j).start()

    def pass_mir(k):
        for j in (0, 1):
            from_mir(k, j).wait_recv()
            to_y(4 + k, j).start()
            to_s(4 + k, j).start()

    for i in range(3):
        pass_y(i)

    @pl.when(inner)
    def _():
        pass_mir(0)

    @pl.when(jnp.logical_not(inner))
    def _():
        for k in range(4):
            for j in (0, 1):
                to_mir(k, j).start()

    pass_y(3)
    win_y(1 - y).wait_recv()
    win_s(c).start()
    win_s(1 - c).wait_recv()

    def h_copy(t, s, k, j):
        src, dst = H.at[t % RING, s, :, span(0, j)], H.at[t % RING, s, :, span(k, j)]
        return rc(src, dst, s_h.at[t, s, k - 1, j], r_h.at[t, s, k - 1, j], kdev(k))

    def wait_h(t, s):
        for k in (1, 2, 3):
            for j in (0, 1):
                h_copy(t, s, k, j).wait_recv()

    def gates(t, s, first):
        keep = None if first else keep_of(t, s)
        feature = mm(letter(t, s), emb_t[...], NT).astype(BF)
        for j in (0, 1):
            pre = []
            for g in range(4):
                drive = mm(feature, WIN[j, g // 2, g % 2], NN)
                if not first:
                    drive = drive + keep * mm(H[(t - 1) % RING, s], W[4 * j + g], NN)
                pre.append(drive)
            s_i, s_f, t_g, s_o = sigmoid(pre[0]), sigmoid(pre[1]), jnp.tanh(pre[2]), sigmoid(pre[3])
            cell = s_i * t_g
            if not first:
                cell = s_f * (C[t - 1, s, j] * keep) + cell
            for g, v in enumerate((s_i, s_f, t_g, s_o)):
                A[t, s, 4 * j + g] = v
            C[t, s, j] = cell
            H[t % RING, s, :, span(0, j)] = (s_o * jnp.tanh(cell)).astype(BF)
            for k in (3, 1, 2):
                h_copy(t, s, k, j).start()

    @pl.loop(0, 2)
    def _(s):
        gates(0, s, True)

    @pl.when(jnp.logical_not(inner))
    def _():
        pass_mir(0)

    for k in (1, 2, 3):
        pass_mir(k)

    def dec_mir(k, far):
        b = place(k, far, y, c)
        return rc(d_slot(b), d_slot(b), s_dm.at[k], r_dm.at[k], mir)

    def dec_y(i, yy):
        b = group_block(i, yy, c)
        return rc(d_slot(b), d_slot(b), s_dy.at[i], r_dy.at[i], ydev)

    def dec_s(i, cc):
        b = group_block(i % 8, y + (i // 8) * (1 - 2 * y), cc)
        return rc(d_slot(b), d_slot(b), s_ds.at[i], r_ds.at[i], sib)

    own_dec.wait()
    dec_mir(0, 0).start()
    dec_y(0, y).start()
    dec_s(0, c).start()
    for k in (1, 2, 3):
        da(k).wait_recv()
        dec_mir(k, 0).start()
        dec_y(k, y).start()
        dec_s(k, c).start()

    for i in (4, 5, 6, 7):
        pass_y(i)

    @pl.loop(0, 16)
    def _(i):
        for j in (0, 1):
            from_s(i, j).wait_recv()

    def released(t, s):
        hid_copy(t, s).wait()
        for k in (1, 2, 3):
            for j in (0, 1):
                h_copy(t, s, k, j).wait_send()

    def forward(t, s):
        wait_h(t - 1, s)

        @pl.when(t >= RING - 1)
        def _():
            released(t - (RING - 1), s)

        gates(t, s, False)

    row = lax.broadcasted_iota(jnp.int32, (128, 256), 0)
    col = lax.broadcasted_iota(jnp.int32, (128, 256), 1)

    def select(cc):
        yy = y + (row // 64) * (1 - 2 * y)
        return jnp.where(col == 64 * (2 * yy + cc) + row % 64, 1.0, 0.0).astype(BF)

    def lane_slot(t, s):
        return pl.ds(pl.multiple_of((2 * t + s) * rows, rows), rows)

    def ht_copy(t, s, slot):
        return rc(HSEND.at[slot], HTS.at[:, :, lane_slot(t, s)], s_ht.at[t, s], r_ht.at[t, s], sib)

    def hid_copy(t, s):
        mine = H.at[t % RING, s, pl.ds(pl.multiple_of(32 * member(0), 32), 32), :]
        return pltpu.make_async_copy(mine, out_hid.at[s * steps + t], hid_sem.at[t, s])

    def logits_of(t, s):
        scores = mm(H[t % RING, s], WDEC[...], NN) + bias_dec[0:1, :]
        top = jnp.max(scores, axis=1, keepdims=True)
        shifted = jnp.exp(scores - top)
        summed = jnp.sum(shifted, axis=1, keepdims=True)
        goal = jnp.where(column(16 + t, s) == wide, 1.0, 0.0)
        picked = jnp.sum(goal * scores, axis=1, keepdims=True)
        LV[...] += jnp.broadcast_to(top + jnp.log(summed) - picked, (rows, 128))
        DL[t, s] = (shifted / summed - goal).astype(BF)

    def decoder_side(t, s):
        hid_copy(t, s).start()
        grad = DL[t, s]
        BD[...] += mm(jnp.ones((8, rows), BF), grad, NN)
        for j in (0, 1):
            GWD[j] += mm(H[t % RING, s, :, span(0, j)], grad, TN).reshape(2, 2, 64, VPAD)

    def transposed_side(t, s):
        slot = s
        mine, other = select(c), select(1 - c)

        @pl.when(t >= 1)
        def _():
            ht_copy(t - 1, s, slot).wait_send()

        for tile in range(8):
            part = H[t % RING, s, :, 256 * tile : 256 * (tile + 1)]
            HT[tile, :, lane_slot(t, s)] = mm(mine, part, NT).astype(BF)
            HSEND[slot, tile] = mm(other, part, NT).astype(BF)
        ht_copy(t, s, slot).start()

    def decoder_mirror():
        @pl.loop(0, 4)
        def _(k):
            dec_mir(k, 1).wait_recv()
            dec_y(4 + k, y).start()
            dec_s(4 + k, c).start()

    def decoder_rest():
        @pl.loop(0, 8)
        def _(i):
            k, j = i // 2, i % 2
            to_mir(k, j).wait_send()
            to_y(i, 0).wait_send()
            to_y(i, 1).wait_send()

        @pl.loop(0, 16)
        def _(i):
            to_s(i, 0).wait_send()
            to_s(i, 1).wait_send()

        @pl.loop(0, 8)
        def _(i):
            dec_y(i, 1 - y).wait_recv()
            dec_s(8 + i, c).start()

        @pl.loop(0, 16)
        def _(i):
            dec_s(i, 1 - c).wait_recv()

    def aside(t, s):
        logits_of(t, s)
        decoder_side(t, s)
        transposed_side(t, s)

    @pl.loop(2, 2 * steps)
    def _(i):
        t, s = i // 2, i % 2
        forward(t, s)

        @pl.when(i == 3)
        def _():
            decoder_mirror()

        @pl.when(i == 5)
        def _():
            decoder_rest()

        @pl.when(i >= 5)
        def _():
            @pl.loop(i - 4 - (13 - i) // 8, i - 3)
            def _(n):
                aside(n // 2, n % 2)


    def d_copy(t, s):
        return rc(D.at[:, t - 1, s], DS.at[:, t - 1, s], s_d.at[t, s], r_d.at[t, s], sib)

    def turn():
        def rows_of(q):
            return slice(256 * q, 256 * (q + 1))

        def swap(p, q):
            upper, lower = W[p, rows_of(q), :].T, W[q, rows_of(p), :].T
            W[p, rows_of(q), :] = lower
            W[q, rows_of(p), :] = upper

        for p in range(8):
            W[p, rows_of(p), :] = W[p, rows_of(p), :].T
            for q in range(p):
                swap(p, q)

    def cell_back(t, s, oldest):
        keep = keep_of(t, s)
        for j in (0, 1):
            up = WDEC[span(0, j), :]
            dh = mm(DL[t, s], up, NT)
            rest = PR[(t + 1) % 2, s, 0, j].astype(F32) + PR[(t + 1) % 2, s, 1, j].astype(F32)
            dh = dh + (OWN[s, j] + rest)
            s_i, s_f, t_g, s_o = (A[t, s, 4 * j + g] for g in range(4))
            t_c = jnp.tanh(C[t, s, j])
            d_o = dh * t_c
            d_c = dh * s_o * (1.0 - t_c * t_c) + DCN[s, j]
            d_i = d_c * t_g * s_i * (1.0 - s_i)
            d_g = d_c * s_i * (1.0 - t_g * t_g)
            d_o = d_o * s_o * (1.0 - s_o)
            if oldest:
                d_f = jnp.zeros_like(d_i)
            else:
                d_f = d_c * (C[t - 1, s, j] * keep) * s_f * (1.0 - s_f)
                DCN[s, j] = keep * (d_c * s_f)
            for g, v in enumerate((d_i, d_f, d_g, d_o)):
                low = v.astype(BF)
                DRAW[4 * j + g] = low
                if not oldest:
                    D[4 * j + g, t - 1, s] = low * keep.astype(BF)

    def part_rows(h):
        return slice(64 * h, 64 * (h + 1))

    def pr_half(t, s, k, h):
        src, dst = STG.at[s, k - 1, :, part_rows(h)], PR.at[t % 2, s, k - 1, :, part_rows(h)]
        return rc(src, dst, s_ph.at[t, s, k - 1, h], r_ph.at[t, s, k - 1, h], kdev(k))

    def owed_copy(t, s, n):
        return rc(STG.at[s, 2, :, part_rows(n)], CB.at[s, n], s_cb.at[t, s, n], r_cb.at[t, s, n], kdev(1 + n))

    def pr_each(act):
        for k in (1, 2):
            for h in (0, 1):
                act(k, h)

    def pr_arrived(t, s):
        pr_each(lambda k, h: pr_half(t, s, k, h).wait_recv())

    def pr_left(t, s):
        pr_each(lambda k, h: pr_half(t, s, k, h).wait_send())
        for n in (0, 1):
            owed_copy(t, s, n).wait_send()

    def product_back(t, s):
        left = jnp.concatenate([D[q, t - 1, s] for q in range(8)], axis=1)
        for k, j in ((3, 0), (3, 1), (1, 0), (1, 1), (2, 0), (2, 1), (0, 0), (0, 1)):
            total = mm(left, W[2 * k + j], NN)
            if k == 0:
                OWN[s, j] = total
                continue
            STG[s, k - 1, j] = total.astype(BF)
            if k < 3:
                PEND[k - 1, j] = total[part_rows(2 - k)]
            elif j == 1:
                owed_copy(t, s, 0).start()
                owed_copy(t, s, 1).start()
        for k in (1, 2):
            pr_half(t, s, k, k - 1).start()

    def add_owed(t, s):
        for k in (2, 1):
            h = 2 - k
            owed_copy(t, s, h).wait_recv()
            STG[s, k - 1, :, part_rows(h)] = (PEND[k - 1] + CB[s, h].astype(F32)).astype(BF)
            pr_half(t, s, k, h).start()

    def input_side(t, s):
        onehot = letter(t, s)
        feat_t = mm(emb_t[...], onehot, NT).astype(BF)
        inputs = []
        for q in range(8):
            jj, gy, gc = q // 4, (q // 2) % 2, q % 2
            DWI[jj, gy, gc] += mm(feat_t, DRAW[q], NN)
            inputs.append(WIN[jj, gy, gc])
        grad_t = mm(jnp.concatenate(inputs, axis=1), jnp.concatenate([DRAW[q] for q in range(8)], axis=1), NT)
        high = grad_t.astype(BF)
        low = (grad_t - high.astype(F32)).astype(BF)
        EMBT[...] += mm(high, onehot, NN) + mm(low, onehot, NN)

    def gd_s():
        return rc(GWD.at[:, :, 1 - c], GIS.at[:, :, 0:64], s_gd.at[0], r_gd.at[0], sib)

    def gd_y():
        return rc(GWD.at[:, 1 - y, c], GY, s_gd.at[1], r_gd.at[1], ydev)

    def gd_m():
        return rc(SGM, GM, s_gd.at[2], r_gd.at[2], mir)

    turn()

    @pl.loop(0, 2 * (steps - 1))
    def _(i):
        t, s = last - i // 2, i % 2

        @pl.when(i < 2)
        def _():
            wait_h(t, s)
            logits_of(last, s)

        @pl.when(i >= 2)
        def _():
            pr_arrived(t + 1, s)

        cell_back(t, s, False)

        @pl.when(i >= 1)
        def _():
            add_owed(t + 1 - s, 1 - s)

        @pl.when(i >= 2)
        def _():
            pr_left(t + 1, s)

        product_back(t, s)
        d_copy(t, s).start()

        @pl.when(i < 2 * (steps - 1) - 1)
        def _():
            input_side(t, s)

        @pl.when(i < 2)
        def _():
            logits_of(last - 1, s)

        @pl.when(jnp.logical_and(i >= 2, i < 4))
        def _():
            decoder_side(last - 1, s)
            transposed_side(last - 1, s)

        @pl.when(i == 4)
        def _():
            @pl.loop(0, 2)
            def _(n):
                decoder_side(last, n)

            gd_s().start()

        @pl.when(i == 5)
        def _():
            gd_s().wait_recv()
            GWD[:, :, c] += GIS[:, :, 0:64]
            gd_y().start()

        @pl.when(i == 7)
        def _():
            gd_y().wait_recv()
            GWD[:, y, c] += GY[...]
            SGM[...] = GWD[1 - zh, y, c].astype(BF)
            gd_m().start()

        @pl.when(i == 9)
        def _():
            gd_m().wait_recv()
            out_dec[...] = GWD[zh, y, c] + GM[...].astype(F32)

    @pl.loop(0, 2 * (steps - 1))
    def _(i):
        ht_copy(i // 2, i % 2, 0).wait_recv()
        d_copy(1 + i // 2, i % 2).wait_recv()

    depth = 2 * (steps - 1) * rows

    def kept(q):
        return A.at[2 + q // 4, (q % 4) // 2, :, pl.ds(pl.multiple_of(64 * (q % 2), 64), 64), :]

    def tile_of(q):
        k, near = q % 4, q // 4
        return 2 * k + 1 - zh + near * (2 * zh - 1)

    def ry_copy(p, q):
        return rc(SY.at[p % 4], RY.at[q], s_ry.at[p], r_ry.at[q], ydev)

    def pieces(k):
        return (1, 2, 2, 4)[k]

    def piece(k, n):
        size = 8 // pieces(k)
        return slice(size * n, size * (n + 1))

    def rm_copy(k, n):
        at = (0, 1, 3, 5)[k] + n
        return rc(SM.at[k, piece(k, n)], RM.at[k, piece(k, n)], s_rm.at[at], r_rm.at[at], mir)

    def ry_first(n):
        return rc(SY.at[0, piece(3, n)], RY.at[3, piece(3, n)], s_ry.at[8 + n], r_ry.at[8 + n], ydev)

    def ry_second(n):
        return rc(SY.at[1, piece(2, n)], RY.at[2, piece(2, n)], s_ry.at[12 + n], r_ry.at[12 + n], ydev)

    def ry_sent(p):
        @pl.when(p == 0)
        def _():
            for n in range(4):
                ry_first(n).wait_send()

        @pl.when(p == 1)
        def _():
            for n in range(2):
                ry_second(n).wait_send()

        @pl.when(p > 1)
        def _():
            ry_copy(p, order(p)).wait_send()

    def ra_copy(k, n):
        at = (0, 0, 2, 3)[k] + n
        rows_of_q = piece(k, n) if k == 1 else slice(0, 8)
        return rc(SM.at[k, rows_of_q], out_recv.at[k - 1, rows_of_q], s_ra.at[at], r_ra.at[at], kdev(k))

    def ra_pieces(k):
        return 2 if k == 1 else 1

    def order(p):
        return 3 - p + 8 * (p // 4)

    def make_tile(p):
        q = order(p)
        tile = tile_of(q)
        left, right = HT[tile], HTS[tile]
        hold = kept(q)

        @pl.when(p >= 4)
        def _():
            ry_sent(p - 4)

        for n in range(8):
            grad = mm(left, D[n].reshape(depth, 256), NN) + mm(right, DS[n].reshape(depth, 256), NN)
            hold[n] = grad[:64]
            SY[p % 4, n] = grad[64:].astype(BF)
            if n % 2 == 1:
                @pl.when(p == 0)
                def _(n=n):
                    ry_first(n // 2).start()

            if n % 4 == 3:
                @pl.when(p == 1)
                def _(n=n):
                    ry_second(n // 4).start()

        @pl.when(p > 1)
        def _():
            ry_copy(p, q).start()

    def add_y(q):
        ry_copy(0, q).wait_recv()
        hold = kept(q)
        hold[...] = hold[...] + RY[q].astype(F32)

    def pass_first(n):
        ry_first(n).wait_recv()
        SM[3, piece(3, n)] = (kept(3)[piece(3, n)] + RY[3, piece(3, n)].astype(F32)).astype(BF)
        rm_copy(3, n).start()

    def pass_on(k):
        if k == 3:
            for n in range(4):
                pass_first(n)
            return
        if k == 2:
            for n in range(2):
                ry_second(n).wait_recv()
                SM[2, piece(2, n)] = (kept(2)[piece(2, n)] + RY[2, piece(2, n)].astype(F32)).astype(BF)
                rm_copy(2, n).start()
            return
        add_y(k)
        for n in range(pieces(k)):
            SM[k, piece(k, n)] = kept(k)[piece(k, n)].astype(BF)
            rm_copy(k, n).start()

    def finish(k):
        add_y(4 + k)
        if k != 1:
            for n in range(pieces(k)):
                rm_copy(k, n).wait_recv()
        if k == 0:
            out_own[...] = kept(4)[...] + RM[0].astype(F32)
            return
        for n in range(ra_pieces(k)):
            part = piece(1, n) if k == 1 else slice(0, 8)
            if k == 1:
                rm_copy(k, n).wait_recv()
                rm_copy(k, n).wait_send()
            else:
                for m in range(pieces(k)):
                    rm_copy(k, m).wait_send()
            SM[k, part] = (kept(4 + k)[part] + RM[k, part].astype(F32)).astype(BF)
            ra_copy(k, n).start()

    def settle(p):
        q = order(p)
        pass_on(q) if q < 4 else finish(q - 4)

    outer = jnp.logical_not(inner)

    def core_rows(cc):
        return pl.ds(pl.multiple_of(64 * cc, 64), 64)

    def piece_rows(xx):
        return pl.ds(pl.multiple_of(64 * c + 32 * xx, 32), 32)

    def sm_core():
        return rc(out_small.at[core_rows(1 - c)], RS1, s_sm.at[0], r_sm.at[0], sib)

    def sm_group(k):
        xx = kx(k)
        return rc(out_small.at[piece_rows(xx)], RS2.at[k - 1], s_sm.at[k], r_sm.at[k], kdev(k))

    def sm_quarter(n):
        return rc(PIECE if n == 0 else PAIR, RS3.at[n], s_sm.at[4 + n], r_sm.at[4 + n], (ydev, mir)[n])

    def sm_spread(k):
        return rc(TOTAL, RS4.at[k - 1], s_sm.at[6 + k], r_sm.at[6 + k], kdev(k))

    def sm_last():
        return rc(out_small.at[core_rows(c)], RS5, s_sm.at[10], r_sm.at[10], sib)

    def sm_step1():
        sm_core().wait_recv()
        out_small[core_rows(c)] = out_small[core_rows(c)] + RS1[...]

        @pl.when(outer)
        def _():
            sm_group(1).start()

        @pl.when(inner)
        def _():
            sm_group(2).start()
            sm_group(3).start()

    def sm_step2():
        @pl.when(outer)
        def _():
            for k in (1, 2, 3):
                sm_group(k).wait_recv()
            PIECE[...] = (out_small[piece_rows(x)] + RS2[0]) + (RS2[1] + RS2[2])
            sm_quarter(0).start()

    def sm_step_mir():
        @pl.when(outer)
        def _():
            sm_quarter(0).wait_recv()
            PAIR[...] = PIECE[...] + RS3[0]
            sm_quarter(1).start()

    def sm_step3():
        @pl.when(outer)
        def _():
            sm_quarter(1).wait_recv()
            TOTAL[...] = PAIR[...] + RS3[1]
            for k in (1, 2, 3):
                sm_spread(k).start()

    def sm_step4():
        sm_core().wait_send()

        @pl.when(outer)
        def _():
            sm_group(1).wait_send()
            sm_spread(1).wait_recv()
            out_small[piece_rows(1 - x)] = RS4[0]
            out_small[piece_rows(x)] = TOTAL[...]

        @pl.when(inner)
        def _():
            for k in (2, 3):
                sm_group(k).wait_send()
                sm_spread(k).wait_recv()
                out_small[piece_rows(kx(k))] = RS4[k - 1]

        sm_last().start()

    def sm_step5():
        sm_last().wait_recv()
        out_small[core_rows(1 - c)] = RS5[...]

    live = pl.ds(0, 104)

    def gi_s():
        return rc(DWI.at[:, :, 1 - c, live], GIS.at[:, :, :, 0:256], s_gi.at[0], r_gi.at[0], sib)

    def gi_y():
        return rc(SIY, IY, s_gi.at[1], r_gi.at[1], ydev)

    def gi_m():
        return rc(SIM, IM, s_gi.at[2], r_gi.at[2], mir)

    def gi_p():
        return rc(DWI.at[y, zh, c, live], out_in, s_gi.at[3], r_gi.at[3], back)

    def first_position():
        @pl.loop(0, 2)
        def _(s):
            pr_arrived(1, s)
            cell_back(0, s, True)
            input_side(0, s)

            @pl.when(jnp.logical_and(inner, s == 0))
            def _():
                pass_first(2)

        leader = jnp.logical_and(x == 0, a == 0)
        high_row = lax.broadcasted_iota(jnp.int32, (8, VPAD), 0)
        loss = jnp.sum(LV[...], axis=0, keepdims=True)
        loss = jnp.concatenate([loss] * (VPAD // 128), axis=1)
        extra = jnp.where(high_row == 0, BD[...], jnp.where(high_row == 1, loss, 0.0))
        out_small[...] = EMBT[...]
        out_small[SMALL - 8 : SMALL] = jnp.where(leader, extra, 0.0)
        sm_core().start()
        gi_s().start()

    @pl.loop(0, 8)
    def _(p):
        make_tile(p)

        @pl.when(p == 0)
        def _():
            add_owed(1, 1)

        @pl.when(p == 1)
        def _():
            @pl.when(inner)
            def _():
                pass_first(0)

            input_side(1, 1)

            @pl.when(inner)
            def _():
                pass_first(1)

            first_position()
            sm_step1()
            @pl.when(inner)
            def _():
                pass_first(3)
                settle(1)

            gi_s().wait_recv()
            DWI[:, :, c, 0:104] = DWI[:, :, c, 0:104] + GIS[:, :, :, 0:256]
            sm_step2()
            SIY[...] = DWI[1 - y, :, c, 0:112].astype(BF)
            gi_y().start()

            @pl.when(outer)
            def _():
                settle(0)

        @pl.when(p == 2)
        def _():
            @pl.when(outer)
            def _():
                settle(1)

            sm_step_mir()

        @pl.when(p == 3)
        def _():
            gi_y().wait_recv()
            DWI[y, :, c, 0:104] = DWI[y, :, c, 0:104] + IY[...].astype(F32)[:, 0:104]
            SIM[...] = DWI[y, 1 - zh, c, 0:112].astype(BF)
            gi_m().start()

        @pl.when(p == 4)
        def _():
            settle(2)
            sm_step3()

        @pl.when(p == 5)
        def _():
            settle(3)

    settle(4)
    settle(5)
    sm_step4()
    settle(6)
    gi_m().wait_recv()
    DWI[y, zh, c, 0:104] = DWI[y, zh, c, 0:104] + IM[...].astype(F32)[0:104]

    @pl.when(moved)
    def _():
        gi_p().start()

    @pl.when(stays)
    def _():
        out_in[...] = DWI[y, zh, c, 0:104]

    sm_step5()
    settle(7)

    for k in (1, 2, 3):
        for j in (0, 1):
            wa(k, j).wait_send()
        ids_copy(k, member(0)).wait_send()
        da(k).wait_send()
        for n in range(ra_pieces(k)):
            ra_copy(k, n).wait()
    rm_copy(0, 0).wait_send()

    @pl.when(moved)
    def _():
        gi_p().wait()
        win_perm(x, z // 2, z % 2).wait_send()

    for s in range(2):
        pr_left(1, s)
    win_mir(zh).wait_send()
    win_y(y).wait_send()
    win_s(c).wait_send()
    @pl.when(outer)
    def _():
        sm_quarter(0).wait_send()
        sm_quarter(1).wait_send()
        for k in (1, 2, 3):
            sm_spread(k).wait_send()

    for copy in (gd_s, gd_y, gd_m, gi_s, gi_y, gi_m, sm_last):
        copy().wait_send()
    for s in range(2):
        ht_copy(last - 1, s, s).wait_send()

    @pl.loop(0, 4)
    def _(k):
        dec_mir(k, 0).wait_send()

    @pl.loop(0, 8)
    def _(i):
        dec_y(i, y).wait_send()

    for p in range(4, 8):
        ry_copy(p, order(p)).wait_send()

    @pl.loop(0, 16)
    def _(i):
        dec_s(i, c).wait_send()

    @pl.loop(2 * (steps - RING + 1), 2 * steps)
    def _(i):
        released(i // 2, i % 2)

    @pl.loop(0, 2 * (steps - 1))
    def _(i):
        d_copy(1 + i // 2, i % 2).wait_send()


def output_kernel(
    characters, own, recv, g_in, g_dec, hid_in, small, hid, table, o_in, o_bias, o_rec, o_dec, o_bias_dec, loss,
    h_buf, own_buf, recv_buf, rec_buf, in_buf, dec_buf, small_buf, t_buf, i_buf, b_buf, d_buf, bd_buf, l_buf, in_sem, out_sem,
):
    dp = lax.axis_index("dp")
    z, x = dp // 2, dp % 2
    a = z + (z // 2) * (3 - 2 * z)

    def cols(k, j, g):
        xk, ak = x + (k % 2) * (1 - 2 * x), a + (k // 2) * (1 - 2 * a)
        ub = 2 * (ak + j * (3 - 2 * ak)) + xk
        return pl.ds(pl.multiple_of(256 * (8 * g + ub), 256), 256)

    def load(n, src, dst):
        copy = pltpu.make_async_copy(src, dst, in_sem.at[n])
        copy.start()
        return copy

    def store(n, src, dst):
        copy = pltpu.make_async_copy(src, dst, out_sem.at[n])
        copy.start()
        return copy

    hid_loads = [
        load(p, hid_in.at[:, :, 256 * p : 256 * (p + 1)], h_buf.at[:, :, cols(p // 2, p % 2, 0)]) for p in range(8)
    ]
    rec_loads = [load(8, own, own_buf), load(9, recv, recv_buf)]
    small_loads = [load(10, small, small_buf), load(11, g_in, in_buf), load(12, g_dec, dec_buf)]
    for copy in hid_loads:
        copy.wait()
    stores = [store(0, h_buf, hid)]
    for copy in rec_loads:
        copy.wait()
    for k in range(4):
        for j in (0, 1):
            for g in range(4):
                part = own_buf[4 * j + g] if k == 0 else recv_buf[k - 1, 4 * j + g].astype(F32)
                rec_buf[:, cols(k, j, g)] = part
    stores.append(store(1, rec_buf, o_rec))
    for copy in small_loads:
        copy.wait()
    vocab, emb = table.shape
    t_buf[...] = small_buf[0:SMALL, :].T[:vocab, :emb]
    i_buf[...] = in_buf[0:emb, :]
    b_buf[...] = in_buf[emb, :]
    d_buf[...] = dec_buf[:, :vocab]
    bd_buf[...] = small_buf[SMALL - 8, :vocab]
    l_buf[...] = small_buf[SMALL - 7 : SMALL - 6, 0:1] / characters
    pairs = ((t_buf, table), (i_buf, o_in), (b_buf, o_bias), (d_buf, o_dec), (bd_buf, o_bias_dec), (l_buf, loss))
    for n, (src, dst) in enumerate(pairs):
        stores.append(store(2 + n, src, dst))
    for copy in stores:
        copy.wait()


def fused(chars, resets, targets, embed, w_in, bias_in, w_rec, w_dec, bias_dec):
    micro, count, steps = chars.shape
    own_rows, gate_cols = w_rec.shape
    vocab, emb = embed.shape
    width = gate_cols // 4
    members = 4
    rows = count * members
    vm = pl.BlockSpec(memory_space=pltpu.VMEM)
    hbm = pl.BlockSpec(memory_space=pl.ANY)
    dma = pltpu.SemaphoreType.DMA
    n = steps - 1
    scratch = [
        pltpu.VMEM((8, width, 256), BF),
        pltpu.VMEM((2, 2, 2, EPAD, 256), BF),
        pltpu.VMEM((width, VPAD), BF),
        pltpu.VMEM((micro, members, count, 24), jnp.int32),
        pltpu.VMEM((RING, micro, rows, width), BF),
        pltpu.VMEM((8, 128, 2 * n * rows), BF),
        pltpu.VMEM((8, 128, 2 * n * rows), BF),
        pltpu.VMEM((2, 8, 128, rows), BF),
        pltpu.VMEM((steps, micro, 8, rows, 256), F32),
        pltpu.VMEM((steps, micro, 2, rows, 256), F32),
        pltpu.VMEM((8, n, micro, rows, 256), BF),
        pltpu.VMEM((8, n, micro, rows, 256), BF),
        pltpu.VMEM((8, rows, 256), BF),
        pltpu.VMEM((steps, micro, rows, VPAD), BF),
        pltpu.VMEM(w_in.shape, BF),
        pltpu.VMEM(bias_in.shape, BF),
        pltpu.VMEM(w_dec.shape, BF),
        pltpu.VMEM(embed.shape, BF),
        pltpu.VMEM(bias_dec.shape, BF),
        pltpu.VMEM((steps, micro, count), jnp.int32),
        pltpu.VMEM((steps, micro, count), jnp.int32),
        pltpu.VMEM((steps, micro, count), jnp.int32),
        dma((8,)),
        pltpu.VMEM((micro, count, 24), jnp.int32),
        pltpu.VMEM((EPAD, 256), BF),
        pltpu.VMEM((EPAD, VPAD), BF),
        pltpu.VMEM((own_rows, VPAD), BF),
        pltpu.VMEM((8, VPAD), F32),
        pltpu.VMEM((2, micro, 2, 2, rows, 256), BF),
        pltpu.VMEM((micro, 3, 2, rows, 256), BF),
        pltpu.VMEM((micro, 2, 2, rows // 2, 256), BF),
        pltpu.VMEM((2, 2, rows // 2, 256), F32),
        pltpu.VMEM((micro, 2, rows, 256), F32),
        pltpu.VMEM((micro, 2, rows, 256), F32),
        pltpu.VMEM((4, 8, 64, 256), BF),
        pltpu.VMEM((8, 8, 64, 256), BF),
        pltpu.VMEM((4, 8, 64, 256), BF),
        pltpu.VMEM((4, 8, 64, 256), BF),
        pltpu.VMEM((EPAD, VPAD), F32),
        pltpu.VMEM((rows, 128), F32),
        pltpu.VMEM((8, VPAD), F32),
        pltpu.VMEM((2, 2, 2, 64, VPAD), F32),
        pltpu.VMEM((2, 2, 104, VPAD), F32),
        pltpu.VMEM((2, 64, VPAD), F32),
        pltpu.VMEM((64, VPAD), BF),
        pltpu.VMEM((64, VPAD), BF),
        pltpu.VMEM((2, 2, 2, EPAD, 256), F32),
        pltpu.VMEM((2, 112, 256), BF),
        pltpu.VMEM((2, 112, 256), BF),
        pltpu.VMEM((112, 256), BF),
        pltpu.VMEM((112, 256), BF),
        pltpu.VMEM((64, VPAD), F32),
        pltpu.VMEM((3, 32, VPAD), F32),
        pltpu.VMEM((2, 32, VPAD), F32),
        pltpu.VMEM((3, 32, VPAD), F32),
        pltpu.VMEM((64, VPAD), F32),
        pltpu.VMEM((32, VPAD), F32),
        pltpu.VMEM((32, VPAD), F32),
        pltpu.VMEM((32, VPAD), F32),
    ]
    shapes = [
        (3,), (4,), (3, 2), (4, 2), (8, 2), (16, 2), (3,), (4,), (8,), (16,),
        (steps, 2, 3, 2), (n, 2), (steps, 2),
        (steps, 2, 2, 2), (steps, 2, 2), (3,), (4,), (11,), (14,), (9,), (4,),
    ]
    for shape in shapes:
        scratch += [dma(shape), dma(shape)]
    scratch += [dma((12,)), dma((steps, 2))]
    out_own, out_recv, out_in, out_dec, out_hid, out_small = pl.pallas_call(
        functools.partial(lstm_kernel, steps, rows),
        out_shape=(
            jax.ShapeDtypeStruct((8, own_rows, 256), F32),
            jax.ShapeDtypeStruct((3, 8, own_rows, 256), BF),
            jax.ShapeDtypeStruct((104, 256), F32),
            jax.ShapeDtypeStruct((own_rows, VPAD), F32),
            jax.ShapeDtypeStruct((micro * steps, count, width), BF),
            jax.ShapeDtypeStruct((EPAD, VPAD), F32),
        ),
        in_specs=[hbm] * 9,
        out_specs=(vm, hbm, vm, vm, hbm, vm),
        scratch_shapes=scratch,
        compiler_params=pltpu.CompilerParams(
            collective_id=0, has_side_effects=True, vmem_limit_bytes=66 * 1000 * 1000
        ),
    )(
        w_rec, w_in, bias_in, w_dec, embed, bias_dec,
        chars.transpose(2, 0, 1), resets.transpose(2, 0, 1), targets.transpose(2, 0, 1),
    )
    everyone = lax.axis_size(("dp", "fsdp"))
    hid, table, g_in, g_bias, g_rec, g_dec, g_bias_dec, loss = pl.pallas_call(
        functools.partial(output_kernel, float(micro * count * steps * everyone)),
        out_shape=(
            jax.ShapeDtypeStruct((micro * steps, count, width), BF),
            jax.ShapeDtypeStruct((vocab, emb), F32),
            jax.ShapeDtypeStruct((emb, 256), F32),
            jax.ShapeDtypeStruct((256,), F32),
            jax.ShapeDtypeStruct((own_rows, gate_cols), F32),
            jax.ShapeDtypeStruct((own_rows, vocab), F32),
            jax.ShapeDtypeStruct((vocab,), F32),
            jax.ShapeDtypeStruct((1, 1), F32),
        ),
        in_specs=[hbm] * 6,
        out_specs=(hbm,) * 8,
        scratch_shapes=[
            pltpu.VMEM((micro * steps, count, width), BF),
            pltpu.VMEM((8, own_rows, 256), F32),
            pltpu.VMEM((3, 8, own_rows, 256), BF),
            pltpu.VMEM((own_rows, gate_cols), F32),
            pltpu.VMEM((104, 256), F32),
            pltpu.VMEM((own_rows, VPAD), F32),
            pltpu.VMEM((EPAD, VPAD), F32),
            pltpu.VMEM((vocab, emb), F32),
            pltpu.VMEM((emb, 256), F32),
            pltpu.VMEM((256,), F32),
            pltpu.VMEM((own_rows, vocab), F32),
            pltpu.VMEM((vocab,), F32),
            pltpu.VMEM((1, 1), F32),
            dma((13,)),
            dma((8,)),
        ],
    )(out_own, out_recv, out_in, out_dec, out_hid, out_small)
    return (
        loss.reshape(()),
        hid.reshape(micro, steps, count, width).transpose(0, 2, 1, 3),
        table,
        g_in,
        g_bias,
        g_rec,
        g_dec,
        g_bias_dec,
    )


def dot_plain(left, right):
    return jnp.dot(left, right, preferred_element_type=jnp.float32)


def dot_right_t(left, right):
    return lax.dot_general(
        left, right, (((1,), (1,)), ((), ())), preferred_element_type=jnp.float32
    )


def dot_left_t(left, right):
    return lax.dot_general(
        left, right, (((0,), (0,)), ((), ())), preferred_element_type=jnp.float32
    )


def lstm_forward(weights, embed, bias_dec, ids, marks, goals):
    w_rec, w_dec, w_in, bias_in = weights
    count, steps = ids.shape
    width = w_rec.shape[0]
    letters = jnp.arange(embed.shape[0], dtype=jnp.int32)
    onehot = (ids.T.reshape(-1)[:, None] == letters[None, :]).astype(jnp.bfloat16)
    feature = dot_plain(onehot, embed).astype(jnp.bfloat16)
    drives = (dot_plain(feature, w_in) + bias_in.astype(jnp.float32)).reshape(steps, count, -1)
    keeps = (1 - marks.T).astype(jnp.float32)[:, :, None]

    def advance(state, slot):
        hidden_now, cell = state
        drive, keep_now = slot
        prev_hidden = hidden_now * keep_now.astype(jnp.bfloat16)
        prev_cell = cell * keep_now
        pre = drive + dot_plain(prev_hidden, w_rec)
        gin, gforget, gcand, gout = jnp.split(pre, 4, axis=1)
        cell_new = jax.nn.sigmoid(gforget) * prev_cell + jax.nn.sigmoid(gin) * jnp.tanh(gcand)
        hid_new = (jax.nn.sigmoid(gout) * jnp.tanh(cell_new)).astype(jnp.bfloat16)
        return ((hid_new, cell_new), (pre, prev_hidden, prev_cell, cell_new, hid_new))

    start = (jnp.zeros((count, width), jnp.bfloat16), jnp.zeros((count, width), jnp.float32))
    state, saved = lax.scan(advance, start, (drives, keeps))
    pres, prev_hiddens, prev_cells, cells, hiddens = saved
    flat_hidden = hiddens.reshape(steps * count, width)
    logits = dot_plain(flat_hidden, w_dec) + bias_dec.astype(jnp.float32)
    top = jnp.max(logits, axis=1, keepdims=True)
    shifted = jnp.exp(logits - top)
    summed = jnp.sum(shifted, axis=1, keepdims=True)
    goal_hot = (goals.T.reshape(-1)[:, None] == letters[None, :]).astype(jnp.float32)
    loss_part = jnp.sum(top[:, 0] + jnp.log(summed[:, 0])) - jnp.sum(goal_hot * logits)
    d_logits = (shifted / summed - goal_hot).astype(jnp.bfloat16)
    kept = (pres, prev_hiddens, prev_cells, cells, keeps, flat_hidden, d_logits, feature, onehot)
    return (kept, loss_part, jnp.transpose(hiddens, (1, 0, 2)))


def lstm_backward(weights, kept):
    w_rec, w_dec, w_in, bias_in = weights
    pres, prev_hiddens, prev_cells, cells, keeps, flat_hidden, d_logits, feature, onehot = kept
    steps, count, width = cells.shape
    from_dec = dot_right_t(d_logits, w_dec).reshape(steps, count, width)

    def retreat(carry, slot):
        grad_h, grad_c = carry
        pre, prev_cell, cell, extra, keep_now = slot
        gin, gforget, gcand, gout = jnp.split(pre, 4, axis=1)
        sig_in = jax.nn.sigmoid(gin)
        sig_forget = jax.nn.sigmoid(gforget)
        sig_out = jax.nn.sigmoid(gout)
        tan_cand = jnp.tanh(gcand)
        tan_cell = jnp.tanh(cell)
        grad_hid = extra + grad_h
        grad_out = grad_hid * tan_cell
        grad_cell = grad_c + grad_hid * sig_out * (1.0 - tan_cell * tan_cell)
        d_pre = jnp.concatenate(
            [
                grad_cell * tan_cand * sig_in * (1.0 - sig_in),
                grad_cell * prev_cell * sig_forget * (1.0 - sig_forget),
                grad_cell * sig_in * (1.0 - tan_cand * tan_cand),
                grad_out * sig_out * (1.0 - sig_out),
            ],
            axis=1,
        ).astype(jnp.bfloat16)
        back_h = dot_right_t(d_pre, w_rec) * keep_now
        back_c = grad_cell * sig_forget * keep_now
        return ((back_h, back_c), d_pre)

    start = (jnp.zeros((count, width), jnp.float32), jnp.zeros((count, width), jnp.float32))
    state, d_pres = lax.scan(
        retreat, start, (pres, prev_cells, cells, from_dec, keeps), reverse=True
    )
    flat_pre = d_pres.reshape(steps * count, -1)
    grad_dec = dot_left_t(flat_hidden, d_logits)
    grad_in = dot_left_t(feature, flat_pre)
    grad_bias = jnp.sum(flat_pre.astype(jnp.float32), axis=0)
    grad_feature = dot_right_t(flat_pre, w_in)
    grad_table = lax.dot_general(
        onehot.astype(jnp.float32),
        grad_feature,
        (((0,), (0,)), ((), ())),
        precision=lax.Precision.HIGHEST,
        preferred_element_type=jnp.float32,
    )
    grad_bias_out = jnp.sum(d_logits.astype(jnp.float32), axis=0)
    flat_prev = prev_hiddens.reshape(steps * count, width)
    return (grad_dec, grad_in, grad_bias, grad_table, grad_bias_out, flat_prev, flat_pre)


def general(chars, resets, targets, embed, w_in, bias_in, w_rec, w_dec, bias_dec):
    micro, count, steps = chars.shape
    everyone = lax.axis_size(("dp", "fsdp"))
    sums = None
    prev_list = []
    pre_list = []
    hidden_list = []
    for index in range(micro):
        forward_set = (
            lax.all_gather(w_rec, ("dp", "fsdp"), axis=0, tiled=True),
            lax.all_gather(w_dec, ("dp", "fsdp"), axis=0, tiled=True),
            lax.all_gather(w_in, ("dp", "fsdp"), axis=1, tiled=True),
            lax.all_gather(bias_in, ("dp", "fsdp"), axis=0, tiled=True),
        )
        kept, loss_part, hiddens = lstm_forward(
            forward_set, embed, bias_dec, chars[index], resets[index], targets[index]
        )
        backward_set = (
            lax.all_gather(w_rec, ("dp", "fsdp"), axis=0, tiled=True),
            lax.all_gather(w_dec, ("dp", "fsdp"), axis=0, tiled=True),
            lax.all_gather(w_in, ("dp", "fsdp"), axis=1, tiled=True),
            lax.all_gather(bias_in, ("dp", "fsdp"), axis=0, tiled=True),
        )
        grad_dec, grad_in, grad_bias, grad_table, grad_bias_out, flat_prev, flat_pre = (
            lstm_backward(backward_set, kept)
        )
        pieces = (grad_dec, grad_in, grad_bias, grad_table, grad_bias_out, loss_part)
        if sums is None:
            sums = pieces
        else:
            sums = tuple((first + second for first, second in zip(sums, pieces)))
        prev_list.append(flat_prev)
        pre_list.append(flat_pre)
        hidden_list.append(hiddens)
    prev_all = jnp.concatenate(prev_list, axis=0)
    pre_all = jnp.concatenate(pre_list, axis=0)
    grad_w_rec = lax.psum_scatter(
        dot_left_t(prev_all, pre_all), ("dp", "fsdp"), scatter_dimension=0, tiled=True
    )
    grad_w_dec, grad_w_in, grad_bias_in = (
        lax.psum_scatter(sums[0], ("dp", "fsdp"), scatter_dimension=0, tiled=True),
        lax.psum_scatter(sums[1], ("dp", "fsdp"), scatter_dimension=1, tiled=True),
        lax.psum_scatter(sums[2], ("dp", "fsdp"), scatter_dimension=0, tiled=True),
    )
    grad_embed, grad_bias_dec, total = lax.psum((sums[3], sums[4], sums[5]), ("dp", "fsdp"))
    loss = total / (micro * count * steps * everyone)
    hidden = jnp.stack(hidden_list, axis=0)
    return (
        loss,
        hidden,
        grad_embed,
        grad_w_in,
        grad_bias_in,
        grad_w_rec,
        grad_w_dec,
        grad_bias_dec,
    )


def solution(mesh):
    per_device = fused if (mesh.shape["dp"], mesh.shape["fsdp"]) == (8, 4) else general
    return jax.shard_map(
        per_device,
        mesh=mesh,
        in_specs=(
            P(None, ("dp", "fsdp"), None),
            P(None, ("dp", "fsdp"), None),
            P(None, ("dp", "fsdp"), None),
            P(),
            P(None, ("dp", "fsdp")),
            P(("dp", "fsdp")),
            P(("dp", "fsdp"), None),
            P(("dp", "fsdp"), None),
            P(),
        ),
        out_specs=(
            P(),
            P(None, ("dp", "fsdp"), None, None),
            P(),
            P(None, ("dp", "fsdp")),
            P(("dp", "fsdp")),
            P(("dp", "fsdp"), None),
            P(("dp", "fsdp"), None),
            P(),
        ),
        check_vma=False,
    )
```

```python
import functools

import jax
import jax.numpy as jnp
from jax import lax
from jax.experimental import pallas as pl
from jax.experimental.pallas import tpu as pltpu
from jax.sharding import PartitionSpec as P

MESH = pl.DeviceIdType.MESH
NN = ((1,), (0,))
NT = ((1,), (1,))
TN = ((0,), (0,))
F32 = jnp.float32
BF = jnp.bfloat16

VPAD = 384
EPAD = 128
RING = 4
SMALL = 112


def mm(left, right, dims):
    return lax.dot_general(left, right, (dims, ((), ())), preferred_element_type=F32)


def sigmoid(v):
    return 0.5 * jnp.tanh(0.5 * v) + 0.5


def lstm_kernel(
    steps, rows,
    w_rec, w_in_hbm, b_in_hbm, w_dec_hbm, emb_hbm, bias_hbm, chars_hbm, resets_hbm, targets_hbm,
    out_own, out_recv, out_in, out_dec, out_hid, out_small,
    W, WIN, WDEC, IDS, H, HT, HTS, HSEND, A, C, D, DS, DRAW, DL,
    w_in_raw, b_in_raw, w_dec_raw, emb_raw, bias_raw, chars_in, resets_in, targets_in, load_sem, ids_in, w_in, emb_t, w_dec, bias_dec, PR, STG, CB, PEND, OWN, DCN, SY, RY, SM, RM, EMBT, LV, BD, GWD, GIS, GY, SGM, GM, DWI, SIY, IY, SIM, IM, RS1, RS2, RS3, RS4, RS5, PIECE, PAIR, TOTAL,
    s_ids, r_ids, s_win, r_win, s_wa, r_wa, s_wm, r_wm, s_wy, r_wy, s_ws, r_ws,
    s_da, r_da, s_dm, r_dm, s_dy, r_dy, s_ds, r_ds, s_h, r_h, s_ht, r_ht, s_d, r_d,
    s_ph, r_ph, s_cb, r_cb, s_gd, r_gd, s_gi, r_gi, s_sm, r_sm, s_ry, r_ry, s_rm, r_rm, s_ra, r_ra,
    l_sem, hid_sem,
):
    last = steps - 1
    dp, fs = lax.axis_index("dp"), lax.axis_index("fsdp")
    z, x, y, c = dp // 2, dp % 2, fs // 2, fs % 2
    zh = z // 2
    a = z + zh * (3 - 2 * z)

    def dev(zz, xx, yy, cc):
        return (zz * 2 + xx, yy * 2 + cc)

    def kx(k):
        return x + (k % 2) * (1 - 2 * x)

    def kz(k):
        return z + (k // 2) * (1 - 2 * (z % 2))

    def ka(k):
        return a + (k // 2) * (1 - 2 * a)

    def kdev(k):
        return dev(kz(k), kx(k), y, c)

    def member(k):
        return 2 * kx(k) + ka(k)

    def unit_block(k, j):
        return 2 * (ka(k) + j * (3 - 2 * ka(k))) + kx(k)

    def lanes(ub):
        return pl.ds(pl.multiple_of(256 * ub, 256), 256)

    def place(k, far, yy, cc):
        return 4 * (2 * k + zh + far * (1 - 2 * zh)) + 2 * yy + cc

    def span(k, j):
        return slice(256 * (2 * k + j), 256 * (2 * k + j + 1))

    mir, ydev, sib = dev(3 - z, x, y, c), dev(z, x, 1 - y, c), dev(z, x, y, 1 - c)
    side = x + y - 2 * x * y
    perm = dev(side + zh * (3 - 2 * side), c, x, z % 2)
    back = dev(2 * zh + c, y, a + y - 2 * a * y, x)
    stays = jnp.logical_and(perm[0] == dp, perm[1] == fs)
    moved = jnp.logical_not(stays)

    def rc(src, dst, ss, rs, to):
        return pltpu.make_async_remote_copy(
            src_ref=src, dst_ref=dst, send_sem=ss, recv_sem=rs, device_id=to, device_id_type=MESH
        )

    barrier = pltpu.get_barrier_semaphore()

    def greet(to):
        pl.semaphore_signal(barrier, inc=1, device_id=to, device_id_type=MESH)

    for k in (1, 2, 3):
        greet(kdev(k))
    for to in (mir, ydev, sib):
        greet(to)

    @pl.when(moved)
    def _():
        greet(perm)
        greet(back)

    pairs = (
        (w_in_hbm, w_in_raw), (b_in_hbm, b_in_raw), (w_dec_hbm, w_dec_raw), (emb_hbm, emb_raw), (bias_hbm, bias_raw),
        (chars_hbm, chars_in), (resets_hbm, resets_in), (targets_hbm, targets_in),
    )
    loads = [pltpu.make_async_copy(src, dst, load_sem.at[n]) for n, (src, dst) in enumerate(pairs)]
    for load in loads:
        load.start()
    for load in loads:
        load.wait()
    emb, vocab = emb_raw.shape[1], emb_raw.shape[0]
    w_in[...] = jnp.zeros_like(w_in)
    w_in[0:emb, :] = w_in_raw[...]
    tail = emb // 16 * 16
    part = w_in[tail : tail + 16, :].astype(F32)
    bias_row = b_in_raw[...].astype(F32).reshape(1, 256)
    part = jnp.where(lax.broadcasted_iota(jnp.int32, (16, 256), 0) == emb - tail, bias_row, part)
    w_in[tail : tail + 16, :] = part.astype(BF)
    for s in range(2):
        stack = jnp.concatenate(
            [v for ref in (chars_in, resets_in, targets_in) for v in (ref[:, s, :], jnp.zeros((8 - steps, 32), jnp.int32))],
            axis=0,
        ).astype(F32)
        wide_stack = jnp.concatenate([stack, jnp.zeros((24, 96), F32)], axis=1)
        ids_in[s] = wide_stack.T[:32, :].astype(jnp.int32)
    pl.semaphore_wait(barrier, 6 + 2 * moved.astype(jnp.int32))


    def d_slot(b):
        return WDEC.at[pl.ds(pl.multiple_of(64 * b, 64), 64), :]

    def w_cols(ub, g):
        return w_rec.at[:, lanes(8 * g + ub)]

    def w_part(j, g, b):
        return W.at[4 * j + g, pl.ds(pl.multiple_of(64 * b, 64), 64), :]

    def wa_start(k):
        for j in (0, 1):
            for g in range(4):
                rc(w_cols(unit_block(k, j), g), w_part(j, g, place(k, 0, y, c)), s_wa.at[k - 1, j], r_wa.at[k - 1, j], kdev(k)).start()

    def wa(k, j):
        b = place(k, 0, y, c)
        part = W.at[pl.ds(4 * j, 4), pl.ds(pl.multiple_of(64 * b, 64), 64), :]
        return rc(part, part, s_wa.at[k - 1, j], r_wa.at[k - 1, j], kdev(k))

    def ids_copy(k, mem):
        return rc(ids_in, IDS.at[:, mem], s_ids.at[k - 1], r_ids.at[k - 1], kdev(k))

    def own_w(j, g):
        return pltpu.make_async_copy(w_cols(unit_block(0, j), g), w_part(j, g, place(0, 0, y, c)), l_sem.at[4 * j + g])

    for j in (0, 1):
        for g in range(4):
            own_w(j, g).start()
    for k in (1, 2, 3):
        ids_copy(k, member(0)).start()

    def win_perm(jj, gy, gc):
        return rc(w_in, WIN.at[jj, gy, gc], s_win.at[0], r_win.at[0], perm)

    def win_local():
        return pltpu.make_async_copy(w_in, WIN.at[x, z // 2, z % 2], l_sem.at[8])

    @pl.when(moved)
    def _():
        win_perm(x, z // 2, z % 2).start()

    @pl.when(stays)
    def _():
        win_local().start()

    for k in (1, 2, 3):
        wa_start(k)

    def w_half(j, b):
        return W.at[pl.ds(4 * j, 4), pl.ds(pl.multiple_of(64 * b, 64), 64), :]

    def to_mir(k, j):
        b = place(k, 0, y, c)
        return rc(w_half(j, b), w_half(j, b), s_wm.at[k, j], r_wm.at[k, j], mir)

    def from_mir(k, j):
        b = place(k, 1, y, c)
        return rc(w_half(j, b), w_half(j, b), s_wm.at[k, j], r_wm.at[k, j], mir)

    def group_block(i, yy, cc):
        return place(i % 4, i // 4, yy, cc)

    def to_y(i, j):
        b = group_block(i, y, c)
        return rc(w_half(j, b), w_half(j, b), s_wy.at[i, j], r_wy.at[i, j], ydev)

    def from_y(i, j):
        b = group_block(i, 1 - y, c)
        return rc(w_half(j, b), w_half(j, b), s_wy.at[i, j], r_wy.at[i, j], ydev)

    def to_s(i, j):
        b = group_block(i % 8, y + (i // 8) * (1 - 2 * y), c)
        return rc(w_half(j, b), w_half(j, b), s_ws.at[i, j], r_ws.at[i, j], sib)

    def from_s(i, j):
        b = group_block(i % 8, y + (i // 8) * (1 - 2 * y), 1 - c)
        return rc(w_half(j, b), w_half(j, b), s_ws.at[i, j], r_ws.at[i, j], sib)

    for j in (0, 1):
        for g in range(4):
            own_w(j, g).wait()
    inner = a == 1

    @pl.when(inner)
    def _():
        for j in (0, 1):
            to_mir(0, j).start()

    for j in (0, 1):
        to_y(0, j).start()
        to_s(0, j).start()

    def win_mir(jj):
        return rc(WIN.at[y, jj, c], WIN.at[y, jj, c], s_win.at[1], r_win.at[1], mir)

    def win_y(yy):
        return rc(WIN.at[yy, :, c], WIN.at[yy, :, c], s_win.at[2], r_win.at[2], ydev)

    def win_s(cc):
        return rc(WIN.at[:, :, cc], WIN.at[:, :, cc], s_win.at[3], r_win.at[3], sib)

    @pl.when(moved)
    def _():
        win_perm(y, zh, c).wait_recv()

    @pl.when(stays)
    def _():
        win_local().wait()

    win_mir(zh).start()


    IDS[:, member(0)] = ids_in[...]

    def own_blocks(k):
        for j in (0, 1):
            wa(k, j).wait_recv()
            to_y(k, j).start()

            @pl.when(inner)
            def _(j=j):
                to_mir(k, j).start()

            to_s(k, j).start()

    own_blocks(1)
    own_blocks(2)
    own_blocks(3)

    def da(k):
        return rc(w_dec, d_slot(place(k, 0, y, c)), s_da.at[k - 1], r_da.at[k - 1], kdev(k))

    HSEND[0, 0 : VPAD // 128] = jnp.zeros((VPAD // 128, 128, rows), BF)
    for n in range(VPAD // 128):
        held = min(128, vocab - 128 * n)
        HSEND[0, n, 0:held, 0:emb] = emb_raw[128 * n : 128 * n + held, :]
    unit = jnp.where(
        lax.broadcasted_iota(jnp.int32, (EPAD, EPAD), 0) == lax.broadcasted_iota(jnp.int32, (EPAD, EPAD), 1), 1.0, 0.0
    ).astype(BF)
    turned = mm(unit, HSEND[0, 0 : VPAD // 128].reshape(VPAD, EPAD), NT)
    emb_t[...] = jnp.where(lax.broadcasted_iota(jnp.int32, (EPAD, VPAD), 0) == emb, 1.0, turned).astype(BF)
    w_dec[...] = jnp.zeros_like(w_dec)
    w_dec[:, :vocab] = w_dec_raw[...]
    bias_dec[...] = jnp.full_like(bias_dec, -1e30)
    bias_dec[0:1, :vocab] = bias_raw[...].astype(F32).reshape(1, vocab)
    for k in (1, 2, 3):
        da(k).start()
    own_dec = pltpu.make_async_copy(w_dec, d_slot(place(0, 0, y, c)), l_sem.at[9])
    own_dec.start()

    for k in (1, 2, 3):
        ids_copy(k, member(k)).wait_recv()
    lane = lax.broadcasted_iota(jnp.int32, (rows, 24), 1)
    wide = lax.broadcasted_iota(jnp.int32, (rows, VPAD), 1).astype(F32)

    def column(at, s):
        packed = IDS[s].reshape(rows, 24)
        return jnp.sum(jnp.where(lane == at, packed, 0).astype(F32), axis=1, keepdims=True)

    def keep_of(t, s):
        return 1.0 - column(8 + t, s)

    def letter(t, s):
        return jnp.where(column(t, s) == wide, 1.0, 0.0).astype(BF)

    EMBT[...] = jnp.zeros_like(EMBT)
    LV[...] = jnp.zeros_like(LV)
    BD[...] = jnp.zeros_like(BD)
    GWD[...] = jnp.zeros_like(GWD)
    DWI[...] = jnp.zeros_like(DWI)
    DCN[...] = jnp.zeros_like(DCN)
    OWN[...] = jnp.zeros_like(OWN)
    PR[0] = jnp.zeros(PR.shape[1:], BF)

    win_mir(1 - zh).wait_recv()

    win_y(y).start()
    def pass_y(i):
        for j in (0, 1):
            from_y(i, j).wait_recv()
            to_s(8 + i, j).start()

    def pass_mir(k):
        for j in (0, 1):
            from_mir(k, j).wait_recv()
            to_y(4 + k, j).start()
            to_s(4 + k, j).start()

    for i in range(3):
        pass_y(i)

    @pl.when(inner)
    def _():
        pass_mir(0)

    @pl.when(jnp.logical_not(inner))
    def _():
        for k in range(4):
            for j in (0, 1):
                to_mir(k, j).start()

    pass_y(3)
    win_y(1 - y).wait_recv()
    win_s(c).start()
    win_s(1 - c).wait_recv()

    def h_copy(t, s, k, j):
        src, dst = H.at[t % RING, s, :, span(0, j)], H.at[t % RING, s, :, span(k, j)]
        return rc(src, dst, s_h.at[t, s, k - 1, j], r_h.at[t, s, k - 1, j], kdev(k))

    def wait_h(t, s):
        for k in (1, 2, 3):
            for j in (0, 1):
                h_copy(t, s, k, j).wait_recv()

    def gates(t, s, first):
        keep = None if first else keep_of(t, s)
        feature = mm(letter(t, s), emb_t[...], NT).astype(BF)
        for j in (0, 1):
            pre = []
            for g in range(4):
                drive = mm(feature, WIN[j, g // 2, g % 2], NN)
                if not first:
                    drive = drive + keep * mm(H[(t - 1) % RING, s], W[4 * j + g], NN)
                pre.append(drive)
            s_i, s_f, t_g, s_o = sigmoid(pre[0]), sigmoid(pre[1]), jnp.tanh(pre[2]), sigmoid(pre[3])
            cell = s_i * t_g
            if not first:
                cell = s_f * (C[t - 1, s, j] * keep) + cell
            for g, v in enumerate((s_i, s_f, t_g, s_o)):
                A[t, s, 4 * j + g] = v
            C[t, s, j] = cell
            H[t % RING, s, :, span(0, j)] = (s_o * jnp.tanh(cell)).astype(BF)
            for k in (3, 1, 2):
                h_copy(t, s, k, j).start()

    @pl.loop(0, 2)
    def _(s):
        gates(0, s, True)

    @pl.when(jnp.logical_not(inner))
    def _():
        pass_mir(0)

    for k in (1, 2, 3):
        pass_mir(k)

    def dec_mir(k, far):
        b = place(k, far, y, c)
        return rc(d_slot(b), d_slot(b), s_dm.at[k], r_dm.at[k], mir)

    def dec_y(i, yy):
        b = group_block(i, yy, c)
        return rc(d_slot(b), d_slot(b), s_dy.at[i], r_dy.at[i], ydev)

    def dec_s(i, cc):
        b = group_block(i % 8, y + (i // 8) * (1 - 2 * y), cc)
        return rc(d_slot(b), d_slot(b), s_ds.at[i], r_ds.at[i], sib)

    own_dec.wait()
    dec_y(0, y).start()
    dec_s(0, c).start()
    for k in (1, 2, 3):
        da(k).wait_recv()
        dec_y(k, y).start()
        dec_s(k, c).start()

    for i in (4, 5, 6, 7):
        pass_y(i)

    @pl.loop(0, 16)
    def _(i):
        for j in (0, 1):
            from_s(i, j).wait_recv()

    def released(t, s):
        hid_copy(t, s).wait()
        for k in (1, 2, 3):
            for j in (0, 1):
                h_copy(t, s, k, j).wait_send()

    def forward(t, s):
        wait_h(t - 1, s)

        @pl.when(t >= RING - 1)
        def _():
            released(t - (RING - 1), s)

        gates(t, s, False)

    row = lax.broadcasted_iota(jnp.int32, (128, 256), 0)
    col = lax.broadcasted_iota(jnp.int32, (128, 256), 1)

    def select(cc):
        yy = y + (row // 64) * (1 - 2 * y)
        return jnp.where(col == 64 * (2 * yy + cc) + row % 64, 1.0, 0.0).astype(BF)

    def lane_slot(t, s):
        return pl.ds(pl.multiple_of((2 * t + s) * rows, rows), rows)

    def ht_copy(t, s, slot):
        return rc(HSEND.at[slot], HTS.at[:, :, lane_slot(t, s)], s_ht.at[t, s], r_ht.at[t, s], sib)

    def hid_copy(t, s):
        mine = H.at[t % RING, s, pl.ds(pl.multiple_of(32 * member(0), 32), 32), :]
        return pltpu.make_async_copy(mine, out_hid.at[s * steps + t], hid_sem.at[t, s])

    def logits_of(t, s):
        scores = mm(H[t % RING, s], WDEC[...], NN) + bias_dec[0:1, :]
        top = jnp.max(scores, axis=1, keepdims=True)
        shifted = jnp.exp(scores - top)
        summed = jnp.sum(shifted, axis=1, keepdims=True)
        goal = jnp.where(column(16 + t, s) == wide, 1.0, 0.0)
        picked = jnp.sum(goal * scores, axis=1, keepdims=True)
        LV[...] += jnp.broadcast_to(top + jnp.log(summed) - picked, (rows, 128))
        DL[t, s] = (shifted / summed - goal).astype(BF)

    def decoder_side(t, s):
        hid_copy(t, s).start()
        grad = DL[t, s]
        BD[...] += mm(jnp.ones((8, rows), BF), grad, NN)
        for j in (0, 1):
            GWD[j] += mm(H[t % RING, s, :, span(0, j)], grad, TN).reshape(2, 2, 64, VPAD)

    def transposed_side(t, s):
        slot = s
        mine, other = select(c), select(1 - c)

        @pl.when(t >= 1)
        def _():
            ht_copy(t - 1, s, slot).wait_send()

        for tile in range(8):
            part = H[t % RING, s, :, 256 * tile : 256 * (tile + 1)]
            HT[tile, :, lane_slot(t, s)] = mm(mine, part, NT).astype(BF)
            HSEND[slot, tile] = mm(other, part, NT).astype(BF)
        ht_copy(t, s, slot).start()

    def decoder_mirror():
        @pl.loop(0, 4)
        def _(k):
            dec_mir(k, 1).wait_recv()
            dec_y(4 + k, y).start()
            dec_s(4 + k, c).start()

    def decoder_rest():
        @pl.loop(0, 8)
        def _(i):
            k, j = i // 2, i % 2
            to_mir(k, j).wait_send()
            to_y(i, 0).wait_send()
            to_y(i, 1).wait_send()

        @pl.loop(0, 16)
        def _(i):
            to_s(i, 0).wait_send()
            to_s(i, 1).wait_send()

        @pl.loop(0, 8)
        def _(i):
            dec_y(i, 1 - y).wait_recv()
            dec_s(8 + i, c).start()

        @pl.loop(0, 16)
        def _(i):
            dec_s(i, 1 - c).wait_recv()

    def aside(t, s):
        logits_of(t, s)
        decoder_side(t, s)
        transposed_side(t, s)

    @pl.loop(2, 2 * steps)
    def _(i):
        t, s = i // 2, i % 2
        forward(t, s)

        @pl.when(i == 2)
        def _():
            @pl.loop(0, 4)
            def _(k):
                dec_mir(k, 0).start()

        @pl.when(i == 4)
        def _():
            decoder_mirror()

        @pl.when(i == 5)
        def _():
            decoder_rest()

        @pl.when(i >= 5)
        def _():
            @pl.loop(i - 4 - (13 - i) // 8, i - 3)
            def _(n):
                aside(n // 2, n % 2)


    def d_copy(t, s):
        return rc(D.at[:, t - 1, s], DS.at[:, t - 1, s], s_d.at[t, s], r_d.at[t, s], sib)

    def turn():
        def rows_of(q):
            return slice(256 * q, 256 * (q + 1))

        def swap(p, q):
            upper, lower = W[p, rows_of(q), :].T, W[q, rows_of(p), :].T
            W[p, rows_of(q), :] = lower
            W[q, rows_of(p), :] = upper

        for p in range(8):
            W[p, rows_of(p), :] = W[p, rows_of(p), :].T
            for q in range(p):
                swap(p, q)

    def cell_back(t, s, oldest):
        keep = keep_of(t, s)
        for j in (0, 1):
            up = WDEC[span(0, j), :]
            dh = mm(DL[t, s], up, NT)
            rest = PR[(t + 1) % 2, s, 0, j].astype(F32) + PR[(t + 1) % 2, s, 1, j].astype(F32)
            dh = dh + (OWN[s, j] + rest)
            s_i, s_f, t_g, s_o = (A[t, s, 4 * j + g] for g in range(4))
            t_c = jnp.tanh(C[t, s, j])
            d_o = dh * t_c
            d_c = dh * s_o * (1.0 - t_c * t_c) + DCN[s, j]
            d_i = d_c * t_g * s_i * (1.0 - s_i)
            d_g = d_c * s_i * (1.0 - t_g * t_g)
            d_o = d_o * s_o * (1.0 - s_o)
            if oldest:
                d_f = jnp.zeros_like(d_i)
            else:
                d_f = d_c * (C[t - 1, s, j] * keep) * s_f * (1.0 - s_f)
                DCN[s, j] = keep * (d_c * s_f)
            for g, v in enumerate((d_i, d_f, d_g, d_o)):
                low = v.astype(BF)
                DRAW[4 * j + g] = low
                if not oldest:
                    D[4 * j + g, t - 1, s] = low * keep.astype(BF)

    def part_rows(h):
        return slice(64 * h, 64 * (h + 1))

    def pr_half(t, s, k, h):
        src, dst = STG.at[s, k - 1, :, part_rows(h)], PR.at[t % 2, s, k - 1, :, part_rows(h)]
        return rc(src, dst, s_ph.at[t, s, k - 1, h], r_ph.at[t, s, k - 1, h], kdev(k))

    def owed_copy(t, s, n):
        return rc(STG.at[s, 2, :, part_rows(n)], CB.at[s, n], s_cb.at[t, s, n], r_cb.at[t, s, n], kdev(1 + n))

    def pr_each(act):
        for k in (1, 2):
            for h in (0, 1):
                act(k, h)

    def pr_arrived(t, s):
        pr_each(lambda k, h: pr_half(t, s, k, h).wait_recv())

    def pr_left(t, s):
        pr_each(lambda k, h: pr_half(t, s, k, h).wait_send())
        for n in (0, 1):
            owed_copy(t, s, n).wait_send()

    def product_back(t, s):
        left = jnp.concatenate([D[q, t - 1, s] for q in range(8)], axis=1)
        for k, j in ((3, 0), (3, 1), (1, 0), (1, 1), (2, 0), (2, 1), (0, 0), (0, 1)):
            total = mm(left, W[2 * k + j], NN)
            if k == 0:
                OWN[s, j] = total
                continue
            STG[s, k - 1, j] = total.astype(BF)
            if k < 3:
                PEND[k - 1, j] = total[part_rows(2 - k)]
            elif j == 1:
                owed_copy(t, s, 0).start()
                owed_copy(t, s, 1).start()
        for k in (1, 2):
            pr_half(t, s, k, k - 1).start()

    def add_owed(t, s):
        for k in (2, 1):
            h = 2 - k
            owed_copy(t, s, h).wait_recv()
            STG[s, k - 1, :, part_rows(h)] = (PEND[k - 1] + CB[s, h].astype(F32)).astype(BF)
            pr_half(t, s, k, h).start()

    def input_side(t, s):
        onehot = letter(t, s)
        feat_t = mm(emb_t[...], onehot, NT).astype(BF)
        inputs = []
        for q in range(8):
            jj, gy, gc = q // 4, (q // 2) % 2, q % 2
            DWI[jj, gy, gc] += mm(feat_t, DRAW[q], NN)
            inputs.append(WIN[jj, gy, gc])
        grad_t = mm(jnp.concatenate(inputs, axis=1), jnp.concatenate([DRAW[q] for q in range(8)], axis=1), NT)
        high = grad_t.astype(BF)
        low = (grad_t - high.astype(F32)).astype(BF)
        EMBT[...] += mm(high, onehot, NN) + mm(low, onehot, NN)

    def gd_s():
        return rc(GWD.at[:, :, 1 - c], GIS.at[:, :, 0:64], s_gd.at[0], r_gd.at[0], sib)

    def gd_y():
        return rc(GWD.at[:, 1 - y, c], GY, s_gd.at[1], r_gd.at[1], ydev)

    def gd_m():
        return rc(SGM, GM, s_gd.at[2], r_gd.at[2], mir)

    turn()

    @pl.loop(0, 2 * (steps - 1))
    def _(i):
        t, s = last - i // 2, i % 2

        @pl.when(i < 2)
        def _():
            wait_h(t, s)
            logits_of(last, s)

        @pl.when(i >= 2)
        def _():
            pr_arrived(t + 1, s)

        cell_back(t, s, False)

        @pl.when(i >= 1)
        def _():
            add_owed(t + 1 - s, 1 - s)

        @pl.when(i >= 2)
        def _():
            pr_left(t + 1, s)

        product_back(t, s)
        d_copy(t, s).start()

        @pl.when(i < 2 * (steps - 1) - 1)
        def _():
            input_side(t, s)

        @pl.when(i < 2)
        def _():
            logits_of(last - 1, s)

        @pl.when(jnp.logical_and(i >= 2, i < 4))
        def _():
            decoder_side(last - 1, s)
            transposed_side(last - 1, s)

        @pl.when(i == 4)
        def _():
            @pl.loop(0, 2)
            def _(n):
                decoder_side(last, n)

            gd_s().start()

        @pl.when(i == 5)
        def _():
            gd_s().wait_recv()
            GWD[:, :, c] += GIS[:, :, 0:64]
            gd_y().start()

        @pl.when(i == 7)
        def _():
            gd_y().wait_recv()
            GWD[:, y, c] += GY[...]
            SGM[...] = GWD[1 - zh, y, c].astype(BF)
            gd_m().start()

        @pl.when(i == 9)
        def _():
            gd_m().wait_recv()
            out_dec[...] = GWD[zh, y, c] + GM[...].astype(F32)

    @pl.loop(0, 2 * (steps - 1))
    def _(i):
        ht_copy(i // 2, i % 2, 0).wait_recv()
        d_copy(1 + i // 2, i % 2).wait_recv()

    depth = 2 * (steps - 1) * rows

    def kept(q):
        return A.at[2 + q // 4, (q % 4) // 2, :, pl.ds(pl.multiple_of(64 * (q % 2), 64), 64), :]

    def tile_of(q):
        k, near = q % 4, q // 4
        return 2 * k + 1 - zh + near * (2 * zh - 1)

    def ry_copy(p, q):
        return rc(SY.at[p % 4], RY.at[q], s_ry.at[p], r_ry.at[q], ydev)

    def pieces(k):
        return (1, 2, 2, 4)[k]

    def piece(k, n):
        size = 8 // pieces(k)
        return slice(size * n, size * (n + 1))

    def rm_copy(k, n):
        at = (0, 1, 3, 5)[k] + n
        return rc(SM.at[k, piece(k, n)], RM.at[k, piece(k, n)], s_rm.at[at], r_rm.at[at], mir)

    def ry_first(n):
        return rc(SY.at[0, piece(3, n)], RY.at[3, piece(3, n)], s_ry.at[8 + n], r_ry.at[8 + n], ydev)

    def ry_second(n):
        return rc(SY.at[1, piece(2, n)], RY.at[2, piece(2, n)], s_ry.at[12 + n], r_ry.at[12 + n], ydev)

    def ry_sent(p):
        @pl.when(p == 0)
        def _():
            for n in range(4):
                ry_first(n).wait_send()

        @pl.when(p == 1)
        def _():
            for n in range(2):
                ry_second(n).wait_send()

        @pl.when(p > 1)
        def _():
            ry_copy(p, order(p)).wait_send()

    def ra_copy(k, n):
        at = (0, 0, 2, 3)[k] + n
        rows_of_q = piece(k, n) if k == 1 else slice(0, 8)
        return rc(SM.at[k, rows_of_q], out_recv.at[k - 1, rows_of_q], s_ra.at[at], r_ra.at[at], kdev(k))

    def ra_pieces(k):
        return 2 if k == 1 else 1

    def order(p):
        return 3 - p + 8 * (p // 4)

    def make_tile(p):
        q = order(p)
        tile = tile_of(q)
        left, right = HT[tile], HTS[tile]
        hold = kept(q)

        @pl.when(p >= 4)
        def _():
            ry_sent(p - 4)

        for n in range(8):
            grad = mm(left, D[n].reshape(depth, 256), NN) + mm(right, DS[n].reshape(depth, 256), NN)
            hold[n] = grad[:64]
            SY[p % 4, n] = grad[64:].astype(BF)
            if n % 2 == 1:
                @pl.when(p == 0)
                def _(n=n):
                    ry_first(n // 2).start()

            if n % 4 == 3:
                @pl.when(p == 1)
                def _(n=n):
                    ry_second(n // 4).start()

        @pl.when(p > 1)
        def _():
            ry_copy(p, q).start()

    def add_y(q):
        ry_copy(0, q).wait_recv()
        hold = kept(q)
        hold[...] = hold[...] + RY[q].astype(F32)

    def pass_first(n):
        ry_first(n).wait_recv()
        SM[3, piece(3, n)] = (kept(3)[piece(3, n)] + RY[3, piece(3, n)].astype(F32)).astype(BF)
        rm_copy(3, n).start()

    def pass_on(k):
        if k == 3:
            for n in range(4):
                pass_first(n)
            return
        if k == 2:
            for n in range(2):
                ry_second(n).wait_recv()
                SM[2, piece(2, n)] = (kept(2)[piece(2, n)] + RY[2, piece(2, n)].astype(F32)).astype(BF)
                rm_copy(2, n).start()
            return
        add_y(k)
        for n in range(pieces(k)):
            SM[k, piece(k, n)] = kept(k)[piece(k, n)].astype(BF)
            rm_copy(k, n).start()

    def finish(k):
        add_y(4 + k)
        if k != 1:
            for n in range(pieces(k)):
                rm_copy(k, n).wait_recv()
        if k == 0:
            out_own[...] = kept(4)[...] + RM[0].astype(F32)
            return
        for n in range(ra_pieces(k)):
            part = piece(1, n) if k == 1 else slice(0, 8)
            if k == 1:
                rm_copy(k, n).wait_recv()
                rm_copy(k, n).wait_send()
            else:
                for m in range(pieces(k)):
                    rm_copy(k, m).wait_send()
            SM[k, part] = (kept(4 + k)[part] + RM[k, part].astype(F32)).astype(BF)
            ra_copy(k, n).start()

    def settle(p):
        q = order(p)
        pass_on(q) if q < 4 else finish(q - 4)

    outer = jnp.logical_not(inner)

    def core_rows(cc):
        return pl.ds(pl.multiple_of(64 * cc, 64), 64)

    def piece_rows(xx):
        return pl.ds(pl.multiple_of(64 * c + 32 * xx, 32), 32)

    def sm_core():
        return rc(out_small.at[core_rows(1 - c)], RS1, s_sm.at[0], r_sm.at[0], sib)

    def sm_group(k):
        xx = kx(k)
        return rc(out_small.at[piece_rows(xx)], RS2.at[k - 1], s_sm.at[k], r_sm.at[k], kdev(k))

    def sm_quarter(n):
        return rc(PIECE if n == 0 else PAIR, RS3.at[n], s_sm.at[4 + n], r_sm.at[4 + n], (ydev, mir)[n])

    def sm_spread(k):
        return rc(TOTAL, RS4.at[k - 1], s_sm.at[6 + k], r_sm.at[6 + k], kdev(k))

    def sm_last():
        return rc(out_small.at[core_rows(c)], RS5, s_sm.at[10], r_sm.at[10], sib)

    def sm_step1():
        sm_core().wait_recv()
        out_small[core_rows(c)] = out_small[core_rows(c)] + RS1[...]

        @pl.when(outer)
        def _():
            sm_group(1).start()

        @pl.when(inner)
        def _():
            sm_group(2).start()
            sm_group(3).start()

    def sm_step2():
        @pl.when(outer)
        def _():
            for k in (1, 2, 3):
                sm_group(k).wait_recv()
            PIECE[...] = (out_small[piece_rows(x)] + RS2[0]) + (RS2[1] + RS2[2])
            sm_quarter(0).start()

    def sm_step_mir():
        @pl.when(outer)
        def _():
            sm_quarter(0).wait_recv()
            PAIR[...] = PIECE[...] + RS3[0]
            sm_quarter(1).start()

    def sm_step3():
        @pl.when(outer)
        def _():
            sm_quarter(1).wait_recv()
            TOTAL[...] = PAIR[...] + RS3[1]
            for k in (1, 2, 3):
                sm_spread(k).start()

    def sm_step4():
        sm_core().wait_send()

        @pl.when(outer)
        def _():
            sm_group(1).wait_send()
            sm_spread(1).wait_recv()
            out_small[piece_rows(1 - x)] = RS4[0]
            out_small[piece_rows(x)] = TOTAL[...]

        @pl.when(inner)
        def _():
            for k in (2, 3):
                sm_group(k).wait_send()
                sm_spread(k).wait_recv()
                out_small[piece_rows(kx(k))] = RS4[k - 1]

        sm_last().start()

    def sm_step5():
        sm_last().wait_recv()
        out_small[core_rows(1 - c)] = RS5[...]

    live = pl.ds(0, 104)

    def gi_s():
        return rc(DWI.at[:, :, 1 - c, live], GIS.at[:, :, :, 0:256], s_gi.at[0], r_gi.at[0], sib)

    def gi_y():
        return rc(SIY, IY, s_gi.at[1], r_gi.at[1], ydev)

    def gi_m():
        return rc(SIM, IM, s_gi.at[2], r_gi.at[2], mir)

    def gi_p():
        return rc(DWI.at[y, zh, c, live], out_in, s_gi.at[3], r_gi.at[3], back)

    def first_position():
        @pl.loop(0, 2)
        def _(s):
            pr_arrived(1, s)
            cell_back(0, s, True)
            input_side(0, s)

            @pl.when(jnp.logical_and(inner, s == 0))
            def _():
                pass_first(2)

        leader = jnp.logical_and(x == 0, a == 0)
        high_row = lax.broadcasted_iota(jnp.int32, (8, VPAD), 0)
        loss = jnp.sum(LV[...], axis=0, keepdims=True)
        loss = jnp.concatenate([loss] * (VPAD // 128), axis=1)
        extra = jnp.where(high_row == 0, BD[...], jnp.where(high_row == 1, loss, 0.0))
        out_small[...] = EMBT[...]
        out_small[SMALL - 8 : SMALL] = jnp.where(leader, extra, 0.0)
        sm_core().start()
        gi_s().start()

    @pl.loop(0, 8)
    def _(p):
        make_tile(p)

        @pl.when(p == 0)
        def _():
            add_owed(1, 1)

        @pl.when(p == 1)
        def _():
            @pl.when(inner)
            def _():
                pass_first(0)

            input_side(1, 1)

            @pl.when(inner)
            def _():
                pass_first(1)

            first_position()
            sm_step1()
            @pl.when(inner)
            def _():
                pass_first(3)
                settle(1)

            gi_s().wait_recv()
            DWI[:, :, c, 0:104] = DWI[:, :, c, 0:104] + GIS[:, :, :, 0:256]
            sm_step2()
            SIY[...] = DWI[1 - y, :, c, 0:112].astype(BF)
            gi_y().start()

            @pl.when(outer)
            def _():
                settle(0)

        @pl.when(p == 2)
        def _():
            @pl.when(outer)
            def _():
                settle(1)

            sm_step_mir()

        @pl.when(p == 3)
        def _():
            gi_y().wait_recv()
            DWI[y, :, c, 0:104] = DWI[y, :, c, 0:104] + IY[...].astype(F32)[:, 0:104]
            SIM[...] = DWI[y, 1 - zh, c, 0:112].astype(BF)
            gi_m().start()

        @pl.when(p == 4)
        def _():
            settle(2)
            sm_step3()

        @pl.when(p == 5)
        def _():
            settle(3)

    settle(4)
    settle(5)
    sm_step4()
    settle(6)
    gi_m().wait_recv()
    DWI[y, zh, c, 0:104] = DWI[y, zh, c, 0:104] + IM[...].astype(F32)[0:104]

    @pl.when(moved)
    def _():
        gi_p().start()

    @pl.when(stays)
    def _():
        out_in[...] = DWI[y, zh, c, 0:104]

    sm_step5()
    settle(7)

    for k in (1, 2, 3):
        for j in (0, 1):
            wa(k, j).wait_send()
        ids_copy(k, member(0)).wait_send()
        da(k).wait_send()
        for n in range(ra_pieces(k)):
            ra_copy(k, n).wait()
    rm_copy(0, 0).wait_send()

    @pl.when(moved)
    def _():
        gi_p().wait()
        win_perm(x, z // 2, z % 2).wait_send()

    for s in range(2):
        pr_left(1, s)
    win_mir(zh).wait_send()
    win_y(y).wait_send()
    win_s(c).wait_send()
    @pl.when(outer)
    def _():
        sm_quarter(0).wait_send()
        sm_quarter(1).wait_send()
        for k in (1, 2, 3):
            sm_spread(k).wait_send()

    for copy in (gd_s, gd_y, gd_m, gi_s, gi_y, gi_m, sm_last):
        copy().wait_send()
    for s in range(2):
        ht_copy(last - 1, s, s).wait_send()

    @pl.loop(0, 4)
    def _(k):
        dec_mir(k, 0).wait_send()

    @pl.loop(0, 8)
    def _(i):
        dec_y(i, y).wait_send()

    for p in range(4, 8):
        ry_copy(p, order(p)).wait_send()

    @pl.loop(0, 16)
    def _(i):
        dec_s(i, c).wait_send()

    @pl.loop(2 * (steps - RING + 1), 2 * steps)
    def _(i):
        released(i // 2, i % 2)

    @pl.loop(0, 2 * (steps - 1))
    def _(i):
        d_copy(1 + i // 2, i % 2).wait_send()


def output_kernel(
    characters, own, recv, g_in, g_dec, hid_in, small, hid, table, o_in, o_bias, o_rec, o_dec, o_bias_dec, loss,
    h_buf, own_buf, recv_buf, rec_buf, in_buf, dec_buf, small_buf, t_buf, i_buf, b_buf, d_buf, bd_buf, l_buf, in_sem, out_sem,
):
    dp = lax.axis_index("dp")
    z, x = dp // 2, dp % 2
    a = z + (z // 2) * (3 - 2 * z)

    def cols(k, j, g):
        xk, ak = x + (k % 2) * (1 - 2 * x), a + (k // 2) * (1 - 2 * a)
        ub = 2 * (ak + j * (3 - 2 * ak)) + xk
        return pl.ds(pl.multiple_of(256 * (8 * g + ub), 256), 256)

    def load(n, src, dst):
        copy = pltpu.make_async_copy(src, dst, in_sem.at[n])
        copy.start()
        return copy

    def store(n, src, dst):
        copy = pltpu.make_async_copy(src, dst, out_sem.at[n])
        copy.start()
        return copy

    hid_loads = [
        load(p, hid_in.at[:, :, 256 * p : 256 * (p + 1)], h_buf.at[:, :, cols(p // 2, p % 2, 0)]) for p in range(8)
    ]
    rec_loads = [load(8, own, own_buf), load(9, recv, recv_buf)]
    small_loads = [load(10, small, small_buf), load(11, g_in, in_buf), load(12, g_dec, dec_buf)]
    for copy in hid_loads:
        copy.wait()
    stores = [store(0, h_buf, hid)]
    for copy in rec_loads:
        copy.wait()
    for k in range(4):
        for j in (0, 1):
            for g in range(4):
                part = own_buf[4 * j + g] if k == 0 else recv_buf[k - 1, 4 * j + g].astype(F32)
                rec_buf[:, cols(k, j, g)] = part
    stores.append(store(1, rec_buf, o_rec))
    for copy in small_loads:
        copy.wait()
    vocab, emb = table.shape
    t_buf[...] = small_buf[0:SMALL, :].T[:vocab, :emb]
    i_buf[...] = in_buf[0:emb, :]
    b_buf[...] = in_buf[emb, :]
    d_buf[...] = dec_buf[:, :vocab]
    bd_buf[...] = small_buf[SMALL - 8, :vocab]
    l_buf[...] = small_buf[SMALL - 7 : SMALL - 6, 0:1] / characters
    pairs = ((t_buf, table), (i_buf, o_in), (b_buf, o_bias), (d_buf, o_dec), (bd_buf, o_bias_dec), (l_buf, loss))
    for n, (src, dst) in enumerate(pairs):
        stores.append(store(2 + n, src, dst))
    for copy in stores:
        copy.wait()


def fused(chars, resets, targets, embed, w_in, bias_in, w_rec, w_dec, bias_dec):
    micro, count, steps = chars.shape
    own_rows, gate_cols = w_rec.shape
    vocab, emb = embed.shape
    width = gate_cols // 4
    members = 4
    rows = count * members
    vm = pl.BlockSpec(memory_space=pltpu.VMEM)
    hbm = pl.BlockSpec(memory_space=pl.ANY)
    dma = pltpu.SemaphoreType.DMA
    n = steps - 1
    scratch = [
        pltpu.VMEM((8, width, 256), BF),
        pltpu.VMEM((2, 2, 2, EPAD, 256), BF),
        pltpu.VMEM((width, VPAD), BF),
        pltpu.VMEM((micro, members, count, 24), jnp.int32),
        pltpu.VMEM((RING, micro, rows, width), BF),
        pltpu.VMEM((8, 128, 2 * n * rows), BF),
        pltpu.VMEM((8, 128, 2 * n * rows), BF),
        pltpu.VMEM((2, 8, 128, rows), BF),
        pltpu.VMEM((steps, micro, 8, rows, 256), F32),
        pltpu.VMEM((steps, micro, 2, rows, 256), F32),
        pltpu.VMEM((8, n, micro, rows, 256), BF),
        pltpu.VMEM((8, n, micro, rows, 256), BF),
        pltpu.VMEM((8, rows, 256), BF),
        pltpu.VMEM((steps, micro, rows, VPAD), BF),
        pltpu.VMEM(w_in.shape, BF),
        pltpu.VMEM(bias_in.shape, BF),
        pltpu.VMEM(w_dec.shape, BF),
        pltpu.VMEM(embed.shape, BF),
        pltpu.VMEM(bias_dec.shape, BF),
        pltpu.VMEM((steps, micro, count), jnp.int32),
        pltpu.VMEM((steps, micro, count), jnp.int32),
        pltpu.VMEM((steps, micro, count), jnp.int32),
        dma((8,)),
        pltpu.VMEM((micro, count, 24), jnp.int32),
        pltpu.VMEM((EPAD, 256), BF),
        pltpu.VMEM((EPAD, VPAD), BF),
        pltpu.VMEM((own_rows, VPAD), BF),
        pltpu.VMEM((8, VPAD), F32),
        pltpu.VMEM((2, micro, 2, 2, rows, 256), BF),
        pltpu.VMEM((micro, 3, 2, rows, 256), BF),
        pltpu.VMEM((micro, 2, 2, rows // 2, 256), BF),
        pltpu.VMEM((2, 2, rows // 2, 256), F32),
        pltpu.VMEM((micro, 2, rows, 256), F32),
        pltpu.VMEM((micro, 2, rows, 256), F32),
        pltpu.VMEM((4, 8, 64, 256), BF),
        pltpu.VMEM((8, 8, 64, 256), BF),
        pltpu.VMEM((4, 8, 64, 256), BF),
        pltpu.VMEM((4, 8, 64, 256), BF),
        pltpu.VMEM((EPAD, VPAD), F32),
        pltpu.VMEM((rows, 128), F32),
        pltpu.VMEM((8, VPAD), F32),
        pltpu.VMEM((2, 2, 2, 64, VPAD), F32),
        pltpu.VMEM((2, 2, 104, VPAD), F32),
        pltpu.VMEM((2, 64, VPAD), F32),
        pltpu.VMEM((64, VPAD), BF),
        pltpu.VMEM((64, VPAD), BF),
        pltpu.VMEM((2, 2, 2, EPAD, 256), F32),
        pltpu.VMEM((2, 112, 256), BF),
        pltpu.VMEM((2, 112, 256), BF),
        pltpu.VMEM((112, 256), BF),
        pltpu.VMEM((112, 256), BF),
        pltpu.VMEM((64, VPAD), F32),
        pltpu.VMEM((3, 32, VPAD), F32),
        pltpu.VMEM((2, 32, VPAD), F32),
        pltpu.VMEM((3, 32, VPAD), F32),
        pltpu.VMEM((64, VPAD), F32),
        pltpu.VMEM((32, VPAD), F32),
        pltpu.VMEM((32, VPAD), F32),
        pltpu.VMEM((32, VPAD), F32),
    ]
    shapes = [
        (3,), (4,), (3, 2), (4, 2), (8, 2), (16, 2), (3,), (4,), (8,), (16,),
        (steps, 2, 3, 2), (n, 2), (steps, 2),
        (steps, 2, 2, 2), (steps, 2, 2), (3,), (4,), (11,), (14,), (9,), (4,),
    ]
    for shape in shapes:
        scratch += [dma(shape), dma(shape)]
    scratch += [dma((12,)), dma((steps, 2))]
    out_own, out_recv, out_in, out_dec, out_hid, out_small = pl.pallas_call(
        functools.partial(lstm_kernel, steps, rows),
        out_shape=(
            jax.ShapeDtypeStruct((8, own_rows, 256), F32),
            jax.ShapeDtypeStruct((3, 8, own_rows, 256), BF),
            jax.ShapeDtypeStruct((104, 256), F32),
            jax.ShapeDtypeStruct((own_rows, VPAD), F32),
            jax.ShapeDtypeStruct((micro * steps, count, width), BF),
            jax.ShapeDtypeStruct((EPAD, VPAD), F32),
        ),
        in_specs=[hbm] * 9,
        out_specs=(vm, hbm, vm, vm, hbm, vm),
        scratch_shapes=scratch,
        compiler_params=pltpu.CompilerParams(
            collective_id=0, has_side_effects=True, vmem_limit_bytes=66 * 1000 * 1000
        ),
    )(
        w_rec, w_in, bias_in, w_dec, embed, bias_dec,
        chars.transpose(2, 0, 1), resets.transpose(2, 0, 1), targets.transpose(2, 0, 1),
    )
    everyone = lax.axis_size(("dp", "fsdp"))
    hid, table, g_in, g_bias, g_rec, g_dec, g_bias_dec, loss = pl.pallas_call(
        functools.partial(output_kernel, float(micro * count * steps * everyone)),
        out_shape=(
            jax.ShapeDtypeStruct((micro * steps, count, width), BF),
            jax.ShapeDtypeStruct((vocab, emb), F32),
            jax.ShapeDtypeStruct((emb, 256), F32),
            jax.ShapeDtypeStruct((256,), F32),
            jax.ShapeDtypeStruct((own_rows, gate_cols), F32),
            jax.ShapeDtypeStruct((own_rows, vocab), F32),
            jax.ShapeDtypeStruct((vocab,), F32),
            jax.ShapeDtypeStruct((1, 1), F32),
        ),
        in_specs=[hbm] * 6,
        out_specs=(hbm,) * 8,
        scratch_shapes=[
            pltpu.VMEM((micro * steps, count, width), BF),
            pltpu.VMEM((8, own_rows, 256), F32),
            pltpu.VMEM((3, 8, own_rows, 256), BF),
            pltpu.VMEM((own_rows, gate_cols), F32),
            pltpu.VMEM((104, 256), F32),
            pltpu.VMEM((own_rows, VPAD), F32),
            pltpu.VMEM((EPAD, VPAD), F32),
            pltpu.VMEM((vocab, emb), F32),
            pltpu.VMEM((emb, 256), F32),
            pltpu.VMEM((256,), F32),
            pltpu.VMEM((own_rows, vocab), F32),
            pltpu.VMEM((vocab,), F32),
            pltpu.VMEM((1, 1), F32),
            dma((13,)),
            dma((8,)),
        ],
    )(out_own, out_recv, out_in, out_dec, out_hid, out_small)
    return (
        loss.reshape(()),
        hid.reshape(micro, steps, count, width).transpose(0, 2, 1, 3),
        table,
        g_in,
        g_bias,
        g_rec,
        g_dec,
        g_bias_dec,
    )


def dot_plain(left, right):
    return jnp.dot(left, right, preferred_element_type=jnp.float32)


def dot_right_t(left, right):
    return lax.dot_general(
        left, right, (((1,), (1,)), ((), ())), preferred_element_type=jnp.float32
    )


def dot_left_t(left, right):
    return lax.dot_general(
        left, right, (((0,), (0,)), ((), ())), preferred_element_type=jnp.float32
    )


def lstm_forward(weights, embed, bias_dec, ids, marks, goals):
    w_rec, w_dec, w_in, bias_in = weights
    count, steps = ids.shape
    width = w_rec.shape[0]
    letters = jnp.arange(embed.shape[0], dtype=jnp.int32)
    onehot = (ids.T.reshape(-1)[:, None] == letters[None, :]).astype(jnp.bfloat16)
    feature = dot_plain(onehot, embed).astype(jnp.bfloat16)
    drives = (dot_plain(feature, w_in) + bias_in.astype(jnp.float32)).reshape(steps, count, -1)
    keeps = (1 - marks.T).astype(jnp.float32)[:, :, None]

    def advance(state, slot):
        hidden_now, cell = state
        drive, keep_now = slot
        prev_hidden = hidden_now * keep_now.astype(jnp.bfloat16)
        prev_cell = cell * keep_now
        pre = drive + dot_plain(prev_hidden, w_rec)
        gin, gforget, gcand, gout = jnp.split(pre, 4, axis=1)
        cell_new = jax.nn.sigmoid(gforget) * prev_cell + jax.nn.sigmoid(gin) * jnp.tanh(gcand)
        hid_new = (jax.nn.sigmoid(gout) * jnp.tanh(cell_new)).astype(jnp.bfloat16)
        return ((hid_new, cell_new), (pre, prev_hidden, prev_cell, cell_new, hid_new))

    start = (jnp.zeros((count, width), jnp.bfloat16), jnp.zeros((count, width), jnp.float32))
    state, saved = lax.scan(advance, start, (drives, keeps))
    pres, prev_hiddens, prev_cells, cells, hiddens = saved
    flat_hidden = hiddens.reshape(steps * count, width)
    logits = dot_plain(flat_hidden, w_dec) + bias_dec.astype(jnp.float32)
    top = jnp.max(logits, axis=1, keepdims=True)
    shifted = jnp.exp(logits - top)
    summed = jnp.sum(shifted, axis=1, keepdims=True)
    goal_hot = (goals.T.reshape(-1)[:, None] == letters[None, :]).astype(jnp.float32)
    loss_part = jnp.sum(top[:, 0] + jnp.log(summed[:, 0])) - jnp.sum(goal_hot * logits)
    d_logits = (shifted / summed - goal_hot).astype(jnp.bfloat16)
    kept = (pres, prev_hiddens, prev_cells, cells, keeps, flat_hidden, d_logits, feature, onehot)
    return (kept, loss_part, jnp.transpose(hiddens, (1, 0, 2)))


def lstm_backward(weights, kept):
    w_rec, w_dec, w_in, bias_in = weights
    pres, prev_hiddens, prev_cells, cells, keeps, flat_hidden, d_logits, feature, onehot = kept
    steps, count, width = cells.shape
    from_dec = dot_right_t(d_logits, w_dec).reshape(steps, count, width)

    def retreat(carry, slot):
        grad_h, grad_c = carry
        pre, prev_cell, cell, extra, keep_now = slot
        gin, gforget, gcand, gout = jnp.split(pre, 4, axis=1)
        sig_in = jax.nn.sigmoid(gin)
        sig_forget = jax.nn.sigmoid(gforget)
        sig_out = jax.nn.sigmoid(gout)
        tan_cand = jnp.tanh(gcand)
        tan_cell = jnp.tanh(cell)
        grad_hid = extra + grad_h
        grad_out = grad_hid * tan_cell
        grad_cell = grad_c + grad_hid * sig_out * (1.0 - tan_cell * tan_cell)
        d_pre = jnp.concatenate(
            [
                grad_cell * tan_cand * sig_in * (1.0 - sig_in),
                grad_cell * prev_cell * sig_forget * (1.0 - sig_forget),
                grad_cell * sig_in * (1.0 - tan_cand * tan_cand),
                grad_out * sig_out * (1.0 - sig_out),
            ],
            axis=1,
        ).astype(jnp.bfloat16)
        back_h = dot_right_t(d_pre, w_rec) * keep_now
        back_c = grad_cell * sig_forget * keep_now
        return ((back_h, back_c), d_pre)

    start = (jnp.zeros((count, width), jnp.float32), jnp.zeros((count, width), jnp.float32))
    state, d_pres = lax.scan(
        retreat, start, (pres, prev_cells, cells, from_dec, keeps), reverse=True
    )
    flat_pre = d_pres.reshape(steps * count, -1)
    grad_dec = dot_left_t(flat_hidden, d_logits)
    grad_in = dot_left_t(feature, flat_pre)
    grad_bias = jnp.sum(flat_pre.astype(jnp.float32), axis=0)
    grad_feature = dot_right_t(flat_pre, w_in)
    grad_table = lax.dot_general(
        onehot.astype(jnp.float32),
        grad_feature,
        (((0,), (0,)), ((), ())),
        precision=lax.Precision.HIGHEST,
        preferred_element_type=jnp.float32,
    )
    grad_bias_out = jnp.sum(d_logits.astype(jnp.float32), axis=0)
    flat_prev = prev_hiddens.reshape(steps * count, width)
    return (grad_dec, grad_in, grad_bias, grad_table, grad_bias_out, flat_prev, flat_pre)


def general(chars, resets, targets, embed, w_in, bias_in, w_rec, w_dec, bias_dec):
    micro, count, steps = chars.shape
    everyone = lax.axis_size(("dp", "fsdp"))
    sums = None
    prev_list = []
    pre_list = []
    hidden_list = []
    for index in range(micro):
        forward_set = (
            lax.all_gather(w_rec, ("dp", "fsdp"), axis=0, tiled=True),
            lax.all_gather(w_dec, ("dp", "fsdp"), axis=0, tiled=True),
            lax.all_gather(w_in, ("dp", "fsdp"), axis=1, tiled=True),
            lax.all_gather(bias_in, ("dp", "fsdp"), axis=0, tiled=True),
        )
        kept, loss_part, hiddens = lstm_forward(
            forward_set, embed, bias_dec, chars[index], resets[index], targets[index]
        )
        backward_set = (
            lax.all_gather(w_rec, ("dp", "fsdp"), axis=0, tiled=True),
            lax.all_gather(w_dec, ("dp", "fsdp"), axis=0, tiled=True),
            lax.all_gather(w_in, ("dp", "fsdp"), axis=1, tiled=True),
            lax.all_gather(bias_in, ("dp", "fsdp"), axis=0, tiled=True),
        )
        grad_dec, grad_in, grad_bias, grad_table, grad_bias_out, flat_prev, flat_pre = (
            lstm_backward(backward_set, kept)
        )
        pieces = (grad_dec, grad_in, grad_bias, grad_table, grad_bias_out, loss_part)
        if sums is None:
            sums = pieces
        else:
            sums = tuple((first + second for first, second in zip(sums, pieces)))
        prev_list.append(flat_prev)
        pre_list.append(flat_pre)
        hidden_list.append(hiddens)
    prev_all = jnp.concatenate(prev_list, axis=0)
    pre_all = jnp.concatenate(pre_list, axis=0)
    grad_w_rec = lax.psum_scatter(
        dot_left_t(prev_all, pre_all), ("dp", "fsdp"), scatter_dimension=0, tiled=True
    )
    grad_w_dec, grad_w_in, grad_bias_in = (
        lax.psum_scatter(sums[0], ("dp", "fsdp"), scatter_dimension=0, tiled=True),
        lax.psum_scatter(sums[1], ("dp", "fsdp"), scatter_dimension=1, tiled=True),
        lax.psum_scatter(sums[2], ("dp", "fsdp"), scatter_dimension=0, tiled=True),
    )
    grad_embed, grad_bias_dec, total = lax.psum((sums[3], sums[4], sums[5]), ("dp", "fsdp"))
    loss = total / (micro * count * steps * everyone)
    hidden = jnp.stack(hidden_list, axis=0)
    return (
        loss,
        hidden,
        grad_embed,
        grad_w_in,
        grad_bias_in,
        grad_w_rec,
        grad_w_dec,
        grad_bias_dec,
    )


def solution(mesh):
    per_device = fused if (mesh.shape["dp"], mesh.shape["fsdp"]) == (8, 4) else general
    return jax.shard_map(
        per_device,
        mesh=mesh,
        in_specs=(
            P(None, ("dp", "fsdp"), None),
            P(None, ("dp", "fsdp"), None),
            P(None, ("dp", "fsdp"), None),
            P(),
            P(None, ("dp", "fsdp")),
            P(("dp", "fsdp")),
            P(("dp", "fsdp"), None),
            P(("dp", "fsdp"), None),
            P(),
        ),
        out_specs=(
            P(),
            P(None, ("dp", "fsdp"), None, None),
            P(),
            P(None, ("dp", "fsdp")),
            P(("dp", "fsdp")),
            P(("dp", "fsdp"), None),
            P(("dp", "fsdp"), None),
            P(),
        ),
        check_vma=False,
    )
```
